512 devices in a mesh: ref: 32 (over y_hi, x, core), dom: 16 (over z, y_lo).
Axes of the slice: x: 4, y: 8 (y_hi: 4, y_lo: 2; y = y_hi * 2 + y_lo), z: 8, core: 2. Of those that a mesh axis runs over, the one named last changes fastest.
Arguments:
- particles: bfloat16 [4096, 2, 2048], P(('ref', 'dom')), may hold values from -16 to 16
- classes: int32 [4096], P(('ref', 'dom')), may hold values from 0 to 15
- template_spectra: bfloat16 [192, 2, 2048], P('ref', None, 'dom'), may hold values from -0.796875 to 0.796875
- transfer_magnitude: float32 [16, 2048], replicated, may hold values from 0.1 to 1
- offsets: int32 [64, 2], replicated, may hold values from -4 to 4
Outputs:
- log_likelihood: float32 [4096], P(('ref', 'dom'))
- new_refs: float32 [192, 2, 2048], P('ref', None, 'dom')
The draws below stay inside these ranges and needn't reach their ends.
All inputs are finite; a program needn't handle non-finite values.
Results may differ from the reference program's by a relative error of at most 0.012.
Values may be sent and summed in bfloat16 or wider, within the bound.
No kernel may reach another device: no remote copies, remote signals or barrier semaphores. Data moves between devices by JAX's collectives and lax.ppermute only.
A program may use at most 64 MiB of HBM per device.

```python
import math
import jax
import jax.numpy as jnp
from jax import lax

BOX = 64
F = 2048
SHIFTS = 64
NCTF = 16
REFS = 192
P_DEV = 8
PARTICLES = 4096
N_REF = 32
N_DOM = 16


def shared_offsets(key):
    offset_key = jax.random.fold_in(key, 101)
    return jax.random.randint(offset_key, (SHIFTS, 2), -4, 5, dtype=jnp.int32)


def shared_references(key):
    ref_key = jax.random.fold_in(key, 102)
    key_scale = jax.random.fold_in(ref_key, 0)
    key_gauss = jax.random.fold_in(ref_key, 1)
    key_bright = jax.random.fold_in(ref_key, 3)
    faint = jnp.exp(jax.random.uniform(key_scale, (REFS, 1, 1), jnp.float32, math.log(0.05), math.log(0.12)))
    bright = jax.random.uniform(key_bright, (REFS, 1, 1), jnp.float32, 0.25, 0.35)
    strong_rows = (jnp.arange(REFS, dtype=jnp.int32) % 4 == 0)[:, None, None]
    scales = jnp.where(strong_rows, bright, faint)
    gauss = jax.random.normal(key_gauss, (REFS, 2, F), jnp.float32)
    return jnp.clip(gauss * scales, -0.796875, 0.796875)


def phase_from(offsets):
    half_side = BOX // 2
    positions = jnp.arange(F, dtype=jnp.int32)
    row_index = positions // half_side
    freq_x = jnp.where(row_index < half_side, row_index, row_index - BOX)
    freq_y = positions % half_side
    turn_count = (offsets[:, 0:1] * freq_x[None, :] + offsets[:, 1:2] * freq_y[None, :]) % BOX
    angles = turn_count.astype(jnp.float32) * (2.0 * math.pi / BOX)
    return (jnp.cos(angles), jnp.sin(angles))


def draw_offsets(key, part):
    return shared_offsets(key)


def draw_template_spectra(key, part):
    return shared_references(key).astype(jnp.bfloat16)


def drawn_rows(base_key, keys):
    references = shared_references(base_key)
    cos_table, sin_table = phase_from(shared_offsets(base_key))
    picked = 4 * jax.random.randint(keys[2], (PARTICLES,), 0, (REFS + 3) // 4, dtype=jnp.int32)
    first_shift = jax.random.randint(keys[3], (PARTICLES,), 0, SHIFTS, dtype=jnp.int32)
    second_shift = jax.random.randint(keys[4], (PARTICLES,), 0, SHIFTS, dtype=jnp.int32)
    strength = (6.0 + 14.0 * jax.random.uniform(keys[5], (PARTICLES, 1), jnp.float32)) * (128.0 / F)
    chosen = references[picked]

    def shifted(shift_index):
        cos_rows = cos_table[shift_index]
        sin_rows = sin_table[shift_index]
        real_part = chosen[:, 0] * cos_rows - chosen[:, 1] * sin_rows
        imag_part = chosen[:, 0] * sin_rows + chosen[:, 1] * cos_rows
        return jnp.stack([real_part * strength, imag_part * strength], axis=1)
    return shifted(first_shift) + shifted(second_shift)


def draw_particles(key, part):
    base_key = key
    key = jax.random.fold_in(key, 3)
    keys = jax.random.split(key, 7)
    marked = (jnp.arange(PARTICLES, dtype=jnp.int32) % 8 == 0)[:, None, None]
    noise_part = jax.random.normal(keys[1], (PARTICLES, 2, F), jnp.float32)
    aligned = drawn_rows(base_key, keys)
    values = jnp.where(marked, aligned + 0.3 * noise_part, noise_part)
    return jnp.clip(values, -16.0, 16.0).astype(jnp.bfloat16)


def touch_ends(array, stream_key, low, top_value):
    place = [jax.random.randint(jax.random.fold_in(stream_key, axis), (), 0, length) for axis, length in enumerate(array.shape)]
    widest = array.shape.index(max(array.shape))
    beside = place[:widest] + [(place[widest] + 1) % array.shape[widest]] + place[widest + 1:]
    return array.at[tuple(place)].set(low).at[tuple(beside)].set(top_value)


def setup_inputs(seed: int = 0) -> dict:
    splits = jax.random.split(jax.random.key(seed), 6)
    particles = draw_particles(jax.random.fold_in(splits[5], 71), 0)
    classes = touch_ends(jax.random.randint(splits[1], (PARTICLES,), 0, NCTF), jax.random.fold_in(splits[1], 1), 0, NCTF - 1).astype(jnp.int32)
    template_spectra = draw_template_spectra(jax.random.fold_in(splits[5], 71), 0)
    transfer_magnitude = jnp.clip(jax.random.uniform(splits[3], (NCTF, F), jnp.float32, 0.1, 1.0), 0.1, 1.0)
    offsets = draw_offsets(jax.random.fold_in(splits[5], 71), 0)
    return dict(particles=particles, classes=classes, template_spectra=template_spectra, transfer_magnitude=transfer_magnitude, offsets=offsets)


highest = lax.Precision.HIGHEST
ridge_term = 1.0


def phase_tables(offsets):
    half_side = BOX // 2
    positions = jnp.arange(F, dtype=jnp.int32)
    row_index = positions // half_side
    freq_x = jnp.where(row_index < half_side, row_index, row_index - BOX)
    freq_y = positions % half_side
    turn_count = (offsets[:, 0:1] * freq_x[None, :] + offsets[:, 1:2] * freq_y[None, :]) % BOX
    angles = turn_count.astype(jnp.float32) * (2.0 * math.pi / BOX)
    return jnp.cos(angles), jnp.sin(angles)


def make_templates(template_slab, cos_table, sin_table):
    template_entries = template_slab.astype(jnp.float32)
    real_part = template_entries[:, 0, None, :]
    imag_part = template_entries[:, 1, None, :]
    shifted_real = real_part * cos_table[None] - imag_part * sin_table[None]
    shifted_imag = real_part * sin_table[None] + imag_part * cos_table[None]
    stacked = jnp.stack([shifted_real, shifted_imag], axis=2).astype(jnp.bfloat16)
    return stacked.reshape(template_slab.shape[0] * cos_table.shape[0], 2 * cos_table.shape[1])


def log_weight_costs(template_slab, transfer_magnitude):
    template_entries = template_slab.astype(jnp.float32)
    power_sum = template_entries[:, 0] ** 2 + template_entries[:, 1] ** 2
    return 0.5 * jnp.dot(transfer_magnitude * transfer_magnitude, power_sum.T, precision=highest)


def fitness_slab(weighted, one_hot, templates, log_weight_cost):
    linear = lax.dot_general(weighted, templates, (((1,), (1,)), ((), ())), preferred_element_type=jnp.float32)
    chosen = jnp.dot(one_hot, log_weight_cost, precision=highest)
    row_count = weighted.shape[0]
    shaped = linear.reshape(row_count, log_weight_cost.shape[1], -1) - chosen[:, :, None]
    return shaped.reshape(row_count, -1)


def reference(particles, classes, template_spectra, transfer_magnitude, offsets):
    cos_table, sin_table = phase_tables(offsets)
    contrast_rows = transfer_magnitude[classes]
    weighted = (particles.astype(jnp.float32) * contrast_rows[:, None, :]).astype(jnp.bfloat16)
    weighted = weighted.reshape(PARTICLES, 2 * F)
    one_hot = (classes[:, None] == jnp.arange(NCTF, dtype=jnp.int32)[None, :]).astype(jnp.float32)
    templates = make_templates(template_spectra, cos_table, sin_table)
    log_weight_cost = log_weight_costs(template_spectra, transfer_magnitude)
    block_rows = P_DEV * N_REF
    weighted_blocks = weighted.reshape(N_DOM, block_rows, 2 * F)
    hot_blocks = one_hot.reshape(N_DOM, block_rows, NCTF)

    def visit_block(running, block_input):
        image_totals, occupancy = running
        block_weighted, block_hot = block_input
        scores = fitness_slab(block_weighted, block_hot, templates, log_weight_cost)
        top_score = jnp.max(scores, axis=1)
        log_norm = top_score + jnp.log(jnp.sum(jnp.exp(scores - top_score[:, None]), axis=1))
        posterior = jnp.exp(scores - log_norm[:, None]).astype(jnp.bfloat16)
        image_totals = image_totals + lax.dot_general(posterior, block_weighted, (((0,), (0,)), ((), ())), preferred_element_type=jnp.float32)
        weight_sums = jnp.sum(posterior.astype(jnp.float32).reshape(block_rows, REFS, SHIFTS), axis=2)
        occupancy = occupancy + jnp.dot(weight_sums.T, block_hot, precision=highest)
        return (image_totals, occupancy), log_norm

    start = (jnp.zeros((REFS * SHIFTS, 2 * F), jnp.float32), jnp.zeros((REFS, NCTF), jnp.float32))
    (image_totals, occupancy), log_blocks = lax.scan(visit_block, start, (weighted_blocks, hot_blocks))
    image_totals = image_totals.reshape(REFS, SHIFTS, 2, F)
    real_sum = jnp.sum(image_totals[:, :, 0] * cos_table[None] + image_totals[:, :, 1] * sin_table[None], axis=1)
    imag_sum = jnp.sum(image_totals[:, :, 1] * cos_table[None] - image_totals[:, :, 0] * sin_table[None], axis=1)
    denominator = jnp.dot(occupancy, transfer_magnitude * transfer_magnitude, precision=highest)
    new_refs = jnp.stack([real_sum, imag_sum], axis=1) / (denominator[:, None, :] + ridge_term)
    return log_blocks.reshape(PARTICLES), new_refs
```

```python
import math

import jax
import jax.numpy as jnp
import numpy as np
from jax import lax
from jax.sharding import Mesh
from jax.sharding import PartitionSpec as P

BOX = 64
F = 2048
SHIFTS = 64
NCTF = 16
LANES = 128

highest = lax.Precision.HIGHEST
ridge_term = 1.0


def phase_tables(offsets):
    half_side = BOX // 2
    positions = jnp.arange(F, dtype=jnp.int32)
    row_index = positions // half_side
    freq_x = jnp.where(row_index < half_side, row_index, row_index - BOX)
    freq_y = positions % half_side
    turn_count = (offsets[:, 0:1] * freq_x[None, :] + offsets[:, 1:2] * freq_y[None, :]) % BOX
    angles = turn_count.astype(jnp.float32) * (2.0 * math.pi / BOX)
    return (jnp.cos(angles), jnp.sin(angles))


def class_table(classes):
    return (classes[:, None] == jnp.arange(NCTF, dtype=jnp.int32)[None, :]).astype(jnp.float32)


def everyone(block, axis):
    count = lax.axis_size(axis)
    copies = jnp.broadcast_to(block[None], (count,) + block.shape)
    return lax.all_to_all(copies, axis, 0, 0)


def body(particles, classes, template_spectra, transfer_magnitude, offsets):
    rows = particles.shape[0]
    own_refs = template_spectra.shape[0]
    chunks = F // LANES
    contrast = jnp.dot(class_table(classes), transfer_magnitude, precision=highest)
    weighted = (particles.astype(jnp.float32) * contrast[:, None, :]).astype(jnp.bfloat16)
    weighted = weighted.reshape(rows, 2, chunks, LANES).swapaxes(1, 2).reshape(rows, 2 * F)
    tags = jnp.broadcast_to(classes.astype(jnp.bfloat16)[:, None], (rows, LANES))
    packet = jnp.concatenate([weighted, tags], axis=1)

    spectra = everyone(template_spectra.reshape(own_refs * 2, LANES), ("yh", "dom"))
    packets = everyone(packet, "xc")
    packets = packets.reshape(-1, 2 * F + LANES)
    weighted = packets[:, : 2 * F]
    hot = class_table(packets[:, 2 * F].astype(jnp.int32))
    count = weighted.shape[0]

    spectra = spectra.reshape(-1, chunks, own_refs, 2, LANES).astype(jnp.float32)
    spectra = spectra.transpose(0, 2, 1, 3, 4).reshape(-1, chunks, 2, LANES)
    refs = spectra.shape[0]
    cos_table, sin_table = phase_tables(offsets)
    cos_table = cos_table.reshape(1, SHIFTS, chunks, LANES)
    sin_table = sin_table.reshape(1, SHIFTS, chunks, LANES)
    real, imag = spectra[:, None, :, 0], spectra[:, None, :, 1]
    templates = jnp.stack(
        [real * cos_table - imag * sin_table, real * sin_table + imag * cos_table], axis=3
    ).astype(jnp.bfloat16)
    templates = templates.reshape(refs * SHIFTS, 2 * F)
    squared = transfer_magnitude * transfer_magnitude
    power = (spectra[:, :, 0] ** 2 + spectra[:, :, 1] ** 2).reshape(refs, F)
    penalty = 0.5 * jnp.dot(power, squared.T, precision=highest)

    scores = lax.dot_general(
        templates, weighted, (((1,), (1,)), ((), ())), preferred_element_type=jnp.float32
    )
    cost = jnp.dot(penalty, hot.T, precision=highest)
    scores = scores.reshape(refs, SHIFTS, count) - cost[:, None, :]
    top = jnp.max(scores, axis=(0, 1))
    total = jnp.sum(jnp.exp(scores - top), axis=(0, 1))
    stats = everyone(jnp.concatenate([top, total]), "xc")
    tops, sums = stats[:, :count], stats[:, count:]
    top_all = jnp.max(tops, axis=0)
    log_all = top_all + jnp.log(jnp.sum(sums * jnp.exp(tops - top_all), axis=0))
    posterior = jnp.exp(scores - log_all).astype(jnp.bfloat16)

    totals = lax.dot_general(
        posterior.reshape(refs * SHIFTS, count),
        weighted,
        (((1,), (0,)), ((), ())),
        preferred_element_type=jnp.float32,
    ).reshape(refs, SHIFTS, chunks, 2, LANES)
    t_real, t_imag = totals[:, :, :, 0], totals[:, :, :, 1]
    real_sum = jnp.sum(t_real * cos_table + t_imag * sin_table, axis=1)
    imag_sum = jnp.sum(t_imag * cos_table - t_real * sin_table, axis=1)
    occupancy = jnp.dot(jnp.sum(posterior.astype(jnp.float32), axis=1), hot, precision=highest)

    groups = refs // own_refs
    sums = jnp.stack([real_sum, imag_sum], axis=1).reshape(groups, own_refs * 2, chunks, LANES)
    sums = sums.transpose(0, 2, 1, 3).reshape(groups * chunks, own_refs * 2, LANES)
    shares = occupancy.reshape(groups, 1, 1, own_refs * NCTF)
    shares = jnp.pad(shares, ((0, 0), (0, 0), (0, 0), (0, LANES - own_refs * NCTF)))
    shares = jnp.broadcast_to(shares, (groups, chunks, 1, LANES)).reshape(-1, 1, LANES)
    parts = lax.all_to_all(jnp.concatenate([sums, shares], axis=1), ("yh", "dom"), 0, 0)
    parts = jnp.sum(parts, axis=0)
    aligned = parts[: own_refs * 2].reshape(own_refs, 2, LANES)
    occupancy = parts[own_refs * 2, : own_refs * NCTF].reshape(own_refs, NCTF)
    own = lax.dynamic_slice_in_dim(squared, lax.axis_index("dom") * LANES, LANES, 1)
    denominator = jnp.dot(occupancy, own, precision=highest)
    new_refs = aligned / (denominator[:, None, :] + ridge_term)
    log_own = lax.dynamic_slice_in_dim(log_all, lax.axis_index("xc") * rows, rows, 0)
    return (log_own, new_refs)


def solution(mesh):
    devices = mesh.devices
    inner = Mesh(devices.reshape(4, devices.shape[0] // 4, devices.shape[1]), ("yh", "xc", "dom"))
    whole = ("yh", "xc", "dom")
    refs = ("yh", "xc")
    return jax.shard_map(
        body,
        mesh=inner,
        in_specs=(P(whole, None, None), P(whole), P(refs, None, "dom"), P(), P()),
        out_specs=(P(whole), P(refs, None, "dom")),
        check_vma=False,
    )
```

```python
import functools
import math

import jax
import jax.numpy as jnp
from jax import lax
from jax.experimental import pallas as pl
from jax.experimental.pallas import tpu as pltpu
from jax.sharding import Mesh
from jax.sharding import PartitionSpec as P

BOX = 64
F = 2048
SHIFTS = 64
NCTF = 16
LANES = 128
CHUNKS = F // LANES
STEPS = 4
ROWS = 16

highest = lax.Precision.HIGHEST
ridge_term = 1.0
f32 = jnp.float32
bf16 = jnp.bfloat16
whole_vmem = pl.BlockSpec(memory_space=pltpu.VMEM)
vmem_bytes = 40 * 1024 * 1024


def phase_tables(offsets):
    half_side = BOX // 2
    positions = jnp.arange(F, dtype=jnp.int32)
    row_index = positions // half_side
    freq_x = jnp.where(row_index < half_side, row_index, row_index - BOX)
    freq_y = positions % half_side
    turn_count = (offsets[:, 0:1] * freq_x[None, :] + offsets[:, 1:2] * freq_y[None, :]) % BOX
    angles = turn_count.astype(f32) * (2.0 * math.pi / BOX)
    return (jnp.cos(angles), jnp.sin(angles))


def prep_kernel(classes_ref, particles_ref, transfer_ref, spectra_ref, packet_ref, copies_ref):
    rows = particles_ref.shape[0]
    own_refs = spectra_ref.shape[0]
    spectra = spectra_ref[...].reshape(own_refs * 2, LANES)
    spare = jnp.zeros((ROWS - own_refs * 2, LANES), bf16)
    spectra = jnp.concatenate([spectra, spare], axis=0)
    copies_ref[...] = jnp.broadcast_to(spectra[None], copies_ref.shape)
    place = lax.broadcasted_iota(jnp.int32, (rows, 1), 0)
    labels = jnp.zeros((rows, 1), jnp.int32)
    for i in range(rows):
        labels = jnp.where(place == i, classes_ref[i], labels)
    contrast = jnp.zeros((rows, F), f32)
    for c in range(NCTF):
        contrast = jnp.where(labels == c, transfer_ref[c : c + 1, :], contrast)
    values = particles_ref[...].astype(f32)
    real = (values[:, 0, :] * contrast).astype(bf16)
    imag = (values[:, 1, :] * contrast).astype(bf16)
    pieces = []
    for d in range(CHUNKS):
        pieces.append(real[:, d * LANES : (d + 1) * LANES])
        pieces.append(imag[:, d * LANES : (d + 1) * LANES])
    pieces.append(jnp.broadcast_to(labels.astype(f32), (rows, LANES)).astype(bf16))
    packet = jnp.concatenate(pieces, axis=1)
    packet_ref[...] = jnp.broadcast_to(packet[None], packet_ref.shape)


def prep(classes, particles, transfer, spectra, near, far):
    rows = particles.shape[0]
    return pl.pallas_call(
        prep_kernel,
        out_shape=(
            jax.ShapeDtypeStruct((near, rows, 2 * F + LANES), bf16),
            jax.ShapeDtypeStruct((far, ROWS, LANES), bf16),
        ),
        in_specs=[pl.BlockSpec(memory_space=pltpu.SMEM)] + [whole_vmem] * 3,
        out_specs=(whole_vmem, whole_vmem),
        name="prep",
    )(classes, particles, transfer, spectra)


def template_kernel(own_refs, spectra_ref, cos_ref, sin_ref, templates_ref, power_ref):
    groups = spectra_ref.shape[0]

    def chunk(j, carry):
        lanes = pl.ds(pl.multiple_of(j * LANES, LANES), LANES)
        real_lanes = pl.ds(pl.multiple_of(j * 2 * LANES, LANES), LANES)
        imag_lanes = pl.ds(pl.multiple_of(j * 2 * LANES + LANES, LANES), LANES)
        cos, sin = cos_ref[:, lanes], sin_ref[:, lanes]
        powers = []
        for g in range(groups):
            block = spectra_ref[g, j].astype(f32)
            for i in range(own_refs):
                real, imag = block[2 * i : 2 * i + 1], block[2 * i + 1 : 2 * i + 2]
                place = (g * own_refs + i) * SHIFTS
                templates_ref[place : place + SHIFTS, real_lanes] = (
                    real * cos - imag * sin
                ).astype(bf16)
                templates_ref[place : place + SHIFTS, imag_lanes] = (
                    real * sin + imag * cos
                ).astype(bf16)
                powers.append(real * real + imag * imag)
        power_ref[:, lanes] = jnp.concatenate(powers, axis=0)
        return carry

    lax.fori_loop(0, CHUNKS // STEPS, chunk, 0)


def make_templates(spectra, cos_table, sin_table, own_refs):
    groups = spectra.shape[0]
    refs = groups * own_refs
    part = CHUNKS // STEPS
    return pl.pallas_call(
        functools.partial(template_kernel, own_refs),
        grid=(STEPS,),
        out_shape=(
            jax.ShapeDtypeStruct((refs * SHIFTS, 2 * F), bf16),
            jax.ShapeDtypeStruct((refs, F), f32),
        ),
        in_specs=[
            pl.BlockSpec((groups, part, ROWS, LANES), lambda k: (0, k, 0, 0)),
            pl.BlockSpec((SHIFTS, part * LANES), lambda k: (0, k)),
            pl.BlockSpec((SHIFTS, part * LANES), lambda k: (0, k)),
        ],
        out_specs=(
            pl.BlockSpec((refs * SHIFTS, part * 2 * LANES), lambda k: (0, k)),
            pl.BlockSpec((refs, part * LANES), lambda k: (0, k)),
        ),
        compiler_params=pltpu.CompilerParams(vmem_limit_bytes=vmem_bytes),
        name="templates",
    )(spectra, cos_table, sin_table)


def label_table(tags):
    lane = lax.broadcasted_iota(jnp.int32, tags.shape, 1) % NCTF
    return (tags.astype(f32) == lane.astype(f32)).astype(f32)


def score_kernel(refs, templates_ref, weighted_ref, tags_ref, penalty_ref, scores_ref, stats_ref):
    step = pl.program_id(0)
    part = lax.dot_general(
        templates_ref[...],
        weighted_ref[...],
        (((1,), (1,)), ((), ())),
        preferred_element_type=f32,
    )

    @pl.when(step == 0)
    def _():
        hot = label_table(tags_ref[...])[:, :NCTF]
        cost = lax.dot_general(
            penalty_ref[...], hot, (((1,), (1,)), ((), ())), precision=highest
        )
        for r in range(refs):
            place = slice(r * SHIFTS, (r + 1) * SHIFTS)
            scores_ref[place, :] = part[place] - cost[r : r + 1]

    @pl.when(step > 0)
    def _():
        scores_ref[...] += part

    @pl.when(step == STEPS - 1)
    def _():
        scores = scores_ref[...]
        top = jnp.max(scores, axis=0, keepdims=True)
        total = jnp.sum(jnp.exp(scores - top), axis=0, keepdims=True)
        stats = jnp.concatenate([top, total], axis=0)
        stats_ref[...] = jnp.broadcast_to(stats[None], stats_ref.shape)


def make_scores(templates, packets, penalty, near):
    refs = penalty.shape[0]
    count = packets.shape[0]
    width = 2 * F // STEPS
    return pl.pallas_call(
        functools.partial(score_kernel, refs),
        grid=(STEPS,),
        out_shape=(
            jax.ShapeDtypeStruct((refs * SHIFTS, count), f32),
            jax.ShapeDtypeStruct((near, 2, count), f32),
        ),
        in_specs=[
            pl.BlockSpec((refs * SHIFTS, width), lambda k: (0, k)),
            pl.BlockSpec((count, width), lambda k: (0, k)),
            pl.BlockSpec((count, LANES), lambda k: (0, 2 * CHUNKS)),
            pl.BlockSpec((refs, NCTF), lambda k: (0, 0)),
        ],
        out_specs=(
            pl.BlockSpec((refs * SHIFTS, count), lambda k: (0, 0)),
            pl.BlockSpec((near, 2, count), lambda k: (0, 0, 0)),
        ),
        compiler_params=pltpu.CompilerParams(vmem_limit_bytes=vmem_bytes),
        name="scores",
    )(templates, packets, packets, penalty)


def back_kernel(
    own_refs, scores_ref, stats_ref, packets_ref, cos_ref, sin_ref, parts_ref, log_ref, posterior_ref
):
    groups = parts_ref.shape[0]
    refs = groups * own_refs
    count = packets_ref.shape[0]
    tops, sums = stats_ref[:, 0, :], stats_ref[:, 1, :]
    top = jnp.max(tops, axis=0, keepdims=True)
    total = jnp.sum(sums * jnp.exp(tops - top), axis=0, keepdims=True)
    log_all = top + jnp.log(total)
    log_ref[...] = log_all
    weights = []
    for r in range(refs):
        place = slice(r * SHIFTS, (r + 1) * SHIFTS)
        posterior = jnp.exp(scores_ref[place, :] - log_all).astype(bf16)
        posterior_ref[place, :] = posterior
        weights.append(jnp.sum(posterior.astype(f32), axis=0, keepdims=True))
    weights = jnp.concatenate(weights, axis=0)
    hot = label_table(packets_ref[:, 2 * F :])
    spread = jnp.dot(weights, hot, precision=highest)
    lane = lax.broadcasted_iota(jnp.int32, (refs, LANES), 1) // NCTF
    row = lax.broadcasted_iota(jnp.int32, (refs, LANES), 0) % own_refs
    spread = jnp.where(lane == row, spread, 0.0)
    shares = []
    for g in range(groups):
        share = jnp.sum(spread[g * own_refs : (g + 1) * own_refs], axis=0, keepdims=True)
        high = share.astype(bf16).astype(f32)
        spare = jnp.zeros((ROWS - 2 * own_refs - 2, LANES), f32)
        shares.append(jnp.concatenate([high, share - high, spare], axis=0))

    def chunk(d, carry):
        lanes = pl.ds(pl.multiple_of(d * LANES, LANES), LANES)
        wide = pl.ds(pl.multiple_of(d * 2 * LANES, 2 * LANES), 2 * LANES)
        cos, sin = cos_ref[:, lanes], sin_ref[:, lanes]
        totals = jnp.dot(posterior_ref[...], packets_ref[:, wide], preferred_element_type=f32)
        for g in range(groups):
            rows = []
            for i in range(own_refs):
                place = (g * own_refs + i) * SHIFTS
                real = totals[place : place + SHIFTS, :LANES]
                imag = totals[place : place + SHIFTS, LANES:]
                rows.append(jnp.sum(real * cos + imag * sin, axis=0, keepdims=True))
                rows.append(jnp.sum(imag * cos - real * sin, axis=0, keepdims=True))
            parts_ref[g, d] = jnp.concatenate(rows + [shares[g]], axis=0).astype(bf16)
        return carry

    lax.fori_loop(0, CHUNKS, chunk, 0)


def back_project(scores, stats, packets, cos_table, sin_table, own_refs):
    count = packets.shape[0]
    groups = scores.shape[0] // SHIFTS // own_refs
    return pl.pallas_call(
        functools.partial(back_kernel, own_refs),
        out_shape=(
            jax.ShapeDtypeStruct((groups, CHUNKS, ROWS, LANES), bf16),
            jax.ShapeDtypeStruct((1, count), f32),
        ),
        in_specs=[whole_vmem] * 5,
        out_specs=(whole_vmem, whole_vmem),
        scratch_shapes=[pltpu.VMEM((scores.shape[0], count), bf16)],
        compiler_params=pltpu.CompilerParams(vmem_limit_bytes=vmem_bytes),
        name="back",
    )(scores, stats, packets, cos_table, sin_table)


def finish_kernel(parts_ref, transfer_ref, out_ref):
    own_refs = out_ref.shape[0]
    sums = jnp.sum(parts_ref[...].astype(f32), axis=0)
    share = sums[2 * own_refs : 2 * own_refs + 1] + sums[2 * own_refs + 1 : 2 * own_refs + 2]
    lane = lax.broadcasted_iota(jnp.int32, (own_refs, LANES), 1) // NCTF
    row = lax.broadcasted_iota(jnp.int32, (own_refs, LANES), 0)
    shares = jnp.where(lane == row, share, 0.0)
    own = transfer_ref[...]
    squared = jnp.concatenate([own * own] * (LANES // NCTF), axis=0)
    denominator = jnp.dot(shares, squared, precision=highest) + ridge_term
    for i in range(own_refs):
        out_ref[i] = sums[2 * i : 2 * i + 2] / denominator[i : i + 1]


def finish(parts, transfer, own_refs):
    return pl.pallas_call(
        finish_kernel,
        out_shape=jax.ShapeDtypeStruct((own_refs, 2, LANES), f32),
        in_specs=[whole_vmem] * 2,
        out_specs=whole_vmem,
        name="finish",
    )(parts, transfer)


def body(near_axes, far_axes, particles, classes, template_spectra, transfer_magnitude, offsets):
    rows = particles.shape[0]
    own_refs = template_spectra.shape[0]
    near, far = lax.axis_size(near_axes), lax.axis_size(far_axes)
    packet, copies = prep(classes, particles, transfer_magnitude, template_spectra, near, far)
    spectra = lax.all_to_all(copies, far_axes, 0, 0)
    packets = lax.all_to_all(packet, near_axes, 0, 0)
    cos_table, sin_table = phase_tables(offsets)
    packets = packets.reshape(near * rows, 2 * F + LANES)
    spectra = spectra.reshape(-1, CHUNKS, ROWS, LANES)
    templates, power = make_templates(spectra, cos_table, sin_table, own_refs)
    squared = transfer_magnitude * transfer_magnitude
    penalty = 0.5 * jnp.dot(power, squared.T, precision=highest)
    scores, stats = make_scores(templates, packets, penalty, near)
    stats = lax.all_to_all(stats, near_axes, 0, 0)
    parts, log_all = back_project(scores, stats, packets, cos_table, sin_table, own_refs)
    parts = lax.all_to_all(parts.reshape(far, ROWS, LANES), far_axes, 0, 0)
    own = lax.dynamic_slice_in_dim(
        transfer_magnitude, lax.axis_index("dom") * LANES, LANES, 1
    )
    new_refs = finish(parts, own, own_refs)
    log_own = lax.dynamic_slice_in_dim(log_all[0], lax.axis_index(near_axes) * rows, rows, 0)
    return (log_own, new_refs)


def solution(mesh):
    devices = mesh.devices
    names = ("tg", "wg", "xc", "dom")
    inner = Mesh(devices.reshape(2, 2, 8, devices.shape[1]), names)
    refs = ("tg", "wg", "xc")
    return jax.shard_map(
        functools.partial(body, ("wg", "xc"), ("tg", "dom")),
        mesh=inner,
        in_specs=(P(names, None, None), P(names), P(refs, None, "dom"), P(), P()),
        out_specs=(P(names), P(refs, None, "dom")),
        check_vma=False,
    )
```

```python
import functools
import math

import jax
import jax.numpy as jnp
from jax import lax
from jax.experimental import pallas as pl
from jax.experimental.pallas import tpu as pltpu
from jax.sharding import Mesh
from jax.sharding import PartitionSpec as P

BOX = 64
F = 2048
SHIFTS = 64
NCTF = 16
LANES = 128
CHUNKS = F // LANES
ROWS = 16

highest = lax.Precision.HIGHEST
ridge_term = 1.0
f32 = jnp.float32
bf16 = jnp.bfloat16
whole_vmem = pl.BlockSpec(memory_space=pltpu.VMEM)
vmem_bytes = 40 * 1024 * 1024


def phase_tables(offsets):
    half_side = BOX // 2
    positions = jnp.arange(F, dtype=jnp.int32)
    row_index = positions // half_side
    freq_x = jnp.where(row_index < half_side, row_index, row_index - BOX)
    freq_y = positions % half_side
    turn_count = (offsets[:, 0:1] * freq_x[None, :] + offsets[:, 1:2] * freq_y[None, :]) % BOX
    angles = turn_count.astype(f32) * (2.0 * math.pi / BOX)
    return (jnp.cos(angles), jnp.sin(angles))


def copies_kernel(spectra_ref, copies_ref):
    own_refs = spectra_ref.shape[0]
    spectra = spectra_ref[...].reshape(own_refs * 2, LANES)
    spare = jnp.zeros((ROWS - own_refs * 2, LANES), bf16)
    spectra = jnp.concatenate([spectra, spare], axis=0)
    copies_ref[...] = jnp.broadcast_to(spectra[None], copies_ref.shape)


def make_copies(spectra, far):
    return pl.pallas_call(
        copies_kernel,
        out_shape=jax.ShapeDtypeStruct((far, ROWS, LANES), bf16),
        in_specs=[whole_vmem],
        out_specs=whole_vmem,
        name="copies",
    )(spectra)


def modulate_kernel(classes_ref, particles_ref, transfer_ref, packet_ref):
    rows = particles_ref.shape[0]
    place = lax.broadcasted_iota(jnp.int32, (rows, 1), 0)
    labels = jnp.zeros((rows, 1), jnp.int32)
    for i in range(rows):
        labels = jnp.where(place == i, classes_ref[i], labels)
    contrast = jnp.zeros((rows, F), f32)
    for c in range(NCTF):
        contrast = jnp.where(labels == c, transfer_ref[c : c + 1, :], contrast)
    values = particles_ref[...].astype(f32)
    real = (values[:, 0, :] * contrast).astype(bf16)
    imag = (values[:, 1, :] * contrast).astype(bf16)
    for d in range(CHUNKS):
        lanes = slice(d * LANES, (d + 1) * LANES)
        packet_ref[:, 2 * d * LANES : (2 * d + 1) * LANES] = real[:, lanes]
        packet_ref[:, (2 * d + 1) * LANES : (2 * d + 2) * LANES] = imag[:, lanes]
    tags = jnp.broadcast_to(labels.astype(f32), (rows, LANES))
    packet_ref[:, 2 * F :] = tags.astype(bf16)


def modulate(classes, particles, transfer):
    rows = particles.shape[0]
    return pl.pallas_call(
        modulate_kernel,
        out_shape=jax.ShapeDtypeStruct((rows, 2 * F + LANES), bf16),
        in_specs=[pl.BlockSpec(memory_space=pltpu.SMEM)] + [whole_vmem] * 2,
        out_specs=whole_vmem,
        name="modulate",
    )(classes, particles, transfer)


def arrange_kernel(place_ref, *refs):
    count = len(refs) - 1
    for k in range(count):
        refs[count][lax.rem(place_ref[0] + count - k, count)] = refs[k][...]


def arrange(place, packets):
    return pl.pallas_call(
        arrange_kernel,
        out_shape=jax.ShapeDtypeStruct((len(packets),) + packets[0].shape, bf16),
        in_specs=[pl.BlockSpec(memory_space=pltpu.SMEM)] + [whole_vmem] * len(packets),
        out_specs=whole_vmem,
        name="arrange",
    )(place, *packets)


def label_table(tags):
    lane = lax.broadcasted_iota(jnp.int32, tags.shape, 1) % NCTF
    return (tags.astype(f32) == lane.astype(f32)).astype(f32)


def score_kernel(
    own_refs,
    side_ref,
    spectra_ref,
    cos_ref,
    sin_ref,
    own_ref,
    other_ref,
    transfer_ref,
    odds_ref,
    stats_ref,
    weighted_ref,
    templates_ref,
    power_ref,
):
    groups = spectra_ref.shape[0]
    refs = groups * own_refs
    half = own_ref.shape[0]
    side = side_ref[0]

    def build(d, slot):
        lanes = pl.ds(pl.multiple_of(d * LANES, LANES), LANES)
        cos, sin = cos_ref[:, lanes], sin_ref[:, lanes]
        powers = []
        for g in range(groups):
            block = spectra_ref[g, d].astype(f32)
            for i in range(own_refs):
                real, imag = block[2 * i : 2 * i + 1], block[2 * i + 1 : 2 * i + 2]
                place = (g * own_refs + i) * SHIFTS
                templates_ref[slot, place : place + SHIFTS, :LANES] = (
                    real * cos - imag * sin
                ).astype(bf16)
                templates_ref[slot, place : place + SHIFTS, LANES:] = (
                    real * sin + imag * cos
                ).astype(bf16)
                powers.append(real * real + imag * imag)
        power_ref[:, lanes] = jnp.concatenate(powers, axis=0)

    def product(d, slot):
        wide = pl.ds(pl.multiple_of(d * 2 * LANES, 2 * LANES), 2 * LANES)
        return lax.dot_general(
            templates_ref[slot],
            weighted_ref[:, wide],
            (((1,), (1,)), ((), ())),
            preferred_element_type=f32,
        )

    build(0, 0)
    own, other = own_ref[...], other_ref[...]
    weighted_ref[:half, :] = jnp.where(side == 0, own, other)
    weighted_ref[half:, :] = jnp.where(side == 0, other, own)
    odds_ref[...] = jnp.zeros_like(odds_ref)

    def pair(k, carry):
        d = 2 * k
        odds_ref[...] += product(d, 0)
        build(d + 1, 1)
        odds_ref[...] += product(d + 1, 1)
        build(lax.rem(d + 2, CHUNKS), 0)
        return carry

    lax.fori_loop(0, CHUNKS // 2, pair, 0)
    transfer = transfer_ref[...]
    penalty = 0.5 * lax.dot_general(
        power_ref[...], transfer * transfer, (((1,), (1,)), ((), ())), precision=highest
    )
    hot = label_table(weighted_ref[:, 2 * F :])[:, :NCTF]
    cost = lax.dot_general(penalty, hot, (((1,), (1,)), ((), ())), precision=highest)
    top = None
    for r in range(refs):
        place = slice(r * SHIFTS, (r + 1) * SHIFTS)
        scores = odds_ref[place, :] - cost[r : r + 1]
        odds_ref[place, :] = scores
        high = jnp.max(scores, axis=0, keepdims=True)
        top = high if top is None else jnp.maximum(top, high)
    odds = jnp.exp(odds_ref[...] - top)
    odds_ref[...] = odds
    total = jnp.sum(odds, axis=0, keepdims=True)
    stats = jnp.concatenate([top, total], axis=0)
    spare = jnp.zeros((2, LANES - stats.shape[1]), f32)
    stats = jnp.concatenate([stats, spare], axis=1)
    stats_ref[...] = jnp.broadcast_to(stats[None], stats_ref.shape)


def make_scores(side, spectra, cos_table, sin_table, own, other, transfer, own_refs, near):
    groups = spectra.shape[0]
    refs = groups * own_refs
    count = 2 * own.shape[0]
    return pl.pallas_call(
        functools.partial(score_kernel, own_refs),
        out_shape=(
            jax.ShapeDtypeStruct((refs * SHIFTS, count), f32),
            jax.ShapeDtypeStruct((near, 2, LANES), f32),
            jax.ShapeDtypeStruct((count, own.shape[1]), bf16),
        ),
        in_specs=[pl.BlockSpec(memory_space=pltpu.SMEM)] + [whole_vmem] * 6,
        out_specs=(whole_vmem, whole_vmem, whole_vmem),
        scratch_shapes=[
            pltpu.VMEM((2, refs * SHIFTS, 2 * LANES), bf16),
            pltpu.VMEM((refs, F), f32),
        ],
        compiler_params=pltpu.CompilerParams(vmem_limit_bytes=vmem_bytes),
        name="scores",
    )(side, spectra, cos_table, sin_table, own, other, transfer)


def back_kernel(
    own_refs,
    slot_ref,
    odds_ref,
    stats_ref,
    packets_ref,
    cos_ref,
    sin_ref,
    parts_ref,
    log_ref,
    posterior_ref,
):
    groups = parts_ref.shape[0]
    refs = groups * own_refs
    count = odds_ref.shape[1]
    tops, sums = stats_ref[:, 0, :count], stats_ref[:, 1, :count]
    top = jnp.max(tops, axis=0, keepdims=True)
    total = jnp.sum(sums * jnp.exp(tops - top), axis=0, keepdims=True)
    log_all = top + jnp.log(total)
    log_ref[...] = log_all
    scale = jnp.exp(stats_ref[slot_ref[0]][0:1, :count] - log_all)
    weights = []
    for r in range(refs):
        place = slice(r * SHIFTS, (r + 1) * SHIFTS)
        posterior = (odds_ref[place, :] * scale).astype(bf16)
        posterior_ref[place, :] = posterior
        weights.append(jnp.sum(posterior.astype(f32), axis=0, keepdims=True))
    weights = jnp.concatenate(weights, axis=0)
    hot = label_table(packets_ref[:, 2 * F :])
    spread = jnp.dot(weights, hot, precision=highest)
    lane = lax.broadcasted_iota(jnp.int32, (refs, LANES), 1) // NCTF
    row = lax.broadcasted_iota(jnp.int32, (refs, LANES), 0) % own_refs
    spread = jnp.where(lane == row, spread, 0.0)
    shares = []
    for g in range(groups):
        share = jnp.sum(spread[g * own_refs : (g + 1) * own_refs], axis=0, keepdims=True)
        high = share.astype(bf16).astype(f32)
        spare = jnp.zeros((ROWS - 2 * own_refs - 2, LANES), f32)
        shares.append(jnp.concatenate([high, share - high, spare], axis=0))

    def chunk(d, carry):
        lanes = pl.ds(pl.multiple_of(d * LANES, LANES), LANES)
        wide = pl.ds(pl.multiple_of(d * 2 * LANES, 2 * LANES), 2 * LANES)
        cos, sin = cos_ref[:, lanes], sin_ref[:, lanes]
        totals = jnp.dot(posterior_ref[...], packets_ref[:, wide], preferred_element_type=f32)
        for g in range(groups):
            rows = []
            for i in range(own_refs):
                place = (g * own_refs + i) * SHIFTS
                real = totals[place : place + SHIFTS, :LANES]
                imag = totals[place : place + SHIFTS, LANES:]
                rows.append(jnp.sum(real * cos + imag * sin, axis=0, keepdims=True))
                rows.append(jnp.sum(imag * cos - real * sin, axis=0, keepdims=True))
            parts_ref[g, d] = jnp.concatenate(rows + [shares[g]], axis=0).astype(bf16)
        return carry

    lax.fori_loop(0, CHUNKS, chunk, 0)


def back_project(slot, odds, stats, packets, cos_table, sin_table, own_refs):
    count = packets.shape[0]
    groups = odds.shape[0] // SHIFTS // own_refs
    return pl.pallas_call(
        functools.partial(back_kernel, own_refs),
        out_shape=(
            jax.ShapeDtypeStruct((groups, CHUNKS, ROWS, LANES), bf16),
            jax.ShapeDtypeStruct((1, count), f32),
        ),
        in_specs=[pl.BlockSpec(memory_space=pltpu.SMEM)] + [whole_vmem] * 5,
        out_specs=(whole_vmem, whole_vmem),
        scratch_shapes=[pltpu.VMEM((odds.shape[0], count), bf16)],
        compiler_params=pltpu.CompilerParams(vmem_limit_bytes=vmem_bytes),
        name="back",
    )(slot, odds, stats, packets, cos_table, sin_table)


def finish_kernel(parts_ref, transfer_ref, out_ref):
    own_refs = out_ref.shape[0]
    sums = jnp.sum(parts_ref[...].astype(f32), axis=0)
    share = sums[2 * own_refs : 2 * own_refs + 1] + sums[2 * own_refs + 1 : 2 * own_refs + 2]
    lane = lax.broadcasted_iota(jnp.int32, (own_refs, LANES), 1) // NCTF
    row = lax.broadcasted_iota(jnp.int32, (own_refs, LANES), 0)
    shares = jnp.where(lane == row, share, 0.0)
    own = transfer_ref[...]
    squared = jnp.concatenate([own * own] * (LANES // NCTF), axis=0)
    denominator = jnp.dot(shares, squared, precision=highest) + ridge_term
    for i in range(own_refs):
        out_ref[i] = sums[2 * i : 2 * i + 2] / denominator[i : i + 1]


def finish(parts, transfer, own_refs):
    return pl.pallas_call(
        finish_kernel,
        out_shape=jax.ShapeDtypeStruct((own_refs, 2, LANES), f32),
        in_specs=[whole_vmem] * 2,
        out_specs=whole_vmem,
        name="finish",
    )(parts, transfer)


def shifted(value, axis, steps):
    count = lax.axis_size(axis)
    pairs = [(source, (source + steps) % count) for source in range(count)]
    return lax.ppermute(value, axis, pairs)


def body(particles, classes, template_spectra, transfer_magnitude, offsets):
    rows = particles.shape[0]
    own_refs = template_spectra.shape[0]
    near_axes, far_axes = ("core", "x"), ("yh", "dom")
    near, far = lax.axis_size(near_axes), lax.axis_size(far_axes)
    copies = make_copies(template_spectra, far)
    copies, particles = lax.optimization_barrier((copies, particles))
    spectra = lax.all_to_all(copies, far_axes, 0, 0)
    packet = modulate(classes, particles, transfer_magnitude)
    packets = [packet] + [shifted(packet, "x", k) for k in range(1, lax.axis_size("x"))]
    own = arrange(lax.axis_index("x")[None], packets)
    other = shifted(own, "core", 1)
    cos_table, sin_table = phase_tables(offsets)
    width = packet.shape[1]
    own, other = own.reshape(-1, width), other.reshape(-1, width)
    spectra = spectra.reshape(-1, CHUNKS, ROWS, LANES)
    side = lax.axis_index("core")[None]
    odds, stats, weighted = make_scores(
        side, spectra, cos_table, sin_table, own, other, transfer_magnitude, own_refs, near
    )
    stats = lax.all_to_all(stats, near_axes, 0, 0)
    slot = lax.axis_index(near_axes)
    parts, log_all = back_project(
        slot[None], odds, stats, weighted, cos_table, sin_table, own_refs
    )
    parts = lax.all_to_all(parts.reshape(far, ROWS, LANES), far_axes, 0, 0)
    own_transfer = lax.dynamic_slice_in_dim(
        transfer_magnitude, lax.axis_index("dom") * LANES, LANES, 1
    )
    new_refs = finish(parts, own_transfer, own_refs)
    log_own = lax.dynamic_slice_in_dim(log_all[0], slot * rows, rows, 0)
    return (log_own, new_refs)


def solution(mesh):
    devices = mesh.devices
    names = ("yh", "x", "core", "dom")
    inner = Mesh(devices.reshape(4, 4, 2, devices.shape[1]), names)
    refs = ("yh", "x", "core")
    return jax.shard_map(
        body,
        mesh=inner,
        in_specs=(P(names, None, None), P(names), P(refs, None, "dom"), P(), P()),
        out_specs=(P(names), P(refs, None, "dom")),
        check_vma=False,
    )
```

```python
import functools
import math

import jax
import jax.numpy as jnp
from jax import lax
from jax.experimental import pallas as pl
from jax.experimental.pallas import tpu as pltpu
from jax.sharding import Mesh
from jax.sharding import PartitionSpec as P

BOX = 64
F = 2048
SHIFTS = 64
NCTF = 16
LANES = 128
CHUNKS = F // LANES
ROWS = 16
UNIT = 2

highest = lax.Precision.HIGHEST
ridge_term = 1.0
f32 = jnp.float32
bf16 = jnp.bfloat16
whole_vmem = pl.BlockSpec(memory_space=pltpu.VMEM)


def room(mib):
    return pltpu.CompilerParams(vmem_limit_bytes=mib * 1024 * 1024)


def phase_tables(offsets):
    half_side = BOX // 2
    positions = jnp.arange(F, dtype=jnp.int32)
    row_index = positions // half_side
    freq_x = jnp.where(row_index < half_side, row_index, row_index - BOX)
    freq_y = positions % half_side
    turn_count = (offsets[:, 0:1] * freq_x[None, :] + offsets[:, 1:2] * freq_y[None, :]) % BOX
    angles = turn_count.astype(f32) * (2.0 * math.pi / BOX)
    return (jnp.cos(angles), jnp.sin(angles))


def modulate_kernel(classes_ref, particles_ref, transfer_ref, packet_ref):
    rows = particles_ref.shape[0]
    place = lax.broadcasted_iota(jnp.int32, (rows, 1), 0)
    labels = jnp.zeros((rows, 1), jnp.int32)
    for i in range(rows):
        labels = jnp.where(place == i, classes_ref[i], labels)
    contrast = jnp.zeros((rows, F), f32)
    for c in range(NCTF):
        contrast = jnp.where(labels == c, transfer_ref[c : c + 1, :], contrast)
    values = particles_ref[...].astype(f32)
    real = (values[:, 0, :] * contrast).astype(bf16)
    imag = (values[:, 1, :] * contrast).astype(bf16)
    for d in range(CHUNKS):
        lanes = slice(d * LANES, (d + 1) * LANES)
        packet_ref[:, 2 * d * LANES : (2 * d + 1) * LANES] = real[:, lanes]
        packet_ref[:, (2 * d + 1) * LANES : (2 * d + 2) * LANES] = imag[:, lanes]
    tags = jnp.broadcast_to(labels.astype(f32), (rows, LANES))
    packet_ref[:, 2 * F :] = tags.astype(bf16)


def modulate(classes, particles, transfer):
    rows = particles.shape[0]
    return pl.pallas_call(
        modulate_kernel,
        out_shape=jax.ShapeDtypeStruct((rows, 2 * F + LANES), bf16),
        in_specs=[pl.BlockSpec(memory_space=pltpu.SMEM)] + [whole_vmem] * 2,
        out_specs=whole_vmem,
        compiler_params=room(4),
        name="modulate",
    )(classes, particles, transfer)


def arrange_kernel(place_ref, *refs):
    count = len(refs) - 1
    for k in range(count):
        refs[count][lax.rem(place_ref[0] + count - k, count)] = refs[k][...]


def arrange(place, packets):
    return pl.pallas_call(
        arrange_kernel,
        out_shape=jax.ShapeDtypeStruct((len(packets),) + packets[0].shape, bf16),
        in_specs=[pl.BlockSpec(memory_space=pltpu.SMEM)] + [whole_vmem] * len(packets),
        out_specs=whole_vmem,
        compiler_params=room(4),
        name="arrange",
    )(place, *packets)


def label_table(tags):
    lane = lax.broadcasted_iota(jnp.int32, tags.shape, 1) % NCTF
    return (tags.astype(f32) == lane.astype(f32)).astype(f32)


def score_kernel(
    own_refs,
    side_ref,
    spectra_ref,
    cos_ref,
    sin_ref,
    own_ref,
    other_ref,
    transfer_ref,
    odds_ref,
    stats_ref,
    weighted_ref,
    templates_ref,
    penalty_ref,
):
    groups = spectra_ref.shape[0]
    refs = groups * own_refs
    half = own_ref.shape[0]
    side = side_ref[0]

    def build(u, slot):
        for j in range(UNIT):
            d = u * UNIT + j
            lanes = pl.ds(pl.multiple_of(d * LANES, LANES), LANES)
            cos, sin = cos_ref[:, lanes], sin_ref[:, lanes]
            left, right = 2 * j * LANES, (2 * j + 1) * LANES
            for g in range(groups):
                block = spectra_ref[g, d].astype(f32)
                for i in range(own_refs):
                    real, imag = block[i, 0:1], block[i, 1:2]
                    place = (g * own_refs + i) * SHIFTS
                    templates_ref[slot, place : place + SHIFTS, left:right] = (
                        real * cos - imag * sin
                    ).astype(bf16)
                    templates_ref[slot, place : place + SHIFTS, right : right + LANES] = (
                        real * sin + imag * cos
                    ).astype(bf16)

    def product(u, slot):
        for j in range(UNIT):
            d = u * UNIT + j
            lanes = pl.ds(pl.multiple_of(d * LANES, LANES), LANES)
            transfer = transfer_ref[:, lanes]
            squared = transfer * transfer
            for g in range(groups):
                block = spectra_ref[g, d].astype(f32)
                for i in range(own_refs):
                    real, imag = block[i, 0:1], block[i, 1:2]
                    place = (g * own_refs + i) * NCTF
                    penalty_ref[place : place + NCTF, :] += (real * real + imag * imag) * squared
        width = 2 * UNIT * LANES
        wide = pl.ds(pl.multiple_of(u * width, width), width)
        odds_ref[...] += lax.dot_general(
            templates_ref[slot],
            weighted_ref[:, wide],
            (((1,), (1,)), ((), ())),
            preferred_element_type=f32,
        )

    build(0, 0)
    own, other = own_ref[...], other_ref[...]
    weighted_ref[:half, :] = jnp.where(side == 0, own, other)
    weighted_ref[half:, :] = jnp.where(side == 0, other, own)
    odds_ref[...] = jnp.zeros_like(odds_ref)
    penalty_ref[...] = jnp.zeros_like(penalty_ref)
    units = CHUNKS // UNIT

    def pair(k, carry):
        u = 2 * k
        product(u, 0)
        build(u + 1, 1)
        product(u + 1, 1)
        build(lax.rem(u + 2, units), 0)
        return carry

    lax.fori_loop(0, units // 2, pair, 0)
    tags = weighted_ref[:, 2 * F :].astype(f32).T[:NCTF]
    hot = (tags == lax.broadcasted_iota(jnp.int32, tags.shape, 0).astype(f32)).astype(f32)
    top = None
    for r in range(refs):
        charge = jnp.sum(penalty_ref[r * NCTF : (r + 1) * NCTF, :], axis=1, keepdims=True)
        cost = 0.5 * jnp.sum(charge * hot, axis=0, keepdims=True)
        place = slice(r * SHIFTS, (r + 1) * SHIFTS)
        scores = odds_ref[place, :] - cost
        odds_ref[place, :] = scores
        high = jnp.max(scores, axis=0, keepdims=True)
        top = high if top is None else jnp.maximum(top, high)
    odds = jnp.exp(odds_ref[...] - top)
    odds_ref[...] = odds
    total = jnp.sum(odds, axis=0, keepdims=True)
    stats = jnp.concatenate([top, total], axis=0)
    spare = jnp.zeros((2, LANES - stats.shape[1]), f32)
    stats = jnp.concatenate([stats, spare], axis=1)
    stats_ref[...] = jnp.broadcast_to(stats[None], stats_ref.shape)


def make_scores(side, spectra, cos_table, sin_table, own, other, transfer, own_refs, near):
    groups = spectra.shape[0]
    refs = groups * own_refs
    count = 2 * own.shape[0]
    return pl.pallas_call(
        functools.partial(score_kernel, own_refs),
        out_shape=(
            jax.ShapeDtypeStruct((refs * SHIFTS, count), f32),
            jax.ShapeDtypeStruct((near, 2, LANES), f32),
            jax.ShapeDtypeStruct((count, own.shape[1]), bf16),
        ),
        in_specs=[pl.BlockSpec(memory_space=pltpu.SMEM)] + [whole_vmem] * 6,
        out_specs=(whole_vmem, whole_vmem, whole_vmem),
        scratch_shapes=[
            pltpu.VMEM((2, refs * SHIFTS, 2 * UNIT * LANES), bf16),
            pltpu.VMEM((refs * NCTF, LANES), f32),
        ],
        compiler_params=room(24),
        name="scores",
    )(side, spectra, cos_table, sin_table, own, other, transfer)


def back_kernel(
    own_refs,
    slot_ref,
    odds_ref,
    stats_ref,
    packets_ref,
    cos_ref,
    sin_ref,
    parts_ref,
    log_ref,
    posterior_ref,
):
    groups = parts_ref.shape[0]
    refs = groups * own_refs
    count = odds_ref.shape[1]
    tops, sums = stats_ref[:, 0, :count], stats_ref[:, 1, :count]
    top = jnp.max(tops, axis=0, keepdims=True)
    total = jnp.sum(sums * jnp.exp(tops - top), axis=0, keepdims=True)
    log_all = top + jnp.log(total)
    log_ref[...] = log_all
    scale = jnp.exp(stats_ref[slot_ref[0]][0:1, :count] - log_all)
    weights = []
    for r in range(refs):
        place = slice(r * SHIFTS, (r + 1) * SHIFTS)
        posterior = (odds_ref[place, :] * scale).astype(bf16)
        posterior_ref[place, :] = posterior
        weights.append(jnp.sum(posterior.astype(f32), axis=0, keepdims=True))
    weights = jnp.concatenate(weights, axis=0)
    hot = label_table(packets_ref[:, 2 * F :])
    spread = jnp.dot(weights, hot, precision=highest)
    lane = lax.broadcasted_iota(jnp.int32, (refs, LANES), 1) // NCTF
    row = lax.broadcasted_iota(jnp.int32, (refs, LANES), 0) % own_refs
    spread = jnp.where(lane == row, spread, 0.0)
    shares = []
    for g in range(groups):
        share = jnp.sum(spread[g * own_refs : (g + 1) * own_refs], axis=0, keepdims=True)
        high = share.astype(bf16).astype(f32)
        spare = jnp.zeros((ROWS - 2 * own_refs - 2, LANES), f32)
        shares.append(jnp.concatenate([high, share - high, spare], axis=0))

    def chunk(d, carry):
        lanes = pl.ds(pl.multiple_of(d * LANES, LANES), LANES)
        wide = pl.ds(pl.multiple_of(d * 2 * LANES, 2 * LANES), 2 * LANES)
        cos, sin = cos_ref[:, lanes], sin_ref[:, lanes]
        totals = jnp.dot(posterior_ref[...], packets_ref[:, wide], preferred_element_type=f32)
        for g in range(groups):
            rows = []
            for i in range(own_refs):
                place = (g * own_refs + i) * SHIFTS
                real = totals[place : place + SHIFTS, :LANES]
                imag = totals[place : place + SHIFTS, LANES:]
                rows.append(jnp.sum(real * cos + imag * sin, axis=0, keepdims=True))
                rows.append(jnp.sum(imag * cos - real * sin, axis=0, keepdims=True))
            parts_ref[g, d] = jnp.concatenate(rows + [shares[g]], axis=0).astype(bf16)
        return carry

    lax.fori_loop(0, CHUNKS, chunk, 0)


def back_project(slot, odds, stats, packets, cos_table, sin_table, own_refs):
    count = packets.shape[0]
    groups = odds.shape[0] // SHIFTS // own_refs
    return pl.pallas_call(
        functools.partial(back_kernel, own_refs),
        out_shape=(
            jax.ShapeDtypeStruct((groups, CHUNKS, ROWS, LANES), bf16),
            jax.ShapeDtypeStruct((1, count), f32),
        ),
        in_specs=[pl.BlockSpec(memory_space=pltpu.SMEM)] + [whole_vmem] * 5,
        out_specs=(whole_vmem, whole_vmem),
        scratch_shapes=[pltpu.VMEM((odds.shape[0], count), bf16)],
        compiler_params=room(24),
        name="back",
    )(slot, odds, stats, packets, cos_table, sin_table)


def finish_kernel(parts_ref, transfer_ref, out_ref):
    own_refs = out_ref.shape[0]
    sums = jnp.sum(parts_ref[...].astype(f32), axis=0)
    share = sums[2 * own_refs : 2 * own_refs + 1] + sums[2 * own_refs + 1 : 2 * own_refs + 2]
    lane = lax.broadcasted_iota(jnp.int32, (own_refs, LANES), 1) // NCTF
    row = lax.broadcasted_iota(jnp.int32, (own_refs, LANES), 0)
    shares = jnp.where(lane == row, share, 0.0)
    own = transfer_ref[...]
    squared = jnp.concatenate([own * own] * (LANES // NCTF), axis=0)
    denominator = jnp.dot(shares, squared, precision=highest) + ridge_term
    for i in range(own_refs):
        out_ref[i] = sums[2 * i : 2 * i + 2] / denominator[i : i + 1]


def finish(parts, transfer, own_refs):
    return pl.pallas_call(
        finish_kernel,
        out_shape=jax.ShapeDtypeStruct((own_refs, 2, LANES), f32),
        in_specs=[whole_vmem] * 2,
        out_specs=whole_vmem,
        compiler_params=room(4),
        name="finish",
    )(parts, transfer)


def shifted(value, axis, steps):
    count = lax.axis_size(axis)
    pairs = [(source, (source + steps) % count) for source in range(count)]
    return lax.ppermute(value, axis, pairs)


def body(particles, classes, template_spectra, transfer_magnitude, offsets):
    rows = particles.shape[0]
    own_refs = template_spectra.shape[0]
    near_axes, far_axes = ("core", "x"), ("yh", "dom")
    near, far = lax.axis_size(near_axes), lax.axis_size(far_axes)
    copies = jnp.broadcast_to(template_spectra[None], (far,) + template_spectra.shape)
    copies, particles = lax.optimization_barrier((copies, particles))
    spectra = lax.all_to_all(copies, far_axes, 0, 0)
    packet = modulate(classes, particles, transfer_magnitude)
    packets = [packet] + [shifted(packet, "x", k) for k in range(1, lax.axis_size("x"))]
    own = arrange(lax.axis_index("x")[None], packets)
    own, spectra = lax.optimization_barrier((own, spectra))
    other = shifted(own, "core", 1)
    cos_table, sin_table = phase_tables(offsets)
    width = packet.shape[1]
    own, other = own.reshape(-1, width), other.reshape(-1, width)
    spectra = spectra.reshape(-1, CHUNKS, own_refs, 2, LANES)
    side = lax.axis_index("core")[None]
    odds, stats, weighted = make_scores(
        side, spectra, cos_table, sin_table, own, other, transfer_magnitude, own_refs, near
    )
    stats = lax.all_to_all(stats, near_axes, 0, 0)
    slot = lax.axis_index(near_axes)
    parts, log_all = back_project(
        slot[None], odds, stats, weighted, cos_table, sin_table, own_refs
    )
    parts = lax.all_to_all(parts.reshape(far, ROWS, LANES), far_axes, 0, 0)
    own_transfer = lax.dynamic_slice_in_dim(
        transfer_magnitude, lax.axis_index("dom") * LANES, LANES, 1
    )
    new_refs = finish(parts, own_transfer, own_refs)
    log_own = lax.dynamic_slice_in_dim(log_all[0], slot * rows, rows, 0)
    return (log_own, new_refs)


def solution(mesh):
    devices = mesh.devices
    names = ("yh", "x", "core", "dom")
    inner = Mesh(devices.reshape(4, 4, 2, devices.shape[1]), names)
    refs = ("yh", "x", "core")
    return jax.shard_map(
        body,
        mesh=inner,
        in_specs=(P(names, None, None), P(names), P(refs, None, "dom"), P(), P()),
        out_specs=(P(names), P(refs, None, "dom")),
        check_vma=False,
    )
```

```python
import functools
import math

import jax
import jax.numpy as jnp
from jax import lax
from jax.experimental import pallas as pl
from jax.experimental.pallas import tpu as pltpu
from jax.sharding import Mesh
from jax.sharding import PartitionSpec as P

BOX = 64
F = 2048
SHIFTS = 64
NCTF = 16
LANES = 128
CHUNKS = F // LANES
ROWS = 16
UNIT = 2
BATCH = 2

highest = lax.Precision.HIGHEST
ridge_term = 1.0
f32 = jnp.float32
bf16 = jnp.bfloat16
whole_vmem = pl.BlockSpec(memory_space=pltpu.VMEM)


def room(mib):
    return pltpu.CompilerParams(vmem_limit_bytes=mib * 1024 * 1024)


def phase_tables(offsets):
    half_side = BOX // 2
    positions = jnp.arange(F, dtype=jnp.int32)
    row_index = positions // half_side
    freq_x = jnp.where(row_index < half_side, row_index, row_index - BOX)
    freq_y = positions % half_side
    turn_count = (offsets[:, 0:1] * freq_x[None, :] + offsets[:, 1:2] * freq_y[None, :]) % BOX
    angles = turn_count.astype(f32) * (2.0 * math.pi / BOX)
    return (jnp.cos(angles), jnp.sin(angles))


def modulate_kernel(classes_ref, particles_ref, transfer_ref, packet_ref):
    rows = particles_ref.shape[0]
    place = lax.broadcasted_iota(jnp.int32, (rows, 1), 0)
    labels = jnp.zeros((rows, 1), jnp.int32)
    for i in range(rows):
        labels = jnp.where(place == i, classes_ref[i], labels)
    contrast = jnp.zeros((rows, F), f32)
    for c in range(NCTF):
        contrast = jnp.where(labels == c, transfer_ref[c : c + 1, :], contrast)
    values = particles_ref[...].astype(f32)
    real = (values[:, 0, :] * contrast).astype(bf16)
    imag = (values[:, 1, :] * contrast).astype(bf16)
    for d in range(CHUNKS):
        lanes = slice(d * LANES, (d + 1) * LANES)
        packet_ref[:, 2 * d * LANES : (2 * d + 1) * LANES] = real[:, lanes]
        packet_ref[:, (2 * d + 1) * LANES : (2 * d + 2) * LANES] = imag[:, lanes]
    tags = jnp.broadcast_to(labels.astype(f32), (rows, LANES))
    packet_ref[:, 2 * F :] = tags.astype(bf16)


def modulate(classes, particles, transfer):
    rows = particles.shape[0]
    return pl.pallas_call(
        modulate_kernel,
        out_shape=jax.ShapeDtypeStruct((rows, 2 * F + LANES), bf16),
        in_specs=[pl.BlockSpec(memory_space=pltpu.SMEM)] + [whole_vmem] * 2,
        out_specs=whole_vmem,
        compiler_params=room(4),
        name="modulate",
    )(classes, particles, transfer)


def arrange_kernel(place_ref, *refs):
    count = len(refs) - 1
    for k in range(count):
        refs[count][lax.rem(place_ref[0] + count - k, count)] = refs[k][...]


def arrange(place, packets):
    return pl.pallas_call(
        arrange_kernel,
        out_shape=jax.ShapeDtypeStruct((len(packets),) + packets[0].shape, bf16),
        in_specs=[pl.BlockSpec(memory_space=pltpu.SMEM)] + [whole_vmem] * len(packets),
        out_specs=whole_vmem,
        compiler_params=room(4),
        name="arrange",
    )(place, *packets)


def label_table(tags):
    lane = lax.broadcasted_iota(jnp.int32, tags.shape, 1) % NCTF
    return (tags.astype(f32) == lane.astype(f32)).astype(f32)


def score_kernel(
    own_refs,
    side_ref,
    spectra_ref,
    cos_ref,
    sin_ref,
    own_ref,
    other_ref,
    transfer_ref,
    odds_ref,
    stats_ref,
    weighted_ref,
    penalty_ref,
):
    groups = spectra_ref.shape[0]
    refs = groups * own_refs
    half = own_ref.shape[0]
    side = side_ref[0]

    own, other = own_ref[...], other_ref[...]
    weighted_ref[:half, :] = jnp.where(side == 0, own, other)
    weighted_ref[half:, :] = jnp.where(side == 0, other, own)
    odds_ref[...] = jnp.zeros_like(odds_ref)
    penalty_ref[...] = jnp.zeros_like(penalty_ref)
    width = 2 * UNIT * LANES

    def unit(u, carry):
        wide = pl.ds(pl.multiple_of(u * width, width), width)
        weighted = weighted_ref[:, wide]
        tables = []
        for j in range(UNIT):
            lanes = pl.ds(pl.multiple_of((u * UNIT + j) * LANES, LANES), LANES)
            transfer = transfer_ref[:, lanes]
            tables.append((cos_ref[:, lanes], sin_ref[:, lanes], transfer * transfer))
        for g in range(groups):
            blocks = [spectra_ref[g, u * UNIT + j].astype(f32) for j in range(UNIT)]
            for first in range(0, own_refs, BATCH):
                rows = []
                for i in range(first, first + BATCH):
                    pieces = []
                    power = 0.0
                    for j in range(UNIT):
                        cos, sin, squared = tables[j]
                        real, imag = blocks[j][i, 0:1], blocks[j][i, 1:2]
                        pieces.append((real * cos - imag * sin).astype(bf16))
                        pieces.append((real * sin + imag * cos).astype(bf16))
                        power = power + (real * real + imag * imag) * squared
                    place = (g * own_refs + i) * NCTF
                    penalty_ref[place : place + NCTF, :] += power
                    rows.append(jnp.concatenate(pieces, axis=1))
                place = (g * own_refs + first) * SHIFTS
                odds_ref[place : place + BATCH * SHIFTS, :] += lax.dot_general(
                    jnp.concatenate(rows, axis=0),
                    weighted,
                    (((1,), (1,)), ((), ())),
                    preferred_element_type=f32,
                )
        return carry

    lax.fori_loop(0, CHUNKS // UNIT, unit, 0)
    tags = weighted_ref[:, 2 * F :].astype(f32).T[:NCTF]
    hot = (tags == lax.broadcasted_iota(jnp.int32, tags.shape, 0).astype(f32)).astype(f32)
    top = None
    for r in range(refs):
        charge = jnp.sum(penalty_ref[r * NCTF : (r + 1) * NCTF, :], axis=1, keepdims=True)
        cost = 0.5 * jnp.sum(charge * hot, axis=0, keepdims=True)
        place = slice(r * SHIFTS, (r + 1) * SHIFTS)
        scores = odds_ref[place, :] - cost
        odds_ref[place, :] = scores
        high = jnp.max(scores, axis=0, keepdims=True)
        top = high if top is None else jnp.maximum(top, high)
    odds = jnp.exp(odds_ref[...] - top)
    odds_ref[...] = odds
    total = jnp.sum(odds, axis=0, keepdims=True)
    stats = jnp.concatenate([top, total], axis=0)
    spare = jnp.zeros((2, LANES - stats.shape[1]), f32)
    stats = jnp.concatenate([stats, spare], axis=1)
    stats_ref[...] = jnp.broadcast_to(stats[None], stats_ref.shape)


def make_scores(side, spectra, cos_table, sin_table, own, other, transfer, own_refs, near):
    groups = spectra.shape[0]
    refs = groups * own_refs
    count = 2 * own.shape[0]
    return pl.pallas_call(
        functools.partial(score_kernel, own_refs),
        out_shape=(
            jax.ShapeDtypeStruct((refs * SHIFTS, count), f32),
            jax.ShapeDtypeStruct((near, 2, LANES), f32),
            jax.ShapeDtypeStruct((count, own.shape[1]), bf16),
        ),
        in_specs=[pl.BlockSpec(memory_space=pltpu.SMEM)] + [whole_vmem] * 6,
        out_specs=(whole_vmem, whole_vmem, whole_vmem),
        scratch_shapes=[
            pltpu.VMEM((refs * NCTF, LANES), f32),
        ],
        compiler_params=room(24),
        name="scores",
    )(side, spectra, cos_table, sin_table, own, other, transfer)


def back_kernel(
    own_refs,
    slot_ref,
    odds_ref,
    stats_ref,
    packets_ref,
    cos_ref,
    sin_ref,
    parts_ref,
    log_ref,
    posterior_ref,
):
    groups = parts_ref.shape[0]
    refs = groups * own_refs
    count = odds_ref.shape[1]
    tops, sums = stats_ref[:, 0, :count], stats_ref[:, 1, :count]
    top = jnp.max(tops, axis=0, keepdims=True)
    total = jnp.sum(sums * jnp.exp(tops - top), axis=0, keepdims=True)
    log_all = top + jnp.log(total)
    own_rows = log_ref.shape[1]
    own_log = jnp.zeros_like(log_ref)
    for k in range(count // own_rows):
        piece = log_all[:, k * own_rows : (k + 1) * own_rows]
        own_log = jnp.where(slot_ref[0] == k, piece, own_log)
    log_ref[...] = own_log
    scale = jnp.exp(stats_ref[slot_ref[0]][0:1, :count] - log_all)
    weights = []
    for r in range(refs):
        place = slice(r * SHIFTS, (r + 1) * SHIFTS)
        posterior = (odds_ref[place, :] * scale).astype(bf16)
        posterior_ref[place, :] = posterior
        weights.append(jnp.sum(posterior.astype(f32), axis=0, keepdims=True))
    weights = jnp.concatenate(weights, axis=0)
    high = weights.astype(bf16)
    low = (weights - high.astype(f32)).astype(bf16)
    hot = label_table(packets_ref[:, 2 * F :]).astype(bf16)
    spread = jnp.dot(jnp.concatenate([high, low], axis=0), hot, preferred_element_type=f32)
    spread = spread[:refs] + spread[refs:]
    lane = lax.broadcasted_iota(jnp.int32, (refs, LANES), 1) // NCTF
    row = lax.broadcasted_iota(jnp.int32, (refs, LANES), 0) % own_refs
    spread = jnp.where(lane == row, spread, 0.0)
    shares = []
    for g in range(groups):
        share = jnp.sum(spread[g * own_refs : (g + 1) * own_refs], axis=0, keepdims=True)
        high = share.astype(bf16).astype(f32)
        spare = jnp.zeros((ROWS - 2 * own_refs - 2, LANES), f32)
        shares.append(jnp.concatenate([high, share - high, spare], axis=0))

    def chunk(d, carry):
        lanes = pl.ds(pl.multiple_of(d * LANES, LANES), LANES)
        wide = pl.ds(pl.multiple_of(d * 2 * LANES, 2 * LANES), 2 * LANES)
        cos, sin = cos_ref[:, lanes], sin_ref[:, lanes]
        weighted = packets_ref[:, wide]
        for g in range(groups):
            rows = []
            for first in range(0, own_refs, BATCH):
                place = (g * own_refs + first) * SHIFTS
                totals = jnp.dot(
                    posterior_ref[place : place + BATCH * SHIFTS, :],
                    weighted,
                    preferred_element_type=f32,
                )
                for i in range(BATCH):
                    real = totals[i * SHIFTS : (i + 1) * SHIFTS, :LANES]
                    imag = totals[i * SHIFTS : (i + 1) * SHIFTS, LANES:]
                    rows.append(jnp.sum(real * cos + imag * sin, axis=0, keepdims=True))
                    rows.append(jnp.sum(imag * cos - real * sin, axis=0, keepdims=True))
            parts_ref[g, d] = jnp.concatenate(rows + [shares[g]], axis=0).astype(bf16)
        return carry

    lax.fori_loop(0, CHUNKS, chunk, 0)


def back_project(slot, odds, stats, packets, cos_table, sin_table, own_refs, rows):
    count = packets.shape[0]
    groups = odds.shape[0] // SHIFTS // own_refs
    return pl.pallas_call(
        functools.partial(back_kernel, own_refs),
        out_shape=(
            jax.ShapeDtypeStruct((groups, CHUNKS, ROWS, LANES), bf16),
            jax.ShapeDtypeStruct((1, rows), f32),
        ),
        in_specs=[pl.BlockSpec(memory_space=pltpu.SMEM)] + [whole_vmem] * 5,
        out_specs=(whole_vmem, whole_vmem),
        scratch_shapes=[pltpu.VMEM((odds.shape[0], count), bf16)],
        compiler_params=room(24),
        name="back",
    )(slot, odds, stats, packets, cos_table, sin_table)


def finish_kernel(place_ref, parts_ref, transfer_ref, out_ref):
    own_refs = out_ref.shape[0]
    sums = jnp.sum(parts_ref[...].astype(f32), axis=0)
    share = sums[2 * own_refs : 2 * own_refs + 1] + sums[2 * own_refs + 1 : 2 * own_refs + 2]
    lane = lax.broadcasted_iota(jnp.int32, (own_refs, LANES), 1) // NCTF
    row = lax.broadcasted_iota(jnp.int32, (own_refs, LANES), 0)
    shares = jnp.where(lane == row, share, 0.0)
    own = transfer_ref[:, pl.ds(pl.multiple_of(place_ref[0] * LANES, LANES), LANES)]
    squared = jnp.concatenate([own * own] * (LANES // NCTF), axis=0)
    denominator = jnp.dot(shares, squared, precision=highest) + ridge_term
    for i in range(own_refs):
        out_ref[i] = sums[2 * i : 2 * i + 2] / denominator[i : i + 1]


def finish(place, parts, transfer, own_refs):
    return pl.pallas_call(
        finish_kernel,
        out_shape=jax.ShapeDtypeStruct((own_refs, 2, LANES), f32),
        in_specs=[pl.BlockSpec(memory_space=pltpu.SMEM)] + [whole_vmem] * 2,
        out_specs=whole_vmem,
        compiler_params=room(4),
        name="finish",
    )(place, parts, transfer)


def shifted(value, axis, steps):
    count = lax.axis_size(axis)
    pairs = [(source, (source + steps) % count) for source in range(count)]
    return lax.ppermute(value, axis, pairs)


def body(particles, classes, template_spectra, transfer_magnitude, offsets):
    rows = particles.shape[0]
    own_refs = template_spectra.shape[0]
    near_axes, far_axes = ("core", "x"), ("yh", "dom")
    near, far = lax.axis_size(near_axes), lax.axis_size(far_axes)
    copies = jnp.broadcast_to(template_spectra[None], (far,) + template_spectra.shape)
    spectra = lax.all_to_all(copies, far_axes, 0, 0)
    packet = modulate(classes, particles, transfer_magnitude)
    left, right = shifted(packet, "x", 1), shifted(packet, "x", -1)
    packets = [packet, left, shifted(left, "x", 1), right]
    own = arrange(lax.axis_index("x")[None], packets)
    other = shifted(own, "core", 1)
    cos_table, sin_table = phase_tables(offsets)
    width = packet.shape[1]
    own, other = own.reshape(-1, width), other.reshape(-1, width)
    spectra = spectra.reshape(-1, CHUNKS, own_refs, 2, LANES)
    side = lax.axis_index("core")[None]
    odds, stats, weighted = make_scores(
        side, spectra, cos_table, sin_table, own, other, transfer_magnitude, own_refs, near
    )
    stats = lax.all_to_all(stats, near_axes, 0, 0)
    slot = lax.axis_index(near_axes)
    parts, log_own = back_project(
        slot[None], odds, stats, weighted, cos_table, sin_table, own_refs, rows
    )
    parts = lax.all_to_all(parts.reshape(far, ROWS, LANES), far_axes, 0, 0)
    place = lax.axis_index("dom")[None]
    new_refs = finish(place, parts, transfer_magnitude, own_refs)
    return (log_own.reshape(rows), new_refs)


def solution(mesh):
    devices = mesh.devices
    names = ("yh", "x", "core", "dom")
    inner = Mesh(devices.reshape(4, 4, 2, devices.shape[1]), names)
    refs = ("yh", "x", "core")
    return jax.shard_map(
        body,
        mesh=inner,
        in_specs=(P(names, None, None), P(names), P(refs, None, "dom"), P(), P()),
        out_specs=(P(names), P(refs, None, "dom")),
        check_vma=False,
    )
```

```python
import functools
import math

import jax
import jax.numpy as jnp
from jax import lax
from jax.experimental import pallas as pl
from jax.experimental.pallas import tpu as pltpu
from jax.sharding import Mesh
from jax.sharding import PartitionSpec as P

BOX = 64
F = 2048
SHIFTS = 64
NCTF = 16
LANES = 128
CHUNKS = F // LANES
ROWS = 16
UNIT = 2
UNROLL = 2
BATCH = 2

highest = lax.Precision.HIGHEST
ridge_term = 1.0
f32 = jnp.float32
bf16 = jnp.bfloat16
whole_vmem = pl.BlockSpec(memory_space=pltpu.VMEM)


def room(mib):
    return pltpu.CompilerParams(vmem_limit_bytes=mib * 1024 * 1024)


def phase_tables(offsets):
    half_side = BOX // 2
    positions = jnp.arange(F, dtype=jnp.int32)
    row_index = positions // half_side
    freq_x = jnp.where(row_index < half_side, row_index, row_index - BOX)
    freq_y = positions % half_side
    turn_count = (offsets[:, 0:1] * freq_x[None, :] + offsets[:, 1:2] * freq_y[None, :]) % BOX
    angles = turn_count.astype(f32) * (2.0 * math.pi / BOX)
    return (jnp.cos(angles), jnp.sin(angles))


def prep_kernel(classes_ref, particles_ref, transfer_ref, spectra_ref, packet_ref, copies_ref):
    rows = particles_ref.shape[0]
    copies_ref[...] = jnp.broadcast_to(spectra_ref[...][None], copies_ref.shape)
    place = lax.broadcasted_iota(jnp.int32, (rows, 1), 0)
    labels = jnp.zeros((rows, 1), jnp.int32)
    for i in range(rows):
        labels = jnp.where(place == i, classes_ref[i], labels)
    contrast = jnp.zeros((rows, F), f32)
    for c in range(NCTF):
        contrast = jnp.where(labels == c, transfer_ref[c : c + 1, :], contrast)
    values = particles_ref[...].astype(f32)
    real = (values[:, 0, :] * contrast).astype(bf16)
    imag = (values[:, 1, :] * contrast).astype(bf16)
    for d in range(CHUNKS):
        lanes = slice(d * LANES, (d + 1) * LANES)
        packet_ref[:, 2 * d * LANES : (2 * d + 1) * LANES] = real[:, lanes]
        packet_ref[:, (2 * d + 1) * LANES : (2 * d + 2) * LANES] = imag[:, lanes]
    tags = jnp.broadcast_to(labels.astype(f32), (rows, LANES))
    packet_ref[:, 2 * F :] = tags.astype(bf16)


def prep(classes, particles, transfer, spectra, far):
    rows = particles.shape[0]
    return pl.pallas_call(
        prep_kernel,
        out_shape=(
            jax.ShapeDtypeStruct((rows, 2 * F + LANES), bf16),
            jax.ShapeDtypeStruct((far,) + spectra.shape, bf16),
        ),
        in_specs=[pl.BlockSpec(memory_space=pltpu.SMEM)] + [whole_vmem] * 3,
        out_specs=(whole_vmem, whole_vmem),
        compiler_params=room(60),
        name="prep",
    )(classes, particles, transfer, spectra)


def arrange_kernel(place_ref, later_ref, *refs):
    count = len(refs) - 1
    for k in range(count):
        refs[count][lax.rem(place_ref[0] + count - k, count)] = refs[k][...]


def arrange(place, later, packets):
    return pl.pallas_call(
        arrange_kernel,
        out_shape=jax.ShapeDtypeStruct((len(packets),) + packets[0].shape, bf16),
        in_specs=[pl.BlockSpec(memory_space=pltpu.SMEM)] * 2 + [whole_vmem] * len(packets),
        out_specs=whole_vmem,
        compiler_params=room(4),
        name="arrange",
    )(place, later, *packets)


def fold(values):
    return jnp.sum(values.reshape(values.shape[0] // 8, 8, values.shape[1]), axis=0)


def row_sums(tiles):
    row = lax.broadcasted_iota(jnp.int32, tiles[0].shape, 0)
    for bit in (1, 2, 4):
        even = (row // bit) % 2 == 0
        merged = []
        for a, b in zip(tiles[::2], tiles[1::2]):
            merged.append(
                jnp.where(even, a, b) + pltpu.roll(jnp.where(even, b, a), 8 - bit, 0)
            )
        tiles = merged
    return tiles[0]


def label_table(tags):
    lane = lax.broadcasted_iota(jnp.int32, tags.shape, 1) % NCTF
    return (tags.astype(f32) == lane.astype(f32)).astype(f32)


def score_kernel(
    own_refs,
    side_ref,
    spectra_ref,
    cos_ref,
    sin_ref,
    own_ref,
    other_ref,
    transfer_ref,
    odds_ref,
    stats_ref,
    weighted_ref,
    penalty_ref,
):
    groups = spectra_ref.shape[0]
    refs = groups * own_refs
    half = own_ref.shape[0]
    side = side_ref[0]

    own, other = own_ref[...], other_ref[...]
    weighted_ref[:half, :] = jnp.where(side == 0, own, other)
    weighted_ref[half:, :] = jnp.where(side == 0, other, own)
    odds_ref[...] = jnp.zeros_like(odds_ref)
    penalty_ref[...] = jnp.zeros_like(penalty_ref)
    width = 2 * UNIT * LANES

    def unit(u):
        wide = pl.ds(pl.multiple_of(u * width, width), width)
        weighted = weighted_ref[:, wide]
        tables = []
        for j in range(UNIT):
            lanes = pl.ds(pl.multiple_of((u * UNIT + j) * LANES, LANES), LANES)
            transfer = transfer_ref[:, lanes]
            tables.append((cos_ref[:, lanes], sin_ref[:, lanes], transfer * transfer))
        for g in range(groups):
            blocks = [spectra_ref[g, u * UNIT + j].astype(f32) for j in range(UNIT)]
            for first in range(0, own_refs, BATCH):
                rows = []
                for i in range(first, first + BATCH):
                    pieces = []
                    power = 0.0
                    for j in range(UNIT):
                        cos, sin, squared = tables[j]
                        real, imag = blocks[j][i, 0:1], blocks[j][i, 1:2]
                        pieces.append((real * cos - imag * sin).astype(bf16))
                        pieces.append((real * sin + imag * cos).astype(bf16))
                        power = power + (real * real + imag * imag) * squared
                    place = (g * own_refs + i) * NCTF
                    penalty_ref[place : place + NCTF, :] += power
                    rows.append(jnp.concatenate(pieces, axis=1))
                place = (g * own_refs + first) * SHIFTS
                odds_ref[place : place + BATCH * SHIFTS, :] += lax.dot_general(
                    jnp.concatenate(rows, axis=0),
                    weighted,
                    (((1,), (1,)), ((), ())),
                    preferred_element_type=f32,
                )

    def units(k, carry):
        for j in range(UNROLL):
            unit(k * UNROLL + j)
        return carry

    lax.fori_loop(0, CHUNKS // UNIT // UNROLL, units, 0)
    tags = weighted_ref[:, 2 * F :].astype(f32).T[:NCTF]
    hot = (tags == lax.broadcasted_iota(jnp.int32, tags.shape, 0).astype(f32)).astype(f32)
    top = None
    for r in range(refs):
        charge = jnp.sum(penalty_ref[r * NCTF : (r + 1) * NCTF, :], axis=1, keepdims=True)
        cost = 0.5 * jnp.sum(charge * hot, axis=0, keepdims=True)
        place = slice(r * SHIFTS, (r + 1) * SHIFTS)
        scores = odds_ref[place, :] - cost
        odds_ref[place, :] = scores
        high = jnp.max(scores, axis=0, keepdims=True)
        top = high if top is None else jnp.maximum(top, high)
    odds = jnp.exp(odds_ref[...] - top)
    odds_ref[...] = odds
    total = jnp.sum(odds, axis=0, keepdims=True)
    stats = jnp.concatenate([top, total], axis=0)
    spare = jnp.zeros((2, LANES - stats.shape[1]), f32)
    stats = jnp.concatenate([stats, spare], axis=1)
    stats_ref[...] = jnp.broadcast_to(stats[None], stats_ref.shape)


def make_scores(side, spectra, cos_table, sin_table, own, other, transfer, own_refs, near):
    groups = spectra.shape[0]
    refs = groups * own_refs
    count = 2 * own.shape[0]
    return pl.pallas_call(
        functools.partial(score_kernel, own_refs),
        out_shape=(
            jax.ShapeDtypeStruct((refs * SHIFTS, count), f32),
            jax.ShapeDtypeStruct((near, 2, LANES), f32),
            jax.ShapeDtypeStruct((count, own.shape[1]), bf16),
        ),
        in_specs=[pl.BlockSpec(memory_space=pltpu.SMEM)] + [whole_vmem] * 6,
        out_specs=(whole_vmem, whole_vmem, whole_vmem),
        scratch_shapes=[
            pltpu.VMEM((refs * NCTF, LANES), f32),
        ],
        compiler_params=room(24),
        name="scores",
    )(side, spectra, cos_table, sin_table, own, other, transfer)


def back_kernel(
    own_refs,
    place_ref,
    side_ref,
    odds_ref,
    stats_ref,
    packets_ref,
    cos_ref,
    sin_ref,
    parts_ref,
    log_ref,
    posterior_ref,
):
    groups = parts_ref.shape[0]
    refs = groups * own_refs
    count = odds_ref.shape[1]
    slot = side_ref[0] * (stats_ref.shape[0] // 2) + place_ref[0]
    tops, sums = stats_ref[:, 0, :count], stats_ref[:, 1, :count]
    top = jnp.max(tops, axis=0, keepdims=True)
    total = jnp.sum(sums * jnp.exp(tops - top), axis=0, keepdims=True)
    log_all = top + jnp.log(total)
    own_rows = log_ref.shape[1]
    own_log = jnp.zeros_like(log_ref)
    for k in range(count // own_rows):
        piece = log_all[:, k * own_rows : (k + 1) * own_rows]
        own_log = jnp.where(slot == k, piece, own_log)
    log_ref[...] = own_log
    scale = jnp.exp(stats_ref[slot][0:1, :count] - log_all)
    weights = []
    for r in range(refs):
        place = slice(r * SHIFTS, (r + 1) * SHIFTS)
        posterior = (odds_ref[place, :] * scale).astype(bf16)
        posterior_ref[place, :] = posterior
        weights.append(jnp.sum(posterior.astype(f32), axis=0, keepdims=True))
    weights = jnp.concatenate(weights, axis=0)
    high = weights.astype(bf16)
    low = (weights - high.astype(f32)).astype(bf16)
    hot = label_table(packets_ref[:, 2 * F :]).astype(bf16)
    spread = jnp.dot(jnp.concatenate([high, low], axis=0), hot, preferred_element_type=f32)
    spread = spread[:refs] + spread[refs:]
    lane = lax.broadcasted_iota(jnp.int32, (refs, LANES), 1) // NCTF
    row = lax.broadcasted_iota(jnp.int32, (refs, LANES), 0) % own_refs
    spread = jnp.where(lane == row, spread, 0.0)
    shares = []
    for g in range(groups):
        share = jnp.sum(spread[g * own_refs : (g + 1) * own_refs], axis=0, keepdims=True)
        high = share.astype(bf16).astype(f32)
        before = jnp.zeros((2 * own_refs, LANES), f32)
        after = jnp.zeros((ROWS - 2 * own_refs - 2, LANES), f32)
        shares.append(jnp.concatenate([before, high, share - high, after], axis=0))

    def chunk(d):
        lanes = pl.ds(pl.multiple_of(d * LANES, LANES), LANES)
        wide = pl.ds(pl.multiple_of(d * 2 * LANES, 2 * LANES), 2 * LANES)
        cos, sin = cos_ref[:, lanes], sin_ref[:, lanes]
        weighted = packets_ref[:, wide]
        for g in range(groups):
            rows = []
            for first in range(0, own_refs, BATCH):
                place = (g * own_refs + first) * SHIFTS
                totals = jnp.dot(
                    posterior_ref[place : place + BATCH * SHIFTS, :],
                    weighted,
                    preferred_element_type=f32,
                )
                for i in range(BATCH):
                    real = totals[i * SHIFTS : (i + 1) * SHIFTS, :LANES]
                    imag = totals[i * SHIFTS : (i + 1) * SHIFTS, LANES:]
                    rows.append(fold(real * cos + imag * sin))
                    rows.append(fold(imag * cos - real * sin))
            blank = [jnp.zeros((8, LANES), f32)] * (ROWS - len(rows))
            rows = rows + blank
            sums = jnp.concatenate([row_sums(rows[:8]), row_sums(rows[8:])], axis=0)
            parts_ref[g, d] = (sums + shares[g]).astype(bf16)

    def chunks(k, carry):
        for j in range(UNROLL):
            chunk(k * UNROLL + j)
        return carry

    lax.fori_loop(0, CHUNKS // UNROLL, chunks, 0)


def back_project(place, side, odds, stats, packets, cos_table, sin_table, own_refs, rows):
    count = packets.shape[0]
    groups = odds.shape[0] // SHIFTS // own_refs
    return pl.pallas_call(
        functools.partial(back_kernel, own_refs),
        out_shape=(
            jax.ShapeDtypeStruct((groups, CHUNKS, ROWS, LANES), bf16),
            jax.ShapeDtypeStruct((1, rows), f32),
        ),
        in_specs=[pl.BlockSpec(memory_space=pltpu.SMEM)] * 2 + [whole_vmem] * 5,
        out_specs=(whole_vmem, whole_vmem),
        scratch_shapes=[pltpu.VMEM((odds.shape[0], count), bf16)],
        compiler_params=room(24),
        name="back",
    )(place, side, odds, stats, packets, cos_table, sin_table)


def finish_kernel(place_ref, parts_ref, transfer_ref, out_ref):
    own_refs = out_ref.shape[0]
    sums = jnp.sum(parts_ref[...].astype(f32), axis=0)
    share = sums[2 * own_refs : 2 * own_refs + 1] + sums[2 * own_refs + 1 : 2 * own_refs + 2]
    lane = lax.broadcasted_iota(jnp.int32, (own_refs, LANES), 1) // NCTF
    row = lax.broadcasted_iota(jnp.int32, (own_refs, LANES), 0)
    shares = jnp.where(lane == row, share, 0.0)
    own = transfer_ref[:, pl.ds(pl.multiple_of(place_ref[0] * LANES, LANES), LANES)]
    squared = jnp.concatenate([own * own] * (LANES // NCTF), axis=0)
    denominator = jnp.dot(shares, squared, precision=highest) + ridge_term
    for i in range(own_refs):
        out_ref[i] = sums[2 * i : 2 * i + 2] / denominator[i : i + 1]


def finish(place, parts, transfer, own_refs):
    return pl.pallas_call(
        finish_kernel,
        out_shape=jax.ShapeDtypeStruct((own_refs, 2, LANES), f32),
        in_specs=[pl.BlockSpec(memory_space=pltpu.SMEM)] + [whole_vmem] * 2,
        out_specs=whole_vmem,
        compiler_params=room(4),
        name="finish",
    )(place, parts, transfer)


def shifted(value, axis, steps):
    count = lax.axis_size(axis)
    pairs = [(source, (source + steps) % count) for source in range(count)]
    return lax.ppermute(value, axis, pairs)


def body(particles, classes, template_spectra, transfer_magnitude, offsets):
    rows = particles.shape[0]
    own_refs = template_spectra.shape[0]
    near_axes, far_axes = ("core", "x"), ("yh", "dom")
    near, far = lax.axis_size(near_axes), lax.axis_size(far_axes)
    packet, copies = prep(classes, particles, transfer_magnitude, template_spectra, far)
    spectra = lax.all_to_all(copies, far_axes, 0, 0)
    left, right = shifted(packet, "x", 1), shifted(packet, "x", -1)
    packets = [packet, left, shifted(left, "x", 1), right]
    place, side, part = [lax.axis_index(name)[None] for name in ("x", "core", "dom")]
    own = arrange(place, part, packets)
    other = shifted(own, "core", 1)
    cos_table, sin_table = phase_tables(offsets)
    width = packet.shape[1]
    own, other = own.reshape(-1, width), other.reshape(-1, width)
    spectra = spectra.reshape(-1, CHUNKS, own_refs, 2, LANES)
    odds, stats, weighted = make_scores(
        side, spectra, cos_table, sin_table, own, other, transfer_magnitude, own_refs, near
    )
    stats = lax.all_to_all(stats, near_axes, 0, 0)
    parts, log_own = back_project(
        place, side, odds, stats, weighted, cos_table, sin_table, own_refs, rows
    )
    parts = lax.all_to_all(parts.reshape(far, ROWS, LANES), far_axes, 0, 0)
    new_refs = finish(part, parts, transfer_magnitude, own_refs)
    return (log_own.reshape(rows), new_refs)


def solution(mesh):
    devices = mesh.devices
    names = ("yh", "x", "core", "dom")
    inner = Mesh(devices.reshape(4, 4, 2, devices.shape[1]), names)
    refs = ("yh", "x", "core")
    return jax.shard_map(
        body,
        mesh=inner,
        in_specs=(P(names, None, None), P(names), P(refs, None, "dom"), P(), P()),
        out_specs=(P(names), P(refs, None, "dom")),
        check_vma=False,
    )
```

```python
import functools
import math

import jax
import jax.numpy as jnp
from jax import lax
from jax.experimental import pallas as pl
from jax.experimental.pallas import tpu as pltpu
from jax.sharding import Mesh
from jax.sharding import PartitionSpec as P

BOX = 64
F = 2048
SHIFTS = 64
NCTF = 16
LANES = 128
CHUNKS = F // LANES
ROWS = 16
UNIT = 2
UNROLL = 4
BATCH = 2

highest = lax.Precision.HIGHEST
ridge_term = 1.0
f32 = jnp.float32
bf16 = jnp.bfloat16
whole_vmem = pl.BlockSpec(memory_space=pltpu.VMEM)


def room(mib):
    return pltpu.CompilerParams(vmem_limit_bytes=mib * 1024 * 1024)


def phase_tables(offsets):
    half_side = BOX // 2
    positions = jnp.arange(F, dtype=jnp.int32)
    row_index = positions // half_side
    freq_x = jnp.where(row_index < half_side, row_index, row_index - BOX)
    freq_y = positions % half_side
    turn_count = (offsets[:, 0:1] * freq_x[None, :] + offsets[:, 1:2] * freq_y[None, :]) % BOX
    angles = turn_count.astype(f32) * (2.0 * math.pi / BOX)
    return (jnp.cos(angles), jnp.sin(angles))


def prep_kernel(classes_ref, particles_ref, transfer_ref, spectra_ref, packet_ref, copies_ref):
    rows = particles_ref.shape[0]
    copies_ref[...] = jnp.broadcast_to(spectra_ref[...][None], copies_ref.shape)
    place = lax.broadcasted_iota(jnp.int32, (rows, 1), 0)
    labels = jnp.zeros((rows, 1), jnp.int32)
    for i in range(rows):
        labels = jnp.where(place == i, classes_ref[i], labels)
    contrast = jnp.zeros((rows, F), f32)
    for c in range(NCTF):
        contrast = jnp.where(labels == c, transfer_ref[c : c + 1, :], contrast)
    values = particles_ref[...].astype(f32)
    real = (values[:, 0, :] * contrast).astype(bf16)
    imag = (values[:, 1, :] * contrast).astype(bf16)
    for d in range(CHUNKS):
        lanes = slice(d * LANES, (d + 1) * LANES)
        packet_ref[:, 2 * d * LANES : (2 * d + 1) * LANES] = real[:, lanes]
        packet_ref[:, (2 * d + 1) * LANES : (2 * d + 2) * LANES] = imag[:, lanes]
    tags = jnp.broadcast_to(labels.astype(f32), (rows, LANES))
    packet_ref[:, 2 * F :] = tags.astype(bf16)


def prep(classes, particles, transfer, spectra, far):
    rows = particles.shape[0]
    return pl.pallas_call(
        prep_kernel,
        out_shape=(
            jax.ShapeDtypeStruct((rows, 2 * F + LANES), bf16),
            jax.ShapeDtypeStruct((far,) + spectra.shape, bf16),
        ),
        in_specs=[pl.BlockSpec(memory_space=pltpu.SMEM)] + [whole_vmem] * 3,
        out_specs=(whole_vmem, whole_vmem),
        compiler_params=room(60),
        name="prep",
    )(classes, particles, transfer, spectra)


def arrange_kernel(place_ref, side_ref, later_ref, *refs):
    count = len(refs) - 1
    for k in range(count):
        step = jnp.where(side_ref[0] == 0, count - k, k)
        refs[count][lax.rem(place_ref[0] + step, count)] = refs[k][...]


def arrange(place, side, later, packets):
    rows, width = packets[0].shape
    ordered = pl.pallas_call(
        arrange_kernel,
        out_shape=jax.ShapeDtypeStruct((len(packets), rows, width), bf16),
        in_specs=[pl.BlockSpec(memory_space=pltpu.SMEM)] * 3 + [whole_vmem] * len(packets),
        out_specs=whole_vmem,
        compiler_params=room(4),
        name="arrange",
    )(place, side, later, *packets)
    return ordered.reshape(len(packets) * rows, width)


def fold(values):
    return jnp.sum(values.reshape(values.shape[0] // 8, 8, values.shape[1]), axis=0)


def row_sums(tiles):
    row = lax.broadcasted_iota(jnp.int32, tiles[0].shape, 0)
    for bit in (1, 2, 4):
        even = (row // bit) % 2 == 0
        merged = []
        for a, b in zip(tiles[::2], tiles[1::2]):
            merged.append(
                jnp.where(even, a, b) + pltpu.roll(jnp.where(even, b, a), 8 - bit, 0)
            )
        tiles = merged
    return tiles[0]


def label_table(tags):
    lane = lax.broadcasted_iota(jnp.int32, tags.shape, 1) % NCTF
    return (tags.astype(f32) == lane.astype(f32)).astype(f32)


def score_kernel(
    own_refs,
    side_ref,
    spectra_ref,
    cos_ref,
    sin_ref,
    own_ref,
    other_ref,
    transfer_ref,
    odds_ref,
    stats_ref,
    weighted_ref,
    penalty_ref,
):
    groups = spectra_ref.shape[0]
    refs = groups * own_refs
    half = own_ref.shape[0]
    side = side_ref[0]

    own, other = own_ref[...], other_ref[...]
    weighted_ref[:half, :] = jnp.where(side == 0, own, other)
    weighted_ref[half:, :] = jnp.where(side == 0, other, own)
    odds_ref[...] = jnp.zeros_like(odds_ref)
    penalty_ref[...] = jnp.zeros_like(penalty_ref)
    width = 2 * UNIT * LANES

    def unit(u):
        wide = pl.ds(pl.multiple_of(u * width, width), width)
        weighted = weighted_ref[:, wide]
        tables = []
        for j in range(UNIT):
            lanes = pl.ds(pl.multiple_of((u * UNIT + j) * LANES, LANES), LANES)
            transfer = transfer_ref[:, lanes]
            tables.append((cos_ref[:, lanes], sin_ref[:, lanes], transfer * transfer))
        for g in range(groups):
            blocks = [spectra_ref[g, u * UNIT + j].astype(f32) for j in range(UNIT)]
            for first in range(0, own_refs, BATCH):
                rows = []
                for i in range(first, first + BATCH):
                    pieces = []
                    power = 0.0
                    for j in range(UNIT):
                        cos, sin, squared = tables[j]
                        real, imag = blocks[j][i, 0:1], blocks[j][i, 1:2]
                        pieces.append((real * cos - imag * sin).astype(bf16))
                        pieces.append((real * sin + imag * cos).astype(bf16))
                        power = power + (real * real + imag * imag) * squared
                    place = (g * own_refs + i) * NCTF
                    penalty_ref[place : place + NCTF, :] += power
                    rows.append(jnp.concatenate(pieces, axis=1))
                place = (g * own_refs + first) * SHIFTS
                odds_ref[place : place + BATCH * SHIFTS, :] += lax.dot_general(
                    jnp.concatenate(rows, axis=0),
                    weighted,
                    (((1,), (1,)), ((), ())),
                    preferred_element_type=f32,
                )

    def units(k, carry):
        for j in range(UNROLL):
            unit(k * UNROLL + j)
        return carry

    lax.fori_loop(0, CHUNKS // UNIT // UNROLL, units, 0)
    tags = weighted_ref[:, 2 * F :].astype(f32).T[:NCTF]
    hot = (tags == lax.broadcasted_iota(jnp.int32, tags.shape, 0).astype(f32)).astype(f32)
    top = None
    for r in range(refs):
        charge = jnp.sum(penalty_ref[r * NCTF : (r + 1) * NCTF, :], axis=1, keepdims=True)
        cost = 0.5 * jnp.sum(charge * hot, axis=0, keepdims=True)
        place = slice(r * SHIFTS, (r + 1) * SHIFTS)
        scores = odds_ref[place, :] - cost
        odds_ref[place, :] = scores
        high = jnp.max(scores, axis=0, keepdims=True)
        top = high if top is None else jnp.maximum(top, high)
    odds = jnp.exp(odds_ref[...] - top)
    odds_ref[...] = odds
    total = jnp.sum(odds, axis=0, keepdims=True)
    stats = jnp.concatenate([top, total], axis=0)
    stats_ref[...] = jnp.broadcast_to(stats[None], stats_ref.shape)


def make_scores(side, spectra, cos_table, sin_table, own, other, transfer, own_refs, near):
    groups = spectra.shape[0]
    refs = groups * own_refs
    count = 2 * own.shape[0]
    return pl.pallas_call(
        functools.partial(score_kernel, own_refs),
        out_shape=(
            jax.ShapeDtypeStruct((refs * SHIFTS, count), f32),
            jax.ShapeDtypeStruct((near, 2, count), f32),
            jax.ShapeDtypeStruct((count, own.shape[1]), bf16),
        ),
        in_specs=[pl.BlockSpec(memory_space=pltpu.SMEM)] + [whole_vmem] * 6,
        out_specs=(whole_vmem, whole_vmem, whole_vmem),
        scratch_shapes=[
            pltpu.VMEM((refs * NCTF, LANES), f32),
        ],
        compiler_params=room(24),
        name="scores",
    )(side, spectra, cos_table, sin_table, own, other, transfer)


def back_kernel(
    own_refs,
    slot_ref,
    odds_ref,
    stats_ref,
    packets_ref,
    cos_ref,
    sin_ref,
    parts_ref,
    log_ref,
    posterior_ref,
):
    groups = parts_ref.shape[0]
    refs = groups * own_refs
    count = odds_ref.shape[1]
    slot = slot_ref[0]
    tops, sums = stats_ref[:, 0, :count], stats_ref[:, 1, :count]
    top = jnp.max(tops, axis=0, keepdims=True)
    total = jnp.sum(sums * jnp.exp(tops - top), axis=0, keepdims=True)
    log_all = top + jnp.log(total)
    own_rows = log_ref.shape[1]
    own_log = jnp.zeros_like(log_ref)
    for k in range(count // own_rows):
        piece = log_all[:, k * own_rows : (k + 1) * own_rows]
        own_log = jnp.where(slot == k, piece, own_log)
    log_ref[...] = own_log
    scale = jnp.exp(stats_ref[slot][0:1, :count] - log_all)
    weights = []
    for r in range(refs):
        place = slice(r * SHIFTS, (r + 1) * SHIFTS)
        posterior = (odds_ref[place, :] * scale).astype(bf16)
        posterior_ref[place, :] = posterior
        weights.append(jnp.sum(posterior.astype(f32), axis=0, keepdims=True))
    weights = jnp.concatenate(weights, axis=0)
    high = weights.astype(bf16)
    low = (weights - high.astype(f32)).astype(bf16)
    hot = label_table(packets_ref[:, 2 * F :]).astype(bf16)
    spread = jnp.dot(jnp.concatenate([high, low], axis=0), hot, preferred_element_type=f32)
    spread = spread[:refs] + spread[refs:]
    lane = lax.broadcasted_iota(jnp.int32, (refs, LANES), 1) // NCTF
    row = lax.broadcasted_iota(jnp.int32, (refs, LANES), 0) % own_refs
    spread = jnp.where(lane == row, spread, 0.0)
    shares = []
    for g in range(groups):
        share = jnp.sum(spread[g * own_refs : (g + 1) * own_refs], axis=0, keepdims=True)
        high = share.astype(bf16).astype(f32)
        before = jnp.zeros((2 * own_refs, LANES), f32)
        after = jnp.zeros((ROWS - 2 * own_refs - 2, LANES), f32)
        shares.append(jnp.concatenate([before, high, share - high, after], axis=0))

    def chunk(d):
        lanes = pl.ds(pl.multiple_of(d * LANES, LANES), LANES)
        wide = pl.ds(pl.multiple_of(d * 2 * LANES, 2 * LANES), 2 * LANES)
        cos, sin = cos_ref[:, lanes], sin_ref[:, lanes]
        weighted = packets_ref[:, wide]
        for g in range(groups):
            rows = []
            for first in range(0, own_refs, BATCH):
                place = (g * own_refs + first) * SHIFTS
                totals = jnp.dot(
                    posterior_ref[place : place + BATCH * SHIFTS, :],
                    weighted,
                    preferred_element_type=f32,
                )
                for i in range(BATCH):
                    real = totals[i * SHIFTS : (i + 1) * SHIFTS, :LANES]
                    imag = totals[i * SHIFTS : (i + 1) * SHIFTS, LANES:]
                    rows.append(fold(real * cos + imag * sin))
                    rows.append(fold(imag * cos - real * sin))
            blank = [jnp.zeros((8, LANES), f32)] * (ROWS - len(rows))
            rows = rows + blank
            sums = jnp.concatenate([row_sums(rows[:8]), row_sums(rows[8:])], axis=0)
            parts_ref[g, d] = (sums + shares[g]).astype(bf16)

    def chunks(k, carry):
        for j in range(UNROLL):
            chunk(k * UNROLL + j)
        return carry

    lax.fori_loop(0, CHUNKS // UNROLL, chunks, 0)


def back_project(slot, odds, stats, packets, cos_table, sin_table, own_refs, rows):
    count = packets.shape[0]
    groups = odds.shape[0] // SHIFTS // own_refs
    return pl.pallas_call(
        functools.partial(back_kernel, own_refs),
        out_shape=(
            jax.ShapeDtypeStruct((groups, CHUNKS, ROWS, LANES), bf16),
            jax.ShapeDtypeStruct((1, rows), f32),
        ),
        in_specs=[pl.BlockSpec(memory_space=pltpu.SMEM)] + [whole_vmem] * 5,
        out_specs=(whole_vmem, whole_vmem),
        scratch_shapes=[pltpu.VMEM((odds.shape[0], count), bf16)],
        compiler_params=room(24),
        name="back",
    )(slot, odds, stats, packets, cos_table, sin_table)


def finish_kernel(place_ref, parts_ref, transfer_ref, out_ref):
    own_refs = out_ref.shape[0]
    sums = jnp.sum(parts_ref[...].astype(f32), axis=0)
    share = sums[2 * own_refs : 2 * own_refs + 1] + sums[2 * own_refs + 1 : 2 * own_refs + 2]
    lane = lax.broadcasted_iota(jnp.int32, (own_refs, LANES), 1) // NCTF
    row = lax.broadcasted_iota(jnp.int32, (own_refs, LANES), 0)
    shares = jnp.where(lane == row, share, 0.0)
    own = transfer_ref[:, pl.ds(pl.multiple_of(place_ref[0] * LANES, LANES), LANES)]
    squared = jnp.concatenate([own * own] * (LANES // NCTF), axis=0)
    denominator = jnp.dot(shares, squared, precision=highest) + ridge_term
    for i in range(own_refs):
        out_ref[i] = sums[2 * i : 2 * i + 2] / denominator[i : i + 1]


def finish(place, parts, transfer, own_refs):
    return pl.pallas_call(
        finish_kernel,
        out_shape=jax.ShapeDtypeStruct((own_refs, 2, LANES), f32),
        in_specs=[pl.BlockSpec(memory_space=pltpu.SMEM)] + [whole_vmem] * 2,
        out_specs=whole_vmem,
        compiler_params=room(4),
        name="finish",
    )(place, parts, transfer)


def shifted(value, axis, steps):
    count = lax.axis_size(axis)
    pairs = [(source, (source + steps) % count) for source in range(count)]
    return lax.ppermute(value, axis, pairs)


def parted(value, steps):
    count = lax.axis_size("x")
    pairs = []
    for source in range(count):
        pairs.append((2 * source, 2 * ((source + steps) % count)))
        pairs.append((2 * source + 1, 2 * ((source - steps) % count) + 1))
    return lax.ppermute(value, ("x", "core"), pairs)


def body(particles, classes, template_spectra, transfer_magnitude, offsets):
    rows = particles.shape[0]
    own_refs = template_spectra.shape[0]
    near_axes, far_axes = ("core", "x", "yb"), ("ya", "dom")
    near, far = lax.axis_size(near_axes), lax.axis_size(far_axes)
    packet, copies = prep(classes, particles, transfer_magnitude, template_spectra, far)
    spectra = lax.all_to_all(copies, far_axes, 0, 0)
    side, part, slot = [lax.axis_index(name)[None] for name in ("core", "dom", near_axes)]
    pair = [packet, shifted(packet, "yb", 1)]
    packet = arrange(lax.axis_index("yb")[None], side, slot, pair)
    first, second = parted(packet, 1), parted(packet, -1)
    packets = [packet, first, parted(first, 1), second]
    own = arrange(lax.axis_index("x")[None], side, part, packets)
    other = shifted(own, "core", 1)
    cos_table, sin_table = phase_tables(offsets)
    spectra = spectra.reshape(-1, CHUNKS, own_refs, 2, LANES)
    odds, stats, weighted = make_scores(
        side, spectra, cos_table, sin_table, own, other, transfer_magnitude, own_refs, near
    )
    stats = lax.all_to_all(stats, near_axes, 0, 0)
    parts, log_own = back_project(
        slot, odds, stats, weighted, cos_table, sin_table, own_refs, rows
    )
    parts = lax.all_to_all(parts.reshape(far, ROWS, LANES), far_axes, 0, 0)
    new_refs = finish(part, parts, transfer_magnitude, own_refs)
    return (log_own.reshape(rows), new_refs)


def solution(mesh):
    devices = mesh.devices
    names = ("ya", "yb", "x", "core", "dom")
    inner = Mesh(devices.reshape(2, 2, 4, 2, devices.shape[1]), names)
    refs = names[:4]
    return jax.shard_map(
        body,
        mesh=inner,
        in_specs=(P(names, None, None), P(names), P(refs, None, "dom"), P(), P()),
        out_specs=(P(names), P(refs, None, "dom")),
        check_vma=False,
    )
```

```python
import functools
import math

import jax
import jax.numpy as jnp
from jax import lax
from jax.experimental import pallas as pl
from jax.experimental.pallas import tpu as pltpu
from jax.sharding import Mesh
from jax.sharding import PartitionSpec as P

BOX = 64
F = 2048
SHIFTS = 64
NCTF = 16
LANES = 128
CHUNKS = F // LANES
ROWS = 16
UNIT = 2
UNROLL = 4
BATCH = 2

highest = lax.Precision.HIGHEST
ridge_term = 1.0
f32 = jnp.float32
bf16 = jnp.bfloat16
whole_vmem = pl.BlockSpec(memory_space=pltpu.VMEM)


def room(mib):
    return pltpu.CompilerParams(vmem_limit_bytes=mib * 1024 * 1024)


def phase_tables(offsets):
    half_side = BOX // 2
    positions = jnp.arange(F, dtype=jnp.int32)
    row_index = positions // half_side
    freq_x = jnp.where(row_index < half_side, row_index, row_index - BOX)
    freq_y = positions % half_side
    turn_count = (offsets[:, 0:1] * freq_x[None, :] + offsets[:, 1:2] * freq_y[None, :]) % BOX
    angles = turn_count.astype(f32) * (2.0 * math.pi / BOX)
    return (jnp.cos(angles), jnp.sin(angles))


def prep_kernel(classes_ref, particles_ref, transfer_ref, spectra_ref, packet_ref, copies_ref):
    rows = particles_ref.shape[0]
    copies_ref[...] = jnp.broadcast_to(spectra_ref[...][None], copies_ref.shape)
    place = lax.broadcasted_iota(jnp.int32, (rows, 1), 0)
    labels = jnp.zeros((rows, 1), jnp.int32)
    for i in range(rows):
        labels = jnp.where(place == i, classes_ref[i], labels)
    contrast = jnp.zeros((rows, F), f32)
    for c in range(NCTF):
        contrast = jnp.where(labels == c, transfer_ref[c : c + 1, :], contrast)
    values = particles_ref[...].astype(f32)
    real = (values[:, 0, :] * contrast).astype(bf16)
    imag = (values[:, 1, :] * contrast).astype(bf16)
    for d in range(CHUNKS):
        lanes = slice(d * LANES, (d + 1) * LANES)
        packet_ref[:, 2 * d * LANES : (2 * d + 1) * LANES] = real[:, lanes]
        packet_ref[:, (2 * d + 1) * LANES : (2 * d + 2) * LANES] = imag[:, lanes]
    tags = jnp.broadcast_to(labels.astype(f32), (rows, LANES))
    packet_ref[:, 2 * F :] = tags.astype(bf16)


def prep(classes, particles, transfer, spectra, far):
    rows = particles.shape[0]
    return pl.pallas_call(
        prep_kernel,
        out_shape=(
            jax.ShapeDtypeStruct((rows, 2 * F + LANES), bf16),
            jax.ShapeDtypeStruct((far,) + spectra.shape, bf16),
        ),
        in_specs=[pl.BlockSpec(memory_space=pltpu.SMEM)] + [whole_vmem] * 3,
        out_specs=(whole_vmem, whole_vmem),
        compiler_params=room(60),
        name="prep",
    )(classes, particles, transfer, spectra)


def arrange_kernel(place_ref, side_ref, part_ref, slot_ref, *refs):
    count = len(refs) - 1
    for k in range(count):
        step = jnp.where(side_ref[0] == 0, count - k, k)
        refs[count][lax.rem(place_ref[0] + step, count)] = refs[k][...]


def arrange(place, side, part, slot, packets):
    rows, width = packets[0].shape
    ordered = pl.pallas_call(
        arrange_kernel,
        out_shape=jax.ShapeDtypeStruct((len(packets), rows, width), bf16),
        in_specs=[pl.BlockSpec(memory_space=pltpu.SMEM)] * 4 + [whole_vmem] * len(packets),
        out_specs=whole_vmem,
        compiler_params=room(4),
        name="arrange",
    )(place, side, part, slot, *packets)
    return ordered.reshape(len(packets) * rows, width)


def fold(values):
    return jnp.sum(values.reshape(values.shape[0] // 8, 8, values.shape[1]), axis=0)


def row_sums(tiles):
    row = lax.broadcasted_iota(jnp.int32, tiles[0].shape, 0)
    for bit in (1, 2, 4):
        even = (row // bit) % 2 == 0
        merged = []
        for a, b in zip(tiles[::2], tiles[1::2]):
            merged.append(
                jnp.where(even, a, b) + pltpu.roll(jnp.where(even, b, a), 8 - bit, 0)
            )
        tiles = merged
    return tiles[0]


def label_table(tags):
    lane = lax.broadcasted_iota(jnp.int32, tags.shape, 1) % NCTF
    return (tags.astype(f32) == lane.astype(f32)).astype(f32)


def score_kernel(
    own_refs,
    side_ref,
    spectra_ref,
    cos_ref,
    sin_ref,
    own_ref,
    other_ref,
    transfer_ref,
    odds_ref,
    stats_ref,
    weighted_ref,
    penalty_ref,
):
    groups = spectra_ref.shape[0]
    refs = groups * own_refs
    half = own_ref.shape[0]
    side = side_ref[0]

    own, other = own_ref[...], other_ref[...]
    weighted_ref[:half, :] = jnp.where(side == 0, own, other)
    weighted_ref[half:, :] = jnp.where(side == 0, other, own)
    odds_ref[...] = jnp.zeros_like(odds_ref)
    penalty_ref[...] = jnp.zeros_like(penalty_ref)
    width = 2 * UNIT * LANES

    def unit(u):
        wide = pl.ds(pl.multiple_of(u * width, width), width)
        weighted = weighted_ref[:, wide]
        tables = []
        for j in range(UNIT):
            lanes = pl.ds(pl.multiple_of((u * UNIT + j) * LANES, LANES), LANES)
            transfer = transfer_ref[:, lanes]
            tables.append((cos_ref[:, lanes], sin_ref[:, lanes], transfer * transfer))
        for g in range(groups):
            blocks = [spectra_ref[g, u * UNIT + j].astype(f32) for j in range(UNIT)]
            for first in range(0, own_refs, BATCH):
                rows = []
                for i in range(first, first + BATCH):
                    pieces = []
                    power = 0.0
                    for j in range(UNIT):
                        cos, sin, squared = tables[j]
                        real, imag = blocks[j][i, 0:1], blocks[j][i, 1:2]
                        pieces.append((real * cos - imag * sin).astype(bf16))
                        pieces.append((real * sin + imag * cos).astype(bf16))
                        power = power + (real * real + imag * imag) * squared
                    place = (g * own_refs + i) * NCTF
                    penalty_ref[place : place + NCTF, :] += power
                    rows.append(jnp.concatenate(pieces, axis=1))
                place = (g * own_refs + first) * SHIFTS
                odds_ref[place : place + BATCH * SHIFTS, :] += lax.dot_general(
                    jnp.concatenate(rows, axis=0),
                    weighted,
                    (((1,), (1,)), ((), ())),
                    preferred_element_type=f32,
                )

    def units(k, carry):
        for j in range(UNROLL):
            unit(k * UNROLL + j)
        return carry

    lax.fori_loop(0, CHUNKS // UNIT // UNROLL, units, 0)
    tags = weighted_ref[:, 2 * F :].astype(f32).T[:NCTF]
    hot = (tags == lax.broadcasted_iota(jnp.int32, tags.shape, 0).astype(f32)).astype(f32)
    top = None
    for r in range(refs):
        charge = jnp.sum(penalty_ref[r * NCTF : (r + 1) * NCTF, :], axis=1, keepdims=True)
        cost = 0.5 * jnp.sum(charge * hot, axis=0, keepdims=True)
        place = slice(r * SHIFTS, (r + 1) * SHIFTS)
        scores = odds_ref[place, :] - cost
        odds_ref[place, :] = scores
        high = jnp.max(scores, axis=0, keepdims=True)
        top = high if top is None else jnp.maximum(top, high)
    odds = jnp.exp(odds_ref[...] - top)
    odds_ref[...] = odds
    total = jnp.sum(odds, axis=0, keepdims=True)
    stats = jnp.concatenate([top, total], axis=0)
    spare = jnp.zeros((2, LANES - stats.shape[1]), f32)
    stats = jnp.concatenate([stats, spare], axis=1)
    stats_ref[...] = jnp.broadcast_to(stats[None], stats_ref.shape)


def make_scores(side, spectra, cos_table, sin_table, own, other, transfer, own_refs, near):
    groups = spectra.shape[0]
    refs = groups * own_refs
    count = 2 * own.shape[0]
    return pl.pallas_call(
        functools.partial(score_kernel, own_refs),
        out_shape=(
            jax.ShapeDtypeStruct((refs * SHIFTS, count), f32),
            jax.ShapeDtypeStruct((near, 2, LANES), f32),
            jax.ShapeDtypeStruct((count, own.shape[1]), bf16),
        ),
        in_specs=[pl.BlockSpec(memory_space=pltpu.SMEM)] + [whole_vmem] * 6,
        out_specs=(whole_vmem, whole_vmem, whole_vmem),
        scratch_shapes=[
            pltpu.VMEM((refs * NCTF, LANES), f32),
        ],
        compiler_params=room(24),
        name="scores",
    )(side, spectra, cos_table, sin_table, own, other, transfer)


def back_kernel(
    own_refs,
    slot_ref,
    odds_ref,
    stats_ref,
    packets_ref,
    cos_ref,
    sin_ref,
    parts_ref,
    log_ref,
    posterior_ref,
):
    groups = parts_ref.shape[0] // CHUNKS
    refs = groups * own_refs
    count = odds_ref.shape[1]
    slot = slot_ref[0]
    tops, sums = stats_ref[:, 0, :count], stats_ref[:, 1, :count]
    top = jnp.max(tops, axis=0, keepdims=True)
    total = jnp.sum(sums * jnp.exp(tops - top), axis=0, keepdims=True)
    log_all = top + jnp.log(total)
    own_rows = log_ref.shape[1]
    own_log = jnp.zeros_like(log_ref)
    for k in range(count // own_rows):
        piece = log_all[:, k * own_rows : (k + 1) * own_rows]
        own_log = jnp.where(slot == k, piece, own_log)
    log_ref[...] = own_log
    scale = jnp.exp(stats_ref[slot][0:1, :count] - log_all)
    weights = []
    for r in range(refs):
        place = slice(r * SHIFTS, (r + 1) * SHIFTS)
        posterior = (odds_ref[place, :] * scale).astype(bf16)
        posterior_ref[place, :] = posterior
        weights.append(jnp.sum(posterior.astype(f32), axis=0, keepdims=True))
    weights = jnp.concatenate(weights, axis=0)
    high = weights.astype(bf16)
    low = (weights - high.astype(f32)).astype(bf16)
    hot = label_table(packets_ref[:, 2 * F :]).astype(bf16)
    spread = jnp.dot(jnp.concatenate([high, low], axis=0), hot, preferred_element_type=f32)
    spread = spread[:refs] + spread[refs:]
    lane = lax.broadcasted_iota(jnp.int32, (refs, LANES), 1) // NCTF
    row = lax.broadcasted_iota(jnp.int32, (refs, LANES), 0) % own_refs
    spread = jnp.where(lane == row, spread, 0.0)
    shares = []
    for g in range(groups):
        share = jnp.sum(spread[g * own_refs : (g + 1) * own_refs], axis=0, keepdims=True)
        high = share.astype(bf16).astype(f32)
        before = jnp.zeros((2 * own_refs, LANES), f32)
        after = jnp.zeros((ROWS - 2 * own_refs - 2, LANES), f32)
        shares.append(jnp.concatenate([before, high, share - high, after], axis=0))

    def chunk(d):
        lanes = pl.ds(pl.multiple_of(d * LANES, LANES), LANES)
        wide = pl.ds(pl.multiple_of(d * 2 * LANES, 2 * LANES), 2 * LANES)
        cos, sin = cos_ref[:, lanes], sin_ref[:, lanes]
        weighted = packets_ref[:, wide]
        for g in range(groups):
            rows = []
            for first in range(0, own_refs, BATCH):
                place = (g * own_refs + first) * SHIFTS
                totals = jnp.dot(
                    posterior_ref[place : place + BATCH * SHIFTS, :],
                    weighted,
                    preferred_element_type=f32,
                )
                for i in range(BATCH):
                    real = totals[i * SHIFTS : (i + 1) * SHIFTS, :LANES]
                    imag = totals[i * SHIFTS : (i + 1) * SHIFTS, LANES:]
                    rows.append(fold(real * cos + imag * sin))
                    rows.append(fold(imag * cos - real * sin))
            blank = [jnp.zeros((8, LANES), f32)] * (ROWS - len(rows))
            rows = rows + blank
            sums = jnp.concatenate([row_sums(rows[:8]), row_sums(rows[8:])], axis=0)
            line = (CHUNKS // 2 - 1 - d // 2) * 2 * groups + 2 * g + d % 2
            parts_ref[line] = (sums + shares[g]).astype(bf16)

    def chunks(k, carry):
        for j in range(UNROLL):
            chunk(k * UNROLL + j)
        return carry

    lax.fori_loop(0, CHUNKS // UNROLL, chunks, 0)


def back_project(slot, odds, stats, packets, cos_table, sin_table, own_refs, rows):
    count = packets.shape[0]
    groups = odds.shape[0] // SHIFTS // own_refs
    return pl.pallas_call(
        functools.partial(back_kernel, own_refs),
        out_shape=(
            jax.ShapeDtypeStruct((groups * CHUNKS, ROWS, LANES), bf16),
            jax.ShapeDtypeStruct((1, rows), f32),
        ),
        in_specs=[pl.BlockSpec(memory_space=pltpu.SMEM)] + [whole_vmem] * 5,
        out_specs=(whole_vmem, whole_vmem),
        scratch_shapes=[pltpu.VMEM((odds.shape[0], count), bf16)],
        compiler_params=room(24),
        name="back",
    )(slot, odds, stats, packets, cos_table, sin_table)


def finish_kernel(place_ref, parts_ref, transfer_ref, out_ref):
    own_refs = out_ref.shape[0]
    sums = jnp.sum(parts_ref[...].astype(f32), axis=0)
    share = sums[2 * own_refs : 2 * own_refs + 1] + sums[2 * own_refs + 1 : 2 * own_refs + 2]
    lane = lax.broadcasted_iota(jnp.int32, (own_refs, LANES), 1) // NCTF
    row = lax.broadcasted_iota(jnp.int32, (own_refs, LANES), 0)
    shares = jnp.where(lane == row, share, 0.0)
    own = transfer_ref[:, pl.ds(pl.multiple_of(place_ref[0] * LANES, LANES), LANES)]
    squared = jnp.concatenate([own * own] * (LANES // NCTF), axis=0)
    denominator = jnp.dot(shares, squared, precision=highest) + ridge_term
    for i in range(own_refs):
        out_ref[i] = sums[2 * i : 2 * i + 2] / denominator[i : i + 1]


def finish(place, parts, transfer, own_refs):
    return pl.pallas_call(
        finish_kernel,
        out_shape=jax.ShapeDtypeStruct((own_refs, 2, LANES), f32),
        in_specs=[pl.BlockSpec(memory_space=pltpu.SMEM)] + [whole_vmem] * 2,
        out_specs=whole_vmem,
        compiler_params=room(4),
        name="finish",
    )(place, parts, transfer)


def shifted(value, axis, steps):
    count = lax.axis_size(axis)
    pairs = [(source, (source + steps) % count) for source in range(count)]
    return lax.ppermute(value, axis, pairs)


def parted(value, steps):
    count = lax.axis_size("x")
    pairs = []
    for source in range(count):
        pairs.append((2 * source, 2 * ((source + steps) % count)))
        pairs.append((2 * source + 1, 2 * ((source - steps) % count) + 1))
    return lax.ppermute(value, ("x", "core"), pairs)


def early_first(yh, dom):
    order = []
    for z in reversed(range(dom // 2)):
        for y in range(yh):
            order += [y * dom + 2 * z, y * dom + 2 * z + 1]
    return [order]


def body(particles, classes, template_spectra, transfer_magnitude, offsets):
    rows = particles.shape[0]
    own_refs = template_spectra.shape[0]
    near_axes, far_axes = ("core", "x"), ("yh", "dom")
    near, far = lax.axis_size(near_axes), lax.axis_size(far_axes)
    packet, copies = prep(classes, particles, transfer_magnitude, template_spectra, far)
    spectra = lax.all_to_all(copies, far_axes, 0, 0)
    place, side, part = [lax.axis_index(name)[None] for name in ("x", "core", "dom")]
    slot = lax.axis_index(near_axes)[None]
    second, first, third = parted(packet, 2), parted(packet, 1), parted(packet, 3)
    own = arrange(place, side, part, slot, [packet, first, second, third])
    other = shifted(own, "core", 1)
    cos_table, sin_table = phase_tables(offsets)
    spectra = spectra.reshape(-1, CHUNKS, own_refs, 2, LANES)
    odds, stats, weighted = make_scores(
        side, spectra, cos_table, sin_table, own, other, transfer_magnitude, own_refs, near
    )
    stats = lax.all_to_all(stats, near_axes, 0, 0)
    parts, log_own = back_project(
        slot, odds, stats, weighted, cos_table, sin_table, own_refs, rows
    )
    order = early_first(lax.axis_size("yh"), lax.axis_size("dom"))
    parts = lax.all_to_all(parts, far_axes, 0, 0, axis_index_groups=order)
    new_refs = finish(part, parts, transfer_magnitude, own_refs)
    return (log_own.reshape(rows), new_refs)


def solution(mesh):
    devices = mesh.devices
    names = ("yh", "x", "core", "dom")
    inner = Mesh(devices.reshape(4, 4, 2, devices.shape[1]), names)
    refs = names[:3]
    return jax.shard_map(
        body,
        mesh=inner,
        in_specs=(P(names, None, None), P(names), P(refs, None, "dom"), P(), P()),
        out_specs=(P(names), P(refs, None, "dom")),
        check_vma=False,
    )
```

```python
import functools
import math

import jax
import jax.numpy as jnp
from jax import lax
from jax.experimental import pallas as pl
from jax.experimental.pallas import tpu as pltpu
from jax.sharding import Mesh
from jax.sharding import PartitionSpec as P

BOX = 64
F = 2048
SHIFTS = 64
NCTF = 16
LANES = 128
CHUNKS = F // LANES
ROWS = 16
UNIT = 2
UNROLL = 4
BATCH = 2

highest = lax.Precision.HIGHEST
ridge_term = 1.0
f32 = jnp.float32
bf16 = jnp.bfloat16
whole_vmem = pl.BlockSpec(memory_space=pltpu.VMEM)


def room(mib):
    return pltpu.CompilerParams(vmem_limit_bytes=mib * 1024 * 1024)


def phase_tables(offsets):
    half_side = BOX // 2
    positions = jnp.arange(F, dtype=jnp.int32)
    row_index = positions // half_side
    freq_x = jnp.where(row_index < half_side, row_index, row_index - BOX)
    freq_y = positions % half_side
    turn_count = (offsets[:, 0:1] * freq_x[None, :] + offsets[:, 1:2] * freq_y[None, :]) % BOX
    angles = turn_count.astype(f32) * (2.0 * math.pi / BOX)
    return (jnp.cos(angles), jnp.sin(angles))


def prep_kernel(classes_ref, particles_ref, transfer_ref, spectra_ref, packet_ref, copies_ref):
    rows = particles_ref.shape[0]
    copies_ref[...] = jnp.broadcast_to(spectra_ref[...][None], copies_ref.shape)
    place = lax.broadcasted_iota(jnp.int32, (rows, 1), 0)
    labels = jnp.zeros((rows, 1), jnp.int32)
    for i in range(rows):
        labels = jnp.where(place == i, classes_ref[i], labels)
    contrast = jnp.zeros((rows, F), f32)
    for c in range(NCTF):
        contrast = jnp.where(labels == c, transfer_ref[c : c + 1, :], contrast)
    values = particles_ref[...].astype(f32)
    real = (values[:, 0, :] * contrast).astype(bf16)
    imag = (values[:, 1, :] * contrast).astype(bf16)
    for d in range(CHUNKS):
        lanes = slice(d * LANES, (d + 1) * LANES)
        packet_ref[:, 2 * d * LANES : (2 * d + 1) * LANES] = real[:, lanes]
        packet_ref[:, (2 * d + 1) * LANES : (2 * d + 2) * LANES] = imag[:, lanes]
    tags = jnp.broadcast_to(labels.astype(f32), (rows, LANES))
    packet_ref[:, 2 * F :] = tags.astype(bf16)


def prep(classes, particles, transfer, spectra, far):
    rows = particles.shape[0]
    return pl.pallas_call(
        prep_kernel,
        out_shape=(
            jax.ShapeDtypeStruct((rows, 2 * F + LANES), bf16),
            jax.ShapeDtypeStruct((far,) + spectra.shape, bf16),
        ),
        in_specs=[pl.BlockSpec(memory_space=pltpu.SMEM)] + [whole_vmem] * 3,
        out_specs=(whole_vmem, whole_vmem),
        compiler_params=room(60),
        name="prep",
    )(classes, particles, transfer, spectra)


def arrange_kernel(place_ref, side_ref, part_ref, slot_ref, *refs):
    count = len(refs) - 1
    for k in range(count):
        step = jnp.where(side_ref[0] == 0, count - k, k)
        refs[count][lax.rem(place_ref[0] + step, count)] = refs[k][...]


def arrange(place, side, part, slot, packets):
    rows, width = packets[0].shape
    ordered = pl.pallas_call(
        arrange_kernel,
        out_shape=jax.ShapeDtypeStruct((len(packets), rows, width), bf16),
        in_specs=[pl.BlockSpec(memory_space=pltpu.SMEM)] * 4 + [whole_vmem] * len(packets),
        out_specs=whole_vmem,
        compiler_params=room(4),
        name="arrange",
    )(place, side, part, slot, *packets)
    return ordered.reshape(len(packets) * rows, width)


def fold(values):
    return jnp.sum(values.reshape(values.shape[0] // 8, 8, values.shape[1]), axis=0)


def row_sums(tiles):
    row = lax.broadcasted_iota(jnp.int32, tiles[0].shape, 0)
    for bit in (1, 2, 4):
        even = (row // bit) % 2 == 0
        merged = []
        for a, b in zip(tiles[::2], tiles[1::2]):
            merged.append(
                jnp.where(even, a, b) + pltpu.roll(jnp.where(even, b, a), 8 - bit, 0)
            )
        tiles = merged
    return tiles[0]


def label_table(tags):
    lane = lax.broadcasted_iota(jnp.int32, tags.shape, 1) % NCTF
    return (tags.astype(f32) == lane.astype(f32)).astype(f32)


def score_kernel(
    own_refs,
    side_ref,
    spectra_ref,
    cos_ref,
    sin_ref,
    own_ref,
    other_ref,
    transfer_ref,
    odds_ref,
    stats_ref,
    weighted_ref,
    penalty_ref,
):
    groups = spectra_ref.shape[0] // CHUNKS
    refs = groups * own_refs
    half = own_ref.shape[0]
    side = side_ref[0]

    own, other = own_ref[...], other_ref[...]
    weighted_ref[:half, :] = jnp.where(side == 0, own, other)
    weighted_ref[half:, :] = jnp.where(side == 0, other, own)
    odds_ref[...] = jnp.zeros_like(odds_ref)
    penalty_ref[...] = jnp.zeros_like(penalty_ref)
    width = 2 * UNIT * LANES

    def unit(u):
        wide = pl.ds(pl.multiple_of(u * width, width), width)
        weighted = weighted_ref[:, wide]
        tables = []
        for j in range(UNIT):
            lanes = pl.ds(pl.multiple_of((u * UNIT + j) * LANES, LANES), LANES)
            transfer = transfer_ref[:, lanes]
            tables.append((cos_ref[:, lanes], sin_ref[:, lanes], transfer * transfer))
        for g in range(groups):
            blocks = []
            for j in range(UNIT):
                d = u * UNIT + j
                blocks.append(spectra_ref[(d // 2) * 2 * groups + 2 * g + d % 2].astype(f32))
            for first in range(0, own_refs, BATCH):
                rows = []
                for i in range(first, first + BATCH):
                    pieces = []
                    power = 0.0
                    for j in range(UNIT):
                        cos, sin, squared = tables[j]
                        real, imag = blocks[j][i, 0:1], blocks[j][i, 1:2]
                        pieces.append((real * cos - imag * sin).astype(bf16))
                        pieces.append((real * sin + imag * cos).astype(bf16))
                        power = power + (real * real + imag * imag) * squared
                    place = (g * own_refs + i) * NCTF
                    penalty_ref[place : place + NCTF, :] += power
                    rows.append(jnp.concatenate(pieces, axis=1))
                place = (g * own_refs + first) * SHIFTS
                odds_ref[place : place + BATCH * SHIFTS, :] += lax.dot_general(
                    jnp.concatenate(rows, axis=0),
                    weighted,
                    (((1,), (1,)), ((), ())),
                    preferred_element_type=f32,
                )

    def units(k, carry):
        for j in range(UNROLL):
            unit(k * UNROLL + j)
        return carry

    lax.fori_loop(0, CHUNKS // UNIT // UNROLL, units, 0)
    tags = weighted_ref[:, 2 * F :].astype(f32).T[:NCTF]
    hot = (tags == lax.broadcasted_iota(jnp.int32, tags.shape, 0).astype(f32)).astype(f32)
    top = None
    for r in range(refs):
        charge = jnp.sum(penalty_ref[r * NCTF : (r + 1) * NCTF, :], axis=1, keepdims=True)
        cost = 0.5 * jnp.sum(charge * hot, axis=0, keepdims=True)
        place = slice(r * SHIFTS, (r + 1) * SHIFTS)
        scores = odds_ref[place, :] - cost
        odds_ref[place, :] = scores
        high = jnp.max(scores, axis=0, keepdims=True)
        top = high if top is None else jnp.maximum(top, high)
    odds = jnp.exp(odds_ref[...] - top)
    odds_ref[...] = odds
    total = jnp.sum(odds, axis=0, keepdims=True)
    stats = jnp.concatenate([top, total], axis=0)
    spare = jnp.zeros((2, LANES - stats.shape[1]), f32)
    stats = jnp.concatenate([stats, spare], axis=1)
    stats_ref[...] = jnp.broadcast_to(stats[None], stats_ref.shape)


def make_scores(side, spectra, cos_table, sin_table, own, other, transfer, own_refs, near):
    groups = spectra.shape[0] // CHUNKS
    refs = groups * own_refs
    count = 2 * own.shape[0]
    return pl.pallas_call(
        functools.partial(score_kernel, own_refs),
        out_shape=(
            jax.ShapeDtypeStruct((refs * SHIFTS, count), f32),
            jax.ShapeDtypeStruct((near, 2, LANES), f32),
            jax.ShapeDtypeStruct((count, own.shape[1]), bf16),
        ),
        in_specs=[pl.BlockSpec(memory_space=pltpu.SMEM)] + [whole_vmem] * 6,
        out_specs=(whole_vmem, whole_vmem, whole_vmem),
        scratch_shapes=[
            pltpu.VMEM((refs * NCTF, LANES), f32),
        ],
        compiler_params=room(24),
        name="scores",
    )(side, spectra, cos_table, sin_table, own, other, transfer)


def back_kernel(
    own_refs,
    slot_ref,
    odds_ref,
    stats_ref,
    packets_ref,
    cos_ref,
    sin_ref,
    parts_ref,
    log_ref,
    posterior_ref,
):
    groups = parts_ref.shape[0] // CHUNKS
    refs = groups * own_refs
    count = odds_ref.shape[1]
    slot = slot_ref[0]
    tops, sums = stats_ref[:, 0, :count], stats_ref[:, 1, :count]
    top = jnp.max(tops, axis=0, keepdims=True)
    total = jnp.sum(sums * jnp.exp(tops - top), axis=0, keepdims=True)
    log_all = top + jnp.log(total)
    own_rows = log_ref.shape[1]
    own_log = jnp.zeros_like(log_ref)
    for k in range(count // own_rows):
        piece = log_all[:, k * own_rows : (k + 1) * own_rows]
        own_log = jnp.where(slot == k, piece, own_log)
    log_ref[...] = own_log
    scale = jnp.exp(stats_ref[slot][0:1, :count] - log_all)
    weights = []
    for r in range(refs):
        place = slice(r * SHIFTS, (r + 1) * SHIFTS)
        posterior = (odds_ref[place, :] * scale).astype(bf16)
        posterior_ref[place, :] = posterior
        weights.append(jnp.sum(posterior.astype(f32), axis=0, keepdims=True))
    weights = jnp.concatenate(weights, axis=0)
    high = weights.astype(bf16)
    low = (weights - high.astype(f32)).astype(bf16)
    hot = label_table(packets_ref[:, 2 * F :]).astype(bf16)
    spread = jnp.dot(jnp.concatenate([high, low], axis=0), hot, preferred_element_type=f32)
    spread = spread[:refs] + spread[refs:]
    lane = lax.broadcasted_iota(jnp.int32, (refs, LANES), 1) // NCTF
    row = lax.broadcasted_iota(jnp.int32, (refs, LANES), 0) % own_refs
    spread = jnp.where(lane == row, spread, 0.0)
    shares = []
    for g in range(groups):
        share = jnp.sum(spread[g * own_refs : (g + 1) * own_refs], axis=0, keepdims=True)
        high = share.astype(bf16).astype(f32)
        before = jnp.zeros((2 * own_refs, LANES), f32)
        after = jnp.zeros((ROWS - 2 * own_refs - 2, LANES), f32)
        shares.append(jnp.concatenate([before, high, share - high, after], axis=0))

    def chunk(d):
        lanes = pl.ds(pl.multiple_of(d * LANES, LANES), LANES)
        wide = pl.ds(pl.multiple_of(d * 2 * LANES, 2 * LANES), 2 * LANES)
        cos, sin = cos_ref[:, lanes], sin_ref[:, lanes]
        weighted = packets_ref[:, wide]
        for g in range(groups):
            rows = []
            for first in range(0, own_refs, BATCH):
                place = (g * own_refs + first) * SHIFTS
                totals = jnp.dot(
                    posterior_ref[place : place + BATCH * SHIFTS, :],
                    weighted,
                    preferred_element_type=f32,
                )
                for i in range(BATCH):
                    real = totals[i * SHIFTS : (i + 1) * SHIFTS, :LANES]
                    imag = totals[i * SHIFTS : (i + 1) * SHIFTS, LANES:]
                    rows.append(fold(real * cos + imag * sin))
                    rows.append(fold(imag * cos - real * sin))
            blank = [jnp.zeros((8, LANES), f32)] * (ROWS - len(rows))
            rows = rows + blank
            sums = jnp.concatenate([row_sums(rows[:8]), row_sums(rows[8:])], axis=0)
            line = (CHUNKS // 2 - 1 - d // 2) * 2 * groups + 2 * g + d % 2
            parts_ref[line] = (sums + shares[g]).astype(bf16)

    def chunks(k, carry):
        for j in range(UNROLL):
            chunk(k * UNROLL + j)
        return carry

    lax.fori_loop(0, CHUNKS // UNROLL, chunks, 0)


def back_project(slot, odds, stats, packets, cos_table, sin_table, own_refs, rows):
    count = packets.shape[0]
    groups = odds.shape[0] // SHIFTS // own_refs
    return pl.pallas_call(
        functools.partial(back_kernel, own_refs),
        out_shape=(
            jax.ShapeDtypeStruct((groups * CHUNKS, ROWS, LANES), bf16),
            jax.ShapeDtypeStruct((1, rows), f32),
        ),
        in_specs=[pl.BlockSpec(memory_space=pltpu.SMEM)] + [whole_vmem] * 5,
        out_specs=(whole_vmem, whole_vmem),
        scratch_shapes=[pltpu.VMEM((odds.shape[0], count), bf16)],
        compiler_params=room(24),
        name="back",
    )(slot, odds, stats, packets, cos_table, sin_table)


def finish_kernel(place_ref, parts_ref, transfer_ref, out_ref):
    own_refs = out_ref.shape[0]
    sums = jnp.sum(parts_ref[...].astype(f32), axis=0)
    share = sums[2 * own_refs : 2 * own_refs + 1] + sums[2 * own_refs + 1 : 2 * own_refs + 2]
    lane = lax.broadcasted_iota(jnp.int32, (own_refs, LANES), 1) // NCTF
    row = lax.broadcasted_iota(jnp.int32, (own_refs, LANES), 0)
    shares = jnp.where(lane == row, share, 0.0)
    own = transfer_ref[:, pl.ds(pl.multiple_of(place_ref[0] * LANES, LANES), LANES)]
    squared = jnp.concatenate([own * own] * (LANES // NCTF), axis=0)
    denominator = jnp.dot(shares, squared, precision=highest) + ridge_term
    for i in range(own_refs):
        out_ref[i] = sums[2 * i : 2 * i + 2] / denominator[i : i + 1]


def finish(place, parts, transfer, own_refs):
    return pl.pallas_call(
        finish_kernel,
        out_shape=jax.ShapeDtypeStruct((own_refs, 2, LANES), f32),
        in_specs=[pl.BlockSpec(memory_space=pltpu.SMEM)] + [whole_vmem] * 2,
        out_specs=whole_vmem,
        compiler_params=room(4),
        name="finish",
    )(place, parts, transfer)


def shifted(value, axis, steps):
    count = lax.axis_size(axis)
    pairs = [(source, (source + steps) % count) for source in range(count)]
    return lax.ppermute(value, axis, pairs)


def parted(value, steps):
    count = lax.axis_size("x")
    pairs = []
    for source in range(count):
        pairs.append((2 * source, 2 * ((source + steps) % count)))
        pairs.append((2 * source + 1, 2 * ((source - steps) % count) + 1))
    return lax.ppermute(value, ("x", "core"), pairs)


def by_z(yh, dom, backwards):
    order = []
    for z in reversed(range(dom // 2)) if backwards else range(dom // 2):
        for y in range(yh):
            order += [y * dom + 2 * z, y * dom + 2 * z + 1]
    return [order]


def body(particles, classes, template_spectra, transfer_magnitude, offsets):
    rows = particles.shape[0]
    own_refs = template_spectra.shape[0]
    near_axes, far_axes = ("core", "x"), ("yh", "dom")
    near, far = lax.axis_size(near_axes), lax.axis_size(far_axes)
    packet, copies = prep(classes, particles, transfer_magnitude, template_spectra, far)
    sizes = [lax.axis_size(name) for name in far_axes]
    spectra = lax.all_to_all(copies, far_axes, 0, 0, axis_index_groups=by_z(*sizes, False))
    place, side, part = [lax.axis_index(name)[None] for name in ("x", "core", "dom")]
    slot = lax.axis_index(near_axes)[None]
    second, first = parted(packet, 2), parted(packet, 1)
    packet, first = lax.optimization_barrier((packet, first))
    third = parted(packet, 3)
    own = arrange(place, side, part, slot, [packet, first, second, third])
    other = shifted(own, "core", 1)
    cos_table, sin_table = phase_tables(offsets)
    odds, stats, weighted = make_scores(
        side, spectra, cos_table, sin_table, own, other, transfer_magnitude, own_refs, near
    )
    stats = lax.all_to_all(stats, near_axes, 0, 0)
    parts, log_own = back_project(
        slot, odds, stats, weighted, cos_table, sin_table, own_refs, rows
    )
    parts = lax.all_to_all(parts, far_axes, 0, 0, axis_index_groups=by_z(*sizes, True))
    new_refs = finish(part, parts, transfer_magnitude, own_refs)
    return (log_own.reshape(rows), new_refs)


def solution(mesh):
    devices = mesh.devices
    names = ("yh", "x", "core", "dom")
    inner = Mesh(devices.reshape(4, 4, 2, devices.shape[1]), names)
    refs = names[:3]
    return jax.shard_map(
        body,
        mesh=inner,
        in_specs=(P(names, None, None), P(names), P(refs, None, "dom"), P(), P()),
        out_specs=(P(names), P(refs, None, "dom")),
        check_vma=False,
    )
```

```python
import functools
import math

import jax
import jax.numpy as jnp
from jax import lax
from jax.experimental import pallas as pl
from jax.experimental.pallas import tpu as pltpu
from jax.sharding import Mesh
from jax.sharding import PartitionSpec as P

BOX = 64
F = 2048
SHIFTS = 64
NCTF = 16
LANES = 128
CHUNKS = F // LANES
ROWS = 16
UNIT = 2
UNROLL = 4
BATCH = 2

highest = lax.Precision.HIGHEST
ridge_term = 1.0
f32 = jnp.float32
bf16 = jnp.bfloat16
whole_vmem = pl.BlockSpec(memory_space=pltpu.VMEM)


def room(mib):
    return pltpu.CompilerParams(vmem_limit_bytes=mib * 1024 * 1024)


def phase_tables(offsets):
    half_side = BOX // 2
    positions = jnp.arange(F, dtype=jnp.int32)
    row_index = positions // half_side
    freq_x = jnp.where(row_index < half_side, row_index, row_index - BOX)
    freq_y = positions % half_side
    turn_count = (offsets[:, 0:1] * freq_x[None, :] + offsets[:, 1:2] * freq_y[None, :]) % BOX
    angles = turn_count.astype(f32) * (2.0 * math.pi / BOX)
    return (jnp.cos(angles), jnp.sin(angles))


def prep_kernel(classes_ref, particles_ref, transfer_ref, spectra_ref, packet_ref, copies_ref):
    rows = particles_ref.shape[0]
    copies_ref[...] = jnp.broadcast_to(spectra_ref[...][None], copies_ref.shape)
    place = lax.broadcasted_iota(jnp.int32, (rows, 1), 0)
    labels = jnp.zeros((rows, 1), jnp.int32)
    for i in range(rows):
        labels = jnp.where(place == i, classes_ref[i], labels)
    contrast = jnp.zeros((rows, F), f32)
    for c in range(NCTF):
        contrast = jnp.where(labels == c, transfer_ref[c : c + 1, :], contrast)
    values = particles_ref[...].astype(f32)
    real = (values[:, 0, :] * contrast).astype(bf16)
    imag = (values[:, 1, :] * contrast).astype(bf16)
    for d in range(CHUNKS):
        lanes = slice(d * LANES, (d + 1) * LANES)
        packet_ref[:, 2 * d * LANES : (2 * d + 1) * LANES] = real[:, lanes]
        packet_ref[:, (2 * d + 1) * LANES : (2 * d + 2) * LANES] = imag[:, lanes]
    tags = jnp.broadcast_to(labels.astype(f32), (rows, LANES))
    packet_ref[:, 2 * F :] = tags.astype(bf16)


def prep(classes, particles, transfer, spectra, far):
    rows = particles.shape[0]
    return pl.pallas_call(
        prep_kernel,
        out_shape=(
            jax.ShapeDtypeStruct((rows, 2 * F + LANES), bf16),
            jax.ShapeDtypeStruct((far,) + spectra.shape, bf16),
        ),
        in_specs=[pl.BlockSpec(memory_space=pltpu.SMEM)] + [whole_vmem] * 3,
        out_specs=(whole_vmem, whole_vmem),
        compiler_params=room(60),
        name="prep",
    )(classes, particles, transfer, spectra)


def arrange_kernel(place_ref, side_ref, part_ref, slot_ref, *refs):
    count = len(refs) - 1
    for k in range(count):
        step = jnp.where(side_ref[0] == 0, count - k, k)
        refs[count][lax.rem(place_ref[0] + step, count)] = refs[k][...]


def arrange(place, side, part, slot, packets):
    rows, width = packets[0].shape
    ordered = pl.pallas_call(
        arrange_kernel,
        out_shape=jax.ShapeDtypeStruct((len(packets), rows, width), bf16),
        in_specs=[pl.BlockSpec(memory_space=pltpu.SMEM)] * 4 + [whole_vmem] * len(packets),
        out_specs=whole_vmem,
        compiler_params=room(4),
        name="arrange",
    )(place, side, part, slot, *packets)
    return ordered.reshape(len(packets) * rows, width)


def fold(values):
    return jnp.sum(values.reshape(values.shape[0] // 8, 8, values.shape[1]), axis=0)


def row_sums(tiles):
    row = lax.broadcasted_iota(jnp.int32, tiles[0].shape, 0)
    for bit in (1, 2, 4):
        even = (row // bit) % 2 == 0
        merged = []
        for a, b in zip(tiles[::2], tiles[1::2]):
            merged.append(
                jnp.where(even, a, b) + pltpu.roll(jnp.where(even, b, a), 8 - bit, 0)
            )
        tiles = merged
    return tiles[0]


def label_table(tags):
    lane = lax.broadcasted_iota(jnp.int32, tags.shape, 1) % NCTF
    return (tags.astype(f32) == lane.astype(f32)).astype(f32)


def score_kernel(
    own_refs,
    side_ref,
    spectra_ref,
    cos_ref,
    sin_ref,
    own_ref,
    other_ref,
    transfer_ref,
    odds_ref,
    stats_ref,
    weighted_ref,
    penalty_ref,
):
    groups = spectra_ref.shape[0]
    refs = groups * own_refs
    half = own_ref.shape[0]
    side = side_ref[0]

    own, other = own_ref[...], other_ref[...]
    weighted_ref[:half, :] = jnp.where(side == 0, own, other)
    weighted_ref[half:, :] = jnp.where(side == 0, other, own)
    odds_ref[...] = jnp.zeros_like(odds_ref)
    penalty_ref[...] = jnp.zeros_like(penalty_ref)
    width = 2 * UNIT * LANES

    def unit(u):
        wide = pl.ds(pl.multiple_of(u * width, width), width)
        weighted = weighted_ref[:, wide]
        tables = []
        for j in range(UNIT):
            lanes = pl.ds(pl.multiple_of((u * UNIT + j) * LANES, LANES), LANES)
            transfer = transfer_ref[:, lanes]
            tables.append((cos_ref[:, lanes], sin_ref[:, lanes], transfer * transfer))
        for g in range(groups):
            blocks = [spectra_ref[g, u * UNIT + j].astype(f32) for j in range(UNIT)]
            for first in range(0, own_refs, BATCH):
                rows = []
                for i in range(first, first + BATCH):
                    pieces = []
                    power = 0.0
                    for j in range(UNIT):
                        cos, sin, squared = tables[j]
                        real, imag = blocks[j][i, 0:1], blocks[j][i, 1:2]
                        pieces.append((real * cos - imag * sin).astype(bf16))
                        pieces.append((real * sin + imag * cos).astype(bf16))
                        power = power + (real * real + imag * imag) * squared
                    place = (g * own_refs + i) * NCTF
                    penalty_ref[place : place + NCTF, :] += power
                    rows.append(jnp.concatenate(pieces, axis=1))
                place = (g * own_refs + first) * SHIFTS
                odds_ref[place : place + BATCH * SHIFTS, :] += lax.dot_general(
                    jnp.concatenate(rows, axis=0),
                    weighted,
                    (((1,), (1,)), ((), ())),
                    preferred_element_type=f32,
                )

    def units(k, carry):
        for j in range(UNROLL):
            unit(k * UNROLL + j)
        return carry

    lax.fori_loop(0, CHUNKS // UNIT // UNROLL, units, 0)
    tags = weighted_ref[:, 2 * F :].astype(f32).T[:NCTF]
    hot = (tags == lax.broadcasted_iota(jnp.int32, tags.shape, 0).astype(f32)).astype(f32)
    top = None
    for r in range(refs):
        charge = jnp.sum(penalty_ref[r * NCTF : (r + 1) * NCTF, :], axis=1, keepdims=True)
        cost = 0.5 * jnp.sum(charge * hot, axis=0, keepdims=True)
        place = slice(r * SHIFTS, (r + 1) * SHIFTS)
        scores = odds_ref[place, :] - cost
        odds_ref[place, :] = scores
        high = jnp.max(scores, axis=0, keepdims=True)
        top = high if top is None else jnp.maximum(top, high)
    odds = jnp.exp(odds_ref[...] - top)
    odds_ref[...] = odds
    total = jnp.sum(odds, axis=0, keepdims=True)
    stats = jnp.concatenate([top, total], axis=0)
    spare = jnp.zeros((2, LANES - stats.shape[1]), f32)
    stats = jnp.concatenate([stats, spare], axis=1)
    stats_ref[...] = jnp.broadcast_to(stats[None], stats_ref.shape)


def make_scores(side, spectra, cos_table, sin_table, own, other, transfer, own_refs, near):
    groups = spectra.shape[0]
    refs = groups * own_refs
    count = 2 * own.shape[0]
    return pl.pallas_call(
        functools.partial(score_kernel, own_refs),
        out_shape=(
            jax.ShapeDtypeStruct((refs * SHIFTS, count), f32),
            jax.ShapeDtypeStruct((near, 2, LANES), f32),
            jax.ShapeDtypeStruct((count, own.shape[1]), bf16),
        ),
        in_specs=[pl.BlockSpec(memory_space=pltpu.SMEM)] + [whole_vmem] * 6,
        out_specs=(whole_vmem, whole_vmem, whole_vmem),
        scratch_shapes=[
            pltpu.VMEM((refs * NCTF, LANES), f32),
        ],
        compiler_params=room(24),
        name="scores",
    )(side, spectra, cos_table, sin_table, own, other, transfer)


def back_kernel(
    own_refs,
    slot_ref,
    odds_ref,
    stats_ref,
    packets_ref,
    cos_ref,
    sin_ref,
    parts_ref,
    log_ref,
    posterior_ref,
):
    groups = parts_ref.shape[0] // CHUNKS
    refs = groups * own_refs
    count = odds_ref.shape[1]
    slot = slot_ref[0]
    tops, sums = stats_ref[:, 0, :count], stats_ref[:, 1, :count]
    top = jnp.max(tops, axis=0, keepdims=True)
    total = jnp.sum(sums * jnp.exp(tops - top), axis=0, keepdims=True)
    log_all = top + jnp.log(total)
    own_rows = log_ref.shape[1]
    own_log = jnp.zeros_like(log_ref)
    for k in range(count // own_rows):
        piece = log_all[:, k * own_rows : (k + 1) * own_rows]
        own_log = jnp.where(slot == k, piece, own_log)
    log_ref[...] = own_log
    scale = jnp.exp(stats_ref[slot][0:1, :count] - log_all)
    weights = []
    for r in range(refs):
        place = slice(r * SHIFTS, (r + 1) * SHIFTS)
        posterior = (odds_ref[place, :] * scale).astype(bf16)
        posterior_ref[place, :] = posterior
        weights.append(jnp.sum(posterior.astype(f32), axis=0, keepdims=True))
    weights = jnp.concatenate(weights, axis=0)
    high = weights.astype(bf16)
    low = (weights - high.astype(f32)).astype(bf16)
    hot = label_table(packets_ref[:, 2 * F :]).astype(bf16)
    spread = jnp.dot(jnp.concatenate([high, low], axis=0), hot, preferred_element_type=f32)
    spread = spread[:refs] + spread[refs:]
    lane = lax.broadcasted_iota(jnp.int32, (refs, LANES), 1) // NCTF
    row = lax.broadcasted_iota(jnp.int32, (refs, LANES), 0) % own_refs
    spread = jnp.where(lane == row, spread, 0.0)
    shares = []
    for g in range(groups):
        share = jnp.sum(spread[g * own_refs : (g + 1) * own_refs], axis=0, keepdims=True)
        high = share.astype(bf16).astype(f32)
        before = jnp.zeros((2 * own_refs, LANES), f32)
        after = jnp.zeros((ROWS - 2 * own_refs - 2, LANES), f32)
        shares.append(jnp.concatenate([before, high, share - high, after], axis=0))

    def chunk(d):
        lanes = pl.ds(pl.multiple_of(d * LANES, LANES), LANES)
        wide = pl.ds(pl.multiple_of(d * 2 * LANES, 2 * LANES), 2 * LANES)
        cos, sin = cos_ref[:, lanes], sin_ref[:, lanes]
        weighted = packets_ref[:, wide]
        for g in range(groups):
            rows = []
            for first in range(0, own_refs, BATCH):
                place = (g * own_refs + first) * SHIFTS
                totals = jnp.dot(
                    posterior_ref[place : place + BATCH * SHIFTS, :],
                    weighted,
                    preferred_element_type=f32,
                )
                for i in range(BATCH):
                    real = totals[i * SHIFTS : (i + 1) * SHIFTS, :LANES]
                    imag = totals[i * SHIFTS : (i + 1) * SHIFTS, LANES:]
                    rows.append(fold(real * cos + imag * sin))
                    rows.append(fold(imag * cos - real * sin))
            blank = [jnp.zeros((8, LANES), f32)] * (ROWS - len(rows))
            rows = rows + blank
            sums = jnp.concatenate([row_sums(rows[:8]), row_sums(rows[8:])], axis=0)
            line = (CHUNKS // 2 - 1 - d // 2) * 2 * groups + 2 * g + d % 2
            parts_ref[line] = (sums + shares[g]).astype(bf16)

    def chunks(k, carry):
        for j in range(UNROLL):
            chunk(k * UNROLL + j)
        return carry

    lax.fori_loop(0, CHUNKS // UNROLL, chunks, 0)


def back_project(slot, odds, stats, packets, cos_table, sin_table, own_refs, rows):
    count = packets.shape[0]
    groups = odds.shape[0] // SHIFTS // own_refs
    return pl.pallas_call(
        functools.partial(back_kernel, own_refs),
        out_shape=(
            jax.ShapeDtypeStruct((groups * CHUNKS, ROWS, LANES), bf16),
            jax.ShapeDtypeStruct((1, rows), f32),
        ),
        in_specs=[pl.BlockSpec(memory_space=pltpu.SMEM)] + [whole_vmem] * 5,
        out_specs=(whole_vmem, whole_vmem),
        scratch_shapes=[pltpu.VMEM((odds.shape[0], count), bf16)],
        compiler_params=room(24),
        name="back",
    )(slot, odds, stats, packets, cos_table, sin_table)


def finish_kernel(place_ref, parts_ref, transfer_ref, out_ref):
    own_refs = out_ref.shape[0]
    sums = jnp.sum(parts_ref[...].astype(f32), axis=0)
    share = sums[2 * own_refs : 2 * own_refs + 1] + sums[2 * own_refs + 1 : 2 * own_refs + 2]
    lane = lax.broadcasted_iota(jnp.int32, (own_refs, LANES), 1) // NCTF
    row = lax.broadcasted_iota(jnp.int32, (own_refs, LANES), 0)
    shares = jnp.where(lane == row, share, 0.0)
    own = transfer_ref[:, pl.ds(pl.multiple_of(place_ref[0] * LANES, LANES), LANES)]
    squared = jnp.concatenate([own * own] * (LANES // NCTF), axis=0)
    denominator = jnp.dot(shares, squared, precision=highest) + ridge_term
    for i in range(own_refs):
        out_ref[i] = sums[2 * i : 2 * i + 2] / denominator[i : i + 1]


def finish(place, parts, transfer, own_refs):
    return pl.pallas_call(
        finish_kernel,
        out_shape=jax.ShapeDtypeStruct((own_refs, 2, LANES), f32),
        in_specs=[pl.BlockSpec(memory_space=pltpu.SMEM)] + [whole_vmem] * 2,
        out_specs=whole_vmem,
        compiler_params=room(4),
        name="finish",
    )(place, parts, transfer)


def shifted(value, axis, steps):
    count = lax.axis_size(axis)
    pairs = [(source, (source + steps) % count) for source in range(count)]
    return lax.ppermute(value, axis, pairs)


def parted(value, steps):
    count = lax.axis_size("x")
    pairs = []
    for source in range(count):
        pairs.append((2 * source, 2 * ((source + steps) % count)))
        pairs.append((2 * source + 1, 2 * ((source - steps) % count) + 1))
    return lax.ppermute(value, ("x", "core"), pairs)


def early_first(yh, dom):
    order = []
    for z in reversed(range(dom // 2)):
        for y in range(yh):
            order += [y * dom + 2 * z, y * dom + 2 * z + 1]
    return [order]


def body(particles, classes, template_spectra, transfer_magnitude, offsets):
    rows = particles.shape[0]
    own_refs = template_spectra.shape[0]
    near_axes, far_axes = ("core", "x"), ("yh", "dom")
    near, far = lax.axis_size(near_axes), lax.axis_size(far_axes)
    packet, copies = prep(classes, particles, transfer_magnitude, template_spectra, far)
    spectra = lax.all_to_all(copies, far_axes, 0, 0)
    place, side, part = [lax.axis_index(name)[None] for name in ("x", "core", "dom")]
    slot = lax.axis_index(near_axes)[None]
    first, third = parted(packet, 1), parted(packet, 3)
    second = parted(first, 1)
    own = arrange(place, side, part, slot, [packet, first, second, third])
    other = shifted(own, "core", 1)
    cos_table, sin_table = phase_tables(offsets)
    spectra = spectra.reshape(-1, CHUNKS, own_refs, 2, LANES)
    odds, stats, weighted = make_scores(
        side, spectra, cos_table, sin_table, own, other, transfer_magnitude, own_refs, near
    )
    stats = lax.all_to_all(stats, near_axes, 0, 0)
    parts, log_own = back_project(
        slot, odds, stats, weighted, cos_table, sin_table, own_refs, rows
    )
    order = early_first(lax.axis_size("yh"), lax.axis_size("dom"))
    parts = lax.all_to_all(parts, far_axes, 0, 0, axis_index_groups=order)
    new_refs = finish(part, parts, transfer_magnitude, own_refs)
    return (log_own.reshape(rows), new_refs)


def solution(mesh):
    devices = mesh.devices
    names = ("yh", "x", "core", "dom")
    inner = Mesh(devices.reshape(4, 4, 2, devices.shape[1]), names)
    refs = names[:3]
    return jax.shard_map(
        body,
        mesh=inner,
        in_specs=(P(names, None, None), P(names), P(refs, None, "dom"), P(), P()),
        out_specs=(P(names), P(refs, None, "dom")),
        check_vma=False,
    )
```

```python
import functools
import math

import jax
import jax.numpy as jnp
from jax import lax
from jax.experimental import pallas as pl
from jax.experimental.pallas import tpu as pltpu
from jax.sharding import Mesh
from jax.sharding import PartitionSpec as P

BOX = 64
F = 2048
SHIFTS = 64
NCTF = 16
LANES = 128
CHUNKS = F // LANES
ROWS = 16
UNIT = 2
UNROLL = 4
BATCH = 2

highest = lax.Precision.HIGHEST
ridge_term = 1.0
f32 = jnp.float32
bf16 = jnp.bfloat16
whole_vmem = pl.BlockSpec(memory_space=pltpu.VMEM)


def room(mib):
    return pltpu.CompilerParams(vmem_limit_bytes=mib * 1024 * 1024)


def phase_tables(offsets):
    half_side = BOX // 2
    positions = jnp.arange(F, dtype=jnp.int32)
    row_index = positions // half_side
    freq_x = jnp.where(row_index < half_side, row_index, row_index - BOX)
    freq_y = positions % half_side
    turn_count = (offsets[:, 0:1] * freq_x[None, :] + offsets[:, 1:2] * freq_y[None, :]) % BOX
    angles = turn_count.astype(f32) * (2.0 * math.pi / BOX)
    return (jnp.cos(angles), jnp.sin(angles))


def prep_kernel(classes_ref, particles_ref, transfer_ref, spectra_ref, packet_ref, copies_ref):
    rows = particles_ref.shape[0]
    copies_ref[...] = jnp.broadcast_to(spectra_ref[...][None], copies_ref.shape)
    place = lax.broadcasted_iota(jnp.int32, (rows, 1), 0)
    labels = jnp.zeros((rows, 1), jnp.int32)
    for i in range(rows):
        labels = jnp.where(place == i, classes_ref[i], labels)
    contrast = jnp.zeros((rows, F), f32)
    for c in range(NCTF):
        contrast = jnp.where(labels == c, transfer_ref[c : c + 1, :], contrast)
    values = particles_ref[...].astype(f32)
    real = (values[:, 0, :] * contrast).astype(bf16)
    imag = (values[:, 1, :] * contrast).astype(bf16)
    for d in range(CHUNKS):
        lanes = slice(d * LANES, (d + 1) * LANES)
        packet_ref[:, 2 * d * LANES : (2 * d + 1) * LANES] = real[:, lanes]
        packet_ref[:, (2 * d + 1) * LANES : (2 * d + 2) * LANES] = imag[:, lanes]
    tags = jnp.broadcast_to(labels.astype(f32), (rows, LANES))
    packet_ref[:, 2 * F :] = tags.astype(bf16)


def prep(classes, particles, transfer, spectra, far):
    rows = particles.shape[0]
    return pl.pallas_call(
        prep_kernel,
        out_shape=(
            jax.ShapeDtypeStruct((rows, 2 * F + LANES), bf16),
            jax.ShapeDtypeStruct((far,) + spectra.shape, bf16),
        ),
        in_specs=[pl.BlockSpec(memory_space=pltpu.SMEM)] + [whole_vmem] * 3,
        out_specs=(whole_vmem, whole_vmem),
        compiler_params=room(60),
        name="prep",
    )(classes, particles, transfer, spectra)


def arrange_kernel(place_ref, side_ref, part_ref, slot_ref, *refs):
    count = len(refs) - 1
    for k in range(count):
        step = jnp.where(side_ref[0] == 0, count - k, k)
        refs[count][lax.rem(place_ref[0] + step, count)] = refs[k][...]


def arrange(place, side, part, slot, packets):
    rows, width = packets[0].shape
    ordered = pl.pallas_call(
        arrange_kernel,
        out_shape=jax.ShapeDtypeStruct((len(packets), rows, width), bf16),
        in_specs=[pl.BlockSpec(memory_space=pltpu.SMEM)] * 4 + [whole_vmem] * len(packets),
        out_specs=whole_vmem,
        compiler_params=room(4),
        name="arrange",
    )(place, side, part, slot, *packets)
    return ordered.reshape(len(packets) * rows, width)


def fold(values):
    return jnp.sum(values.reshape(values.shape[0] // 8, 8, values.shape[1]), axis=0)


def row_sums(tiles):
    row = lax.broadcasted_iota(jnp.int32, tiles[0].shape, 0)
    for bit in (1, 2, 4):
        even = (row // bit) % 2 == 0
        merged = []
        for a, b in zip(tiles[::2], tiles[1::2]):
            merged.append(
                jnp.where(even, a, b) + pltpu.roll(jnp.where(even, b, a), 8 - bit, 0)
            )
        tiles = merged
    return tiles[0]


def label_table(tags):
    lane = lax.broadcasted_iota(jnp.int32, tags.shape, 1) % NCTF
    return (tags.astype(f32) == lane.astype(f32)).astype(f32)


def score_kernel(
    own_refs,
    side_ref,
    spectra_ref,
    cos_ref,
    sin_ref,
    own_ref,
    other_ref,
    transfer_ref,
    odds_ref,
    stats_ref,
    weighted_ref,
    penalty_ref,
):
    groups = spectra_ref.shape[0] // CHUNKS
    refs = groups * own_refs
    half = own_ref.shape[0]
    side = side_ref[0]

    own, other = own_ref[...], other_ref[...]
    weighted_ref[:half, :] = jnp.where(side == 0, own, other)
    weighted_ref[half:, :] = jnp.where(side == 0, other, own)
    odds_ref[...] = jnp.zeros_like(odds_ref)
    penalty_ref[...] = jnp.zeros_like(penalty_ref)
    width = 2 * UNIT * LANES

    def unit(u):
        wide = pl.ds(pl.multiple_of(u * width, width), width)
        weighted = weighted_ref[:, wide]
        tables = []
        for j in range(UNIT):
            lanes = pl.ds(pl.multiple_of((u * UNIT + j) * LANES, LANES), LANES)
            transfer = transfer_ref[:, lanes]
            tables.append((cos_ref[:, lanes], sin_ref[:, lanes], transfer * transfer))
        for g in range(groups):
            blocks = []
            for j in range(UNIT):
                d = u * UNIT + j
                line = diagonal(side, 2 * g + d % 2, d // 2, CHUNKS // 2)
                blocks.append(spectra_ref[line].astype(f32))
            for first in range(0, own_refs, BATCH):
                rows = []
                for i in range(first, first + BATCH):
                    pieces = []
                    power = 0.0
                    for j in range(UNIT):
                        cos, sin, squared = tables[j]
                        real, imag = blocks[j][i, 0:1], blocks[j][i, 1:2]
                        pieces.append((real * cos - imag * sin).astype(bf16))
                        pieces.append((real * sin + imag * cos).astype(bf16))
                        power = power + (real * real + imag * imag) * squared
                    place = (g * own_refs + i) * NCTF
                    penalty_ref[place : place + NCTF, :] += power
                    rows.append(jnp.concatenate(pieces, axis=1))
                place = (g * own_refs + first) * SHIFTS
                odds_ref[place : place + BATCH * SHIFTS, :] += lax.dot_general(
                    jnp.concatenate(rows, axis=0),
                    weighted,
                    (((1,), (1,)), ((), ())),
                    preferred_element_type=f32,
                )

    def units(k, carry):
        for j in range(UNROLL):
            unit(k * UNROLL + j)
        return carry

    lax.fori_loop(0, CHUNKS // UNIT // UNROLL, units, 0)
    tags = weighted_ref[:, 2 * F :].astype(f32).T[:NCTF]
    hot = (tags == lax.broadcasted_iota(jnp.int32, tags.shape, 0).astype(f32)).astype(f32)
    top = None
    for r in range(refs):
        charge = jnp.sum(penalty_ref[r * NCTF : (r + 1) * NCTF, :], axis=1, keepdims=True)
        cost = 0.5 * jnp.sum(charge * hot, axis=0, keepdims=True)
        place = slice(r * SHIFTS, (r + 1) * SHIFTS)
        scores = odds_ref[place, :] - cost
        odds_ref[place, :] = scores
        high = jnp.max(scores, axis=0, keepdims=True)
        top = high if top is None else jnp.maximum(top, high)
    odds = jnp.exp(odds_ref[...] - top)
    odds_ref[...] = odds
    total = jnp.sum(odds, axis=0, keepdims=True)
    stats = jnp.concatenate([top, total], axis=0)
    spare = jnp.zeros((2, LANES - stats.shape[1]), f32)
    stats = jnp.concatenate([stats, spare], axis=1)
    stats_ref[...] = jnp.broadcast_to(stats[None], stats_ref.shape)


def make_scores(side, spectra, cos_table, sin_table, own, other, transfer, own_refs, near):
    groups = spectra.shape[0] // CHUNKS
    refs = groups * own_refs
    count = 2 * own.shape[0]
    return pl.pallas_call(
        functools.partial(score_kernel, own_refs),
        out_shape=(
            jax.ShapeDtypeStruct((refs * SHIFTS, count), f32),
            jax.ShapeDtypeStruct((near, 2, LANES), f32),
            jax.ShapeDtypeStruct((count, own.shape[1]), bf16),
        ),
        in_specs=[pl.BlockSpec(memory_space=pltpu.SMEM)] + [whole_vmem] * 6,
        out_specs=(whole_vmem, whole_vmem, whole_vmem),
        scratch_shapes=[
            pltpu.VMEM((refs * NCTF, LANES), f32),
        ],
        compiler_params=room(24),
        name="scores",
    )(side, spectra, cos_table, sin_table, own, other, transfer)


def back_kernel(
    own_refs,
    side_ref,
    slot_ref,
    odds_ref,
    stats_ref,
    packets_ref,
    cos_ref,
    sin_ref,
    parts_ref,
    log_ref,
    posterior_ref,
):
    groups = parts_ref.shape[0] // CHUNKS
    refs = groups * own_refs
    count = odds_ref.shape[1]
    slot = slot_ref[0]
    tops, sums = stats_ref[:, 0, :count], stats_ref[:, 1, :count]
    top = jnp.max(tops, axis=0, keepdims=True)
    total = jnp.sum(sums * jnp.exp(tops - top), axis=0, keepdims=True)
    log_all = top + jnp.log(total)
    own_rows = log_ref.shape[1]
    own_log = jnp.zeros_like(log_ref)
    for k in range(count // own_rows):
        piece = log_all[:, k * own_rows : (k + 1) * own_rows]
        own_log = jnp.where(slot == k, piece, own_log)
    log_ref[...] = own_log
    scale = jnp.exp(stats_ref[slot][0:1, :count] - log_all)
    weights = []
    for r in range(refs):
        place = slice(r * SHIFTS, (r + 1) * SHIFTS)
        posterior = (odds_ref[place, :] * scale).astype(bf16)
        posterior_ref[place, :] = posterior
        weights.append(jnp.sum(posterior.astype(f32), axis=0, keepdims=True))
    weights = jnp.concatenate(weights, axis=0)
    high = weights.astype(bf16)
    low = (weights - high.astype(f32)).astype(bf16)
    hot = label_table(packets_ref[:, 2 * F :]).astype(bf16)
    spread = jnp.dot(jnp.concatenate([high, low], axis=0), hot, preferred_element_type=f32)
    spread = spread[:refs] + spread[refs:]
    lane = lax.broadcasted_iota(jnp.int32, (refs, LANES), 1) // NCTF
    row = lax.broadcasted_iota(jnp.int32, (refs, LANES), 0) % own_refs
    spread = jnp.where(lane == row, spread, 0.0)
    shares = []
    for g in range(groups):
        share = jnp.sum(spread[g * own_refs : (g + 1) * own_refs], axis=0, keepdims=True)
        high = share.astype(bf16).astype(f32)
        before = jnp.zeros((2 * own_refs, LANES), f32)
        after = jnp.zeros((ROWS - 2 * own_refs - 2, LANES), f32)
        shares.append(jnp.concatenate([before, high, share - high, after], axis=0))

    def chunk(d):
        lanes = pl.ds(pl.multiple_of(d * LANES, LANES), LANES)
        wide = pl.ds(pl.multiple_of(d * 2 * LANES, 2 * LANES), 2 * LANES)
        cos, sin = cos_ref[:, lanes], sin_ref[:, lanes]
        weighted = packets_ref[:, wide]
        for g in range(groups):
            rows = []
            for first in range(0, own_refs, BATCH):
                place = (g * own_refs + first) * SHIFTS
                totals = jnp.dot(
                    posterior_ref[place : place + BATCH * SHIFTS, :],
                    weighted,
                    preferred_element_type=f32,
                )
                for i in range(BATCH):
                    real = totals[i * SHIFTS : (i + 1) * SHIFTS, :LANES]
                    imag = totals[i * SHIFTS : (i + 1) * SHIFTS, LANES:]
                    rows.append(fold(real * cos + imag * sin))
                    rows.append(fold(imag * cos - real * sin))
            blank = [jnp.zeros((8, LANES), f32)] * (ROWS - len(rows))
            rows = rows + blank
            sums = jnp.concatenate([row_sums(rows[:8]), row_sums(rows[8:])], axis=0)
            line = diagonal(side_ref[0], 2 * g + d % 2, d // 2, CHUNKS // 2)
            parts_ref[line] = (sums + shares[g]).astype(bf16)

    def chunks(k, carry):
        for j in range(UNROLL):
            chunk(k * UNROLL + j)
        return carry

    lax.fori_loop(0, CHUNKS // UNROLL, chunks, 0)


def back_project(side, slot, odds, stats, packets, cos_table, sin_table, own_refs, rows):
    count = packets.shape[0]
    groups = odds.shape[0] // SHIFTS // own_refs
    return pl.pallas_call(
        functools.partial(back_kernel, own_refs),
        out_shape=(
            jax.ShapeDtypeStruct((groups * CHUNKS, ROWS, LANES), bf16),
            jax.ShapeDtypeStruct((1, rows), f32),
        ),
        in_specs=[pl.BlockSpec(memory_space=pltpu.SMEM)] * 2 + [whole_vmem] * 5,
        out_specs=(whole_vmem, whole_vmem),
        scratch_shapes=[pltpu.VMEM((odds.shape[0], count), bf16)],
        compiler_params=room(24),
        name="back",
    )(side, slot, odds, stats, packets, cos_table, sin_table)


def finish_kernel(place_ref, parts_ref, transfer_ref, out_ref):
    own_refs = out_ref.shape[0]
    sums = jnp.sum(parts_ref[...].astype(f32), axis=0)
    share = sums[2 * own_refs : 2 * own_refs + 1] + sums[2 * own_refs + 1 : 2 * own_refs + 2]
    lane = lax.broadcasted_iota(jnp.int32, (own_refs, LANES), 1) // NCTF
    row = lax.broadcasted_iota(jnp.int32, (own_refs, LANES), 0)
    shares = jnp.where(lane == row, share, 0.0)
    own = transfer_ref[:, pl.ds(pl.multiple_of(place_ref[0] * LANES, LANES), LANES)]
    squared = jnp.concatenate([own * own] * (LANES // NCTF), axis=0)
    denominator = jnp.dot(shares, squared, precision=highest) + ridge_term
    for i in range(own_refs):
        out_ref[i] = sums[2 * i : 2 * i + 2] / denominator[i : i + 1]


def finish(place, parts, transfer, own_refs):
    return pl.pallas_call(
        finish_kernel,
        out_shape=jax.ShapeDtypeStruct((own_refs, 2, LANES), f32),
        in_specs=[pl.BlockSpec(memory_space=pltpu.SMEM)] + [whole_vmem] * 2,
        out_specs=whole_vmem,
        compiler_params=room(4),
        name="finish",
    )(place, parts, transfer)


def shifted(value, axis, steps):
    count = lax.axis_size(axis)
    pairs = [(source, (source + steps) % count) for source in range(count)]
    return lax.ppermute(value, axis, pairs)


def parted(value, steps):
    count = lax.axis_size("x")
    pairs = []
    for source in range(count):
        pairs.append((2 * source, 2 * ((source + steps) % count)))
        pairs.append((2 * source + 1, 2 * ((source - steps) % count) + 1))
    return lax.ppermute(value, ("x", "core"), pairs)


def diagonal(side, row, plane, count):
    return count * ((row - plane + count + side * (count // 2)) % count) + plane


def wide_groups(yh, dom):
    count = dom // 2
    groups = []
    for side in range(2):
        group = [0] * (yh * dom)
        for y in range(yh):
            for d in range(dom):
                group[diagonal(side, 2 * y + d % 2, d // 2, count)] = side * yh * dom + y * dom + d
        groups.append(group)
    return groups


def wide_exchange(value):
    groups = wide_groups(lax.axis_size("yh"), lax.axis_size("dom"))
    return lax.all_to_all(value, ("core", "yh", "dom"), 0, 0, axis_index_groups=groups)


def body(particles, classes, template_spectra, transfer_magnitude, offsets):
    rows = particles.shape[0]
    own_refs = template_spectra.shape[0]
    near_axes = ("core", "x")
    near, far = lax.axis_size(near_axes), lax.axis_size(("yh", "dom"))
    packet, copies = prep(classes, particles, transfer_magnitude, template_spectra, far)
    spectra = wide_exchange(copies)
    place, side, part = [lax.axis_index(name)[None] for name in ("x", "core", "dom")]
    slot = lax.axis_index(near_axes)[None]
    second, first, third = parted(packet, 2), parted(packet, 1), parted(packet, 3)
    own = arrange(place, side, part, slot, [packet, first, second, third])
    other = shifted(own, "core", 1)
    cos_table, sin_table = phase_tables(offsets)
    odds, stats, weighted = make_scores(
        side, spectra, cos_table, sin_table, own, other, transfer_magnitude, own_refs, near
    )
    stats = lax.all_to_all(stats, near_axes, 0, 0)
    parts, log_own = back_project(
        side, slot, odds, stats, weighted, cos_table, sin_table, own_refs, rows
    )
    parts = wide_exchange(parts)
    new_refs = finish(part, parts, transfer_magnitude, own_refs)
    return (log_own.reshape(rows), new_refs)


def solution(mesh):
    devices = mesh.devices
    names = ("yh", "x", "core", "dom")
    inner = Mesh(devices.reshape(4, 4, 2, devices.shape[1]), names)
    refs = names[:3]
    return jax.shard_map(
        body,
        mesh=inner,
        in_specs=(P(names, None, None), P(names), P(refs, None, "dom"), P(), P()),
        out_specs=(P(names), P(refs, None, "dom")),
        check_vma=False,
    )
```

```python
import functools
import math

import jax
import jax.numpy as jnp
from jax import lax
from jax.experimental import pallas as pl
from jax.experimental.pallas import tpu as pltpu
from jax.sharding import Mesh
from jax.sharding import PartitionSpec as P

BOX = 64
F = 2048
SHIFTS = 64
NCTF = 16
LANES = 128
CHUNKS = F // LANES
ROWS = 16
UNIT = 2
UNROLL = 4
BATCH = 2

highest = lax.Precision.HIGHEST
ridge_term = 1.0
f32 = jnp.float32
bf16 = jnp.bfloat16
whole_vmem = pl.BlockSpec(memory_space=pltpu.VMEM)


def room(mib):
    return pltpu.CompilerParams(vmem_limit_bytes=mib * 1024 * 1024)


def phase_tables(offsets):
    half_side = BOX // 2
    positions = jnp.arange(F, dtype=jnp.int32)
    row_index = positions // half_side
    freq_x = jnp.where(row_index < half_side, row_index, row_index - BOX)
    freq_y = positions % half_side
    turn_count = (offsets[:, 0:1] * freq_x[None, :] + offsets[:, 1:2] * freq_y[None, :]) % BOX
    angles = turn_count.astype(f32) * (2.0 * math.pi / BOX)
    return (jnp.cos(angles), jnp.sin(angles))


def prep_kernel(classes_ref, particles_ref, transfer_ref, spectra_ref, packet_ref, copies_ref):
    rows = particles_ref.shape[0]
    copies_ref[...] = jnp.broadcast_to(spectra_ref[...][None], copies_ref.shape)
    place = lax.broadcasted_iota(jnp.int32, (rows, 1), 0)
    labels = jnp.zeros((rows, 1), jnp.int32)
    for i in range(rows):
        labels = jnp.where(place == i, classes_ref[i], labels)
    contrast = jnp.zeros((rows, F), f32)
    for c in range(NCTF):
        contrast = jnp.where(labels == c, transfer_ref[c : c + 1, :], contrast)
    values = particles_ref[...].astype(f32)
    real = (values[:, 0, :] * contrast).astype(bf16)
    imag = (values[:, 1, :] * contrast).astype(bf16)
    for d in range(CHUNKS):
        lanes = slice(d * LANES, (d + 1) * LANES)
        packet_ref[:, 2 * d * LANES : (2 * d + 1) * LANES] = real[:, lanes]
        packet_ref[:, (2 * d + 1) * LANES : (2 * d + 2) * LANES] = imag[:, lanes]
    tags = jnp.broadcast_to(labels.astype(f32), (rows, LANES))
    packet_ref[:, 2 * F :] = tags.astype(bf16)


def prep(classes, particles, transfer, spectra, far):
    rows = particles.shape[0]
    return pl.pallas_call(
        prep_kernel,
        out_shape=(
            jax.ShapeDtypeStruct((rows, 2 * F + LANES), bf16),
            jax.ShapeDtypeStruct((far,) + spectra.shape, bf16),
        ),
        in_specs=[pl.BlockSpec(memory_space=pltpu.SMEM)] + [whole_vmem] * 3,
        out_specs=(whole_vmem, whole_vmem),
        compiler_params=room(60),
        name="prep",
    )(classes, particles, transfer, spectra)


def arrange_kernel(place_ref, side_ref, part_ref, slot_ref, *refs):
    count = len(refs) - 1
    for k in range(count):
        step = jnp.where(side_ref[0] == 0, count - k, k)
        refs[count][lax.rem(place_ref[0] + step, count)] = refs[k][...]


def arrange(place, side, part, slot, packets):
    rows, width = packets[0].shape
    ordered = pl.pallas_call(
        arrange_kernel,
        out_shape=jax.ShapeDtypeStruct((len(packets), rows, width), bf16),
        in_specs=[pl.BlockSpec(memory_space=pltpu.SMEM)] * 4 + [whole_vmem] * len(packets),
        out_specs=whole_vmem,
        compiler_params=room(4),
        name="arrange",
    )(place, side, part, slot, *packets)
    return ordered.reshape(len(packets) * rows, width)


def fold(values):
    return jnp.sum(values.reshape(values.shape[0] // 8, 8, values.shape[1]), axis=0)


def row_sums(tiles):
    row = lax.broadcasted_iota(jnp.int32, tiles[0].shape, 0)
    for bit in (1, 2, 4):
        even = (row // bit) % 2 == 0
        merged = []
        for a, b in zip(tiles[::2], tiles[1::2]):
            merged.append(
                jnp.where(even, a, b) + pltpu.roll(jnp.where(even, b, a), 8 - bit, 0)
            )
        tiles = merged
    return tiles[0]


def label_table(tags):
    lane = lax.broadcasted_iota(jnp.int32, tags.shape, 1) % NCTF
    return (tags.astype(f32) == lane.astype(f32)).astype(f32)


def score_kernel(
    own_refs,
    side_ref,
    spectra_ref,
    cos_ref,
    sin_ref,
    own_ref,
    other_ref,
    transfer_ref,
    odds_ref,
    stats_ref,
    weighted_ref,
    penalty_ref,
):
    groups = spectra_ref.shape[0] // CHUNKS
    refs = groups * own_refs
    half = own_ref.shape[0]
    side = side_ref[0]

    own, other = own_ref[...], other_ref[...]
    weighted_ref[:half, :] = jnp.where(side == 0, own, other)
    weighted_ref[half:, :] = jnp.where(side == 0, other, own)
    odds_ref[...] = jnp.zeros_like(odds_ref)
    penalty_ref[...] = jnp.zeros_like(penalty_ref)
    width = 2 * UNIT * LANES

    def unit(u):
        wide = pl.ds(pl.multiple_of(u * width, width), width)
        weighted = weighted_ref[:, wide]
        tables = []
        for j in range(UNIT):
            lanes = pl.ds(pl.multiple_of((u * UNIT + j) * LANES, LANES), LANES)
            transfer = transfer_ref[:, lanes]
            tables.append((cos_ref[:, lanes], sin_ref[:, lanes], transfer * transfer))
        for g in range(groups):
            blocks = []
            for j in range(UNIT):
                d = u * UNIT + j
                line = peer_line(2 * g + d % 2, d // 2, 2 * groups, CHUNKS // 2)
                blocks.append(spectra_ref[line].astype(f32))
            for first in range(0, own_refs, BATCH):
                rows = []
                for i in range(first, first + BATCH):
                    pieces = []
                    power = 0.0
                    for j in range(UNIT):
                        cos, sin, squared = tables[j]
                        real, imag = blocks[j][i, 0:1], blocks[j][i, 1:2]
                        pieces.append((real * cos - imag * sin).astype(bf16))
                        pieces.append((real * sin + imag * cos).astype(bf16))
                        power = power + (real * real + imag * imag) * squared
                    place = (g * own_refs + i) * NCTF
                    penalty_ref[place : place + NCTF, :] += power
                    rows.append(jnp.concatenate(pieces, axis=1))
                place = (g * own_refs + first) * SHIFTS
                odds_ref[place : place + BATCH * SHIFTS, :] += lax.dot_general(
                    jnp.concatenate(rows, axis=0),
                    weighted,
                    (((1,), (1,)), ((), ())),
                    preferred_element_type=f32,
                )

    def units(k, carry):
        for j in range(UNROLL):
            unit(k * UNROLL + j)
        return carry

    lax.fori_loop(0, CHUNKS // UNIT // UNROLL, units, 0)
    tags = weighted_ref[:, 2 * F :].astype(f32).T[:NCTF]
    hot = (tags == lax.broadcasted_iota(jnp.int32, tags.shape, 0).astype(f32)).astype(f32)
    top = None
    for r in range(refs):
        charge = jnp.sum(penalty_ref[r * NCTF : (r + 1) * NCTF, :], axis=1, keepdims=True)
        cost = 0.5 * jnp.sum(charge * hot, axis=0, keepdims=True)
        place = slice(r * SHIFTS, (r + 1) * SHIFTS)
        scores = odds_ref[place, :] - cost
        odds_ref[place, :] = scores
        high = jnp.max(scores, axis=0, keepdims=True)
        top = high if top is None else jnp.maximum(top, high)
    odds = jnp.exp(odds_ref[...] - top)
    odds_ref[...] = odds
    total = jnp.sum(odds, axis=0, keepdims=True)
    stats = jnp.concatenate([top, total], axis=0)
    spare = jnp.zeros((2, LANES - stats.shape[1]), f32)
    stats = jnp.concatenate([stats, spare], axis=1)
    stats_ref[...] = jnp.broadcast_to(stats[None], stats_ref.shape)


def make_scores(side, spectra, cos_table, sin_table, own, other, transfer, own_refs, near):
    groups = spectra.shape[0] // CHUNKS
    refs = groups * own_refs
    count = 2 * own.shape[0]
    return pl.pallas_call(
        functools.partial(score_kernel, own_refs),
        out_shape=(
            jax.ShapeDtypeStruct((refs * SHIFTS, count), f32),
            jax.ShapeDtypeStruct((near, 2, LANES), f32),
            jax.ShapeDtypeStruct((count, own.shape[1]), bf16),
        ),
        in_specs=[pl.BlockSpec(memory_space=pltpu.SMEM)] + [whole_vmem] * 6,
        out_specs=(whole_vmem, whole_vmem, whole_vmem),
        scratch_shapes=[
            pltpu.VMEM((refs * NCTF, LANES), f32),
        ],
        compiler_params=room(24),
        name="scores",
    )(side, spectra, cos_table, sin_table, own, other, transfer)


def back_kernel(
    own_refs,
    slot_ref,
    odds_ref,
    stats_ref,
    packets_ref,
    cos_ref,
    sin_ref,
    parts_ref,
    log_ref,
    posterior_ref,
):
    groups = parts_ref.shape[0] // CHUNKS
    refs = groups * own_refs
    count = odds_ref.shape[1]
    slot = slot_ref[0]
    tops, sums = stats_ref[:, 0, :count], stats_ref[:, 1, :count]
    top = jnp.max(tops, axis=0, keepdims=True)
    total = jnp.sum(sums * jnp.exp(tops - top), axis=0, keepdims=True)
    log_all = top + jnp.log(total)
    own_rows = log_ref.shape[1]
    own_log = jnp.zeros_like(log_ref)
    for k in range(count // own_rows):
        piece = log_all[:, k * own_rows : (k + 1) * own_rows]
        own_log = jnp.where(slot == k, piece, own_log)
    log_ref[...] = own_log
    scale = jnp.exp(stats_ref[slot][0:1, :count] - log_all)
    weights = []
    for r in range(refs):
        place = slice(r * SHIFTS, (r + 1) * SHIFTS)
        posterior = (odds_ref[place, :] * scale).astype(bf16)
        posterior_ref[place, :] = posterior
        weights.append(jnp.sum(posterior.astype(f32), axis=0, keepdims=True))
    weights = jnp.concatenate(weights, axis=0)
    high = weights.astype(bf16)
    low = (weights - high.astype(f32)).astype(bf16)
    hot = label_table(packets_ref[:, 2 * F :]).astype(bf16)
    spread = jnp.dot(jnp.concatenate([high, low], axis=0), hot, preferred_element_type=f32)
    spread = spread[:refs] + spread[refs:]
    lane = lax.broadcasted_iota(jnp.int32, (refs, LANES), 1) // NCTF
    row = lax.broadcasted_iota(jnp.int32, (refs, LANES), 0) % own_refs
    spread = jnp.where(lane == row, spread, 0.0)
    shares = []
    for g in range(groups):
        share = jnp.sum(spread[g * own_refs : (g + 1) * own_refs], axis=0, keepdims=True)
        high = share.astype(bf16).astype(f32)
        before = jnp.zeros((2 * own_refs, LANES), f32)
        after = jnp.zeros((ROWS - 2 * own_refs - 2, LANES), f32)
        shares.append(jnp.concatenate([before, high, share - high, after], axis=0))

    def chunk(d):
        lanes = pl.ds(pl.multiple_of(d * LANES, LANES), LANES)
        wide = pl.ds(pl.multiple_of(d * 2 * LANES, 2 * LANES), 2 * LANES)
        cos, sin = cos_ref[:, lanes], sin_ref[:, lanes]
        weighted = packets_ref[:, wide]
        for g in range(groups):
            rows = []
            for first in range(0, own_refs, BATCH):
                place = (g * own_refs + first) * SHIFTS
                totals = jnp.dot(
                    posterior_ref[place : place + BATCH * SHIFTS, :],
                    weighted,
                    preferred_element_type=f32,
                )
                for i in range(BATCH):
                    real = totals[i * SHIFTS : (i + 1) * SHIFTS, :LANES]
                    imag = totals[i * SHIFTS : (i + 1) * SHIFTS, LANES:]
                    rows.append(fold(real * cos + imag * sin))
                    rows.append(fold(imag * cos - real * sin))
            blank = [jnp.zeros((8, LANES), f32)] * (ROWS - len(rows))
            rows = rows + blank
            sums = jnp.concatenate([row_sums(rows[:8]), row_sums(rows[8:])], axis=0)
            line = peer_line(2 * g + d % 2, d // 2, 2 * groups, CHUNKS // 2)
            parts_ref[line] = (sums + shares[g]).astype(bf16)

    def chunks(k, carry):
        for j in range(UNROLL):
            chunk(k * UNROLL + j)
        return carry

    lax.fori_loop(0, CHUNKS // UNROLL, chunks, 0)


def back_project(slot, odds, stats, packets, cos_table, sin_table, own_refs, rows):
    count = packets.shape[0]
    groups = odds.shape[0] // SHIFTS // own_refs
    return pl.pallas_call(
        functools.partial(back_kernel, own_refs),
        out_shape=(
            jax.ShapeDtypeStruct((groups * CHUNKS, ROWS, LANES), bf16),
            jax.ShapeDtypeStruct((1, rows), f32),
        ),
        in_specs=[pl.BlockSpec(memory_space=pltpu.SMEM)] + [whole_vmem] * 5,
        out_specs=(whole_vmem, whole_vmem),
        scratch_shapes=[pltpu.VMEM((odds.shape[0], count), bf16)],
        compiler_params=room(24),
        name="back",
    )(slot, odds, stats, packets, cos_table, sin_table)


def finish_kernel(place_ref, parts_ref, transfer_ref, out_ref):
    own_refs = out_ref.shape[0]
    sums = jnp.sum(parts_ref[...].astype(f32), axis=0)
    share = sums[2 * own_refs : 2 * own_refs + 1] + sums[2 * own_refs + 1 : 2 * own_refs + 2]
    lane = lax.broadcasted_iota(jnp.int32, (own_refs, LANES), 1) // NCTF
    row = lax.broadcasted_iota(jnp.int32, (own_refs, LANES), 0)
    shares = jnp.where(lane == row, share, 0.0)
    own = transfer_ref[:, pl.ds(pl.multiple_of(place_ref[0] * LANES, LANES), LANES)]
    squared = jnp.concatenate([own * own] * (LANES // NCTF), axis=0)
    denominator = jnp.dot(shares, squared, precision=highest) + ridge_term
    for i in range(own_refs):
        out_ref[i] = sums[2 * i : 2 * i + 2] / denominator[i : i + 1]


def finish(place, parts, transfer, own_refs):
    return pl.pallas_call(
        finish_kernel,
        out_shape=jax.ShapeDtypeStruct((own_refs, 2, LANES), f32),
        in_specs=[pl.BlockSpec(memory_space=pltpu.SMEM)] + [whole_vmem] * 2,
        out_specs=whole_vmem,
        compiler_params=room(4),
        name="finish",
    )(place, parts, transfer)


def shifted(value, axis, steps):
    count = lax.axis_size(axis)
    pairs = [(source, (source + steps) % count) for source in range(count)]
    return lax.ppermute(value, axis, pairs)


def parted(value, steps):
    count = lax.axis_size("x")
    pairs = []
    for source in range(count):
        pairs.append((2 * source, 2 * ((source + steps) % count)))
        pairs.append((2 * source + 1, 2 * ((source - steps) % count) + 1))
    return lax.ppermute(value, ("x", "core"), pairs)


def peer_line(row, plane, rows, planes):
    return (planes - 1 - plane) * rows + (row + rows // 2) % rows


def wide_exchange(value):
    yh, dom = lax.axis_size("yh"), lax.axis_size("dom")
    order = [0] * (yh * dom)
    for y in range(yh):
        for d in range(dom):
            order[peer_line(2 * y + d % 2, d // 2, 2 * yh, dom // 2)] = y * dom + d
    return lax.all_to_all(value, ("yh", "dom"), 0, 0, axis_index_groups=[order])


def body(particles, classes, template_spectra, transfer_magnitude, offsets):
    rows = particles.shape[0]
    own_refs = template_spectra.shape[0]
    near_axes = ("core", "x")
    near, far = lax.axis_size(near_axes), lax.axis_size(("yh", "dom"))
    packet, copies = prep(classes, particles, transfer_magnitude, template_spectra, far)
    spectra = wide_exchange(copies)
    place, side, part = [lax.axis_index(name)[None] for name in ("x", "core", "dom")]
    slot = lax.axis_index(near_axes)[None]
    second, first, third = parted(packet, 2), parted(packet, 1), parted(packet, 3)
    own = arrange(place, side, part, slot, [packet, first, second, third])
    other = shifted(own, "core", 1)
    cos_table, sin_table = phase_tables(offsets)
    odds, stats, weighted = make_scores(
        side, spectra, cos_table, sin_table, own, other, transfer_magnitude, own_refs, near
    )
    stats = lax.all_to_all(stats, near_axes, 0, 0)
    parts, log_own = back_project(
        slot, odds, stats, weighted, cos_table, sin_table, own_refs, rows
    )
    parts = wide_exchange(parts)
    new_refs = finish(part, parts, transfer_magnitude, own_refs)
    return (log_own.reshape(rows), new_refs)


def solution(mesh):
    devices = mesh.devices
    names = ("yh", "x", "core", "dom")
    inner = Mesh(devices.reshape(4, 4, 2, devices.shape[1]), names)
    refs = names[:3]
    return jax.shard_map(
        body,
        mesh=inner,
        in_specs=(P(names, None, None), P(names), P(refs, None, "dom"), P(), P()),
        out_specs=(P(names), P(refs, None, "dom")),
        check_vma=False,
    )
```

```python
import functools
import math

import jax
import jax.numpy as jnp
from jax import lax
from jax.experimental import pallas as pl
from jax.experimental.pallas import tpu as pltpu
from jax.sharding import Mesh
from jax.sharding import PartitionSpec as P

BOX = 64
F = 2048
SHIFTS = 64
NCTF = 16
LANES = 128
CHUNKS = F // LANES
ROWS = 16
UNIT = 2
UNROLL = 4
BATCH = 2

highest = lax.Precision.HIGHEST
ridge_term = 1.0
f32 = jnp.float32
bf16 = jnp.bfloat16
whole_vmem = pl.BlockSpec(memory_space=pltpu.VMEM)


def room(mib):
    return pltpu.CompilerParams(vmem_limit_bytes=mib * 1024 * 1024)


def phase_tables(offsets):
    half_side = BOX // 2
    positions = jnp.arange(F, dtype=jnp.int32)
    row_index = positions // half_side
    freq_x = jnp.where(row_index < half_side, row_index, row_index - BOX)
    freq_y = positions % half_side
    turn_count = (offsets[:, 0:1] * freq_x[None, :] + offsets[:, 1:2] * freq_y[None, :]) % BOX
    angles = turn_count.astype(f32) * (2.0 * math.pi / BOX)
    return (jnp.cos(angles), jnp.sin(angles))


def prep_kernel(classes_ref, particles_ref, transfer_ref, spectra_ref, packet_ref, copies_ref):
    rows = particles_ref.shape[0]
    copies_ref[...] = jnp.broadcast_to(spectra_ref[...][None], copies_ref.shape)
    place = lax.broadcasted_iota(jnp.int32, (rows, 1), 0)
    labels = jnp.zeros((rows, 1), jnp.int32)
    for i in range(rows):
        labels = jnp.where(place == i, classes_ref[i], labels)
    contrast = jnp.zeros((rows, F), f32)
    for c in range(NCTF):
        contrast = jnp.where(labels == c, transfer_ref[c : c + 1, :], contrast)
    values = particles_ref[...].astype(f32)
    real = (values[:, 0, :] * contrast).astype(bf16)
    imag = (values[:, 1, :] * contrast).astype(bf16)
    for d in range(CHUNKS):
        lanes = slice(d * LANES, (d + 1) * LANES)
        packet_ref[:, 2 * d * LANES : (2 * d + 1) * LANES] = real[:, lanes]
        packet_ref[:, (2 * d + 1) * LANES : (2 * d + 2) * LANES] = imag[:, lanes]
    tags = jnp.broadcast_to(labels.astype(f32), (rows, LANES))
    packet_ref[:, 2 * F :] = tags.astype(bf16)


def prep(classes, particles, transfer, spectra, far):
    rows = particles.shape[0]
    return pl.pallas_call(
        prep_kernel,
        out_shape=(
            jax.ShapeDtypeStruct((rows, 2 * F + LANES), bf16),
            jax.ShapeDtypeStruct((far,) + spectra.shape, bf16),
        ),
        in_specs=[pl.BlockSpec(memory_space=pltpu.SMEM)] + [whole_vmem] * 3,
        out_specs=(whole_vmem, whole_vmem),
        compiler_params=room(60),
        name="prep",
    )(classes, particles, transfer, spectra)


def arrange_kernel(place_ref, side_ref, part_ref, slot_ref, *refs):
    count = len(refs) - 1
    for k in range(count):
        step = jnp.where(side_ref[0] == 0, count - k, k)
        refs[count][lax.rem(place_ref[0] + step, count)] = refs[k][...]


def arrange(place, side, part, slot, packets):
    rows, width = packets[0].shape
    ordered = pl.pallas_call(
        arrange_kernel,
        out_shape=jax.ShapeDtypeStruct((len(packets), rows, width), bf16),
        in_specs=[pl.BlockSpec(memory_space=pltpu.SMEM)] * 4 + [whole_vmem] * len(packets),
        out_specs=whole_vmem,
        compiler_params=room(4),
        name="arrange",
    )(place, side, part, slot, *packets)
    return ordered.reshape(len(packets) * rows, width)


def fold(values):
    return jnp.sum(values.reshape(values.shape[0] // 8, 8, values.shape[1]), axis=0)


def row_sums(tiles):
    row = lax.broadcasted_iota(jnp.int32, tiles[0].shape, 0)
    for bit in (1, 2, 4):
        even = (row // bit) % 2 == 0
        merged = []
        for a, b in zip(tiles[::2], tiles[1::2]):
            merged.append(
                jnp.where(even, a, b) + pltpu.roll(jnp.where(even, b, a), 8 - bit, 0)
            )
        tiles = merged
    return tiles[0]


def label_table(tags):
    lane = lax.broadcasted_iota(jnp.int32, tags.shape, 1) % NCTF
    return (tags.astype(f32) == lane.astype(f32)).astype(f32)


def score_kernel(
    own_refs,
    side_ref,
    spectra_ref,
    cos_ref,
    sin_ref,
    own_ref,
    other_ref,
    transfer_ref,
    odds_ref,
    stats_ref,
    weighted_ref,
    penalty_ref,
):
    groups = spectra_ref.shape[0] // CHUNKS
    refs = groups * own_refs
    half = own_ref.shape[0]
    side = side_ref[0]

    own, other = own_ref[...], other_ref[...]
    weighted_ref[:half, :] = jnp.where(side == 0, own, other)
    weighted_ref[half:, :] = jnp.where(side == 0, other, own)
    odds_ref[...] = jnp.zeros_like(odds_ref)
    penalty_ref[...] = jnp.zeros_like(penalty_ref)
    width = 2 * UNIT * LANES

    def unit(u):
        wide = pl.ds(pl.multiple_of(u * width, width), width)
        weighted = weighted_ref[:, wide]
        tables = []
        for j in range(UNIT):
            lanes = pl.ds(pl.multiple_of((u * UNIT + j) * LANES, LANES), LANES)
            transfer = transfer_ref[:, lanes]
            tables.append((cos_ref[:, lanes], sin_ref[:, lanes], transfer * transfer))
        for g in range(groups):
            blocks = []
            for j in range(UNIT):
                d = u * UNIT + j
                line = peer_line(2 * g + d % 2, d // 2, 2 * groups, CHUNKS // 2)
                blocks.append(spectra_ref[line].astype(f32))
            for first in range(0, own_refs, BATCH):
                rows = []
                for i in range(first, first + BATCH):
                    pieces = []
                    power = 0.0
                    for j in range(UNIT):
                        cos, sin, squared = tables[j]
                        real, imag = blocks[j][i, 0:1], blocks[j][i, 1:2]
                        pieces.append((real * cos - imag * sin).astype(bf16))
                        pieces.append((real * sin + imag * cos).astype(bf16))
                        power = power + (real * real + imag * imag) * squared
                    place = (g * own_refs + i) * NCTF
                    penalty_ref[place : place + NCTF, :] += power
                    rows.append(jnp.concatenate(pieces, axis=1))
                place = (g * own_refs + first) * SHIFTS
                odds_ref[place : place + BATCH * SHIFTS, :] += lax.dot_general(
                    jnp.concatenate(rows, axis=0),
                    weighted,
                    (((1,), (1,)), ((), ())),
                    preferred_element_type=f32,
                )

    def units(k, carry):
        for j in range(UNROLL):
            unit(k * UNROLL + j)
        return carry

    lax.fori_loop(0, CHUNKS // UNIT // UNROLL, units, 0)
    tags = weighted_ref[:, 2 * F :].astype(f32).T[:NCTF]
    hot = (tags == lax.broadcasted_iota(jnp.int32, tags.shape, 0).astype(f32)).astype(f32)
    top = None
    for r in range(refs):
        charge = jnp.sum(penalty_ref[r * NCTF : (r + 1) * NCTF, :], axis=1, keepdims=True)
        cost = 0.5 * jnp.sum(charge * hot, axis=0, keepdims=True)
        place = slice(r * SHIFTS, (r + 1) * SHIFTS)
        scores = odds_ref[place, :] - cost
        odds_ref[place, :] = scores
        high = jnp.max(scores, axis=0, keepdims=True)
        top = high if top is None else jnp.maximum(top, high)
    odds = jnp.exp(odds_ref[...] - top)
    odds_ref[...] = odds
    total = jnp.sum(odds, axis=0, keepdims=True)
    stats = jnp.concatenate([top, total], axis=0)
    spare = jnp.zeros((2, LANES - stats.shape[1]), f32)
    stats = jnp.concatenate([stats, spare], axis=1)
    stats_ref[...] = jnp.broadcast_to(stats[None], stats_ref.shape)


def make_scores(side, spectra, cos_table, sin_table, own, other, transfer, own_refs, near):
    groups = spectra.shape[0] // CHUNKS
    refs = groups * own_refs
    count = 2 * own.shape[0]
    return pl.pallas_call(
        functools.partial(score_kernel, own_refs),
        out_shape=(
            jax.ShapeDtypeStruct((refs * SHIFTS, count), f32),
            jax.ShapeDtypeStruct((near, 2, LANES), f32),
            jax.ShapeDtypeStruct((count, own.shape[1]), bf16),
        ),
        in_specs=[pl.BlockSpec(memory_space=pltpu.SMEM)] + [whole_vmem] * 6,
        out_specs=(whole_vmem, whole_vmem, whole_vmem),
        scratch_shapes=[
            pltpu.VMEM((refs * NCTF, LANES), f32),
        ],
        compiler_params=room(24),
        name="scores",
    )(side, spectra, cos_table, sin_table, own, other, transfer)


def back_kernel(
    own_refs,
    slot_ref,
    odds_ref,
    stats_ref,
    packets_ref,
    cos_ref,
    sin_ref,
    parts_ref,
    log_ref,
    posterior_ref,
):
    groups = parts_ref.shape[0] // CHUNKS
    refs = groups * own_refs
    count = odds_ref.shape[1]
    slot = slot_ref[0]
    tops, sums = stats_ref[:, 0, :count], stats_ref[:, 1, :count]
    top = jnp.max(tops, axis=0, keepdims=True)
    total = jnp.sum(sums * jnp.exp(tops - top), axis=0, keepdims=True)
    log_all = top + jnp.log(total)
    own_rows = log_ref.shape[1]
    own_log = jnp.zeros_like(log_ref)
    for k in range(count // own_rows):
        piece = log_all[:, k * own_rows : (k + 1) * own_rows]
        own_log = jnp.where(slot == k, piece, own_log)
    log_ref[...] = own_log
    scale = jnp.exp(stats_ref[slot][0:1, :count] - log_all)
    weights = []
    for r in range(refs):
        place = slice(r * SHIFTS, (r + 1) * SHIFTS)
        posterior = (odds_ref[place, :] * scale).astype(bf16)
        posterior_ref[place, :] = posterior
        weights.append(jnp.sum(posterior.astype(f32), axis=0, keepdims=True))
    weights = jnp.concatenate(weights, axis=0)
    high = weights.astype(bf16)
    low = (weights - high.astype(f32)).astype(bf16)
    hot = label_table(packets_ref[:, 2 * F :]).astype(bf16)
    spread = jnp.dot(jnp.concatenate([high, low], axis=0), hot, preferred_element_type=f32)
    spread = spread[:refs] + spread[refs:]
    lane = lax.broadcasted_iota(jnp.int32, (refs, LANES), 1) // NCTF
    row = lax.broadcasted_iota(jnp.int32, (refs, LANES), 0) % own_refs
    spread = jnp.where(lane == row, spread, 0.0)
    shares = []
    for g in range(groups):
        share = jnp.sum(spread[g * own_refs : (g + 1) * own_refs], axis=0, keepdims=True)
        high = share.astype(bf16).astype(f32)
        before = jnp.zeros((2 * own_refs, LANES), f32)
        after = jnp.zeros((ROWS - 2 * own_refs - 2, LANES), f32)
        shares.append(jnp.concatenate([before, high, share - high, after], axis=0))

    def chunk(d):
        lanes = pl.ds(pl.multiple_of(d * LANES, LANES), LANES)
        wide = pl.ds(pl.multiple_of(d * 2 * LANES, 2 * LANES), 2 * LANES)
        cos, sin = cos_ref[:, lanes], sin_ref[:, lanes]
        weighted = packets_ref[:, wide]
        for g in range(groups):
            rows = []
            for first in range(0, own_refs, BATCH):
                place = (g * own_refs + first) * SHIFTS
                totals = jnp.dot(
                    posterior_ref[place : place + BATCH * SHIFTS, :],
                    weighted,
                    preferred_element_type=f32,
                )
                for i in range(BATCH):
                    real = totals[i * SHIFTS : (i + 1) * SHIFTS, :LANES]
                    imag = totals[i * SHIFTS : (i + 1) * SHIFTS, LANES:]
                    rows.append(fold(real * cos + imag * sin))
                    rows.append(fold(imag * cos - real * sin))
            blank = [jnp.zeros((8, LANES), f32)] * (ROWS - len(rows))
            rows = rows + blank
            sums = jnp.concatenate([row_sums(rows[:8]), row_sums(rows[8:])], axis=0)
            line = peer_line(2 * g + d % 2, d // 2, 2 * groups, CHUNKS // 2)
            parts_ref[line] = (sums + shares[g]).astype(bf16)

    def chunks(k, carry):
        for j in range(UNROLL):
            chunk(k * UNROLL + j)
        return carry

    lax.fori_loop(0, CHUNKS // UNROLL, chunks, 0)


def back_project(slot, odds, stats, packets, cos_table, sin_table, own_refs, rows):
    count = packets.shape[0]
    groups = odds.shape[0] // SHIFTS // own_refs
    return pl.pallas_call(
        functools.partial(back_kernel, own_refs),
        out_shape=(
            jax.ShapeDtypeStruct((groups * CHUNKS, ROWS, LANES), bf16),
            jax.ShapeDtypeStruct((1, rows), f32),
        ),
        in_specs=[pl.BlockSpec(memory_space=pltpu.SMEM)] + [whole_vmem] * 5,
        out_specs=(whole_vmem, whole_vmem),
        scratch_shapes=[pltpu.VMEM((odds.shape[0], count), bf16)],
        compiler_params=room(24),
        name="back",
    )(slot, odds, stats, packets, cos_table, sin_table)


def finish_kernel(place_ref, parts_ref, transfer_ref, out_ref):
    own_refs = out_ref.shape[0]
    sums = jnp.sum(parts_ref[...].astype(f32), axis=0)
    share = sums[2 * own_refs : 2 * own_refs + 1] + sums[2 * own_refs + 1 : 2 * own_refs + 2]
    lane = lax.broadcasted_iota(jnp.int32, (own_refs, LANES), 1) // NCTF
    row = lax.broadcasted_iota(jnp.int32, (own_refs, LANES), 0)
    shares = jnp.where(lane == row, share, 0.0)
    own = transfer_ref[:, pl.ds(pl.multiple_of(place_ref[0] * LANES, LANES), LANES)]
    squared = jnp.concatenate([own * own] * (LANES // NCTF), axis=0)
    denominator = jnp.dot(shares, squared, precision=highest) + ridge_term
    for i in range(own_refs):
        out_ref[i] = sums[2 * i : 2 * i + 2] / denominator[i : i + 1]


def finish(place, parts, transfer, own_refs):
    return pl.pallas_call(
        finish_kernel,
        out_shape=jax.ShapeDtypeStruct((own_refs, 2, LANES), f32),
        in_specs=[pl.BlockSpec(memory_space=pltpu.SMEM)] + [whole_vmem] * 2,
        out_specs=whole_vmem,
        compiler_params=room(4),
        name="finish",
    )(place, parts, transfer)


def shifted(value, axis, steps):
    count = lax.axis_size(axis)
    pairs = [(source, (source + steps) % count) for source in range(count)]
    return lax.ppermute(value, axis, pairs)


def parted(value, steps):
    count = lax.axis_size("x")
    pairs = []
    for source in range(count):
        pairs.append((2 * source, 2 * ((source + steps) % count)))
        pairs.append((2 * source + 1, 2 * ((source - steps) % count) + 1))
    return lax.ppermute(value, ("x", "core"), pairs)


def peer_line(row, plane, rows, planes):
    return (planes - 1 - plane) * rows + (row + rows // 2) % rows


def wide_exchange(value):
    yh, dom = lax.axis_size("yh"), lax.axis_size("dom")
    order = [0] * (yh * dom)
    for y in range(yh):
        for d in range(dom):
            order[peer_line(2 * y + d % 2, d // 2, 2 * yh, dom // 2)] = y * dom + d
    return lax.all_to_all(value, ("yh", "dom"), 0, 0, axis_index_groups=[order])


def body(particles, classes, template_spectra, transfer_magnitude, offsets):
    rows = particles.shape[0]
    own_refs = template_spectra.shape[0]
    near_axes = ("core", "x")
    near, far = lax.axis_size(near_axes), lax.axis_size(("yh", "dom"))
    packet, copies = prep(classes, particles, transfer_magnitude, template_spectra, far)
    spectra = wide_exchange(copies)
    place, side, part = [lax.axis_index(name)[None] for name in ("x", "core", "dom")]
    slot = lax.axis_index(near_axes)[None]
    second, first = parted(packet, 2), parted(packet, 1)
    packet, first = lax.optimization_barrier((packet, first))
    third = parted(packet, 3)
    own = arrange(place, side, part, slot, [packet, first, second, third])
    other = shifted(own, "core", 1)
    cos_table, sin_table = phase_tables(offsets)
    odds, stats, weighted = make_scores(
        side, spectra, cos_table, sin_table, own, other, transfer_magnitude, own_refs, near
    )
    stats = lax.all_to_all(stats, near_axes, 0, 0)
    parts, log_own = back_project(
        slot, odds, stats, weighted, cos_table, sin_table, own_refs, rows
    )
    parts = wide_exchange(parts)
    new_refs = finish(part, parts, transfer_magnitude, own_refs)
    return (log_own.reshape(rows), new_refs)


def solution(mesh):
    devices = mesh.devices
    names = ("yh", "x", "core", "dom")
    inner = Mesh(devices.reshape(4, 4, 2, devices.shape[1]), names)
    refs = names[:3]
    return jax.shard_map(
        body,
        mesh=inner,
        in_specs=(P(names, None, None), P(names), P(refs, None, "dom"), P(), P()),
        out_specs=(P(names), P(refs, None, "dom")),
        check_vma=False,
    )
```

```python
import functools
import math

import jax
import jax.numpy as jnp
from jax import lax
from jax.experimental import pallas as pl
from jax.experimental.pallas import tpu as pltpu
from jax.sharding import Mesh
from jax.sharding import PartitionSpec as P

BOX = 64
F = 2048
SHIFTS = 64
NCTF = 16
LANES = 128
CHUNKS = F // LANES
ROWS = 16
UNIT = 2
UNROLL = 4
BATCH = 2

highest = lax.Precision.HIGHEST
ridge_term = 1.0
f32 = jnp.float32
bf16 = jnp.bfloat16
whole_vmem = pl.BlockSpec(memory_space=pltpu.VMEM)


def room(mib):
    return pltpu.CompilerParams(vmem_limit_bytes=mib * 1024 * 1024)


def phase_tables(offsets):
    half_side = BOX // 2
    positions = jnp.arange(F, dtype=jnp.int32)
    row_index = positions // half_side
    freq_x = jnp.where(row_index < half_side, row_index, row_index - BOX)
    freq_y = positions % half_side
    turn_count = (offsets[:, 0:1] * freq_x[None, :] + offsets[:, 1:2] * freq_y[None, :]) % BOX
    angles = turn_count.astype(f32) * (2.0 * math.pi / BOX)
    return (jnp.cos(angles), jnp.sin(angles))


def prep_kernel(classes_ref, particles_ref, transfer_ref, spectra_ref, packet_ref, copies_ref):
    rows = particles_ref.shape[0]
    copies_ref[...] = jnp.broadcast_to(spectra_ref[...][None], copies_ref.shape)
    place = lax.broadcasted_iota(jnp.int32, (rows, 1), 0)
    labels = jnp.zeros((rows, 1), jnp.int32)
    for i in range(rows):
        labels = jnp.where(place == i, classes_ref[i], labels)
    contrast = jnp.zeros((rows, F), f32)
    for c in range(NCTF):
        contrast = jnp.where(labels == c, transfer_ref[c : c + 1, :], contrast)
    values = particles_ref[...].astype(f32)
    real = (values[:, 0, :] * contrast).astype(bf16)
    imag = (values[:, 1, :] * contrast).astype(bf16)
    for d in range(CHUNKS):
        lanes = slice(d * LANES, (d + 1) * LANES)
        packet_ref[:, 2 * d * LANES : (2 * d + 1) * LANES] = real[:, lanes]
        packet_ref[:, (2 * d + 1) * LANES : (2 * d + 2) * LANES] = imag[:, lanes]
    tags = jnp.broadcast_to(labels.astype(f32), (rows, LANES))
    packet_ref[:, 2 * F :] = tags.astype(bf16)


def prep(classes, particles, transfer, spectra, far):
    rows = particles.shape[0]
    return pl.pallas_call(
        prep_kernel,
        out_shape=(
            jax.ShapeDtypeStruct((rows, 2 * F + LANES), bf16),
            jax.ShapeDtypeStruct((far,) + spectra.shape, bf16),
        ),
        in_specs=[pl.BlockSpec(memory_space=pltpu.SMEM)] + [whole_vmem] * 3,
        out_specs=(whole_vmem, whole_vmem),
        compiler_params=room(60),
        name="prep",
    )(classes, particles, transfer, spectra)


def arrange_kernel(place_ref, side_ref, part_ref, slot_ref, *refs):
    count = len(refs) - 1
    for k in range(count):
        step = jnp.where(side_ref[0] == 0, count - k, k)
        refs[count][lax.rem(place_ref[0] + step, count)] = refs[k][...]


def arrange(place, side, part, slot, packets):
    rows, width = packets[0].shape
    ordered = pl.pallas_call(
        arrange_kernel,
        out_shape=jax.ShapeDtypeStruct((len(packets), rows, width), bf16),
        in_specs=[pl.BlockSpec(memory_space=pltpu.SMEM)] * 4 + [whole_vmem] * len(packets),
        out_specs=whole_vmem,
        compiler_params=room(4),
        name="arrange",
    )(place, side, part, slot, *packets)
    return ordered.reshape(len(packets) * rows, width)


def fold(values):
    return jnp.sum(values.reshape(values.shape[0] // 8, 8, values.shape[1]), axis=0)


def row_sums(tiles):
    row = lax.broadcasted_iota(jnp.int32, tiles[0].shape, 0)
    for bit in (1, 2, 4):
        even = (row // bit) % 2 == 0
        merged = []
        for a, b in zip(tiles[::2], tiles[1::2]):
            merged.append(
                jnp.where(even, a, b) + pltpu.roll(jnp.where(even, b, a), 8 - bit, 0)
            )
        tiles = merged
    return tiles[0]


def label_table(tags):
    lane = lax.broadcasted_iota(jnp.int32, tags.shape, 1) % NCTF
    return (tags.astype(f32) == lane.astype(f32)).astype(f32)


def score_kernel(
    own_refs,
    side_ref,
    spectra_ref,
    cos_ref,
    sin_ref,
    own_ref,
    other_ref,
    transfer_ref,
    odds_ref,
    stats_ref,
    weighted_ref,
    penalty_ref,
):
    groups = spectra_ref.shape[0] // CHUNKS
    refs = groups * own_refs
    half = own_ref.shape[0]
    side = side_ref[0]

    own, other = own_ref[...], other_ref[...]
    weighted_ref[:half, :] = jnp.where(side == 0, own, other)
    weighted_ref[half:, :] = jnp.where(side == 0, other, own)
    odds_ref[...] = jnp.zeros_like(odds_ref)
    penalty_ref[...] = jnp.zeros_like(penalty_ref)
    width = 2 * UNIT * LANES

    def unit(u):
        wide = pl.ds(pl.multiple_of(u * width, width), width)
        weighted = weighted_ref[:, wide]
        tables = []
        for j in range(UNIT):
            lanes = pl.ds(pl.multiple_of((u * UNIT + j) * LANES, LANES), LANES)
            transfer = transfer_ref[:, lanes]
            tables.append((cos_ref[:, lanes], sin_ref[:, lanes], transfer * transfer))
        for g in range(groups):
            blocks = []
            for j in range(UNIT):
                d = u * UNIT + j
                line = slant_line(side, 2 * g + d % 2, d // 2, CHUNKS // 2)
                blocks.append(spectra_ref[line].astype(f32))
            for first in range(0, own_refs, BATCH):
                rows = []
                for i in range(first, first + BATCH):
                    pieces = []
                    power = 0.0
                    for j in range(UNIT):
                        cos, sin, squared = tables[j]
                        real, imag = blocks[j][i, 0:1], blocks[j][i, 1:2]
                        pieces.append((real * cos - imag * sin).astype(bf16))
                        pieces.append((real * sin + imag * cos).astype(bf16))
                        power = power + (real * real + imag * imag) * squared
                    place = (g * own_refs + i) * NCTF
                    penalty_ref[place : place + NCTF, :] += power
                    rows.append(jnp.concatenate(pieces, axis=1))
                place = (g * own_refs + first) * SHIFTS
                odds_ref[place : place + BATCH * SHIFTS, :] += lax.dot_general(
                    jnp.concatenate(rows, axis=0),
                    weighted,
                    (((1,), (1,)), ((), ())),
                    preferred_element_type=f32,
                )

    def units(k, carry):
        for j in range(UNROLL):
            unit(k * UNROLL + j)
        return carry

    lax.fori_loop(0, CHUNKS // UNIT // UNROLL, units, 0)
    tags = weighted_ref[:, 2 * F :].astype(f32).T[:NCTF]
    hot = (tags == lax.broadcasted_iota(jnp.int32, tags.shape, 0).astype(f32)).astype(f32)
    top = None
    for r in range(refs):
        charge = jnp.sum(penalty_ref[r * NCTF : (r + 1) * NCTF, :], axis=1, keepdims=True)
        cost = 0.5 * jnp.sum(charge * hot, axis=0, keepdims=True)
        place = slice(r * SHIFTS, (r + 1) * SHIFTS)
        scores = odds_ref[place, :] - cost
        odds_ref[place, :] = scores
        high = jnp.max(scores, axis=0, keepdims=True)
        top = high if top is None else jnp.maximum(top, high)
    odds = jnp.exp(odds_ref[...] - top)
    odds_ref[...] = odds
    total = jnp.sum(odds, axis=0, keepdims=True)
    stats = jnp.concatenate([top, total], axis=0)
    spare = jnp.zeros((2, LANES - stats.shape[1]), f32)
    stats = jnp.concatenate([stats, spare], axis=1)
    stats_ref[...] = jnp.broadcast_to(stats[None], stats_ref.shape)


def make_scores(side, spectra, cos_table, sin_table, own, other, transfer, own_refs, near):
    groups = spectra.shape[0] // CHUNKS
    refs = groups * own_refs
    count = 2 * own.shape[0]
    return pl.pallas_call(
        functools.partial(score_kernel, own_refs),
        out_shape=(
            jax.ShapeDtypeStruct((refs * SHIFTS, count), f32),
            jax.ShapeDtypeStruct((near, 2, LANES), f32),
            jax.ShapeDtypeStruct((count, own.shape[1]), bf16),
        ),
        in_specs=[pl.BlockSpec(memory_space=pltpu.SMEM)] + [whole_vmem] * 6,
        out_specs=(whole_vmem, whole_vmem, whole_vmem),
        scratch_shapes=[
            pltpu.VMEM((refs * NCTF, LANES), f32),
        ],
        compiler_params=room(24),
        name="scores",
    )(side, spectra, cos_table, sin_table, own, other, transfer)


def back_kernel(
    own_refs,
    slot_ref,
    odds_ref,
    stats_ref,
    packets_ref,
    cos_ref,
    sin_ref,
    parts_ref,
    log_ref,
    posterior_ref,
):
    groups = parts_ref.shape[0] // CHUNKS
    refs = groups * own_refs
    count = odds_ref.shape[1]
    slot = slot_ref[0]
    tops, sums = stats_ref[:, 0, :count], stats_ref[:, 1, :count]
    top = jnp.max(tops, axis=0, keepdims=True)
    total = jnp.sum(sums * jnp.exp(tops - top), axis=0, keepdims=True)
    log_all = top + jnp.log(total)
    own_rows = log_ref.shape[1]
    own_log = jnp.zeros_like(log_ref)
    for k in range(count // own_rows):
        piece = log_all[:, k * own_rows : (k + 1) * own_rows]
        own_log = jnp.where(slot == k, piece, own_log)
    log_ref[...] = own_log
    scale = jnp.exp(stats_ref[slot][0:1, :count] - log_all)
    weights = []
    for r in range(refs):
        place = slice(r * SHIFTS, (r + 1) * SHIFTS)
        posterior = (odds_ref[place, :] * scale).astype(bf16)
        posterior_ref[place, :] = posterior
        weights.append(jnp.sum(posterior.astype(f32), axis=0, keepdims=True))
    weights = jnp.concatenate(weights, axis=0)
    high = weights.astype(bf16)
    low = (weights - high.astype(f32)).astype(bf16)
    hot = label_table(packets_ref[:, 2 * F :]).astype(bf16)
    spread = jnp.dot(jnp.concatenate([high, low], axis=0), hot, preferred_element_type=f32)
    spread = spread[:refs] + spread[refs:]
    lane = lax.broadcasted_iota(jnp.int32, (refs, LANES), 1) // NCTF
    row = lax.broadcasted_iota(jnp.int32, (refs, LANES), 0) % own_refs
    spread = jnp.where(lane == row, spread, 0.0)
    shares = []
    for g in range(groups):
        share = jnp.sum(spread[g * own_refs : (g + 1) * own_refs], axis=0, keepdims=True)
        high = share.astype(bf16).astype(f32)
        before = jnp.zeros((2 * own_refs, LANES), f32)
        after = jnp.zeros((ROWS - 2 * own_refs - 2, LANES), f32)
        shares.append(jnp.concatenate([before, high, share - high, after], axis=0))

    def chunk(d):
        lanes = pl.ds(pl.multiple_of(d * LANES, LANES), LANES)
        wide = pl.ds(pl.multiple_of(d * 2 * LANES, 2 * LANES), 2 * LANES)
        cos, sin = cos_ref[:, lanes], sin_ref[:, lanes]
        weighted = packets_ref[:, wide]
        for g in range(groups):
            rows = []
            for first in range(0, own_refs, BATCH):
                place = (g * own_refs + first) * SHIFTS
                totals = jnp.dot(
                    posterior_ref[place : place + BATCH * SHIFTS, :],
                    weighted,
                    preferred_element_type=f32,
                )
                for i in range(BATCH):
                    real = totals[i * SHIFTS : (i + 1) * SHIFTS, :LANES]
                    imag = totals[i * SHIFTS : (i + 1) * SHIFTS, LANES:]
                    rows.append(fold(real * cos + imag * sin))
                    rows.append(fold(imag * cos - real * sin))
            blank = [jnp.zeros((8, LANES), f32)] * (ROWS - len(rows))
            rows = rows + blank
            sums = jnp.concatenate([row_sums(rows[:8]), row_sums(rows[8:])], axis=0)
            line = peer_line(2 * g + d % 2, d // 2, 2 * groups, CHUNKS // 2)
            parts_ref[line] = (sums + shares[g]).astype(bf16)

    def chunks(k, carry):
        for j in range(UNROLL):
            chunk(k * UNROLL + j)
        return carry

    lax.fori_loop(0, CHUNKS // UNROLL, chunks, 0)


def back_project(slot, odds, stats, packets, cos_table, sin_table, own_refs, rows):
    count = packets.shape[0]
    groups = odds.shape[0] // SHIFTS // own_refs
    return pl.pallas_call(
        functools.partial(back_kernel, own_refs),
        out_shape=(
            jax.ShapeDtypeStruct((groups * CHUNKS, ROWS, LANES), bf16),
            jax.ShapeDtypeStruct((1, rows), f32),
        ),
        in_specs=[pl.BlockSpec(memory_space=pltpu.SMEM)] + [whole_vmem] * 5,
        out_specs=(whole_vmem, whole_vmem),
        scratch_shapes=[pltpu.VMEM((odds.shape[0], count), bf16)],
        compiler_params=room(24),
        name="back",
    )(slot, odds, stats, packets, cos_table, sin_table)


def finish_kernel(place_ref, parts_ref, transfer_ref, out_ref):
    own_refs = out_ref.shape[0]
    sums = jnp.sum(parts_ref[...].astype(f32), axis=0)
    share = sums[2 * own_refs : 2 * own_refs + 1] + sums[2 * own_refs + 1 : 2 * own_refs + 2]
    lane = lax.broadcasted_iota(jnp.int32, (own_refs, LANES), 1) // NCTF
    row = lax.broadcasted_iota(jnp.int32, (own_refs, LANES), 0)
    shares = jnp.where(lane == row, share, 0.0)
    own = transfer_ref[:, pl.ds(pl.multiple_of(place_ref[0] * LANES, LANES), LANES)]
    squared = jnp.concatenate([own * own] * (LANES // NCTF), axis=0)
    denominator = jnp.dot(shares, squared, precision=highest) + ridge_term
    for i in range(own_refs):
        out_ref[i] = sums[2 * i : 2 * i + 2] / denominator[i : i + 1]


def finish(place, parts, transfer, own_refs):
    return pl.pallas_call(
        finish_kernel,
        out_shape=jax.ShapeDtypeStruct((own_refs, 2, LANES), f32),
        in_specs=[pl.BlockSpec(memory_space=pltpu.SMEM)] + [whole_vmem] * 2,
        out_specs=whole_vmem,
        compiler_params=room(4),
        name="finish",
    )(place, parts, transfer)


def shifted(value, axis, steps):
    count = lax.axis_size(axis)
    pairs = [(source, (source + steps) % count) for source in range(count)]
    return lax.ppermute(value, axis, pairs)


def parted(value, steps):
    count = lax.axis_size("x")
    pairs = []
    for source in range(count):
        pairs.append((2 * source, 2 * ((source + steps) % count)))
        pairs.append((2 * source + 1, 2 * ((source - steps) % count) + 1))
    return lax.ppermute(value, ("x", "core"), pairs)


def peer_line(row, plane, rows, planes):
    return (planes - 1 - plane) * rows + (row + rows // 2) % rows


def slant_line(side, row, plane, count):
    column = (plane + 1) % count
    step = count + side * column - (1 - side) * column
    return count * ((row + count // 2 + step) % count) + column


def slanted_exchange(value):
    yh, dom = lax.axis_size("yh"), lax.axis_size("dom")
    groups = []
    for side in range(2):
        order = [0] * (yh * dom)
        for y in range(yh):
            for d in range(dom):
                line = slant_line(side, 2 * y + d % 2, d // 2, dom // 2)
                order[line] = (side * yh + y) * dom + d
        groups.append(order)
    return lax.all_to_all(value, ("core", "yh", "dom"), 0, 0, axis_index_groups=groups)


def wide_exchange(value):
    yh, dom = lax.axis_size("yh"), lax.axis_size("dom")
    order = [0] * (yh * dom)
    for y in range(yh):
        for d in range(dom):
            order[peer_line(2 * y + d % 2, d // 2, 2 * yh, dom // 2)] = y * dom + d
    return lax.all_to_all(value, ("yh", "dom"), 0, 0, axis_index_groups=[order])


def body(particles, classes, template_spectra, transfer_magnitude, offsets):
    rows = particles.shape[0]
    own_refs = template_spectra.shape[0]
    near_axes = ("core", "x")
    near, far = lax.axis_size(near_axes), lax.axis_size(("yh", "dom"))
    packet, copies = prep(classes, particles, transfer_magnitude, template_spectra, far)
    spectra = slanted_exchange(copies)
    place, side, part = [lax.axis_index(name)[None] for name in ("x", "core", "dom")]
    slot = lax.axis_index(near_axes)[None]
    second, first, third = parted(packet, 2), parted(packet, 1), parted(packet, 3)
    own = arrange(place, side, part, slot, [packet, first, second, third])
    other = shifted(own, "core", 1)
    cos_table, sin_table = phase_tables(offsets)
    odds, stats, weighted = make_scores(
        side, spectra, cos_table, sin_table, own, other, transfer_magnitude, own_refs, near
    )
    stats = lax.all_to_all(stats, near_axes, 0, 0)
    parts, log_own = back_project(
        slot, odds, stats, weighted, cos_table, sin_table, own_refs, rows
    )
    parts = wide_exchange(parts)
    new_refs = finish(part, parts, transfer_magnitude, own_refs)
    return (log_own.reshape(rows), new_refs)


def solution(mesh):
    devices = mesh.devices
    names = ("yh", "x", "core", "dom")
    inner = Mesh(devices.reshape(4, 4, 2, devices.shape[1]), names)
    refs = names[:3]
    return jax.shard_map(
        body,
        mesh=inner,
        in_specs=(P(names, None, None), P(names), P(refs, None, "dom"), P(), P()),
        out_specs=(P(names), P(refs, None, "dom")),
        check_vma=False,
    )
```

```python
import functools
import math

import jax
import jax.numpy as jnp
from jax import lax
from jax.experimental import pallas as pl
from jax.experimental.pallas import tpu as pltpu
from jax.sharding import Mesh
from jax.sharding import PartitionSpec as P

BOX = 64
F = 2048
SHIFTS = 64
NCTF = 16
LANES = 128
CHUNKS = F // LANES
ROWS = 16
UNIT = 2
UNROLL = 4
BATCH = 2

highest = lax.Precision.HIGHEST
ridge_term = 1.0
f32 = jnp.float32
bf16 = jnp.bfloat16
whole_vmem = pl.BlockSpec(memory_space=pltpu.VMEM)


def room(mib):
    return pltpu.CompilerParams(vmem_limit_bytes=mib * 1024 * 1024)


def phase_tables(offsets):
    half_side = BOX // 2
    positions = jnp.arange(F, dtype=jnp.int32)
    row_index = positions // half_side
    freq_x = jnp.where(row_index < half_side, row_index, row_index - BOX)
    freq_y = positions % half_side
    turn_count = (offsets[:, 0:1] * freq_x[None, :] + offsets[:, 1:2] * freq_y[None, :]) % BOX
    angles = turn_count.astype(f32) * (2.0 * math.pi / BOX)
    return (jnp.cos(angles), jnp.sin(angles))


def prep_kernel(classes_ref, particles_ref, transfer_ref, spectra_ref, packet_ref, copies_ref):
    rows = particles_ref.shape[0]
    copies_ref[...] = jnp.broadcast_to(spectra_ref[...][None], copies_ref.shape)
    place = lax.broadcasted_iota(jnp.int32, (rows, 1), 0)
    labels = jnp.zeros((rows, 1), jnp.int32)
    for i in range(rows):
        labels = jnp.where(place == i, classes_ref[i], labels)
    contrast = jnp.zeros((rows, F), f32)
    for c in range(NCTF):
        contrast = jnp.where(labels == c, transfer_ref[c : c + 1, :], contrast)
    values = particles_ref[...].astype(f32)
    real = (values[:, 0, :] * contrast).astype(bf16)
    imag = (values[:, 1, :] * contrast).astype(bf16)
    for d in range(CHUNKS):
        lanes = slice(d * LANES, (d + 1) * LANES)
        packet_ref[:, 2 * d * LANES : (2 * d + 1) * LANES] = real[:, lanes]
        packet_ref[:, (2 * d + 1) * LANES : (2 * d + 2) * LANES] = imag[:, lanes]
    tags = jnp.broadcast_to(labels.astype(f32), (rows, LANES))
    packet_ref[:, 2 * F :] = tags.astype(bf16)


def prep(classes, particles, transfer, spectra, far):
    rows = particles.shape[0]
    return pl.pallas_call(
        prep_kernel,
        out_shape=(
            jax.ShapeDtypeStruct((rows, 2 * F + LANES), bf16),
            jax.ShapeDtypeStruct((far,) + spectra.shape, bf16),
        ),
        in_specs=[pl.BlockSpec(memory_space=pltpu.SMEM)] + [whole_vmem] * 3,
        out_specs=(whole_vmem, whole_vmem),
        compiler_params=room(60),
        name="prep",
    )(classes, particles, transfer, spectra)


def local_copy(kernel, blocks, scalars, arrays, name):
    shape = (blocks,) + arrays[0].shape[-2:]
    return pl.pallas_call(
        kernel,
        out_shape=jax.ShapeDtypeStruct(shape, bf16),
        in_specs=[pl.BlockSpec(memory_space=pltpu.SMEM)] * len(scalars) + [whole_vmem] * len(arrays),
        out_specs=whole_vmem,
        compiler_params=room(4),
        name=name,
    )(*scalars, *arrays)


def pair_kernel(side_ref, own_ref, mate_ref, out_ref):
    out_ref[side_ref[0]] = own_ref[...]
    out_ref[1 - side_ref[0]] = mate_ref[...]


def bundle_kernel(near_ref, far_ref, out_ref):
    out_ref[0:2] = near_ref[...]
    out_ref[2] = far_ref[...]


def gather_kernel(place_ref, side_ref, part_ref, slot_ref, pair_ref, own_ref, other_ref, out_ref):
    count = out_ref.shape[0] // 2
    place, side = place_ref[0], side_ref[0]
    below, above = lax.rem(place + count - 1, count), lax.rem(place + 1, count)
    across = lax.rem(place + 2, count)
    mine = jnp.where(side == 0, below, above)
    theirs = jnp.where(side == 0, above, below)
    for k in range(2):
        out_ref[k * count + place] = pair_ref[k]
        out_ref[k * count + mine] = own_ref[k]
        out_ref[k * count + theirs] = other_ref[k]
    out_ref[side * count + across] = own_ref[2]
    out_ref[(1 - side) * count + across] = other_ref[2]


def fold(values):
    return jnp.sum(values.reshape(values.shape[0] // 8, 8, values.shape[1]), axis=0)


def row_sums(tiles):
    row = lax.broadcasted_iota(jnp.int32, tiles[0].shape, 0)
    for bit in (1, 2, 4):
        even = (row // bit) % 2 == 0
        merged = []
        for a, b in zip(tiles[::2], tiles[1::2]):
            merged.append(
                jnp.where(even, a, b) + pltpu.roll(jnp.where(even, b, a), 8 - bit, 0)
            )
        tiles = merged
    return tiles[0]


def label_table(tags):
    lane = lax.broadcasted_iota(jnp.int32, tags.shape, 1) % NCTF
    return (tags.astype(f32) == lane.astype(f32)).astype(f32)


def score_kernel(
    own_refs,
    side_ref,
    spectra_ref,
    cos_ref,
    sin_ref,
    weighted_ref,
    transfer_ref,
    odds_ref,
    stats_ref,
    penalty_ref,
):
    groups = spectra_ref.shape[0] // CHUNKS
    refs = groups * own_refs
    side = side_ref[0]

    odds_ref[...] = jnp.zeros_like(odds_ref)
    penalty_ref[...] = jnp.zeros_like(penalty_ref)
    width = 2 * UNIT * LANES

    def unit(u):
        wide = pl.ds(pl.multiple_of(u * width, width), width)
        weighted = weighted_ref[:, wide]
        tables = []
        for j in range(UNIT):
            lanes = pl.ds(pl.multiple_of((u * UNIT + j) * LANES, LANES), LANES)
            transfer = transfer_ref[:, lanes]
            tables.append((cos_ref[:, lanes], sin_ref[:, lanes], transfer * transfer))
        for g in range(groups):
            blocks = []
            for j in range(UNIT):
                d = u * UNIT + j
                line = slant_line(side, 2 * g + d % 2, d // 2, CHUNKS // 2)
                blocks.append(spectra_ref[line].astype(f32))
            for first in range(0, own_refs, BATCH):
                rows = []
                for i in range(first, first + BATCH):
                    pieces = []
                    power = 0.0
                    for j in range(UNIT):
                        cos, sin, squared = tables[j]
                        real, imag = blocks[j][i, 0:1], blocks[j][i, 1:2]
                        pieces.append((real * cos - imag * sin).astype(bf16))
                        pieces.append((real * sin + imag * cos).astype(bf16))
                        power = power + (real * real + imag * imag) * squared
                    place = (g * own_refs + i) * NCTF
                    penalty_ref[place : place + NCTF, :] += power
                    rows.append(jnp.concatenate(pieces, axis=1))
                place = (g * own_refs + first) * SHIFTS
                odds_ref[place : place + BATCH * SHIFTS, :] += lax.dot_general(
                    jnp.concatenate(rows, axis=0),
                    weighted,
                    (((1,), (1,)), ((), ())),
                    preferred_element_type=f32,
                )

    def units(k, carry):
        for j in range(UNROLL):
            unit(k * UNROLL + j)
        return carry

    lax.fori_loop(0, CHUNKS // UNIT // UNROLL, units, 0)
    tags = weighted_ref[:, 2 * F :].astype(f32).T[:NCTF]
    hot = (tags == lax.broadcasted_iota(jnp.int32, tags.shape, 0).astype(f32)).astype(f32)
    top = None
    for r in range(refs):
        charge = jnp.sum(penalty_ref[r * NCTF : (r + 1) * NCTF, :], axis=1, keepdims=True)
        cost = 0.5 * jnp.sum(charge * hot, axis=0, keepdims=True)
        place = slice(r * SHIFTS, (r + 1) * SHIFTS)
        scores = odds_ref[place, :] - cost
        odds_ref[place, :] = scores
        high = jnp.max(scores, axis=0, keepdims=True)
        top = high if top is None else jnp.maximum(top, high)
    odds = jnp.exp(odds_ref[...] - top)
    odds_ref[...] = odds
    total = jnp.sum(odds, axis=0, keepdims=True)
    stats = jnp.concatenate([top, total], axis=0)
    spare = jnp.zeros((2, LANES - stats.shape[1]), f32)
    stats = jnp.concatenate([stats, spare], axis=1)
    stats_ref[...] = jnp.broadcast_to(stats[None], stats_ref.shape)


def make_scores(side, spectra, cos_table, sin_table, weighted, transfer, own_refs, near):
    groups = spectra.shape[0] // CHUNKS
    refs = groups * own_refs
    count = weighted.shape[0]
    return pl.pallas_call(
        functools.partial(score_kernel, own_refs),
        out_shape=(
            jax.ShapeDtypeStruct((refs * SHIFTS, count), f32),
            jax.ShapeDtypeStruct((near, 2, LANES), f32),
        ),
        in_specs=[pl.BlockSpec(memory_space=pltpu.SMEM)] + [whole_vmem] * 5,
        out_specs=(whole_vmem, whole_vmem),
        scratch_shapes=[
            pltpu.VMEM((refs * NCTF, LANES), f32),
        ],
        compiler_params=room(24),
        name="scores",
    )(side, spectra, cos_table, sin_table, weighted, transfer)


def back_kernel(
    own_refs,
    slot_ref,
    odds_ref,
    stats_ref,
    packets_ref,
    cos_ref,
    sin_ref,
    parts_ref,
    log_ref,
    posterior_ref,
):
    groups = parts_ref.shape[0] // CHUNKS
    refs = groups * own_refs
    count = odds_ref.shape[1]
    slot = slot_ref[0]
    tops, sums = stats_ref[:, 0, :count], stats_ref[:, 1, :count]
    top = jnp.max(tops, axis=0, keepdims=True)
    total = jnp.sum(sums * jnp.exp(tops - top), axis=0, keepdims=True)
    log_all = top + jnp.log(total)
    own_rows = log_ref.shape[1]
    own_log = jnp.zeros_like(log_ref)
    for k in range(count // own_rows):
        piece = log_all[:, k * own_rows : (k + 1) * own_rows]
        own_log = jnp.where(slot == k, piece, own_log)
    log_ref[...] = own_log
    scale = jnp.exp(stats_ref[slot][0:1, :count] - log_all)
    weights = []
    for r in range(refs):
        place = slice(r * SHIFTS, (r + 1) * SHIFTS)
        posterior = (odds_ref[place, :] * scale).astype(bf16)
        posterior_ref[place, :] = posterior
        weights.append(jnp.sum(posterior.astype(f32), axis=0, keepdims=True))
    weights = jnp.concatenate(weights, axis=0)
    high = weights.astype(bf16)
    low = (weights - high.astype(f32)).astype(bf16)
    hot = label_table(packets_ref[:, 2 * F :]).astype(bf16)
    spread = jnp.dot(jnp.concatenate([high, low], axis=0), hot, preferred_element_type=f32)
    spread = spread[:refs] + spread[refs:]
    lane = lax.broadcasted_iota(jnp.int32, (refs, LANES), 1) // NCTF
    row = lax.broadcasted_iota(jnp.int32, (refs, LANES), 0) % own_refs
    spread = jnp.where(lane == row, spread, 0.0)
    shares = []
    for g in range(groups):
        share = jnp.sum(spread[g * own_refs : (g + 1) * own_refs], axis=0, keepdims=True)
        high = share.astype(bf16).astype(f32)
        before = jnp.zeros((2 * own_refs, LANES), f32)
        after = jnp.zeros((ROWS - 2 * own_refs - 2, LANES), f32)
        shares.append(jnp.concatenate([before, high, share - high, after], axis=0))

    def chunk(d):
        lanes = pl.ds(pl.multiple_of(d * LANES, LANES), LANES)
        wide = pl.ds(pl.multiple_of(d * 2 * LANES, 2 * LANES), 2 * LANES)
        cos, sin = cos_ref[:, lanes], sin_ref[:, lanes]
        weighted = packets_ref[:, wide]
        for g in range(groups):
            rows = []
            for first in range(0, own_refs, BATCH):
                place = (g * own_refs + first) * SHIFTS
                totals = jnp.dot(
                    posterior_ref[place : place + BATCH * SHIFTS, :],
                    weighted,
                    preferred_element_type=f32,
                )
                for i in range(BATCH):
                    real = totals[i * SHIFTS : (i + 1) * SHIFTS, :LANES]
                    imag = totals[i * SHIFTS : (i + 1) * SHIFTS, LANES:]
                    rows.append(fold(real * cos + imag * sin))
                    rows.append(fold(imag * cos - real * sin))
            blank = [jnp.zeros((8, LANES), f32)] * (ROWS - len(rows))
            rows = rows + blank
            sums = jnp.concatenate([row_sums(rows[:8]), row_sums(rows[8:])], axis=0)
            line = peer_line(2 * g + d % 2, d // 2, 2 * groups, CHUNKS // 2)
            parts_ref[line] = (sums + shares[g]).astype(bf16)

    def chunks(k, carry):
        for j in range(UNROLL):
            chunk(k * UNROLL + j)
        return carry

    lax.fori_loop(0, CHUNKS // UNROLL, chunks, 0)


def back_project(slot, odds, stats, packets, cos_table, sin_table, own_refs, rows):
    count = packets.shape[0]
    groups = odds.shape[0] // SHIFTS // own_refs
    return pl.pallas_call(
        functools.partial(back_kernel, own_refs),
        out_shape=(
            jax.ShapeDtypeStruct((groups * CHUNKS, ROWS, LANES), bf16),
            jax.ShapeDtypeStruct((1, rows), f32),
        ),
        in_specs=[pl.BlockSpec(memory_space=pltpu.SMEM)] + [whole_vmem] * 5,
        out_specs=(whole_vmem, whole_vmem),
        scratch_shapes=[pltpu.VMEM((odds.shape[0], count), bf16)],
        compiler_params=room(24),
        name="back",
    )(slot, odds, stats, packets, cos_table, sin_table)


def finish_kernel(place_ref, parts_ref, transfer_ref, out_ref):
    own_refs = out_ref.shape[0]
    sums = jnp.sum(parts_ref[...].astype(f32), axis=0)
    share = sums[2 * own_refs : 2 * own_refs + 1] + sums[2 * own_refs + 1 : 2 * own_refs + 2]
    lane = lax.broadcasted_iota(jnp.int32, (own_refs, LANES), 1) // NCTF
    row = lax.broadcasted_iota(jnp.int32, (own_refs, LANES), 0)
    shares = jnp.where(lane == row, share, 0.0)
    own = transfer_ref[:, pl.ds(pl.multiple_of(place_ref[0] * LANES, LANES), LANES)]
    squared = jnp.concatenate([own * own] * (LANES // NCTF), axis=0)
    denominator = jnp.dot(shares, squared, precision=highest) + ridge_term
    for i in range(own_refs):
        out_ref[i] = sums[2 * i : 2 * i + 2] / denominator[i : i + 1]


def finish(place, parts, transfer, own_refs):
    return pl.pallas_call(
        finish_kernel,
        out_shape=jax.ShapeDtypeStruct((own_refs, 2, LANES), f32),
        in_specs=[pl.BlockSpec(memory_space=pltpu.SMEM)] + [whole_vmem] * 2,
        out_specs=whole_vmem,
        compiler_params=room(4),
        name="finish",
    )(place, parts, transfer)


def shifted(value, axis, steps):
    count = lax.axis_size(axis)
    pairs = [(source, (source + steps) % count) for source in range(count)]
    return lax.ppermute(value, axis, pairs)


def parted(value, steps):
    count = lax.axis_size("x")
    pairs = []
    for source in range(count):
        pairs.append((2 * source, 2 * ((source + steps) % count)))
        pairs.append((2 * source + 1, 2 * ((source - steps) % count) + 1))
    return lax.ppermute(value, ("x", "core"), pairs)


def peer_line(row, plane, rows, planes):
    ranks = (4, 1, 3, 6, 7, 5, 2, 0)
    rank = sum((plane == z) * r for z, r in enumerate(ranks[:planes]))
    return rank * rows + (row + rows // 2) % rows


def slant_line(side, row, plane, count):
    column = (plane + 1) % count
    step = count + side * column - (1 - side) * column
    return count * ((row + count // 2 + step) % count) + column


def slanted_exchange(value):
    yh, dom = lax.axis_size("yh"), lax.axis_size("dom")
    groups = []
    for side in range(2):
        order = [0] * (yh * dom)
        for y in range(yh):
            for d in range(dom):
                line = slant_line(side, 2 * y + d % 2, d // 2, dom // 2)
                order[line] = (side * yh + y) * dom + d
        groups.append(order)
    return lax.all_to_all(value, ("core", "yh", "dom"), 0, 0, axis_index_groups=groups)


def wide_exchange(value):
    yh, dom = lax.axis_size("yh"), lax.axis_size("dom")
    order = [0] * (yh * dom)
    for y in range(yh):
        for d in range(dom):
            order[peer_line(2 * y + d % 2, d // 2, 2 * yh, dom // 2)] = y * dom + d
    return lax.all_to_all(value, ("yh", "dom"), 0, 0, axis_index_groups=[order])


def body(particles, classes, template_spectra, transfer_magnitude, offsets):
    rows = particles.shape[0]
    own_refs = template_spectra.shape[0]
    near_axes = ("core", "x")
    near, far = lax.axis_size(near_axes), lax.axis_size(("yh", "dom"))
    packet, copies = prep(classes, particles, transfer_magnitude, template_spectra, far)
    place, side, part = [lax.axis_index(name)[None] for name in ("x", "core", "dom")]
    slot = lax.axis_index(near_axes)[None]
    mate = shifted(packet, "core", 1)
    far_packet = parted(packet, 2)
    pair = local_copy(pair_kernel, 2, [side], [packet, mate], "pair")
    copies, pair = lax.optimization_barrier((copies, pair))
    spectra = slanted_exchange(copies)
    own = local_copy(bundle_kernel, 3, [], [parted(pair, 1), far_packet], "bundle")
    own, offsets = lax.optimization_barrier((own, offsets))
    other = shifted(own, "core", 1)
    spots = [place, side, part, slot]
    weighted = local_copy(gather_kernel, near, spots, [pair, own, other], "gather")
    weighted = weighted.reshape(near * rows, weighted.shape[-1])
    cos_table, sin_table = phase_tables(offsets)
    odds, stats = make_scores(
        side, spectra, cos_table, sin_table, weighted, transfer_magnitude, own_refs, near
    )
    stats = lax.all_to_all(stats, near_axes, 0, 0)
    parts, log_own = back_project(
        slot, odds, stats, weighted, cos_table, sin_table, own_refs, rows
    )
    parts = wide_exchange(parts)
    new_refs = finish(part, parts, transfer_magnitude, own_refs)
    return (log_own.reshape(rows), new_refs)


def solution(mesh):
    devices = mesh.devices
    names = ("yh", "x", "core", "dom")
    inner = Mesh(devices.reshape(4, 4, 2, devices.shape[1]), names)
    refs = names[:3]
    return jax.shard_map(
        body,
        mesh=inner,
        in_specs=(P(names, None, None), P(names), P(refs, None, "dom"), P(), P()),
        out_specs=(P(names), P(refs, None, "dom")),
        check_vma=False,
    )
```

```python
import functools
import math

import jax
import jax.numpy as jnp
from jax import lax
from jax.experimental import pallas as pl
from jax.experimental.pallas import tpu as pltpu
from jax.sharding import Mesh
from jax.sharding import PartitionSpec as P

BOX = 64
F = 2048
SHIFTS = 64
NCTF = 16
LANES = 128
CHUNKS = F // LANES
ROWS = 16
UNIT = 2
UNROLL = 4
BATCH = 2

highest = lax.Precision.HIGHEST
ridge_term = 1.0
f32 = jnp.float32
bf16 = jnp.bfloat16
whole_vmem = pl.BlockSpec(memory_space=pltpu.VMEM)


def room(mib):
    return pltpu.CompilerParams(vmem_limit_bytes=mib * 1024 * 1024)


def phase_tables(offsets):
    half_side = BOX // 2
    positions = jnp.arange(F, dtype=jnp.int32)
    row_index = positions // half_side
    freq_x = jnp.where(row_index < half_side, row_index, row_index - BOX)
    freq_y = positions % half_side
    turn_count = (offsets[:, 0:1] * freq_x[None, :] + offsets[:, 1:2] * freq_y[None, :]) % BOX
    angles = turn_count.astype(f32) * (2.0 * math.pi / BOX)
    cos, sin = jnp.cos(angles), jnp.sin(angles)
    return (cos, sin + cos, sin - cos)


def prep_kernel(classes_ref, particles_ref, transfer_ref, spectra_ref, packet_ref, copies_ref):
    rows = particles_ref.shape[0]
    copies_ref[...] = jnp.broadcast_to(spectra_ref[...][None], copies_ref.shape)
    place = lax.broadcasted_iota(jnp.int32, (rows, 1), 0)
    labels = jnp.zeros((rows, 1), jnp.int32)
    for i in range(rows):
        labels = jnp.where(place == i, classes_ref[i], labels)
    contrast = jnp.zeros((rows, F), f32)
    for c in range(NCTF):
        contrast = jnp.where(labels == c, transfer_ref[c : c + 1, :], contrast)
    values = particles_ref[...].astype(f32)
    real = (values[:, 0, :] * contrast).astype(bf16)
    imag = (values[:, 1, :] * contrast).astype(bf16)
    for d in range(CHUNKS):
        lanes = slice(d * LANES, (d + 1) * LANES)
        packet_ref[:, 2 * d * LANES : (2 * d + 1) * LANES] = real[:, lanes]
        packet_ref[:, (2 * d + 1) * LANES : (2 * d + 2) * LANES] = imag[:, lanes]
    tags = jnp.broadcast_to(labels.astype(f32), (rows, LANES))
    packet_ref[:, 2 * F :] = tags.astype(bf16)


def prep(classes, particles, transfer, spectra, far):
    rows = particles.shape[0]
    return pl.pallas_call(
        prep_kernel,
        out_shape=(
            jax.ShapeDtypeStruct((rows, 2 * F + LANES), bf16),
            jax.ShapeDtypeStruct((far,) + spectra.shape, bf16),
        ),
        in_specs=[pl.BlockSpec(memory_space=pltpu.SMEM)] + [whole_vmem] * 3,
        out_specs=(whole_vmem, whole_vmem),
        compiler_params=room(60),
        name="prep",
    )(classes, particles, transfer, spectra)


def arrange_kernel(place_ref, side_ref, part_ref, slot_ref, *refs):
    count = len(refs) - 1
    for k in range(count):
        step = jnp.where(side_ref[0] == 0, count - k, k)
        refs[count][lax.rem(place_ref[0] + step, count)] = refs[k][...]


def arrange(place, side, part, slot, packets):
    rows, width = packets[0].shape
    ordered = pl.pallas_call(
        arrange_kernel,
        out_shape=jax.ShapeDtypeStruct((len(packets), rows, width), bf16),
        in_specs=[pl.BlockSpec(memory_space=pltpu.SMEM)] * 4 + [whole_vmem] * len(packets),
        out_specs=whole_vmem,
        compiler_params=room(4),
        name="arrange",
    )(place, side, part, slot, *packets)
    return ordered.reshape(len(packets) * rows, width)


def fold(values):
    return jnp.sum(values.reshape(values.shape[0] // 8, 8, values.shape[1]), axis=0)


def row_sums(tiles):
    row = lax.broadcasted_iota(jnp.int32, tiles[0].shape, 0)
    for bit in (1, 2, 4):
        even = (row // bit) % 2 == 0
        merged = []
        for a, b in zip(tiles[::2], tiles[1::2]):
            merged.append(
                jnp.where(even, a, b) + pltpu.roll(jnp.where(even, b, a), 8 - bit, 0)
            )
        tiles = merged
    return tiles[0]


def label_table(tags):
    lane = lax.broadcasted_iota(jnp.int32, tags.shape, 1) % NCTF
    return (tags.astype(f32) == lane.astype(f32)).astype(f32)


def score_kernel(
    own_refs,
    side_ref,
    spectra_ref,
    cos_ref,
    plus_ref,
    minus_ref,
    own_ref,
    other_ref,
    transfer_ref,
    odds_ref,
    mass_ref,
    stats_ref,
    weighted_ref,
    scores_ref,
    penalty_ref,
):
    groups = spectra_ref.shape[0] // CHUNKS
    refs = groups * own_refs
    half = own_ref.shape[0]
    side = side_ref[0]

    own, other = own_ref[...], other_ref[...]
    weighted_ref[:half, :] = jnp.where(side == 0, own, other)
    weighted_ref[half:, :] = jnp.where(side == 0, other, own)
    scores_ref[...] = jnp.zeros_like(scores_ref)
    penalty_ref[...] = jnp.zeros_like(penalty_ref)
    width = 2 * UNIT * LANES

    def unit(u):
        wide = pl.ds(pl.multiple_of(u * width, width), width)
        weighted = weighted_ref[:, wide]
        tables = []
        for j in range(UNIT):
            lanes = pl.ds(pl.multiple_of((u * UNIT + j) * LANES, LANES), LANES)
            transfer = transfer_ref[:, lanes]
            turns = (cos_ref[:, lanes], plus_ref[:, lanes], minus_ref[:, lanes])
            tables.append(turns + (transfer * transfer,))
        for g in range(groups):
            blocks = []
            for j in range(UNIT):
                d = u * UNIT + j
                line = slant_line(side, 2 * g + d % 2, d // 2, CHUNKS // 2)
                blocks.append(spectra_ref[line].astype(f32))
            for first in range(0, own_refs, BATCH):
                rows = []
                for i in range(first, first + BATCH):
                    pieces = []
                    power = 0.0
                    for j in range(UNIT):
                        cos, plus, minus, squared = tables[j]
                        real, imag = blocks[j][i, 0:1], blocks[j][i, 1:2]
                        both = (real + imag) * cos
                        pieces.append((both - imag * plus).astype(bf16))
                        pieces.append((both + real * minus).astype(bf16))
                        power = power + (real * real + imag * imag) * squared
                    place = (g * own_refs + i) * NCTF
                    penalty_ref[place : place + NCTF, :] += power
                    rows.append(jnp.concatenate(pieces, axis=1))
                place = (g * own_refs + first) * SHIFTS
                scores_ref[place : place + BATCH * SHIFTS, :] += lax.dot_general(
                    jnp.concatenate(rows, axis=0),
                    weighted,
                    (((1,), (1,)), ((), ())),
                    preferred_element_type=f32,
                )

    def units(k, carry):
        for j in range(UNROLL):
            unit(k * UNROLL + j)
        return carry

    lax.fori_loop(0, CHUNKS // UNIT // UNROLL, units, 0)
    tags = weighted_ref[:, 2 * F :].astype(f32).T[:NCTF]
    hot = (tags == lax.broadcasted_iota(jnp.int32, tags.shape, 0).astype(f32)).astype(f32)
    top = None
    for r in range(refs):
        charge = jnp.sum(penalty_ref[r * NCTF : (r + 1) * NCTF, :], axis=1, keepdims=True)
        cost = 0.5 * jnp.sum(charge * hot, axis=0, keepdims=True)
        place = slice(r * SHIFTS, (r + 1) * SHIFTS)
        scores = scores_ref[place, :] - cost
        scores_ref[place, :] = scores
        high = jnp.max(scores, axis=0, keepdims=True)
        top = high if top is None else jnp.maximum(top, high)
    total = jnp.zeros_like(top)
    masses = []
    for r in range(refs):
        place = slice(r * SHIFTS, (r + 1) * SHIFTS)
        odds = jnp.exp(scores_ref[place, :] - top)
        total = total + jnp.sum(odds, axis=0, keepdims=True)
        odds = odds.astype(bf16)
        odds_ref[place, :] = odds
        masses.append(jnp.sum(odds.astype(f32), axis=0, keepdims=True))
    mass_ref[...] = jnp.concatenate(masses, axis=0)
    stats = jnp.concatenate([top, total], axis=0)
    spare = jnp.zeros((2, LANES - stats.shape[1]), f32)
    stats = jnp.concatenate([stats, spare], axis=1)
    stats_ref[...] = jnp.broadcast_to(stats[None], stats_ref.shape)


def make_scores(side, spectra, tables, own, other, transfer, own_refs, near):
    groups = spectra.shape[0] // CHUNKS
    refs = groups * own_refs
    count = 2 * own.shape[0]
    return pl.pallas_call(
        functools.partial(score_kernel, own_refs),
        out_shape=(
            jax.ShapeDtypeStruct((refs * SHIFTS, count), bf16),
            jax.ShapeDtypeStruct((refs, count), f32),
            jax.ShapeDtypeStruct((near, 2, LANES), f32),
            jax.ShapeDtypeStruct((count, own.shape[1]), bf16),
        ),
        in_specs=[pl.BlockSpec(memory_space=pltpu.SMEM)] + [whole_vmem] * 7,
        out_specs=(whole_vmem,) * 4,
        scratch_shapes=[
            pltpu.VMEM((refs * SHIFTS, count), f32),
            pltpu.VMEM((refs * NCTF, LANES), f32),
        ],
        compiler_params=room(24),
        name="scores",
    )(side, spectra, *tables, own, other, transfer)


def back_kernel(
    own_refs,
    slot_ref,
    odds_ref,
    mass_ref,
    stats_ref,
    packets_ref,
    cos_ref,
    plus_ref,
    minus_ref,
    parts_ref,
    log_ref,
):
    groups = parts_ref.shape[0] // CHUNKS
    refs = groups * own_refs
    count = odds_ref.shape[1]
    slot = slot_ref[0]
    tops, sums = stats_ref[:, 0, :count], stats_ref[:, 1, :count]
    top = jnp.max(tops, axis=0, keepdims=True)
    total = jnp.sum(sums * jnp.exp(tops - top), axis=0, keepdims=True)
    log_all = top + jnp.log(total)
    own_rows = log_ref.shape[1]
    own_log = jnp.zeros_like(log_ref)
    for k in range(count // own_rows):
        piece = log_all[:, k * own_rows : (k + 1) * own_rows]
        own_log = jnp.where(slot == k, piece, own_log)
    log_ref[...] = own_log
    scale = jnp.exp(stats_ref[slot][0:1, :count] - log_all)
    weights = mass_ref[...] * scale
    column = jnp.broadcast_to(scale, (LANES, count)).T
    column = jnp.concatenate([column, column], axis=1)
    high = weights.astype(bf16)
    low = (weights - high.astype(f32)).astype(bf16)
    hot = label_table(packets_ref[:, 2 * F :]).astype(bf16)
    spread = jnp.dot(jnp.concatenate([high, low], axis=0), hot, preferred_element_type=f32)
    spread = spread[:refs] + spread[refs:]
    lane = lax.broadcasted_iota(jnp.int32, (refs, LANES), 1) // NCTF
    row = lax.broadcasted_iota(jnp.int32, (refs, LANES), 0) % own_refs
    spread = jnp.where(lane == row, spread, 0.0)
    shares = []
    for g in range(groups):
        share = jnp.sum(spread[g * own_refs : (g + 1) * own_refs], axis=0, keepdims=True)
        high = share.astype(bf16).astype(f32)
        before = jnp.zeros((2 * own_refs, LANES), f32)
        after = jnp.zeros((ROWS - 2 * own_refs - 2, LANES), f32)
        shares.append(jnp.concatenate([before, high, share - high, after], axis=0))

    def chunk(d):
        lanes = pl.ds(pl.multiple_of(d * LANES, LANES), LANES)
        wide = pl.ds(pl.multiple_of(d * 2 * LANES, 2 * LANES), 2 * LANES)
        cos, plus, minus = cos_ref[:, lanes], plus_ref[:, lanes], minus_ref[:, lanes]
        weighted = (packets_ref[:, wide].astype(f32) * column).astype(bf16)
        for g in range(groups):
            rows = []
            for first in range(0, own_refs, BATCH):
                place = (g * own_refs + first) * SHIFTS
                totals = jnp.dot(
                    odds_ref[place : place + BATCH * SHIFTS, :],
                    weighted,
                    preferred_element_type=f32,
                )
                for i in range(BATCH):
                    real = totals[i * SHIFTS : (i + 1) * SHIFTS, :LANES]
                    imag = totals[i * SHIFTS : (i + 1) * SHIFTS, LANES:]
                    both = fold((real + imag) * cos)
                    rows.append(both + fold(imag * minus))
                    rows.append(both - fold(real * plus))
            blank = [jnp.zeros((8, LANES), f32)] * (ROWS - len(rows))
            rows = rows + blank
            sums = jnp.concatenate([row_sums(rows[:8]), row_sums(rows[8:])], axis=0)
            line = peer_line(2 * g + d % 2, d // 2, 2 * groups, CHUNKS // 2)
            parts_ref[line] = (sums + shares[g]).astype(bf16)

    def chunks(k, carry):
        for j in range(UNROLL):
            chunk(k * UNROLL + j)
        return carry

    lax.fori_loop(0, CHUNKS // UNROLL, chunks, 0)


def back_project(slot, odds, mass, stats, packets, tables, own_refs, rows):
    count = packets.shape[0]
    groups = odds.shape[0] // SHIFTS // own_refs
    return pl.pallas_call(
        functools.partial(back_kernel, own_refs),
        out_shape=(
            jax.ShapeDtypeStruct((groups * CHUNKS, ROWS, LANES), bf16),
            jax.ShapeDtypeStruct((1, rows), f32),
        ),
        in_specs=[pl.BlockSpec(memory_space=pltpu.SMEM)] + [whole_vmem] * 7,
        out_specs=(whole_vmem, whole_vmem),
        compiler_params=room(24),
        name="back",
    )(slot, odds, mass, stats, packets, *tables)


def finish_kernel(place_ref, parts_ref, transfer_ref, out_ref):
    own_refs = out_ref.shape[0]
    sums = jnp.sum(parts_ref[...].astype(f32), axis=0)
    share = sums[2 * own_refs : 2 * own_refs + 1] + sums[2 * own_refs + 1 : 2 * own_refs + 2]
    lane = lax.broadcasted_iota(jnp.int32, (own_refs, LANES), 1) // NCTF
    row = lax.broadcasted_iota(jnp.int32, (own_refs, LANES), 0)
    shares = jnp.where(lane == row, share, 0.0)
    own = transfer_ref[:, pl.ds(pl.multiple_of(place_ref[0] * LANES, LANES), LANES)]
    squared = jnp.concatenate([own * own] * (LANES // NCTF), axis=0)
    denominator = jnp.dot(shares, squared, precision=highest) + ridge_term
    for i in range(own_refs):
        out_ref[i] = sums[2 * i : 2 * i + 2] / denominator[i : i + 1]


def finish(place, parts, transfer, own_refs):
    return pl.pallas_call(
        finish_kernel,
        out_shape=jax.ShapeDtypeStruct((own_refs, 2, LANES), f32),
        in_specs=[pl.BlockSpec(memory_space=pltpu.SMEM)] + [whole_vmem] * 2,
        out_specs=whole_vmem,
        compiler_params=room(4),
        name="finish",
    )(place, parts, transfer)


def shifted(value, axis, steps):
    count = lax.axis_size(axis)
    pairs = [(source, (source + steps) % count) for source in range(count)]
    return lax.ppermute(value, axis, pairs)


def parted(value, steps):
    count = lax.axis_size("x")
    pairs = []
    for source in range(count):
        pairs.append((2 * source, 2 * ((source + steps) % count)))
        pairs.append((2 * source + 1, 2 * ((source - steps) % count) + 1))
    return lax.ppermute(value, ("x", "core"), pairs)


def peer_line(row, plane, rows, planes):
    return (planes - 1 - plane) * rows + (row + rows // 2) % rows


def slant_line(side, row, plane, count):
    column = (plane + 1) % count
    step = count + side * column - (1 - side) * column
    return count * ((row + count // 2 + step) % count) + column


def slanted_exchange(value):
    yh, dom = lax.axis_size("yh"), lax.axis_size("dom")
    groups = []
    for side in range(2):
        order = [0] * (yh * dom)
        for y in range(yh):
            for d in range(dom):
                line = slant_line(side, 2 * y + d % 2, d // 2, dom // 2)
                order[line] = (side * yh + y) * dom + d
        groups.append(order)
    return lax.all_to_all(value, ("core", "yh", "dom"), 0, 0, axis_index_groups=groups)


def wide_exchange(value):
    yh, dom = lax.axis_size("yh"), lax.axis_size("dom")
    order = [0] * (yh * dom)
    for y in range(yh):
        for d in range(dom):
            order[peer_line(2 * y + d % 2, d // 2, 2 * yh, dom // 2)] = y * dom + d
    return lax.all_to_all(value, ("yh", "dom"), 0, 0, axis_index_groups=[order])


def body(particles, classes, template_spectra, transfer_magnitude, offsets):
    rows = particles.shape[0]
    own_refs = template_spectra.shape[0]
    near_axes = ("core", "x")
    near, far = lax.axis_size(near_axes), lax.axis_size(("yh", "dom"))
    packet, copies = prep(classes, particles, transfer_magnitude, template_spectra, far)
    spectra = slanted_exchange(copies)
    place, side, part = [lax.axis_index(name)[None] for name in ("x", "core", "dom")]
    slot = lax.axis_index(near_axes)[None]
    second, first, third = parted(packet, 2), parted(packet, 1), parted(packet, 3)
    own = arrange(place, side, part, slot, [packet, first, second, third])
    other = shifted(own, "core", 1)
    tables = phase_tables(offsets)
    odds, mass, stats, weighted = make_scores(
        side, spectra, tables, own, other, transfer_magnitude, own_refs, near
    )
    stats = lax.all_to_all(stats, near_axes, 0, 0)
    parts, log_own = back_project(
        slot, odds, mass, stats, weighted, tables, own_refs, rows
    )
    parts = wide_exchange(parts)
    new_refs = finish(part, parts, transfer_magnitude, own_refs)
    return (log_own.reshape(rows), new_refs)


def solution(mesh):
    devices = mesh.devices
    names = ("yh", "x", "core", "dom")
    inner = Mesh(devices.reshape(4, 4, 2, devices.shape[1]), names)
    refs = names[:3]
    return jax.shard_map(
        body,
        mesh=inner,
        in_specs=(P(names, None, None), P(names), P(refs, None, "dom"), P(), P()),
        out_specs=(P(names), P(refs, None, "dom")),
        check_vma=False,
    )
```

```python
import functools
import math

import jax
import jax.numpy as jnp
from jax import lax
from jax.experimental import pallas as pl
from jax.experimental.pallas import tpu as pltpu
from jax.sharding import Mesh
from jax.sharding import PartitionSpec as P

BOX = 64
F = 2048
SHIFTS = 64
NCTF = 16
LANES = 128
CHUNKS = F // LANES
ROWS = 16
UNIT = 2
UNROLL = 4
BATCH = 6

highest = lax.Precision.HIGHEST
ridge_term = 1.0
f32 = jnp.float32
bf16 = jnp.bfloat16
whole_vmem = pl.BlockSpec(memory_space=pltpu.VMEM)


def room(mib):
    return pltpu.CompilerParams(vmem_limit_bytes=mib * 1024 * 1024)


def phase_tables(offsets):
    half_side = BOX // 2
    positions = jnp.arange(F, dtype=jnp.int32)
    row_index = positions // half_side
    freq_x = jnp.where(row_index < half_side, row_index, row_index - BOX)
    freq_y = positions % half_side
    turn_count = (offsets[:, 0:1] * freq_x[None, :] + offsets[:, 1:2] * freq_y[None, :]) % BOX
    angles = turn_count.astype(f32) * (2.0 * math.pi / BOX)
    return (jnp.cos(angles), jnp.sin(angles))


def prep_kernel(classes_ref, particles_ref, transfer_ref, spectra_ref, packet_ref, copies_ref):
    rows = particles_ref.shape[0]
    copies_ref[...] = jnp.broadcast_to(spectra_ref[...][None], copies_ref.shape)
    place = lax.broadcasted_iota(jnp.int32, (rows, 1), 0)
    labels = jnp.zeros((rows, 1), jnp.int32)
    for i in range(rows):
        labels = jnp.where(place == i, classes_ref[i], labels)
    contrast = jnp.zeros((rows, F), f32)
    for c in range(NCTF):
        contrast = jnp.where(labels == c, transfer_ref[c : c + 1, :], contrast)
    values = particles_ref[...].astype(f32)
    real = (values[:, 0, :] * contrast).astype(bf16)
    imag = (values[:, 1, :] * contrast).astype(bf16)
    for d in range(CHUNKS):
        lanes = slice(d * LANES, (d + 1) * LANES)
        packet_ref[:, 2 * d * LANES : (2 * d + 1) * LANES] = real[:, lanes]
        packet_ref[:, (2 * d + 1) * LANES : (2 * d + 2) * LANES] = imag[:, lanes]
    tags = jnp.broadcast_to(labels.astype(f32), (rows, LANES))
    packet_ref[:, 2 * F :] = tags.astype(bf16)


def prep(classes, particles, transfer, spectra, far):
    rows = particles.shape[0]
    return pl.pallas_call(
        prep_kernel,
        out_shape=(
            jax.ShapeDtypeStruct((rows, 2 * F + LANES), bf16),
            jax.ShapeDtypeStruct((far,) + spectra.shape, bf16),
        ),
        in_specs=[pl.BlockSpec(memory_space=pltpu.SMEM)] + [whole_vmem] * 3,
        out_specs=(whole_vmem, whole_vmem),
        compiler_params=room(60),
        name="prep",
    )(classes, particles, transfer, spectra)


def arrange_kernel(place_ref, side_ref, part_ref, slot_ref, *refs):
    count = len(refs) - 1
    for k in range(count):
        step = jnp.where(side_ref[0] == 0, count - k, k)
        refs[count][lax.rem(place_ref[0] + step, count)] = refs[k][...]


def arrange(place, side, part, slot, packets):
    rows, width = packets[0].shape
    ordered = pl.pallas_call(
        arrange_kernel,
        out_shape=jax.ShapeDtypeStruct((len(packets), rows, width), bf16),
        in_specs=[pl.BlockSpec(memory_space=pltpu.SMEM)] * 4 + [whole_vmem] * len(packets),
        out_specs=whole_vmem,
        compiler_params=room(4),
        name="arrange",
    )(place, side, part, slot, *packets)
    return ordered.reshape(len(packets) * rows, width)


def fold(values):
    return jnp.sum(values.reshape(values.shape[0] // 8, 8, values.shape[1]), axis=0)


def row_sums(tiles):
    row = lax.broadcasted_iota(jnp.int32, tiles[0].shape, 0)
    for bit in (1, 2, 4):
        even = (row // bit) % 2 == 0
        merged = []
        for a, b in zip(tiles[::2], tiles[1::2]):
            merged.append(
                jnp.where(even, a, b) + pltpu.roll(jnp.where(even, b, a), 8 - bit, 0)
            )
        tiles = merged
    return tiles[0]


def label_table(tags):
    lane = lax.broadcasted_iota(jnp.int32, tags.shape, 1) % NCTF
    return (tags.astype(f32) == lane.astype(f32)).astype(f32)


def score_kernel(
    own_refs,
    side_ref,
    spectra_ref,
    cos_ref,
    sin_ref,
    own_ref,
    other_ref,
    transfer_ref,
    odds_ref,
    stats_ref,
    weighted_ref,
    penalty_ref,
):
    groups = spectra_ref.shape[0] // CHUNKS
    refs = groups * own_refs
    half = own_ref.shape[0]
    side = side_ref[0]

    own, other = own_ref[...], other_ref[...]
    weighted_ref[:half, :] = jnp.where(side == 0, own, other)
    weighted_ref[half:, :] = jnp.where(side == 0, other, own)
    odds_ref[...] = jnp.zeros_like(odds_ref)
    penalty_ref[...] = jnp.zeros_like(penalty_ref)
    width = 2 * UNIT * LANES

    def unit(u):
        wide = pl.ds(pl.multiple_of(u * width, width), width)
        weighted = weighted_ref[:, wide]
        tables = []
        for j in range(UNIT):
            lanes = pl.ds(pl.multiple_of((u * UNIT + j) * LANES, LANES), LANES)
            transfer = transfer_ref[:, lanes]
            tables.append((cos_ref[:, lanes], sin_ref[:, lanes], transfer * transfer))
        for g in range(groups):
            blocks = []
            for j in range(UNIT):
                d = u * UNIT + j
                line = slant_line(side, 2 * g + d % 2, d // 2, CHUNKS // 2)
                blocks.append(spectra_ref[line].astype(f32))
            for first in range(0, own_refs, BATCH):
                rows = []
                for i in range(first, first + BATCH):
                    pieces = []
                    power = 0.0
                    for j in range(UNIT):
                        cos, sin, squared = tables[j]
                        real, imag = blocks[j][i, 0:1], blocks[j][i, 1:2]
                        pieces.append((real * cos - imag * sin).astype(bf16))
                        pieces.append((real * sin + imag * cos).astype(bf16))
                        power = power + (real * real + imag * imag) * squared
                    place = (g * own_refs + i) * NCTF
                    penalty_ref[place : place + NCTF, :] += power
                    rows.append(jnp.concatenate(pieces, axis=1))
                place = (g * own_refs + first) * SHIFTS
                odds_ref[place : place + BATCH * SHIFTS, :] += lax.dot_general(
                    jnp.concatenate(rows, axis=0),
                    weighted,
                    (((1,), (1,)), ((), ())),
                    preferred_element_type=f32,
                )

    def units(k, carry):
        for j in range(UNROLL):
            unit(k * UNROLL + j)
        return carry

    lax.fori_loop(0, CHUNKS // UNIT // UNROLL, units, 0)
    tags = weighted_ref[:, 2 * F :].astype(f32).T[:NCTF]
    hot = (tags == lax.broadcasted_iota(jnp.int32, tags.shape, 0).astype(f32)).astype(f32)
    top = None
    for r in range(refs):
        charge = jnp.sum(penalty_ref[r * NCTF : (r + 1) * NCTF, :], axis=1, keepdims=True)
        cost = 0.5 * jnp.sum(charge * hot, axis=0, keepdims=True)
        place = slice(r * SHIFTS, (r + 1) * SHIFTS)
        scores = odds_ref[place, :] - cost
        odds_ref[place, :] = scores
        high = jnp.max(scores, axis=0, keepdims=True)
        top = high if top is None else jnp.maximum(top, high)
    odds = jnp.exp(odds_ref[...] - top)
    odds_ref[...] = odds
    total = jnp.sum(odds, axis=0, keepdims=True)
    stats = jnp.concatenate([top, total], axis=0)
    spare = jnp.zeros((2, LANES - stats.shape[1]), f32)
    stats = jnp.concatenate([stats, spare], axis=1)
    stats_ref[...] = jnp.broadcast_to(stats[None], stats_ref.shape)


def make_scores(side, spectra, cos_table, sin_table, own, other, transfer, own_refs, near):
    groups = spectra.shape[0] // CHUNKS
    refs = groups * own_refs
    count = 2 * own.shape[0]
    return pl.pallas_call(
        functools.partial(score_kernel, own_refs),
        out_shape=(
            jax.ShapeDtypeStruct((refs * SHIFTS, count), f32),
            jax.ShapeDtypeStruct((near, 2, LANES), f32),
            jax.ShapeDtypeStruct((count, own.shape[1]), bf16),
        ),
        in_specs=[pl.BlockSpec(memory_space=pltpu.SMEM)] + [whole_vmem] * 6,
        out_specs=(whole_vmem, whole_vmem, whole_vmem),
        scratch_shapes=[
            pltpu.VMEM((refs * NCTF, LANES), f32),
        ],
        compiler_params=room(24),
        name="scores",
    )(side, spectra, cos_table, sin_table, own, other, transfer)


def back_kernel(
    own_refs,
    slot_ref,
    odds_ref,
    stats_ref,
    packets_ref,
    cos_ref,
    sin_ref,
    parts_ref,
    log_ref,
    posterior_ref,
):
    groups = parts_ref.shape[0] // CHUNKS
    refs = groups * own_refs
    count = odds_ref.shape[1]
    slot = slot_ref[0]
    tops, sums = stats_ref[:, 0, :count], stats_ref[:, 1, :count]
    top = jnp.max(tops, axis=0, keepdims=True)
    total = jnp.sum(sums * jnp.exp(tops - top), axis=0, keepdims=True)
    log_all = top + jnp.log(total)
    own_rows = log_ref.shape[1]
    own_log = jnp.zeros_like(log_ref)
    for k in range(count // own_rows):
        piece = log_all[:, k * own_rows : (k + 1) * own_rows]
        own_log = jnp.where(slot == k, piece, own_log)
    log_ref[...] = own_log
    scale = jnp.exp(stats_ref[slot][0:1, :count] - log_all)
    weights = []
    for r in range(refs):
        place = slice(r * SHIFTS, (r + 1) * SHIFTS)
        posterior = (odds_ref[place, :] * scale).astype(bf16)
        posterior_ref[place, :] = posterior
        weights.append(jnp.sum(posterior.astype(f32), axis=0, keepdims=True))
    weights = jnp.concatenate(weights, axis=0)
    high = weights.astype(bf16)
    low = (weights - high.astype(f32)).astype(bf16)
    hot = label_table(packets_ref[:, 2 * F :]).astype(bf16)
    spread = jnp.dot(jnp.concatenate([high, low], axis=0), hot, preferred_element_type=f32)
    spread = spread[:refs] + spread[refs:]
    lane = lax.broadcasted_iota(jnp.int32, (refs, LANES), 1) // NCTF
    row = lax.broadcasted_iota(jnp.int32, (refs, LANES), 0) % own_refs
    spread = jnp.where(lane == row, spread, 0.0)
    shares = []
    for g in range(groups):
        share = jnp.sum(spread[g * own_refs : (g + 1) * own_refs], axis=0, keepdims=True)
        high = share.astype(bf16).astype(f32)
        before = jnp.zeros((2 * own_refs, LANES), f32)
        after = jnp.zeros((ROWS - 2 * own_refs - 2, LANES), f32)
        shares.append(jnp.concatenate([before, high, share - high, after], axis=0))

    def chunk(d):
        lanes = pl.ds(pl.multiple_of(d * LANES, LANES), LANES)
        wide = pl.ds(pl.multiple_of(d * 2 * LANES, 2 * LANES), 2 * LANES)
        cos, sin = cos_ref[:, lanes], sin_ref[:, lanes]
        weighted = packets_ref[:, wide]
        for g in range(groups):
            rows = []
            for first in range(0, own_refs, BATCH):
                place = (g * own_refs + first) * SHIFTS
                totals = jnp.dot(
                    posterior_ref[place : place + BATCH * SHIFTS, :],
                    weighted,
                    preferred_element_type=f32,
                )
                for i in range(BATCH):
                    real = totals[i * SHIFTS : (i + 1) * SHIFTS, :LANES]
                    imag = totals[i * SHIFTS : (i + 1) * SHIFTS, LANES:]
                    rows.append(fold(real * cos + imag * sin))
                    rows.append(fold(imag * cos - real * sin))
            blank = [jnp.zeros((8, LANES), f32)] * (ROWS - len(rows))
            rows = rows + blank
            sums = jnp.concatenate([row_sums(rows[:8]), row_sums(rows[8:])], axis=0)
            line = peer_line(2 * g + d % 2, d // 2, 2 * groups, CHUNKS // 2)
            parts_ref[line] = (sums + shares[g]).astype(bf16)

    def chunks(k, carry):
        for j in range(UNROLL):
            chunk(k * UNROLL + j)
        return carry

    lax.fori_loop(0, CHUNKS // UNROLL, chunks, 0)


def back_project(slot, odds, stats, packets, cos_table, sin_table, own_refs, rows):
    count = packets.shape[0]
    groups = odds.shape[0] // SHIFTS // own_refs
    return pl.pallas_call(
        functools.partial(back_kernel, own_refs),
        out_shape=(
            jax.ShapeDtypeStruct((groups * CHUNKS, ROWS, LANES), bf16),
            jax.ShapeDtypeStruct((1, rows), f32),
        ),
        in_specs=[pl.BlockSpec(memory_space=pltpu.SMEM)] + [whole_vmem] * 5,
        out_specs=(whole_vmem, whole_vmem),
        scratch_shapes=[pltpu.VMEM((odds.shape[0], count), bf16)],
        compiler_params=room(24),
        name="back",
    )(slot, odds, stats, packets, cos_table, sin_table)


def finish_kernel(place_ref, parts_ref, transfer_ref, out_ref):
    own_refs = out_ref.shape[0]
    sums = jnp.sum(parts_ref[...].astype(f32), axis=0)
    share = sums[2 * own_refs : 2 * own_refs + 1] + sums[2 * own_refs + 1 : 2 * own_refs + 2]
    lane = lax.broadcasted_iota(jnp.int32, (own_refs, LANES), 1) // NCTF
    row = lax.broadcasted_iota(jnp.int32, (own_refs, LANES), 0)
    shares = jnp.where(lane == row, share, 0.0)
    own = transfer_ref[:, pl.ds(pl.multiple_of(place_ref[0] * LANES, LANES), LANES)]
    squared = jnp.concatenate([own * own] * (LANES // NCTF), axis=0)
    denominator = jnp.dot(shares, squared, precision=highest) + ridge_term
    for i in range(own_refs):
        out_ref[i] = sums[2 * i : 2 * i + 2] / denominator[i : i + 1]


def finish(place, parts, transfer, own_refs):
    return pl.pallas_call(
        finish_kernel,
        out_shape=jax.ShapeDtypeStruct((own_refs, 2, LANES), f32),
        in_specs=[pl.BlockSpec(memory_space=pltpu.SMEM)] + [whole_vmem] * 2,
        out_specs=whole_vmem,
        compiler_params=room(4),
        name="finish",
    )(place, parts, transfer)


def shifted(value, axis, steps):
    count = lax.axis_size(axis)
    pairs = [(source, (source + steps) % count) for source in range(count)]
    return lax.ppermute(value, axis, pairs)


def parted(value, steps):
    count = lax.axis_size("x")
    pairs = []
    for source in range(count):
        pairs.append((2 * source, 2 * ((source + steps) % count)))
        pairs.append((2 * source + 1, 2 * ((source - steps) % count) + 1))
    return lax.ppermute(value, ("x", "core"), pairs)


def peer_line(row, plane, rows, planes):
    return (planes - 1 - plane) * rows + (row + rows // 2) % rows


def slant_line(side, row, plane, count):
    column = (plane + 1) % count
    step = count + side * column - (1 - side) * column
    return count * ((row + count // 2 + step) % count) + column


def slanted_exchange(value):
    yh, dom = lax.axis_size("yh"), lax.axis_size("dom")
    groups = []
    for side in range(2):
        order = [0] * (yh * dom)
        for y in range(yh):
            for d in range(dom):
                line = slant_line(side, 2 * y + d % 2, d // 2, dom // 2)
                order[line] = (side * yh + y) * dom + d
        groups.append(order)
    return lax.all_to_all(value, ("core", "yh", "dom"), 0, 0, axis_index_groups=groups)


def wide_exchange(value):
    yh, dom = lax.axis_size("yh"), lax.axis_size("dom")
    order = [0] * (yh * dom)
    for y in range(yh):
        for d in range(dom):
            order[peer_line(2 * y + d % 2, d // 2, 2 * yh, dom // 2)] = y * dom + d
    return lax.all_to_all(value, ("yh", "dom"), 0, 0, axis_index_groups=[order])


def body(particles, classes, template_spectra, transfer_magnitude, offsets):
    rows = particles.shape[0]
    own_refs = template_spectra.shape[0]
    near_axes = ("core", "x")
    near, far = lax.axis_size(near_axes), lax.axis_size(("yh", "dom"))
    packet, copies = prep(classes, particles, transfer_magnitude, template_spectra, far)
    spectra = slanted_exchange(copies)
    place, side, part = [lax.axis_index(name)[None] for name in ("x", "core", "dom")]
    slot = lax.axis_index(near_axes)[None]
    second, first, third = parted(packet, 2), parted(packet, 1), parted(packet, 3)
    own = arrange(place, side, part, slot, [packet, first, second, third])
    other = shifted(own, "core", 1)
    cos_table, sin_table = phase_tables(offsets)
    odds, stats, weighted = make_scores(
        side, spectra, cos_table, sin_table, own, other, transfer_magnitude, own_refs, near
    )
    stats = lax.all_to_all(stats, near_axes, 0, 0)
    parts, log_own = back_project(
        slot, odds, stats, weighted, cos_table, sin_table, own_refs, rows
    )
    parts = wide_exchange(parts)
    new_refs = finish(part, parts, transfer_magnitude, own_refs)
    return (log_own.reshape(rows), new_refs)


def solution(mesh):
    devices = mesh.devices
    names = ("yh", "x", "core", "dom")
    inner = Mesh(devices.reshape(4, 4, 2, devices.shape[1]), names)
    refs = names[:3]
    return jax.shard_map(
        body,
        mesh=inner,
        in_specs=(P(names, None, None), P(names), P(refs, None, "dom"), P(), P()),
        out_specs=(P(names), P(refs, None, "dom")),
        check_vma=False,
    )
```

```python
import functools
import math

import jax
import jax.numpy as jnp
from jax import lax
from jax.experimental import pallas as pl
from jax.experimental.pallas import tpu as pltpu
from jax.sharding import Mesh
from jax.sharding import PartitionSpec as P

BOX = 64
F = 2048
SHIFTS = 64
NCTF = 16
LANES = 128
CHUNKS = F // LANES
ROWS = 16
UNIT = 2
UNROLL = 4
BATCH = 2

highest = lax.Precision.HIGHEST
ridge_term = 1.0
f32 = jnp.float32
bf16 = jnp.bfloat16
whole_vmem = pl.BlockSpec(memory_space=pltpu.VMEM)


def room(mib):
    return pltpu.CompilerParams(vmem_limit_bytes=mib * 1024 * 1024)


def phase_tables(offsets):
    half_side = BOX // 2
    positions = jnp.arange(F, dtype=jnp.int32)
    row_index = positions // half_side
    freq_x = jnp.where(row_index < half_side, row_index, row_index - BOX)
    freq_y = positions % half_side
    turn_count = (offsets[:, 0:1] * freq_x[None, :] + offsets[:, 1:2] * freq_y[None, :]) % BOX
    angles = turn_count.astype(f32) * (2.0 * math.pi / BOX)
    return (jnp.cos(angles), jnp.sin(angles))


def prep_kernel(classes_ref, particles_ref, transfer_ref, spectra_ref, packet_ref, copies_ref):
    rows = particles_ref.shape[0]
    copies_ref[...] = jnp.broadcast_to(spectra_ref[...][None], copies_ref.shape)
    place = lax.broadcasted_iota(jnp.int32, (rows, 1), 0)
    labels = jnp.zeros((rows, 1), jnp.int32)
    for i in range(rows):
        labels = jnp.where(place == i, classes_ref[i], labels)
    contrast = jnp.zeros((rows, F), f32)
    for c in range(NCTF):
        contrast = jnp.where(labels == c, transfer_ref[c : c + 1, :], contrast)
    values = particles_ref[...].astype(f32)
    real = (values[:, 0, :] * contrast).astype(bf16)
    imag = (values[:, 1, :] * contrast).astype(bf16)
    for d in range(CHUNKS):
        lanes = slice(d * LANES, (d + 1) * LANES)
        packet_ref[:, 2 * d * LANES : (2 * d + 1) * LANES] = real[:, lanes]
        packet_ref[:, (2 * d + 1) * LANES : (2 * d + 2) * LANES] = imag[:, lanes]
    tags = jnp.broadcast_to(labels.astype(f32), (rows, LANES))
    packet_ref[:, 2 * F :] = tags.astype(bf16)


def prep(classes, particles, transfer, spectra, far):
    rows = particles.shape[0]
    return pl.pallas_call(
        prep_kernel,
        out_shape=(
            jax.ShapeDtypeStruct((rows, 2 * F + LANES), bf16),
            jax.ShapeDtypeStruct((far,) + spectra.shape, bf16),
        ),
        in_specs=[pl.BlockSpec(memory_space=pltpu.SMEM)] + [whole_vmem] * 3,
        out_specs=(whole_vmem, whole_vmem),
        compiler_params=room(60),
        name="prep",
    )(classes, particles, transfer, spectra)


def local_copy(kernel, blocks, scalars, arrays, name):
    shape = (blocks,) + arrays[0].shape[-2:]
    return pl.pallas_call(
        kernel,
        out_shape=jax.ShapeDtypeStruct(shape, bf16),
        in_specs=[pl.BlockSpec(memory_space=pltpu.SMEM)] * len(scalars) + [whole_vmem] * len(arrays),
        out_specs=whole_vmem,
        compiler_params=room(4),
        name=name,
    )(*scalars, *arrays)


def pair_kernel(side_ref, own_ref, mate_ref, out_ref):
    out_ref[side_ref[0]] = own_ref[...]
    out_ref[1 - side_ref[0]] = mate_ref[...]


def bundle_kernel(near_ref, far_ref, out_ref):
    out_ref[0:2] = near_ref[...]
    out_ref[2] = far_ref[...]


def gather_kernel(place_ref, side_ref, part_ref, slot_ref, pair_ref, own_ref, other_ref, out_ref):
    count = out_ref.shape[0] // 2
    place, side = place_ref[0], side_ref[0]
    below, above = lax.rem(place + count - 1, count), lax.rem(place + 1, count)
    across = lax.rem(place + 2, count)
    mine = jnp.where(side == 0, below, above)
    theirs = jnp.where(side == 0, above, below)
    for k in range(2):
        out_ref[k * count + place] = pair_ref[k]
        out_ref[k * count + mine] = own_ref[k]
        out_ref[k * count + theirs] = other_ref[k]
    out_ref[side * count + across] = own_ref[2]
    out_ref[(1 - side) * count + across] = other_ref[2]


def fold(values):
    return jnp.sum(values.reshape(values.shape[0] // 8, 8, values.shape[1]), axis=0)


def row_sums(tiles):
    row = lax.broadcasted_iota(jnp.int32, tiles[0].shape, 0)
    for bit in (1, 2, 4):
        even = (row // bit) % 2 == 0
        merged = []
        for a, b in zip(tiles[::2], tiles[1::2]):
            merged.append(
                jnp.where(even, a, b) + pltpu.roll(jnp.where(even, b, a), 8 - bit, 0)
            )
        tiles = merged
    return tiles[0]


def label_table(tags):
    lane = lax.broadcasted_iota(jnp.int32, tags.shape, 1) % NCTF
    return (tags.astype(f32) == lane.astype(f32)).astype(f32)


def score_kernel(
    own_refs,
    side_ref,
    spectra_ref,
    cos_ref,
    sin_ref,
    weighted_ref,
    transfer_ref,
    odds_ref,
    stats_ref,
    penalty_ref,
):
    groups = spectra_ref.shape[0] // CHUNKS
    refs = groups * own_refs
    side = side_ref[0]

    odds_ref[...] = jnp.zeros_like(odds_ref)
    penalty_ref[...] = jnp.zeros_like(penalty_ref)
    width = 2 * UNIT * LANES

    def unit(u):
        wide = pl.ds(pl.multiple_of(u * width, width), width)
        weighted = weighted_ref[:, wide]
        tables = []
        for j in range(UNIT):
            lanes = pl.ds(pl.multiple_of((u * UNIT + j) * LANES, LANES), LANES)
            transfer = transfer_ref[:, lanes]
            tables.append((cos_ref[:, lanes], sin_ref[:, lanes], transfer * transfer))
        for g in range(groups):
            blocks = []
            for j in range(UNIT):
                d = u * UNIT + j
                line = slant_line(side, 2 * g + d % 2, d // 2, CHUNKS // 2)
                blocks.append(spectra_ref[line].astype(f32))
            for first in range(0, own_refs, BATCH):
                rows = []
                for i in range(first, first + BATCH):
                    pieces = []
                    power = 0.0
                    for j in range(UNIT):
                        cos, sin, squared = tables[j]
                        real, imag = blocks[j][i, 0:1], blocks[j][i, 1:2]
                        pieces.append((real * cos - imag * sin).astype(bf16))
                        pieces.append((real * sin + imag * cos).astype(bf16))
                        power = power + (real * real + imag * imag) * squared
                    place = (g * own_refs + i) * NCTF
                    penalty_ref[place : place + NCTF, :] += power
                    rows.append(jnp.concatenate(pieces, axis=1))
                place = (g * own_refs + first) * SHIFTS
                odds_ref[place : place + BATCH * SHIFTS, :] += lax.dot_general(
                    jnp.concatenate(rows, axis=0),
                    weighted,
                    (((1,), (1,)), ((), ())),
                    preferred_element_type=f32,
                )

    def units(k, carry):
        for j in range(UNROLL):
            unit(k * UNROLL + j)
        return carry

    lax.fori_loop(0, CHUNKS // UNIT // UNROLL, units, 0)
    tags = weighted_ref[:, 2 * F :].astype(f32).T[:NCTF]
    hot = (tags == lax.broadcasted_iota(jnp.int32, tags.shape, 0).astype(f32)).astype(f32)
    top = None
    for r in range(refs):
        charge = jnp.sum(penalty_ref[r * NCTF : (r + 1) * NCTF, :], axis=1, keepdims=True)
        cost = 0.5 * jnp.sum(charge * hot, axis=0, keepdims=True)
        place = slice(r * SHIFTS, (r + 1) * SHIFTS)
        scores = odds_ref[place, :] - cost
        odds_ref[place, :] = scores
        high = jnp.max(scores, axis=0, keepdims=True)
        top = high if top is None else jnp.maximum(top, high)
    odds = jnp.exp(odds_ref[...] - top)
    odds_ref[...] = odds
    total = jnp.sum(odds, axis=0, keepdims=True)
    stats = jnp.concatenate([top, total], axis=0)
    spare = jnp.zeros((2, LANES - stats.shape[1]), f32)
    stats = jnp.concatenate([stats, spare], axis=1)
    stats_ref[...] = jnp.broadcast_to(stats[None], stats_ref.shape)


def make_scores(side, spectra, cos_table, sin_table, weighted, transfer, own_refs, near):
    groups = spectra.shape[0] // CHUNKS
    refs = groups * own_refs
    count = weighted.shape[0]
    return pl.pallas_call(
        functools.partial(score_kernel, own_refs),
        out_shape=(
            jax.ShapeDtypeStruct((refs * SHIFTS, count), f32),
            jax.ShapeDtypeStruct((near, 2, LANES), f32),
        ),
        in_specs=[pl.BlockSpec(memory_space=pltpu.SMEM)] + [whole_vmem] * 5,
        out_specs=(whole_vmem, whole_vmem),
        scratch_shapes=[
            pltpu.VMEM((refs * NCTF, LANES), f32),
        ],
        compiler_params=room(24),
        name="scores",
    )(side, spectra, cos_table, sin_table, weighted, transfer)


def back_kernel(
    own_refs,
    slot_ref,
    odds_ref,
    stats_ref,
    packets_ref,
    cos_ref,
    sin_ref,
    parts_ref,
    log_ref,
    posterior_ref,
):
    groups = parts_ref.shape[0] // CHUNKS
    refs = groups * own_refs
    count = odds_ref.shape[1]
    slot = slot_ref[0]
    tops, sums = stats_ref[:, 0, :count], stats_ref[:, 1, :count]
    top = jnp.max(tops, axis=0, keepdims=True)
    total = jnp.sum(sums * jnp.exp(tops - top), axis=0, keepdims=True)
    log_all = top + jnp.log(total)
    own_rows = log_ref.shape[1]
    own_log = jnp.zeros_like(log_ref)
    for k in range(count // own_rows):
        piece = log_all[:, k * own_rows : (k + 1) * own_rows]
        own_log = jnp.where(slot == k, piece, own_log)
    log_ref[...] = own_log
    scale = jnp.exp(stats_ref[slot][0:1, :count] - log_all)
    weights = []
    for r in range(refs):
        place = slice(r * SHIFTS, (r + 1) * SHIFTS)
        posterior = (odds_ref[place, :] * scale).astype(bf16)
        posterior_ref[place, :] = posterior
        weights.append(jnp.sum(posterior.astype(f32), axis=0, keepdims=True))
    weights = jnp.concatenate(weights, axis=0)
    high = weights.astype(bf16)
    low = (weights - high.astype(f32)).astype(bf16)
    hot = label_table(packets_ref[:, 2 * F :]).astype(bf16)
    spread = jnp.dot(jnp.concatenate([high, low], axis=0), hot, preferred_element_type=f32)
    spread = spread[:refs] + spread[refs:]
    lane = lax.broadcasted_iota(jnp.int32, (refs, LANES), 1) // NCTF
    row = lax.broadcasted_iota(jnp.int32, (refs, LANES), 0) % own_refs
    spread = jnp.where(lane == row, spread, 0.0)
    shares = []
    for g in range(groups):
        share = jnp.sum(spread[g * own_refs : (g + 1) * own_refs], axis=0, keepdims=True)
        high = share.astype(bf16).astype(f32)
        before = jnp.zeros((2 * own_refs, LANES), f32)
        after = jnp.zeros((ROWS - 2 * own_refs - 2, LANES), f32)
        shares.append(jnp.concatenate([before, high, share - high, after], axis=0))

    def chunk(d):
        lanes = pl.ds(pl.multiple_of(d * LANES, LANES), LANES)
        wide = pl.ds(pl.multiple_of(d * 2 * LANES, 2 * LANES), 2 * LANES)
        cos, sin = cos_ref[:, lanes], sin_ref[:, lanes]
        weighted = packets_ref[:, wide]
        for g in range(groups):
            rows = []
            for first in range(0, own_refs, BATCH):
                place = (g * own_refs + first) * SHIFTS
                totals = jnp.dot(
                    posterior_ref[place : place + BATCH * SHIFTS, :],
                    weighted,
                    preferred_element_type=f32,
                )
                for i in range(BATCH):
                    real = totals[i * SHIFTS : (i + 1) * SHIFTS, :LANES]
                    imag = totals[i * SHIFTS : (i + 1) * SHIFTS, LANES:]
                    rows.append(fold(real * cos + imag * sin))
                    rows.append(fold(imag * cos - real * sin))
            blank = [jnp.zeros((8, LANES), f32)] * (ROWS - len(rows))
            rows = rows + blank
            sums = jnp.concatenate([row_sums(rows[:8]), row_sums(rows[8:])], axis=0)
            line = peer_line(2 * g + d % 2, d // 2, 2 * groups, CHUNKS // 2)
            parts_ref[line] = (sums + shares[g]).astype(bf16)

    def chunks(k, carry):
        for j in range(UNROLL):
            chunk(k * UNROLL + j)
        return carry

    lax.fori_loop(0, CHUNKS // UNROLL, chunks, 0)


def back_project(slot, odds, stats, packets, cos_table, sin_table, own_refs, rows):
    count = packets.shape[0]
    groups = odds.shape[0] // SHIFTS // own_refs
    return pl.pallas_call(
        functools.partial(back_kernel, own_refs),
        out_shape=(
            jax.ShapeDtypeStruct((groups * CHUNKS, ROWS, LANES), bf16),
            jax.ShapeDtypeStruct((1, rows), f32),
        ),
        in_specs=[pl.BlockSpec(memory_space=pltpu.SMEM)] + [whole_vmem] * 5,
        out_specs=(whole_vmem, whole_vmem),
        scratch_shapes=[pltpu.VMEM((odds.shape[0], count), bf16)],
        compiler_params=room(24),
        name="back",
    )(slot, odds, stats, packets, cos_table, sin_table)


def finish_kernel(place_ref, parts_ref, transfer_ref, out_ref):
    own_refs = out_ref.shape[0]
    sums = jnp.sum(parts_ref[...].astype(f32), axis=0)
    share = sums[2 * own_refs : 2 * own_refs + 1] + sums[2 * own_refs + 1 : 2 * own_refs + 2]
    lane = lax.broadcasted_iota(jnp.int32, (own_refs, LANES), 1) // NCTF
    row = lax.broadcasted_iota(jnp.int32, (own_refs, LANES), 0)
    shares = jnp.where(lane == row, share, 0.0)
    own = transfer_ref[:, pl.ds(pl.multiple_of(place_ref[0] * LANES, LANES), LANES)]
    squared = jnp.concatenate([own * own] * (LANES // NCTF), axis=0)
    denominator = jnp.dot(shares, squared, precision=highest) + ridge_term
    for i in range(own_refs):
        out_ref[i] = sums[2 * i : 2 * i + 2] / denominator[i : i + 1]


def finish(place, parts, transfer, own_refs):
    return pl.pallas_call(
        finish_kernel,
        out_shape=jax.ShapeDtypeStruct((own_refs, 2, LANES), f32),
        in_specs=[pl.BlockSpec(memory_space=pltpu.SMEM)] + [whole_vmem] * 2,
        out_specs=whole_vmem,
        compiler_params=room(4),
        name="finish",
    )(place, parts, transfer)


def shifted(value, axis, steps):
    count = lax.axis_size(axis)
    pairs = [(source, (source + steps) % count) for source in range(count)]
    return lax.ppermute(value, axis, pairs)


def parted(value, steps):
    count = lax.axis_size("x")
    pairs = []
    for source in range(count):
        pairs.append((2 * source, 2 * ((source + steps) % count)))
        pairs.append((2 * source + 1, 2 * ((source - steps) % count) + 1))
    return lax.ppermute(value, ("x", "core"), pairs)


def peer_line(row, plane, rows, planes):
    return (planes - 1 - plane) * rows + (row + rows // 2) % rows


def slant_line(side, row, plane, count):
    column = (plane + 1) % count
    step = count + side * column - (1 - side) * column
    return count * ((row + count // 2 + step) % count) + column


def slanted_exchange(value):
    yh, dom = lax.axis_size("yh"), lax.axis_size("dom")
    groups = []
    for side in range(2):
        order = [0] * (yh * dom)
        for y in range(yh):
            for d in range(dom):
                line = slant_line(side, 2 * y + d % 2, d // 2, dom // 2)
                order[line] = (side * yh + y) * dom + d
        groups.append(order)
    return lax.all_to_all(value, ("core", "yh", "dom"), 0, 0, axis_index_groups=groups)


def wide_exchange(value):
    yh, dom = lax.axis_size("yh"), lax.axis_size("dom")
    order = [0] * (yh * dom)
    for y in range(yh):
        for d in range(dom):
            order[peer_line(2 * y + d % 2, d // 2, 2 * yh, dom // 2)] = y * dom + d
    return lax.all_to_all(value, ("yh", "dom"), 0, 0, axis_index_groups=[order])


def body(particles, classes, template_spectra, transfer_magnitude, offsets):
    rows = particles.shape[0]
    own_refs = template_spectra.shape[0]
    near_axes = ("core", "x")
    near, far = lax.axis_size(near_axes), lax.axis_size(("yh", "dom"))
    packet, copies = prep(classes, particles, transfer_magnitude, template_spectra, far)
    place, side, part = [lax.axis_index(name)[None] for name in ("x", "core", "dom")]
    slot = lax.axis_index(near_axes)[None]
    mate = shifted(packet, "core", 1)
    far_packet = parted(packet, 2)
    pair = local_copy(pair_kernel, 2, [side], [packet, mate], "pair")
    copies, pair, offsets = lax.optimization_barrier((copies, pair, offsets))
    spectra = slanted_exchange(copies)
    own = local_copy(bundle_kernel, 3, [], [parted(pair, 1), far_packet], "bundle")
    other = shifted(own, "core", 1)
    spots = [place, side, part, slot]
    weighted = local_copy(gather_kernel, near, spots, [pair, own, other], "gather")
    weighted = weighted.reshape(near * rows, weighted.shape[-1])
    cos_table, sin_table = phase_tables(offsets)
    odds, stats = make_scores(
        side, spectra, cos_table, sin_table, weighted, transfer_magnitude, own_refs, near
    )
    stats = lax.all_to_all(stats, near_axes, 0, 0)
    parts, log_own = back_project(
        slot, odds, stats, weighted, cos_table, sin_table, own_refs, rows
    )
    parts = wide_exchange(parts)
    new_refs = finish(part, parts, transfer_magnitude, own_refs)
    return (log_own.reshape(rows), new_refs)


def solution(mesh):
    devices = mesh.devices
    names = ("yh", "x", "core", "dom")
    inner = Mesh(devices.reshape(4, 4, 2, devices.shape[1]), names)
    refs = names[:3]
    return jax.shard_map(
        body,
        mesh=inner,
        in_specs=(P(names, None, None), P(names), P(refs, None, "dom"), P(), P()),
        out_specs=(P(names), P(refs, None, "dom")),
        check_vma=False,
    )
```

```python
import functools
import math

import jax
import jax.numpy as jnp
from jax import lax
from jax.experimental import pallas as pl
from jax.experimental.pallas import tpu as pltpu
from jax.sharding import Mesh
from jax.sharding import PartitionSpec as P

BOX = 64
F = 2048
SHIFTS = 64
NCTF = 16
LANES = 128
CHUNKS = F // LANES
ROWS = 16
UNIT = 4
UNROLL = 8
BATCH = 2
WIDE = 6

highest = lax.Precision.HIGHEST
ridge_term = 1.0
f32 = jnp.float32
bf16 = jnp.bfloat16
whole_vmem = pl.BlockSpec(memory_space=pltpu.VMEM)


def room(mib):
    return pltpu.CompilerParams(vmem_limit_bytes=mib * 1024 * 1024)


def phase_tables(offsets):
    half_side = BOX // 2
    positions = jnp.arange(F, dtype=jnp.int32)
    row_index = positions // half_side
    freq_x = jnp.where(row_index < half_side, row_index, row_index - BOX)
    freq_y = positions % half_side
    turn_count = (offsets[:, 0:1] * freq_x[None, :] + offsets[:, 1:2] * freq_y[None, :]) % BOX
    angles = turn_count.astype(f32) * (2.0 * math.pi / BOX)
    return (jnp.cos(angles), jnp.sin(angles))


def prep_kernel(classes_ref, particles_ref, transfer_ref, spectra_ref, packet_ref, copies_ref):
    rows = particles_ref.shape[0]
    copies_ref[...] = jnp.broadcast_to(spectra_ref[...][None], copies_ref.shape)
    place = lax.broadcasted_iota(jnp.int32, (rows, 1), 0)
    labels = jnp.zeros((rows, 1), jnp.int32)
    for i in range(rows):
        labels = jnp.where(place == i, classes_ref[i], labels)
    contrast = jnp.zeros((rows, F), f32)
    for c in range(NCTF):
        contrast = jnp.where(labels == c, transfer_ref[c : c + 1, :], contrast)
    values = particles_ref[...].astype(f32)
    real = (values[:, 0, :] * contrast).astype(bf16)
    imag = (values[:, 1, :] * contrast).astype(bf16)
    for d in range(CHUNKS):
        lanes = slice(d * LANES, (d + 1) * LANES)
        packet_ref[:, 2 * d * LANES : (2 * d + 1) * LANES] = real[:, lanes]
        packet_ref[:, (2 * d + 1) * LANES : (2 * d + 2) * LANES] = imag[:, lanes]
    tags = jnp.broadcast_to(labels.astype(f32), (rows, LANES))
    packet_ref[:, 2 * F :] = tags.astype(bf16)


def prep(classes, particles, transfer, spectra, far):
    rows = particles.shape[0]
    return pl.pallas_call(
        prep_kernel,
        out_shape=(
            jax.ShapeDtypeStruct((rows, 2 * F + LANES), bf16),
            jax.ShapeDtypeStruct((far,) + spectra.shape, bf16),
        ),
        in_specs=[pl.BlockSpec(memory_space=pltpu.SMEM)] + [whole_vmem] * 3,
        out_specs=(whole_vmem, whole_vmem),
        compiler_params=room(60),
        name="prep",
    )(classes, particles, transfer, spectra)


def arrange_kernel(place_ref, side_ref, part_ref, slot_ref, *refs):
    count = len(refs) - 1
    for k in range(count):
        step = jnp.where(side_ref[0] == 0, count - k, k)
        refs[count][lax.rem(place_ref[0] + step, count)] = refs[k][...]


def arrange(place, side, part, slot, packets):
    rows, width = packets[0].shape
    ordered = pl.pallas_call(
        arrange_kernel,
        out_shape=jax.ShapeDtypeStruct((len(packets), rows, width), bf16),
        in_specs=[pl.BlockSpec(memory_space=pltpu.SMEM)] * 4 + [whole_vmem] * len(packets),
        out_specs=whole_vmem,
        compiler_params=room(4),
        name="arrange",
    )(place, side, part, slot, *packets)
    return ordered.reshape(len(packets) * rows, width)


def fold(values):
    return jnp.sum(values.reshape(values.shape[0] // 8, 8, values.shape[1]), axis=0)


def row_sums(tiles):
    row = lax.broadcasted_iota(jnp.int32, tiles[0].shape, 0)
    for bit in (1, 2, 4):
        even = (row // bit) % 2 == 0
        merged = []
        for a, b in zip(tiles[::2], tiles[1::2]):
            merged.append(
                jnp.where(even, a, b) + pltpu.roll(jnp.where(even, b, a), 8 - bit, 0)
            )
        tiles = merged
    return tiles[0]


def label_table(tags):
    lane = lax.broadcasted_iota(jnp.int32, tags.shape, 1) % NCTF
    return (tags.astype(f32) == lane.astype(f32)).astype(f32)


def score_kernel(
    own_refs,
    side_ref,
    spectra_ref,
    cos_ref,
    sin_ref,
    own_ref,
    other_ref,
    transfer_ref,
    odds_ref,
    stats_ref,
    weighted_ref,
    penalty_ref,
):
    groups = spectra_ref.shape[0] // CHUNKS
    refs = groups * own_refs
    half = own_ref.shape[0]
    side = side_ref[0]

    own, other = own_ref[...], other_ref[...]
    weighted_ref[:half, :] = jnp.where(side == 0, own, other)
    weighted_ref[half:, :] = jnp.where(side == 0, other, own)
    odds_ref[...] = jnp.zeros_like(odds_ref)
    penalty_ref[...] = jnp.zeros_like(penalty_ref)
    width = 2 * UNIT * LANES

    def unit(u):
        wide = pl.ds(pl.multiple_of(u * width, width), width)
        weighted = weighted_ref[:, wide]
        tables = []
        for j in range(UNIT):
            lanes = pl.ds(pl.multiple_of((u * UNIT + j) * LANES, LANES), LANES)
            transfer = transfer_ref[:, lanes]
            tables.append((cos_ref[:, lanes], sin_ref[:, lanes], transfer * transfer))
        for g in range(groups):
            blocks = []
            for j in range(UNIT):
                d = u * UNIT + j
                line = slant_line(side, 2 * g + d % 2, d // 2, CHUNKS // 2)
                blocks.append(spectra_ref[line].astype(f32))
            for first in range(0, own_refs, WIDE):
                rows = []
                for i in range(first, first + WIDE):
                    pieces = []
                    power = 0.0
                    for j in range(UNIT):
                        cos, sin, squared = tables[j]
                        real, imag = blocks[j][i, 0:1], blocks[j][i, 1:2]
                        pieces.append((real * cos - imag * sin).astype(bf16))
                        pieces.append((real * sin + imag * cos).astype(bf16))
                        power = power + (real * real + imag * imag) * squared
                    place = (g * own_refs + i) * NCTF
                    penalty_ref[place : place + NCTF, :] += power
                    rows.append(jnp.concatenate(pieces, axis=1))
                place = (g * own_refs + first) * SHIFTS
                odds_ref[place : place + WIDE * SHIFTS, :] += lax.dot_general(
                    jnp.concatenate(rows, axis=0),
                    weighted,
                    (((1,), (1,)), ((), ())),
                    preferred_element_type=f32,
                )

    def units(k, carry):
        unit(2 * k)
        unit(2 * k + 1)
        return carry

    lax.fori_loop(0, CHUNKS // UNIT // 2, units, 0)
    tags = weighted_ref[:, 2 * F :].astype(f32).T[:NCTF]
    hot = (tags == lax.broadcasted_iota(jnp.int32, tags.shape, 0).astype(f32)).astype(f32)
    top = None
    for r in range(refs):
        charge = jnp.sum(penalty_ref[r * NCTF : (r + 1) * NCTF, :], axis=1, keepdims=True)
        cost = 0.5 * jnp.sum(charge * hot, axis=0, keepdims=True)
        place = slice(r * SHIFTS, (r + 1) * SHIFTS)
        scores = odds_ref[place, :] - cost
        odds_ref[place, :] = scores
        high = jnp.max(scores, axis=0, keepdims=True)
        top = high if top is None else jnp.maximum(top, high)
    odds = jnp.exp(odds_ref[...] - top)
    odds_ref[...] = odds
    total = jnp.sum(odds, axis=0, keepdims=True)
    stats = jnp.concatenate([top, total], axis=0)
    spare = jnp.zeros((2, LANES - stats.shape[1]), f32)
    stats = jnp.concatenate([stats, spare], axis=1)
    stats_ref[...] = jnp.broadcast_to(stats[None], stats_ref.shape)


def make_scores(side, spectra, cos_table, sin_table, own, other, transfer, own_refs, near):
    groups = spectra.shape[0] // CHUNKS
    refs = groups * own_refs
    count = 2 * own.shape[0]
    return pl.pallas_call(
        functools.partial(score_kernel, own_refs),
        out_shape=(
            jax.ShapeDtypeStruct((refs * SHIFTS, count), f32),
            jax.ShapeDtypeStruct((near, 2, LANES), f32),
            jax.ShapeDtypeStruct((count, own.shape[1]), bf16),
        ),
        in_specs=[pl.BlockSpec(memory_space=pltpu.SMEM)] + [whole_vmem] * 6,
        out_specs=(whole_vmem, whole_vmem, whole_vmem),
        scratch_shapes=[
            pltpu.VMEM((refs * NCTF, LANES), f32),
        ],
        compiler_params=room(24),
        name="scores",
    )(side, spectra, cos_table, sin_table, own, other, transfer)


def back_kernel(
    own_refs,
    slot_ref,
    odds_ref,
    stats_ref,
    packets_ref,
    cos_ref,
    sin_ref,
    parts_ref,
    log_ref,
    posterior_ref,
):
    groups = parts_ref.shape[0] // CHUNKS
    refs = groups * own_refs
    count = odds_ref.shape[1]
    slot = slot_ref[0]
    tops, sums = stats_ref[:, 0, :count], stats_ref[:, 1, :count]
    top = jnp.max(tops, axis=0, keepdims=True)
    total = jnp.sum(sums * jnp.exp(tops - top), axis=0, keepdims=True)
    log_all = top + jnp.log(total)
    own_rows = log_ref.shape[1]
    own_log = jnp.zeros_like(log_ref)
    for k in range(count // own_rows):
        piece = log_all[:, k * own_rows : (k + 1) * own_rows]
        own_log = jnp.where(slot == k, piece, own_log)
    log_ref[...] = own_log
    scale = jnp.exp(stats_ref[slot][0:1, :count] - log_all)
    weights = []
    for r in range(refs):
        place = slice(r * SHIFTS, (r + 1) * SHIFTS)
        posterior = (odds_ref[place, :] * scale).astype(bf16)
        posterior_ref[place, :] = posterior
        weights.append(jnp.sum(posterior.astype(f32), axis=0, keepdims=True))
    weights = jnp.concatenate(weights, axis=0)
    high = weights.astype(bf16)
    low = (weights - high.astype(f32)).astype(bf16)
    hot = label_table(packets_ref[:, 2 * F :]).astype(bf16)
    spread = jnp.dot(jnp.concatenate([high, low], axis=0), hot, preferred_element_type=f32)
    spread = spread[:refs] + spread[refs:]
    lane = lax.broadcasted_iota(jnp.int32, (refs, LANES), 1) // NCTF
    row = lax.broadcasted_iota(jnp.int32, (refs, LANES), 0) % own_refs
    spread = jnp.where(lane == row, spread, 0.0)
    shares = []
    for g in range(groups):
        share = jnp.sum(spread[g * own_refs : (g + 1) * own_refs], axis=0, keepdims=True)
        high = share.astype(bf16).astype(f32)
        before = jnp.zeros((2 * own_refs, LANES), f32)
        after = jnp.zeros((ROWS - 2 * own_refs - 2, LANES), f32)
        shares.append(jnp.concatenate([before, high, share - high, after], axis=0))

    def chunk(d):
        lanes = pl.ds(pl.multiple_of(d * LANES, LANES), LANES)
        wide = pl.ds(pl.multiple_of(d * 2 * LANES, 2 * LANES), 2 * LANES)
        cos, sin = cos_ref[:, lanes], sin_ref[:, lanes]
        weighted = packets_ref[:, wide]
        for g in range(groups):
            rows = []
            for first in range(0, own_refs, BATCH):
                place = (g * own_refs + first) * SHIFTS
                totals = jnp.dot(
                    posterior_ref[place : place + BATCH * SHIFTS, :],
                    weighted,
                    preferred_element_type=f32,
                )
                for i in range(BATCH):
                    real = totals[i * SHIFTS : (i + 1) * SHIFTS, :LANES]
                    imag = totals[i * SHIFTS : (i + 1) * SHIFTS, LANES:]
                    rows.append(fold(real * cos + imag * sin))
                    rows.append(fold(imag * cos - real * sin))
            blank = [jnp.zeros((8, LANES), f32)] * (ROWS - len(rows))
            rows = rows + blank
            sums = jnp.concatenate([row_sums(rows[:8]), row_sums(rows[8:])], axis=0)
            line = peer_line(2 * g + d % 2, d // 2, 2 * groups, CHUNKS // 2)
            parts_ref[line] = (sums + shares[g]).astype(bf16)

    def chunks(k, carry):
        for j in range(UNROLL):
            chunk(k * UNROLL + j)
        return carry

    lax.fori_loop(0, CHUNKS // UNROLL, chunks, 0)


def back_project(slot, odds, stats, packets, cos_table, sin_table, own_refs, rows):
    count = packets.shape[0]
    groups = odds.shape[0] // SHIFTS // own_refs
    return pl.pallas_call(
        functools.partial(back_kernel, own_refs),
        out_shape=(
            jax.ShapeDtypeStruct((groups * CHUNKS, ROWS, LANES), bf16),
            jax.ShapeDtypeStruct((1, rows), f32),
        ),
        in_specs=[pl.BlockSpec(memory_space=pltpu.SMEM)] + [whole_vmem] * 5,
        out_specs=(whole_vmem, whole_vmem),
        scratch_shapes=[pltpu.VMEM((odds.shape[0], count), bf16)],
        compiler_params=room(24),
        name="back",
    )(slot, odds, stats, packets, cos_table, sin_table)


def finish_kernel(place_ref, parts_ref, transfer_ref, out_ref):
    own_refs = out_ref.shape[0]
    sums = jnp.sum(parts_ref[...].astype(f32), axis=0)
    share = sums[2 * own_refs : 2 * own_refs + 1] + sums[2 * own_refs + 1 : 2 * own_refs + 2]
    lane = lax.broadcasted_iota(jnp.int32, (own_refs, LANES), 1) // NCTF
    row = lax.broadcasted_iota(jnp.int32, (own_refs, LANES), 0)
    shares = jnp.where(lane == row, share, 0.0)
    own = transfer_ref[:, pl.ds(pl.multiple_of(place_ref[0] * LANES, LANES), LANES)]
    squared = jnp.concatenate([own * own] * (LANES // NCTF), axis=0)
    denominator = jnp.dot(shares, squared, precision=highest) + ridge_term
    for i in range(own_refs):
        out_ref[i] = sums[2 * i : 2 * i + 2] / denominator[i : i + 1]


def finish(place, parts, transfer, own_refs):
    return pl.pallas_call(
        finish_kernel,
        out_shape=jax.ShapeDtypeStruct((own_refs, 2, LANES), f32),
        in_specs=[pl.BlockSpec(memory_space=pltpu.SMEM)] + [whole_vmem] * 2,
        out_specs=whole_vmem,
        compiler_params=room(4),
        name="finish",
    )(place, parts, transfer)


def shifted(value, axis, steps):
    count = lax.axis_size(axis)
    pairs = [(source, (source + steps) % count) for source in range(count)]
    return lax.ppermute(value, axis, pairs)


def parted(value, steps):
    count = lax.axis_size("x")
    pairs = []
    for source in range(count):
        pairs.append((2 * source, 2 * ((source + steps) % count)))
        pairs.append((2 * source + 1, 2 * ((source - steps) % count) + 1))
    return lax.ppermute(value, ("x", "core"), pairs)


def peer_line(row, plane, rows, planes):
    return (planes - 1 - plane) * rows + (row + rows // 2) % rows


def slant_line(side, row, plane, count):
    column = (plane + 1) % count
    step = count + side * column - (1 - side) * column
    return count * ((row + count // 2 + step) % count) + column


def slanted_exchange(value):
    yh, dom = lax.axis_size("yh"), lax.axis_size("dom")
    groups = []
    for side in range(2):
        order = [0] * (yh * dom)
        for y in range(yh):
            for d in range(dom):
                line = slant_line(side, 2 * y + d % 2, d // 2, dom // 2)
                order[line] = (side * yh + y) * dom + d
        groups.append(order)
    return lax.all_to_all(value, ("core", "yh", "dom"), 0, 0, axis_index_groups=groups)


def wide_exchange(value):
    yh, dom = lax.axis_size("yh"), lax.axis_size("dom")
    order = [0] * (yh * dom)
    for y in range(yh):
        for d in range(dom):
            order[peer_line(2 * y + d % 2, d // 2, 2 * yh, dom // 2)] = y * dom + d
    return lax.all_to_all(value, ("yh", "dom"), 0, 0, axis_index_groups=[order])


def body(particles, classes, template_spectra, transfer_magnitude, offsets):
    rows = particles.shape[0]
    own_refs = template_spectra.shape[0]
    near_axes = ("core", "x")
    near, far = lax.axis_size(near_axes), lax.axis_size(("yh", "dom"))
    packet, copies = prep(classes, particles, transfer_magnitude, template_spectra, far)
    spectra = slanted_exchange(copies)
    place, side, part = [lax.axis_index(name)[None] for name in ("x", "core", "dom")]
    slot = lax.axis_index(near_axes)[None]
    second, first, third = parted(packet, 2), parted(packet, 1), parted(packet, 3)
    own = arrange(place, side, part, slot, [packet, first, second, third])
    other = shifted(own, "core", 1)
    cos_table, sin_table = phase_tables(offsets)
    odds, stats, weighted = make_scores(
        side, spectra, cos_table, sin_table, own, other, transfer_magnitude, own_refs, near
    )
    stats = lax.all_to_all(stats, near_axes, 0, 0)
    parts, log_own = back_project(
        slot, odds, stats, weighted, cos_table, sin_table, own_refs, rows
    )
    parts = wide_exchange(parts)
    new_refs = finish(part, parts, transfer_magnitude, own_refs)
    return (log_own.reshape(rows), new_refs)


def solution(mesh):
    devices = mesh.devices
    names = ("yh", "x", "core", "dom")
    inner = Mesh(devices.reshape(4, 4, 2, devices.shape[1]), names)
    refs = names[:3]
    return jax.shard_map(
        body,
        mesh=inner,
        in_specs=(P(names, None, None), P(names), P(refs, None, "dom"), P(), P()),
        out_specs=(P(names), P(refs, None, "dom")),
        check_vma=False,
    )
```

```python
import functools
import math

import jax
import jax.numpy as jnp
from jax import lax
from jax.experimental import pallas as pl
from jax.experimental.pallas import tpu as pltpu
from jax.sharding import Mesh
from jax.sharding import PartitionSpec as P

BOX = 64
F = 2048
SHIFTS = 64
NCTF = 16
LANES = 128
CHUNKS = F // LANES
ROWS = 16
UNIT = 4
UNROLL = 8
BATCH = 2
WIDE = 6

highest = lax.Precision.HIGHEST
ridge_term = 1.0
f32 = jnp.float32
bf16 = jnp.bfloat16
whole_vmem = pl.BlockSpec(memory_space=pltpu.VMEM)


def room(mib):
    return pltpu.CompilerParams(vmem_limit_bytes=mib * 1024 * 1024)


def phase_tables(offsets):
    half_side = BOX // 2
    positions = jnp.arange(F, dtype=jnp.int32)
    row_index = positions // half_side
    freq_x = jnp.where(row_index < half_side, row_index, row_index - BOX)
    freq_y = positions % half_side
    turn_count = (offsets[:, 0:1] * freq_x[None, :] + offsets[:, 1:2] * freq_y[None, :]) % BOX
    angles = turn_count.astype(f32) * (2.0 * math.pi / BOX)
    return (jnp.cos(angles), jnp.sin(angles))


def prep_kernel(classes_ref, particles_ref, transfer_ref, spectra_ref, packet_ref, copies_ref):
    rows = particles_ref.shape[0]
    copies_ref[...] = jnp.broadcast_to(spectra_ref[...][None], copies_ref.shape)
    place = lax.broadcasted_iota(jnp.int32, (rows, 1), 0)
    labels = jnp.zeros((rows, 1), jnp.int32)
    for i in range(rows):
        labels = jnp.where(place == i, classes_ref[i], labels)
    contrast = jnp.zeros((rows, F), f32)
    for c in range(NCTF):
        contrast = jnp.where(labels == c, transfer_ref[c : c + 1, :], contrast)
    values = particles_ref[...].astype(f32)
    real = (values[:, 0, :] * contrast).astype(bf16)
    imag = (values[:, 1, :] * contrast).astype(bf16)
    for d in range(CHUNKS):
        lanes = slice(d * LANES, (d + 1) * LANES)
        packet_ref[:, 2 * d * LANES : (2 * d + 1) * LANES] = real[:, lanes]
        packet_ref[:, (2 * d + 1) * LANES : (2 * d + 2) * LANES] = imag[:, lanes]
    tags = jnp.broadcast_to(labels.astype(f32), (rows, LANES))
    packet_ref[:, 2 * F :] = tags.astype(bf16)


def prep(classes, particles, transfer, spectra, far):
    rows = particles.shape[0]
    return pl.pallas_call(
        prep_kernel,
        out_shape=(
            jax.ShapeDtypeStruct((rows, 2 * F + LANES), bf16),
            jax.ShapeDtypeStruct((far,) + spectra.shape, bf16),
        ),
        in_specs=[pl.BlockSpec(memory_space=pltpu.SMEM)] + [whole_vmem] * 3,
        out_specs=(whole_vmem, whole_vmem),
        compiler_params=room(60),
        name="prep",
    )(classes, particles, transfer, spectra)


def arrange_kernel(place_ref, side_ref, part_ref, slot_ref, *refs):
    count = len(refs) - 1
    for k, shift in enumerate((0, 3, 1, 2)):
        step = jnp.where(side_ref[0] == 0, count - shift, shift)
        refs[count][lax.rem(place_ref[0] + step, count)] = refs[k][...]


def arrange(place, side, part, slot, packets):
    rows, width = packets[0].shape
    ordered = pl.pallas_call(
        arrange_kernel,
        out_shape=jax.ShapeDtypeStruct((len(packets), rows, width), bf16),
        in_specs=[pl.BlockSpec(memory_space=pltpu.SMEM)] * 4 + [whole_vmem] * len(packets),
        out_specs=whole_vmem,
        compiler_params=room(4),
        name="arrange",
    )(place, side, part, slot, *packets)
    return ordered.reshape(len(packets) * rows, width)


def fold(values):
    return jnp.sum(values.reshape(values.shape[0] // 8, 8, values.shape[1]), axis=0)


def row_sums(tiles):
    row = lax.broadcasted_iota(jnp.int32, tiles[0].shape, 0)
    for bit in (1, 2, 4):
        even = (row // bit) % 2 == 0
        merged = []
        for a, b in zip(tiles[::2], tiles[1::2]):
            merged.append(
                jnp.where(even, a, b) + pltpu.roll(jnp.where(even, b, a), 8 - bit, 0)
            )
        tiles = merged
    return tiles[0]


def label_table(tags):
    lane = lax.broadcasted_iota(jnp.int32, tags.shape, 1) % NCTF
    return (tags.astype(f32) == lane.astype(f32)).astype(f32)


def score_kernel(
    own_refs,
    side_ref,
    spectra_ref,
    cos_ref,
    sin_ref,
    own_ref,
    other_ref,
    transfer_ref,
    odds_ref,
    stats_ref,
    weighted_ref,
    penalty_ref,
):
    groups = spectra_ref.shape[0] // CHUNKS
    refs = groups * own_refs
    half = own_ref.shape[0]
    side = side_ref[0]

    own, other = own_ref[...], other_ref[...]
    weighted_ref[:half, :] = jnp.where(side == 0, own, other)
    weighted_ref[half:, :] = jnp.where(side == 0, other, own)
    odds_ref[...] = jnp.zeros_like(odds_ref)
    penalty_ref[...] = jnp.zeros_like(penalty_ref)
    width = 2 * UNIT * LANES

    def unit(u):
        wide = pl.ds(pl.multiple_of(u * width, width), width)
        weighted = weighted_ref[:, wide]
        tables = []
        for j in range(UNIT):
            lanes = pl.ds(pl.multiple_of((u * UNIT + j) * LANES, LANES), LANES)
            transfer = transfer_ref[:, lanes]
            tables.append((cos_ref[:, lanes], sin_ref[:, lanes], transfer * transfer))
        for g in range(groups):
            blocks = []
            for j in range(UNIT):
                d = u * UNIT + j
                line = slant_line(side, 2 * g + d % 2, d // 2, CHUNKS // 2)
                blocks.append(spectra_ref[line].astype(f32))
            for first in range(0, own_refs, WIDE):
                rows = []
                for i in range(first, first + WIDE):
                    pieces = []
                    power = 0.0
                    for j in range(UNIT):
                        cos, sin, squared = tables[j]
                        real, imag = blocks[j][i, 0:1], blocks[j][i, 1:2]
                        pieces.append((real * cos - imag * sin).astype(bf16))
                        pieces.append((real * sin + imag * cos).astype(bf16))
                        power = power + (real * real + imag * imag) * squared
                    place = (g * own_refs + i) * NCTF
                    penalty_ref[place : place + NCTF, :] += power
                    rows.append(jnp.concatenate(pieces, axis=1))
                place = (g * own_refs + first) * SHIFTS
                odds_ref[place : place + WIDE * SHIFTS, :] += lax.dot_general(
                    jnp.concatenate(rows, axis=0),
                    weighted,
                    (((1,), (1,)), ((), ())),
                    preferred_element_type=f32,
                )

    def units(k, carry):
        unit(2 * k)
        unit(2 * k + 1)
        return carry

    lax.fori_loop(0, CHUNKS // UNIT // 2, units, 0)
    tags = weighted_ref[:, 2 * F :].astype(f32).T[:NCTF]
    hot = (tags == lax.broadcasted_iota(jnp.int32, tags.shape, 0).astype(f32)).astype(f32)
    top = None
    for r in range(refs):
        charge = jnp.sum(penalty_ref[r * NCTF : (r + 1) * NCTF, :], axis=1, keepdims=True)
        cost = 0.5 * jnp.sum(charge * hot, axis=0, keepdims=True)
        place = slice(r * SHIFTS, (r + 1) * SHIFTS)
        scores = odds_ref[place, :] - cost
        odds_ref[place, :] = scores
        high = jnp.max(scores, axis=0, keepdims=True)
        top = high if top is None else jnp.maximum(top, high)
    odds = jnp.exp(odds_ref[...] - top)
    odds_ref[...] = odds
    total = jnp.sum(odds, axis=0, keepdims=True)
    stats = jnp.concatenate([top, total], axis=0)
    spare = jnp.zeros((2, LANES - stats.shape[1]), f32)
    stats = jnp.concatenate([stats, spare], axis=1)
    stats_ref[...] = jnp.broadcast_to(stats[None], stats_ref.shape)


def make_scores(side, spectra, cos_table, sin_table, own, other, transfer, own_refs, near):
    groups = spectra.shape[0] // CHUNKS
    refs = groups * own_refs
    count = 2 * own.shape[0]
    return pl.pallas_call(
        functools.partial(score_kernel, own_refs),
        out_shape=(
            jax.ShapeDtypeStruct((refs * SHIFTS, count), f32),
            jax.ShapeDtypeStruct((near, 2, LANES), f32),
            jax.ShapeDtypeStruct((count, own.shape[1]), bf16),
        ),
        in_specs=[pl.BlockSpec(memory_space=pltpu.SMEM)] + [whole_vmem] * 6,
        out_specs=(whole_vmem, whole_vmem, whole_vmem),
        scratch_shapes=[
            pltpu.VMEM((refs * NCTF, LANES), f32),
        ],
        compiler_params=room(24),
        name="scores",
    )(side, spectra, cos_table, sin_table, own, other, transfer)


def back_kernel(
    own_refs,
    slot_ref,
    odds_ref,
    stats_ref,
    packets_ref,
    cos_ref,
    sin_ref,
    parts_ref,
    log_ref,
    posterior_ref,
):
    groups = parts_ref.shape[0] // CHUNKS
    refs = groups * own_refs
    count = odds_ref.shape[1]
    slot = slot_ref[0]
    tops, sums = stats_ref[:, 0, :count], stats_ref[:, 1, :count]
    top = jnp.max(tops, axis=0, keepdims=True)
    total = jnp.sum(sums * jnp.exp(tops - top), axis=0, keepdims=True)
    log_all = top + jnp.log(total)
    own_rows = log_ref.shape[1]
    own_log = jnp.zeros_like(log_ref)
    for k in range(count // own_rows):
        piece = log_all[:, k * own_rows : (k + 1) * own_rows]
        own_log = jnp.where(slot == k, piece, own_log)
    log_ref[...] = own_log
    scale = jnp.exp(stats_ref[slot][0:1, :count] - log_all)
    weights = []
    for r in range(refs):
        place = slice(r * SHIFTS, (r + 1) * SHIFTS)
        posterior = (odds_ref[place, :] * scale).astype(bf16)
        posterior_ref[place, :] = posterior
        weights.append(jnp.sum(posterior.astype(f32), axis=0, keepdims=True))
    weights = jnp.concatenate(weights, axis=0)
    high = weights.astype(bf16)
    low = (weights - high.astype(f32)).astype(bf16)
    hot = label_table(packets_ref[:, 2 * F :]).astype(bf16)
    spread = jnp.dot(jnp.concatenate([high, low], axis=0), hot, preferred_element_type=f32)
    spread = spread[:refs] + spread[refs:]
    lane = lax.broadcasted_iota(jnp.int32, (refs, LANES), 1) // NCTF
    row = lax.broadcasted_iota(jnp.int32, (refs, LANES), 0) % own_refs
    spread = jnp.where(lane == row, spread, 0.0)
    shares = []
    for g in range(groups):
        share = jnp.sum(spread[g * own_refs : (g + 1) * own_refs], axis=0, keepdims=True)
        high = share.astype(bf16).astype(f32)
        before = jnp.zeros((2 * own_refs, LANES), f32)
        after = jnp.zeros((ROWS - 2 * own_refs - 2, LANES), f32)
        shares.append(jnp.concatenate([before, high, share - high, after], axis=0))

    def chunk(d):
        lanes = pl.ds(pl.multiple_of(d * LANES, LANES), LANES)
        wide = pl.ds(pl.multiple_of(d * 2 * LANES, 2 * LANES), 2 * LANES)
        cos, sin = cos_ref[:, lanes], sin_ref[:, lanes]
        weighted = packets_ref[:, wide]
        for g in range(groups):
            rows = []
            for first in range(0, own_refs, BATCH):
                place = (g * own_refs + first) * SHIFTS
                totals = jnp.dot(
                    posterior_ref[place : place + BATCH * SHIFTS, :],
                    weighted,
                    preferred_element_type=f32,
                )
                for i in range(BATCH):
                    real = totals[i * SHIFTS : (i + 1) * SHIFTS, :LANES]
                    imag = totals[i * SHIFTS : (i + 1) * SHIFTS, LANES:]
                    rows.append(fold(real * cos + imag * sin))
                    rows.append(fold(imag * cos - real * sin))
            blank = [jnp.zeros((8, LANES), f32)] * (ROWS - len(rows))
            rows = rows + blank
            sums = jnp.concatenate([row_sums(rows[:8]), row_sums(rows[8:])], axis=0)
            line = peer_line(2 * g + d % 2, d // 2, 2 * groups, CHUNKS // 2)
            parts_ref[line] = (sums + shares[g]).astype(bf16)

    def chunks(k, carry):
        for j in range(UNROLL):
            chunk(k * UNROLL + j)
        return carry

    lax.fori_loop(0, CHUNKS // UNROLL, chunks, 0)


def back_project(slot, odds, stats, packets, cos_table, sin_table, own_refs, rows):
    count = packets.shape[0]
    groups = odds.shape[0] // SHIFTS // own_refs
    return pl.pallas_call(
        functools.partial(back_kernel, own_refs),
        out_shape=(
            jax.ShapeDtypeStruct((groups * CHUNKS, ROWS, LANES), bf16),
            jax.ShapeDtypeStruct((1, rows), f32),
        ),
        in_specs=[pl.BlockSpec(memory_space=pltpu.SMEM)] + [whole_vmem] * 5,
        out_specs=(whole_vmem, whole_vmem),
        scratch_shapes=[pltpu.VMEM((odds.shape[0], count), bf16)],
        compiler_params=room(24),
        name="back",
    )(slot, odds, stats, packets, cos_table, sin_table)


def finish_kernel(place_ref, parts_ref, transfer_ref, out_ref):
    own_refs = out_ref.shape[0]
    sums = jnp.sum(parts_ref[...].astype(f32), axis=0)
    share = sums[2 * own_refs : 2 * own_refs + 1] + sums[2 * own_refs + 1 : 2 * own_refs + 2]
    lane = lax.broadcasted_iota(jnp.int32, (own_refs, LANES), 1) // NCTF
    row = lax.broadcasted_iota(jnp.int32, (own_refs, LANES), 0)
    shares = jnp.where(lane == row, share, 0.0)
    own = transfer_ref[:, pl.ds(pl.multiple_of(place_ref[0] * LANES, LANES), LANES)]
    squared = jnp.concatenate([own * own] * (LANES // NCTF), axis=0)
    denominator = jnp.dot(shares, squared, precision=highest) + ridge_term
    for i in range(own_refs):
        out_ref[i] = sums[2 * i : 2 * i + 2] / denominator[i : i + 1]


def finish(place, parts, transfer, own_refs):
    return pl.pallas_call(
        finish_kernel,
        out_shape=jax.ShapeDtypeStruct((own_refs, 2, LANES), f32),
        in_specs=[pl.BlockSpec(memory_space=pltpu.SMEM)] + [whole_vmem] * 2,
        out_specs=whole_vmem,
        compiler_params=room(4),
        name="finish",
    )(place, parts, transfer)


def shifted(value, axis, steps):
    count = lax.axis_size(axis)
    pairs = [(source, (source + steps) % count) for source in range(count)]
    return lax.ppermute(value, axis, pairs)


def parted(value, steps):
    count = lax.axis_size("x")
    pairs = []
    for source in range(count):
        pairs.append((2 * source, 2 * ((source + steps) % count)))
        pairs.append((2 * source + 1, 2 * ((source - steps) % count) + 1))
    return lax.ppermute(value, ("x", "core"), pairs)


def peer_line(row, plane, rows, planes):
    return (planes - 1 - plane) * rows + (row + rows // 2) % rows


def slant_line(side, row, plane, count):
    column = (plane + 1) % count
    step = count + side * column - (1 - side) * column
    return count * ((row + count // 2 + step) % count) + column


def slanted_exchange(value):
    yh, dom = lax.axis_size("yh"), lax.axis_size("dom")
    groups = []
    for side in range(2):
        order = [0] * (yh * dom)
        for y in range(yh):
            for d in range(dom):
                line = slant_line(side, 2 * y + d % 2, d // 2, dom // 2)
                order[line] = (side * yh + y) * dom + d
        groups.append(order)
    return lax.all_to_all(value, ("core", "yh", "dom"), 0, 0, axis_index_groups=groups)


def wide_exchange(value):
    yh, dom = lax.axis_size("yh"), lax.axis_size("dom")
    order = [0] * (yh * dom)
    for y in range(yh):
        for d in range(dom):
            order[peer_line(2 * y + d % 2, d // 2, 2 * yh, dom // 2)] = y * dom + d
    return lax.all_to_all(value, ("yh", "dom"), 0, 0, axis_index_groups=[order])


def body(particles, classes, template_spectra, transfer_magnitude, offsets):
    rows = particles.shape[0]
    own_refs = template_spectra.shape[0]
    near_axes = ("core", "x")
    near, far = lax.axis_size(near_axes), lax.axis_size(("yh", "dom"))
    packet, copies = prep(classes, particles, transfer_magnitude, template_spectra, far)
    spectra = slanted_exchange(copies)
    place, side, part = [lax.axis_index(name)[None] for name in ("x", "core", "dom")]
    slot = lax.axis_index(near_axes)[None]
    second, first, third = parted(packet, 2), parted(packet, 1), parted(packet, 3)
    own = arrange(place, side, part, slot, [packet, third, first, second])
    other = shifted(own, "core", 1)
    cos_table, sin_table = phase_tables(offsets)
    odds, stats, weighted = make_scores(
        side, spectra, cos_table, sin_table, own, other, transfer_magnitude, own_refs, near
    )
    stats = lax.all_to_all(stats, near_axes, 0, 0)
    parts, log_own = back_project(
        slot, odds, stats, weighted, cos_table, sin_table, own_refs, rows
    )
    parts = wide_exchange(parts)
    new_refs = finish(part, parts, transfer_magnitude, own_refs)
    return (log_own.reshape(rows), new_refs)


def solution(mesh):
    devices = mesh.devices
    names = ("yh", "x", "core", "dom")
    inner = Mesh(devices.reshape(4, 4, 2, devices.shape[1]), names)
    refs = names[:3]
    return jax.shard_map(
        body,
        mesh=inner,
        in_specs=(P(names, None, None), P(names), P(refs, None, "dom"), P(), P()),
        out_specs=(P(names), P(refs, None, "dom")),
        check_vma=False,
    )
```

```python
import functools
import math

import jax
import jax.numpy as jnp
from jax import lax
from jax.experimental import pallas as pl
from jax.experimental.pallas import tpu as pltpu
from jax.sharding import Mesh
from jax.sharding import PartitionSpec as P

BOX = 64
F = 2048
SHIFTS = 64
NCTF = 16
LANES = 128
CHUNKS = F // LANES
ROWS = 16
UNIT = 4
UNROLL = 8
BATCH = 2
WIDE = 6

highest = lax.Precision.HIGHEST
ridge_term = 1.0
f32 = jnp.float32
bf16 = jnp.bfloat16
whole_vmem = pl.BlockSpec(memory_space=pltpu.VMEM)


def room(mib):
    return pltpu.CompilerParams(vmem_limit_bytes=mib * 1024 * 1024)


def phase_tables(offsets):
    half_side = BOX // 2
    positions = jnp.arange(F, dtype=jnp.int32)
    row_index = positions // half_side
    freq_x = jnp.where(row_index < half_side, row_index, row_index - BOX)
    freq_y = positions % half_side
    turn_count = (offsets[:, 0:1] * freq_x[None, :] + offsets[:, 1:2] * freq_y[None, :]) % BOX
    angles = turn_count.astype(f32) * (2.0 * math.pi / BOX)
    return (jnp.cos(angles), jnp.sin(angles))


def prep_kernel(classes_ref, particles_ref, transfer_ref, spectra_ref, packet_ref, copies_ref):
    rows = particles_ref.shape[0]
    copies_ref[...] = jnp.broadcast_to(spectra_ref[...][None], copies_ref.shape)
    place = lax.broadcasted_iota(jnp.int32, (rows, 1), 0)
    labels = jnp.zeros((rows, 1), jnp.int32)
    for i in range(rows):
        labels = jnp.where(place == i, classes_ref[i], labels)
    contrast = jnp.zeros((rows, F), f32)
    for c in range(NCTF):
        contrast = jnp.where(labels == c, transfer_ref[c : c + 1, :], contrast)
    values = particles_ref[...].astype(f32)
    real = (values[:, 0, :] * contrast).astype(bf16)
    imag = (values[:, 1, :] * contrast).astype(bf16)
    for d in range(CHUNKS):
        lanes = slice(d * LANES, (d + 1) * LANES)
        packet_ref[:, 2 * d * LANES : (2 * d + 1) * LANES] = real[:, lanes]
        packet_ref[:, (2 * d + 1) * LANES : (2 * d + 2) * LANES] = imag[:, lanes]
    tags = jnp.broadcast_to(labels.astype(f32), (rows, LANES))
    packet_ref[:, 2 * F :] = tags.astype(bf16)


def prep(classes, particles, transfer, spectra, far):
    rows = particles.shape[0]
    return pl.pallas_call(
        prep_kernel,
        out_shape=(
            jax.ShapeDtypeStruct((rows, 2 * F + LANES), bf16),
            jax.ShapeDtypeStruct((far,) + spectra.shape, bf16),
        ),
        in_specs=[pl.BlockSpec(memory_space=pltpu.SMEM)] + [whole_vmem] * 3,
        out_specs=(whole_vmem, whole_vmem),
        compiler_params=room(60),
        name="prep",
    )(classes, particles, transfer, spectra)


def arrange_kernel(place_ref, side_ref, part_ref, slot_ref, *refs):
    count = len(refs) - 1
    for k in range(count):
        step = jnp.where(side_ref[0] == 0, k, count - k)
        refs[count][lax.rem(place_ref[0] + step, count)] = refs[k][...]


def arrange(place, side, part, slot, packets):
    rows, width = packets[0].shape
    ordered = pl.pallas_call(
        arrange_kernel,
        out_shape=jax.ShapeDtypeStruct((len(packets), rows, width), bf16),
        in_specs=[pl.BlockSpec(memory_space=pltpu.SMEM)] * 4 + [whole_vmem] * len(packets),
        out_specs=whole_vmem,
        compiler_params=room(4),
        name="arrange",
    )(place, side, part, slot, *packets)
    return ordered.reshape(len(packets) * rows, width)


def fold(values):
    return jnp.sum(values.reshape(values.shape[0] // 8, 8, values.shape[1]), axis=0)


def row_sums(tiles):
    row = lax.broadcasted_iota(jnp.int32, tiles[0].shape, 0)
    for bit in (1, 2, 4):
        even = (row // bit) % 2 == 0
        merged = []
        for a, b in zip(tiles[::2], tiles[1::2]):
            merged.append(
                jnp.where(even, a, b) + pltpu.roll(jnp.where(even, b, a), 8 - bit, 0)
            )
        tiles = merged
    return tiles[0]


def label_table(tags):
    lane = lax.broadcasted_iota(jnp.int32, tags.shape, 1) % NCTF
    return (tags.astype(f32) == lane.astype(f32)).astype(f32)


def score_kernel(
    own_refs,
    side_ref,
    spectra_ref,
    cos_ref,
    sin_ref,
    own_ref,
    other_ref,
    transfer_ref,
    odds_ref,
    stats_ref,
    weighted_ref,
    penalty_ref,
):
    groups = spectra_ref.shape[0] // CHUNKS
    refs = groups * own_refs
    half = own_ref.shape[0]
    side = side_ref[0]

    own, other = own_ref[...], other_ref[...]
    weighted_ref[:half, :] = jnp.where(side == 0, own, other)
    weighted_ref[half:, :] = jnp.where(side == 0, other, own)
    odds_ref[...] = jnp.zeros_like(odds_ref)
    penalty_ref[...] = jnp.zeros_like(penalty_ref)
    width = 2 * UNIT * LANES

    def unit(u):
        wide = pl.ds(pl.multiple_of(u * width, width), width)
        weighted = weighted_ref[:, wide]
        tables = []
        for j in range(UNIT):
            lanes = pl.ds(pl.multiple_of((u * UNIT + j) * LANES, LANES), LANES)
            transfer = transfer_ref[:, lanes]
            tables.append((cos_ref[:, lanes], sin_ref[:, lanes], transfer * transfer))
        for g in range(groups):
            blocks = []
            for j in range(UNIT):
                d = u * UNIT + j
                line = slant_line(side, 2 * g + d % 2, d // 2, CHUNKS // 2)
                blocks.append(spectra_ref[line].astype(f32))
            for first in range(0, own_refs, WIDE):
                rows = []
                for i in range(first, first + WIDE):
                    pieces = []
                    power = 0.0
                    for j in range(UNIT):
                        cos, sin, squared = tables[j]
                        real, imag = blocks[j][i, 0:1], blocks[j][i, 1:2]
                        pieces.append((real * cos - imag * sin).astype(bf16))
                        pieces.append((real * sin + imag * cos).astype(bf16))
                        power = power + (real * real + imag * imag) * squared
                    place = (g * own_refs + i) * NCTF
                    penalty_ref[place : place + NCTF, :] += power
                    rows.append(jnp.concatenate(pieces, axis=1))
                place = (g * own_refs + first) * SHIFTS
                odds_ref[place : place + WIDE * SHIFTS, :] += lax.dot_general(
                    jnp.concatenate(rows, axis=0),
                    weighted,
                    (((1,), (1,)), ((), ())),
                    preferred_element_type=f32,
                )

    def units(k, carry):
        unit(2 * k)
        unit(2 * k + 1)
        return carry

    lax.fori_loop(0, CHUNKS // UNIT // 2, units, 0)
    tags = weighted_ref[:, 2 * F :].astype(f32).T[:NCTF]
    hot = (tags == lax.broadcasted_iota(jnp.int32, tags.shape, 0).astype(f32)).astype(f32)
    top = None
    for r in range(refs):
        charge = jnp.sum(penalty_ref[r * NCTF : (r + 1) * NCTF, :], axis=1, keepdims=True)
        cost = 0.5 * jnp.sum(charge * hot, axis=0, keepdims=True)
        place = slice(r * SHIFTS, (r + 1) * SHIFTS)
        scores = odds_ref[place, :] - cost
        odds_ref[place, :] = scores
        high = jnp.max(scores, axis=0, keepdims=True)
        top = high if top is None else jnp.maximum(top, high)
    odds = jnp.exp(odds_ref[...] - top)
    odds_ref[...] = odds
    total = jnp.sum(odds, axis=0, keepdims=True)
    stats = jnp.concatenate([top, total], axis=0)
    spare = jnp.zeros((2, LANES - stats.shape[1]), f32)
    stats = jnp.concatenate([stats, spare], axis=1)
    stats_ref[...] = jnp.broadcast_to(stats[None], stats_ref.shape)


def make_scores(side, spectra, cos_table, sin_table, own, other, transfer, own_refs, near):
    groups = spectra.shape[0] // CHUNKS
    refs = groups * own_refs
    count = 2 * own.shape[0]
    return pl.pallas_call(
        functools.partial(score_kernel, own_refs),
        out_shape=(
            jax.ShapeDtypeStruct((refs * SHIFTS, count), f32),
            jax.ShapeDtypeStruct((near, 2, LANES), f32),
            jax.ShapeDtypeStruct((count, own.shape[1]), bf16),
        ),
        in_specs=[pl.BlockSpec(memory_space=pltpu.SMEM)] + [whole_vmem] * 6,
        out_specs=(whole_vmem, whole_vmem, whole_vmem),
        scratch_shapes=[
            pltpu.VMEM((refs * NCTF, LANES), f32),
        ],
        compiler_params=room(24),
        name="scores",
    )(side, spectra, cos_table, sin_table, own, other, transfer)


def back_kernel(
    own_refs,
    slot_ref,
    odds_ref,
    stats_ref,
    packets_ref,
    cos_ref,
    sin_ref,
    parts_ref,
    log_ref,
    posterior_ref,
):
    groups = parts_ref.shape[0] // CHUNKS
    refs = groups * own_refs
    count = odds_ref.shape[1]
    slot = slot_ref[0]
    tops, sums = stats_ref[:, 0, :count], stats_ref[:, 1, :count]
    top = jnp.max(tops, axis=0, keepdims=True)
    total = jnp.sum(sums * jnp.exp(tops - top), axis=0, keepdims=True)
    log_all = top + jnp.log(total)
    own_rows = log_ref.shape[1]
    own_log = jnp.zeros_like(log_ref)
    for k in range(count // own_rows):
        piece = log_all[:, k * own_rows : (k + 1) * own_rows]
        own_log = jnp.where(slot == k, piece, own_log)
    log_ref[...] = own_log
    scale = jnp.exp(stats_ref[slot][0:1, :count] - log_all)
    weights = []
    for r in range(refs):
        place = slice(r * SHIFTS, (r + 1) * SHIFTS)
        posterior = (odds_ref[place, :] * scale).astype(bf16)
        posterior_ref[place, :] = posterior
        weights.append(jnp.sum(posterior.astype(f32), axis=0, keepdims=True))
    weights = jnp.concatenate(weights, axis=0)
    high = weights.astype(bf16)
    low = (weights - high.astype(f32)).astype(bf16)
    hot = label_table(packets_ref[:, 2 * F :]).astype(bf16)
    spread = jnp.dot(jnp.concatenate([high, low], axis=0), hot, preferred_element_type=f32)
    spread = spread[:refs] + spread[refs:]
    lane = lax.broadcasted_iota(jnp.int32, (refs, LANES), 1) // NCTF
    row = lax.broadcasted_iota(jnp.int32, (refs, LANES), 0) % own_refs
    spread = jnp.where(lane == row, spread, 0.0)
    shares = []
    for g in range(groups):
        share = jnp.sum(spread[g * own_refs : (g + 1) * own_refs], axis=0, keepdims=True)
        high = share.astype(bf16).astype(f32)
        before = jnp.zeros((2 * own_refs, LANES), f32)
        after = jnp.zeros((ROWS - 2 * own_refs - 2, LANES), f32)
        shares.append(jnp.concatenate([before, high, share - high, after], axis=0))

    def chunk(d):
        lanes = pl.ds(pl.multiple_of(d * LANES, LANES), LANES)
        wide = pl.ds(pl.multiple_of(d * 2 * LANES, 2 * LANES), 2 * LANES)
        cos, sin = cos_ref[:, lanes], sin_ref[:, lanes]
        weighted = packets_ref[:, wide]
        for g in range(groups):
            rows = []
            for first in range(0, own_refs, BATCH):
                place = (g * own_refs + first) * SHIFTS
                totals = jnp.dot(
                    posterior_ref[place : place + BATCH * SHIFTS, :],
                    weighted,
                    preferred_element_type=f32,
                )
                for i in range(BATCH):
                    real = totals[i * SHIFTS : (i + 1) * SHIFTS, :LANES]
                    imag = totals[i * SHIFTS : (i + 1) * SHIFTS, LANES:]
                    rows.append(fold(real * cos + imag * sin))
                    rows.append(fold(imag * cos - real * sin))
            blank = [jnp.zeros((8, LANES), f32)] * (ROWS - len(rows))
            rows = rows + blank
            sums = jnp.concatenate([row_sums(rows[:8]), row_sums(rows[8:])], axis=0)
            line = peer_line(2 * g + d % 2, d // 2, 2 * groups, CHUNKS // 2)
            parts_ref[line] = (sums + shares[g]).astype(bf16)

    def chunks(k, carry):
        for j in range(UNROLL):
            chunk(k * UNROLL + j)
        return carry

    lax.fori_loop(0, CHUNKS // UNROLL, chunks, 0)


def back_project(slot, odds, stats, packets, cos_table, sin_table, own_refs, rows):
    count = packets.shape[0]
    groups = odds.shape[0] // SHIFTS // own_refs
    return pl.pallas_call(
        functools.partial(back_kernel, own_refs),
        out_shape=(
            jax.ShapeDtypeStruct((groups * CHUNKS, ROWS, LANES), bf16),
            jax.ShapeDtypeStruct((1, rows), f32),
        ),
        in_specs=[pl.BlockSpec(memory_space=pltpu.SMEM)] + [whole_vmem] * 5,
        out_specs=(whole_vmem, whole_vmem),
        scratch_shapes=[pltpu.VMEM((odds.shape[0], count), bf16)],
        compiler_params=room(24),
        name="back",
    )(slot, odds, stats, packets, cos_table, sin_table)


def finish_kernel(place_ref, parts_ref, transfer_ref, out_ref):
    own_refs = out_ref.shape[0]
    sums = jnp.sum(parts_ref[...].astype(f32), axis=0)
    share = sums[2 * own_refs : 2 * own_refs + 1] + sums[2 * own_refs + 1 : 2 * own_refs + 2]
    lane = lax.broadcasted_iota(jnp.int32, (own_refs, LANES), 1) // NCTF
    row = lax.broadcasted_iota(jnp.int32, (own_refs, LANES), 0)
    shares = jnp.where(lane == row, share, 0.0)
    own = transfer_ref[:, pl.ds(pl.multiple_of(place_ref[0] * LANES, LANES), LANES)]
    squared = jnp.concatenate([own * own] * (LANES // NCTF), axis=0)
    denominator = jnp.dot(shares, squared, precision=highest) + ridge_term
    for i in range(own_refs):
        out_ref[i] = sums[2 * i : 2 * i + 2] / denominator[i : i + 1]


def finish(place, parts, transfer, own_refs):
    return pl.pallas_call(
        finish_kernel,
        out_shape=jax.ShapeDtypeStruct((own_refs, 2, LANES), f32),
        in_specs=[pl.BlockSpec(memory_space=pltpu.SMEM)] + [whole_vmem] * 2,
        out_specs=whole_vmem,
        compiler_params=room(4),
        name="finish",
    )(place, parts, transfer)


def shifted(value, axis, steps):
    count = lax.axis_size(axis)
    pairs = [(source, (source + steps) % count) for source in range(count)]
    return lax.ppermute(value, axis, pairs)


def parted(value, steps):
    count = lax.axis_size("x")
    pairs = []
    for source in range(count):
        pairs.append((2 * source, 2 * ((source - steps) % count)))
        pairs.append((2 * source + 1, 2 * ((source + steps) % count) + 1))
    return lax.ppermute(value, ("x", "core"), pairs)


def peer_line(row, plane, rows, planes):
    return (planes - 1 - plane) * rows + (row + rows // 2) % rows


def slant_line(side, row, plane, count):
    column = (plane + 1) % count
    step = count + side * column - (1 - side) * column
    return count * ((row + count // 2 + step) % count) + column


def slanted_exchange(value):
    yh, dom = lax.axis_size("yh"), lax.axis_size("dom")
    groups = []
    for side in range(2):
        order = [0] * (yh * dom)
        for y in range(yh):
            for d in range(dom):
                line = slant_line(side, 2 * y + d % 2, d // 2, dom // 2)
                order[line] = (side * yh + y) * dom + d
        groups.append(order)
    return lax.all_to_all(value, ("core", "yh", "dom"), 0, 0, axis_index_groups=groups)


def wide_exchange(value):
    yh, dom = lax.axis_size("yh"), lax.axis_size("dom")
    order = [0] * (yh * dom)
    for y in range(yh):
        for d in range(dom):
            order[peer_line(2 * y + d % 2, d // 2, 2 * yh, dom // 2)] = y * dom + d
    return lax.all_to_all(value, ("yh", "dom"), 0, 0, axis_index_groups=[order])


def body(particles, classes, template_spectra, transfer_magnitude, offsets):
    rows = particles.shape[0]
    own_refs = template_spectra.shape[0]
    near_axes = ("core", "x")
    near, far = lax.axis_size(near_axes), lax.axis_size(("yh", "dom"))
    packet, copies = prep(classes, particles, transfer_magnitude, template_spectra, far)
    spectra = slanted_exchange(copies)
    place, side, part = [lax.axis_index(name)[None] for name in ("x", "core", "dom")]
    slot = lax.axis_index(near_axes)[None]
    second, first, third = parted(packet, 2), parted(packet, 1), parted(packet, 3)
    own = arrange(place, side, part, slot, [packet, first, second, third])
    other = shifted(own, "core", 1)
    cos_table, sin_table = phase_tables(offsets)
    odds, stats, weighted = make_scores(
        side, spectra, cos_table, sin_table, own, other, transfer_magnitude, own_refs, near
    )
    stats = lax.all_to_all(stats, near_axes, 0, 0)
    parts, log_own = back_project(
        slot, odds, stats, weighted, cos_table, sin_table, own_refs, rows
    )
    parts = wide_exchange(parts)
    new_refs = finish(part, parts, transfer_magnitude, own_refs)
    return (log_own.reshape(rows), new_refs)


def solution(mesh):
    devices = mesh.devices
    names = ("yh", "x", "core", "dom")
    inner = Mesh(devices.reshape(4, 4, 2, devices.shape[1]), names)
    refs = names[:3]
    return jax.shard_map(
        body,
        mesh=inner,
        in_specs=(P(names, None, None), P(names), P(refs, None, "dom"), P(), P()),
        out_specs=(P(names), P(refs, None, "dom")),
        check_vma=False,
    )
```

```python
import functools
import math

import jax
import jax.numpy as jnp
from jax import lax
from jax.experimental import pallas as pl
from jax.experimental.pallas import tpu as pltpu
from jax.sharding import Mesh
from jax.sharding import PartitionSpec as P

BOX = 64
F = 2048
SHIFTS = 64
NCTF = 16
LANES = 128
CHUNKS = F // LANES
ROWS = 16
UNIT = 4
UNROLL = 8
BATCH = 2
WIDE = 6

highest = lax.Precision.HIGHEST
ridge_term = 1.0
f32 = jnp.float32
bf16 = jnp.bfloat16
whole_vmem = pl.BlockSpec(memory_space=pltpu.VMEM)


def room(mib):
    return pltpu.CompilerParams(vmem_limit_bytes=mib * 1024 * 1024)


def phase_tables(offsets):
    half_side = BOX // 2
    positions = jnp.arange(F, dtype=jnp.int32)
    row_index = positions // half_side
    freq_x = jnp.where(row_index < half_side, row_index, row_index - BOX)
    freq_y = positions % half_side
    turn_count = (offsets[:, 0:1] * freq_x[None, :] + offsets[:, 1:2] * freq_y[None, :]) % BOX
    angles = turn_count.astype(f32) * (2.0 * math.pi / BOX)
    return (jnp.cos(angles), jnp.sin(angles))


def prep_kernel(classes_ref, particles_ref, transfer_ref, spectra_ref, packet_ref, copies_ref):
    rows = particles_ref.shape[0]
    copies_ref[...] = jnp.broadcast_to(spectra_ref[...][None], copies_ref.shape)
    place = lax.broadcasted_iota(jnp.int32, (rows, 1), 0)
    labels = jnp.zeros((rows, 1), jnp.int32)
    for i in range(rows):
        labels = jnp.where(place == i, classes_ref[i], labels)
    contrast = jnp.zeros((rows, F), f32)
    for c in range(NCTF):
        contrast = jnp.where(labels == c, transfer_ref[c : c + 1, :], contrast)
    values = particles_ref[...].astype(f32)
    real = (values[:, 0, :] * contrast).astype(bf16)
    imag = (values[:, 1, :] * contrast).astype(bf16)
    for d in range(CHUNKS):
        lanes = slice(d * LANES, (d + 1) * LANES)
        packet_ref[:, 2 * d * LANES : (2 * d + 1) * LANES] = real[:, lanes]
        packet_ref[:, (2 * d + 1) * LANES : (2 * d + 2) * LANES] = imag[:, lanes]
    tags = jnp.broadcast_to(labels.astype(f32), (rows, LANES))
    packet_ref[:, 2 * F :] = tags.astype(bf16)


def prep(classes, particles, transfer, spectra, far):
    rows = particles.shape[0]
    return pl.pallas_call(
        prep_kernel,
        out_shape=(
            jax.ShapeDtypeStruct((rows, 2 * F + LANES), bf16),
            jax.ShapeDtypeStruct((far,) + spectra.shape, bf16),
        ),
        in_specs=[pl.BlockSpec(memory_space=pltpu.SMEM)] + [whole_vmem] * 3,
        out_specs=(whole_vmem, whole_vmem),
        compiler_params=room(60),
        name="prep",
    )(classes, particles, transfer, spectra)


def arrange_kernel(place_ref, side_ref, part_ref, slot_ref, *refs):
    count = len(refs) - 1
    for k in range(count):
        step = jnp.where(side_ref[0] == 0, k, count - k)
        refs[count][lax.rem(place_ref[0] + step, count)] = refs[k][...]


def arrange(place, side, part, slot, packets):
    rows, width = packets[0].shape
    ordered = pl.pallas_call(
        arrange_kernel,
        out_shape=jax.ShapeDtypeStruct((len(packets), rows, width), bf16),
        in_specs=[pl.BlockSpec(memory_space=pltpu.SMEM)] * 4 + [whole_vmem] * len(packets),
        out_specs=whole_vmem,
        compiler_params=room(4),
        name="arrange",
    )(place, side, part, slot, *packets)
    return ordered.reshape(len(packets) * rows, width)


def fold(values):
    return jnp.sum(values.reshape(values.shape[0] // 8, 8, values.shape[1]), axis=0)


def row_sums(tiles):
    row = lax.broadcasted_iota(jnp.int32, tiles[0].shape, 0)
    for bit in (1, 2, 4):
        even = (row // bit) % 2 == 0
        merged = []
        for a, b in zip(tiles[::2], tiles[1::2]):
            merged.append(
                jnp.where(even, a, b) + pltpu.roll(jnp.where(even, b, a), 8 - bit, 0)
            )
        tiles = merged
    return tiles[0]


def label_table(tags):
    lane = lax.broadcasted_iota(jnp.int32, tags.shape, 1) % NCTF
    return (tags.astype(f32) == lane.astype(f32)).astype(f32)


def score_kernel(
    own_refs,
    side_ref,
    spectra_ref,
    cos_ref,
    sin_ref,
    own_ref,
    other_ref,
    transfer_ref,
    odds_ref,
    stats_ref,
    weighted_ref,
    penalty_ref,
):
    groups = spectra_ref.shape[0] // CHUNKS
    refs = groups * own_refs
    half = own_ref.shape[0]
    side = side_ref[0]

    own, other = own_ref[...], other_ref[...]
    weighted_ref[:half, :] = jnp.where(side == 0, own, other)
    weighted_ref[half:, :] = jnp.where(side == 0, other, own)
    odds_ref[...] = jnp.zeros_like(odds_ref)
    penalty_ref[...] = jnp.zeros_like(penalty_ref)
    width = 2 * UNIT * LANES

    def unit(u):
        wide = pl.ds(pl.multiple_of(u * width, width), width)
        weighted = weighted_ref[:, wide]
        tables = []
        for j in range(UNIT):
            lanes = pl.ds(pl.multiple_of((u * UNIT + j) * LANES, LANES), LANES)
            transfer = transfer_ref[:, lanes]
            tables.append((cos_ref[:, lanes], sin_ref[:, lanes], transfer * transfer))
        for g in range(groups):
            blocks = []
            for j in range(UNIT):
                d = u * UNIT + j
                line = slant_line(side, 2 * g + d % 2, d // 2, CHUNKS // 2)
                blocks.append(spectra_ref[line].astype(f32))
            for first in range(0, own_refs, WIDE):
                rows = []
                for i in range(first, first + WIDE):
                    pieces = []
                    power = 0.0
                    for j in range(UNIT):
                        cos, sin, squared = tables[j]
                        real, imag = blocks[j][i, 0:1], blocks[j][i, 1:2]
                        pieces.append((real * cos - imag * sin).astype(bf16))
                        pieces.append((real * sin + imag * cos).astype(bf16))
                        power = power + (real * real + imag * imag) * squared
                    place = (g * own_refs + i) * NCTF
                    penalty_ref[place : place + NCTF, :] += power
                    rows.append(jnp.concatenate(pieces, axis=1))
                place = (g * own_refs + first) * SHIFTS
                odds_ref[place : place + WIDE * SHIFTS, :] += lax.dot_general(
                    jnp.concatenate(rows, axis=0),
                    weighted,
                    (((1,), (1,)), ((), ())),
                    preferred_element_type=f32,
                )

    def units(k, carry):
        unit(2 * k)
        unit(2 * k + 1)
        return carry

    lax.fori_loop(0, CHUNKS // UNIT // 2, units, 0)
    tags = weighted_ref[:, 2 * F :].astype(f32).T[:NCTF]
    hot = (tags == lax.broadcasted_iota(jnp.int32, tags.shape, 0).astype(f32)).astype(f32)
    top = None
    for r in range(refs):
        charge = jnp.sum(penalty_ref[r * NCTF : (r + 1) * NCTF, :], axis=1, keepdims=True)
        cost = 0.5 * jnp.sum(charge * hot, axis=0, keepdims=True)
        place = slice(r * SHIFTS, (r + 1) * SHIFTS)
        scores = odds_ref[place, :] - cost
        odds_ref[place, :] = scores
        high = jnp.max(scores, axis=0, keepdims=True)
        top = high if top is None else jnp.maximum(top, high)
    odds = jnp.exp(odds_ref[...] - top)
    odds_ref[...] = odds
    total = jnp.sum(odds, axis=0, keepdims=True)
    stats = jnp.concatenate([top, total], axis=0)
    spare = jnp.zeros((2, LANES - stats.shape[1]), f32)
    stats = jnp.concatenate([stats, spare], axis=1)
    stats_ref[...] = jnp.broadcast_to(stats[None], stats_ref.shape)


def make_scores(side, spectra, cos_table, sin_table, own, other, transfer, own_refs, near):
    groups = spectra.shape[0] // CHUNKS
    refs = groups * own_refs
    count = 2 * own.shape[0]
    return pl.pallas_call(
        functools.partial(score_kernel, own_refs),
        out_shape=(
            jax.ShapeDtypeStruct((refs * SHIFTS, count), f32),
            jax.ShapeDtypeStruct((near, 2, LANES), f32),
            jax.ShapeDtypeStruct((count, own.shape[1]), bf16),
        ),
        in_specs=[pl.BlockSpec(memory_space=pltpu.SMEM)] + [whole_vmem] * 6,
        out_specs=(whole_vmem, whole_vmem, whole_vmem),
        scratch_shapes=[
            pltpu.VMEM((refs * NCTF, LANES), f32),
        ],
        compiler_params=room(24),
        name="scores",
    )(side, spectra, cos_table, sin_table, own, other, transfer)


def back_kernel(
    own_refs,
    slot_ref,
    odds_ref,
    stats_ref,
    packets_ref,
    cos_ref,
    sin_ref,
    parts_ref,
    log_ref,
    posterior_ref,
):
    groups = parts_ref.shape[0] // CHUNKS
    refs = groups * own_refs
    count = odds_ref.shape[1]
    slot = slot_ref[0]
    tops, sums = stats_ref[:, 0, :count], stats_ref[:, 1, :count]
    top = jnp.max(tops, axis=0, keepdims=True)
    total = jnp.sum(sums * jnp.exp(tops - top), axis=0, keepdims=True)
    log_all = top + jnp.log(total)
    own_rows = log_ref.shape[1]
    own_log = jnp.zeros_like(log_ref)
    for k in range(count // own_rows):
        piece = log_all[:, k * own_rows : (k + 1) * own_rows]
        own_log = jnp.where(slot == k, piece, own_log)
    log_ref[...] = own_log
    scale = jnp.exp(stats_ref[slot][0:1, :count] - log_all)
    weights = []
    for r in range(refs):
        place = slice(r * SHIFTS, (r + 1) * SHIFTS)
        posterior = (odds_ref[place, :] * scale).astype(bf16)
        posterior_ref[place, :] = posterior
        weights.append(jnp.sum(posterior.astype(f32), axis=0, keepdims=True))
    weights = jnp.concatenate(weights, axis=0)
    high = weights.astype(bf16)
    low = (weights - high.astype(f32)).astype(bf16)
    hot = label_table(packets_ref[:, 2 * F :]).astype(bf16)
    spread = jnp.dot(jnp.concatenate([high, low], axis=0), hot, preferred_element_type=f32)
    spread = spread[:refs] + spread[refs:]
    lane = lax.broadcasted_iota(jnp.int32, (refs, LANES), 1) // NCTF
    row = lax.broadcasted_iota(jnp.int32, (refs, LANES), 0) % own_refs
    spread = jnp.where(lane == row, spread, 0.0)
    shares = []
    for g in range(groups):
        share = jnp.sum(spread[g * own_refs : (g + 1) * own_refs], axis=0, keepdims=True)
        high = share.astype(bf16).astype(f32)
        before = jnp.zeros((2 * own_refs, LANES), f32)
        after = jnp.zeros((ROWS - 2 * own_refs - 2, LANES), f32)
        shares.append(jnp.concatenate([before, high, share - high, after], axis=0))

    def chunk(d):
        lanes = pl.ds(pl.multiple_of(d * LANES, LANES), LANES)
        wide = pl.ds(pl.multiple_of(d * 2 * LANES, 2 * LANES), 2 * LANES)
        cos, sin = cos_ref[:, lanes], sin_ref[:, lanes]
        weighted = packets_ref[:, wide]
        for g in range(groups):
            rows = []
            for first in range(0, own_refs, BATCH):
                place = (g * own_refs + first) * SHIFTS
                totals = jnp.dot(
                    posterior_ref[place : place + BATCH * SHIFTS, :],
                    weighted,
                    preferred_element_type=f32,
                )
                for i in range(BATCH):
                    real = totals[i * SHIFTS : (i + 1) * SHIFTS, :LANES]
                    imag = totals[i * SHIFTS : (i + 1) * SHIFTS, LANES:]
                    rows.append(fold(real * cos + imag * sin))
                    rows.append(fold(imag * cos - real * sin))
            blank = [jnp.zeros((8, LANES), f32)] * (ROWS - len(rows))
            rows = rows + blank
            sums = jnp.concatenate([row_sums(rows[:8]), row_sums(rows[8:])], axis=0)
            line = peer_line(2 * g + d % 2, d // 2, 2 * groups, CHUNKS // 2)
            sums = (sums + shares[g]).astype(bf16)
            for i in range(own_refs + 1):
                parts_ref[line, i] = sums[2 * i : 2 * i + 2]

    def chunks(k, carry):
        for j in range(UNROLL):
            chunk(k * UNROLL + j)
        return carry

    lax.fori_loop(0, CHUNKS // UNROLL, chunks, 0)


def back_project(slot, odds, stats, packets, cos_table, sin_table, own_refs, rows):
    count = packets.shape[0]
    groups = odds.shape[0] // SHIFTS // own_refs
    return pl.pallas_call(
        functools.partial(back_kernel, own_refs),
        out_shape=(
            jax.ShapeDtypeStruct((groups * CHUNKS, own_refs + 1, 2, LANES), bf16),
            jax.ShapeDtypeStruct((1, rows), f32),
        ),
        in_specs=[pl.BlockSpec(memory_space=pltpu.SMEM)] + [whole_vmem] * 5,
        out_specs=(whole_vmem, whole_vmem),
        scratch_shapes=[pltpu.VMEM((odds.shape[0], count), bf16)],
        compiler_params=room(24),
        name="back",
    )(slot, odds, stats, packets, cos_table, sin_table)


def finish_kernel(place_ref, parts_ref, transfer_ref, out_ref):
    own_refs = out_ref.shape[0]
    sums = jnp.sum(parts_ref[...].astype(f32), axis=0)
    share = jnp.sum(sums[own_refs], axis=0, keepdims=True)
    lane = lax.broadcasted_iota(jnp.int32, (own_refs, LANES), 1) // NCTF
    row = lax.broadcasted_iota(jnp.int32, (own_refs, LANES), 0)
    shares = jnp.where(lane == row, share, 0.0)
    own = transfer_ref[:, pl.ds(pl.multiple_of(place_ref[0] * LANES, LANES), LANES)]
    squared = jnp.concatenate([own * own] * (LANES // NCTF), axis=0)
    denominator = jnp.dot(shares, squared, precision=highest) + ridge_term
    for i in range(own_refs):
        out_ref[i] = sums[i] / denominator[i : i + 1]


def finish(place, parts, transfer, own_refs):
    return pl.pallas_call(
        finish_kernel,
        out_shape=jax.ShapeDtypeStruct((own_refs, 2, LANES), f32),
        in_specs=[pl.BlockSpec(memory_space=pltpu.SMEM)] + [whole_vmem] * 2,
        out_specs=whole_vmem,
        compiler_params=room(4),
        name="finish",
    )(place, parts, transfer)


def shifted(value, axis, steps):
    count = lax.axis_size(axis)
    pairs = [(source, (source + steps) % count) for source in range(count)]
    return lax.ppermute(value, axis, pairs)


def parted(value, steps):
    count = lax.axis_size("x")
    pairs = []
    for source in range(count):
        pairs.append((2 * source, 2 * ((source - steps) % count)))
        pairs.append((2 * source + 1, 2 * ((source + steps) % count) + 1))
    return lax.ppermute(value, ("x", "core"), pairs)


def peer_line(row, plane, rows, planes):
    return (planes - 1 - plane) * rows + (row + rows // 2) % rows


def slant_line(side, row, plane, count):
    column = (plane + 1) % count
    step = count + side * column - (1 - side) * column
    return count * ((row + count // 2 + step) % count) + column


def slanted_exchange(value):
    yh, dom = lax.axis_size("yh"), lax.axis_size("dom")
    groups = []
    for side in range(2):
        order = [0] * (yh * dom)
        for y in range(yh):
            for d in range(dom):
                line = slant_line(side, 2 * y + d % 2, d // 2, dom // 2)
                order[line] = (side * yh + y) * dom + d
        groups.append(order)
    return lax.all_to_all(value, ("core", "yh", "dom"), 0, 0, axis_index_groups=groups)


def wide_exchange(value):
    yh, dom = lax.axis_size("yh"), lax.axis_size("dom")
    order = [0] * (yh * dom)
    for y in range(yh):
        for d in range(dom):
            order[peer_line(2 * y + d % 2, d // 2, 2 * yh, dom // 2)] = y * dom + d
    return lax.all_to_all(value, ("yh", "dom"), 0, 0, axis_index_groups=[order])


def body(particles, classes, template_spectra, transfer_magnitude, offsets):
    rows = particles.shape[0]
    own_refs = template_spectra.shape[0]
    near_axes = ("core", "x")
    near, far = lax.axis_size(near_axes), lax.axis_size(("yh", "dom"))
    packet, copies = prep(classes, particles, transfer_magnitude, template_spectra, far)
    spectra = slanted_exchange(copies)
    place, side, part = [lax.axis_index(name)[None] for name in ("x", "core", "dom")]
    slot = lax.axis_index(near_axes)[None]
    second, first, third = parted(packet, 2), parted(packet, 1), parted(packet, 3)
    own = arrange(place, side, part, slot, [packet, first, second, third])
    other = shifted(own, "core", 1)
    cos_table, sin_table = phase_tables(offsets)
    odds, stats, weighted = make_scores(
        side, spectra, cos_table, sin_table, own, other, transfer_magnitude, own_refs, near
    )
    stats = lax.all_to_all(stats, near_axes, 0, 0)
    parts, log_own = back_project(
        slot, odds, stats, weighted, cos_table, sin_table, own_refs, rows
    )
    parts = wide_exchange(parts)
    new_refs = finish(part, parts, transfer_magnitude, own_refs)
    return (log_own.reshape(rows), new_refs)


def solution(mesh):
    devices = mesh.devices
    names = ("yh", "x", "core", "dom")
    inner = Mesh(devices.reshape(4, 4, 2, devices.shape[1]), names)
    refs = names[:3]
    return jax.shard_map(
        body,
        mesh=inner,
        in_specs=(P(names, None, None), P(names), P(refs, None, "dom"), P(), P()),
        out_specs=(P(names), P(refs, None, "dom")),
        check_vma=False,
    )
```

```python
import functools
import math

import jax
import jax.numpy as jnp
from jax import lax
from jax.experimental import pallas as pl
from jax.experimental.pallas import tpu as pltpu
from jax.sharding import Mesh
from jax.sharding import PartitionSpec as P

BOX = 64
F = 2048
SHIFTS = 64
NCTF = 16
LANES = 128
CHUNKS = F // LANES
ROWS = 16
UNIT = 4
UNROLL = 16
BATCH = 2
WIDE = 6

highest = lax.Precision.HIGHEST
ridge_term = 1.0
f32 = jnp.float32
bf16 = jnp.bfloat16
whole_vmem = pl.BlockSpec(memory_space=pltpu.VMEM)


def room(mib):
    return pltpu.CompilerParams(vmem_limit_bytes=mib * 1024 * 1024)


def phase_tables(offsets):
    half_side = BOX // 2
    positions = jnp.arange(F, dtype=jnp.int32)
    row_index = positions // half_side
    freq_x = jnp.where(row_index < half_side, row_index, row_index - BOX)
    freq_y = positions % half_side
    turn_count = (offsets[:, 0:1] * freq_x[None, :] + offsets[:, 1:2] * freq_y[None, :]) % BOX
    angles = turn_count.astype(f32) * (2.0 * math.pi / BOX)
    return (jnp.cos(angles), jnp.sin(angles))


def prep_kernel(classes_ref, particles_ref, transfer_ref, spectra_ref, packet_ref, copies_ref):
    rows = particles_ref.shape[0]
    copies_ref[...] = jnp.broadcast_to(spectra_ref[...][None], copies_ref.shape)
    place = lax.broadcasted_iota(jnp.int32, (rows, 1), 0)
    labels = jnp.zeros((rows, 1), jnp.int32)
    for i in range(rows):
        labels = jnp.where(place == i, classes_ref[i], labels)
    contrast = jnp.zeros((rows, F), f32)
    for c in range(NCTF):
        contrast = jnp.where(labels == c, transfer_ref[c : c + 1, :], contrast)
    values = particles_ref[...].astype(f32)
    real = (values[:, 0, :] * contrast).astype(bf16)
    imag = (values[:, 1, :] * contrast).astype(bf16)
    for d in range(CHUNKS):
        lanes = slice(d * LANES, (d + 1) * LANES)
        packet_ref[:, 2 * d * LANES : (2 * d + 1) * LANES] = real[:, lanes]
        packet_ref[:, (2 * d + 1) * LANES : (2 * d + 2) * LANES] = imag[:, lanes]
    tags = jnp.broadcast_to(labels.astype(f32), (rows, LANES))
    packet_ref[:, 2 * F :] = tags.astype(bf16)


def prep(classes, particles, transfer, spectra, far):
    rows = particles.shape[0]
    return pl.pallas_call(
        prep_kernel,
        out_shape=(
            jax.ShapeDtypeStruct((rows, 2 * F + LANES), bf16),
            jax.ShapeDtypeStruct((far,) + spectra.shape, bf16),
        ),
        in_specs=[pl.BlockSpec(memory_space=pltpu.SMEM)] + [whole_vmem] * 3,
        out_specs=(whole_vmem, whole_vmem),
        compiler_params=room(60),
        name="prep",
    )(classes, particles, transfer, spectra)


def arrange_kernel(place_ref, side_ref, part_ref, slot_ref, *refs):
    count = len(refs) - 1
    for k in range(count):
        step = jnp.where(side_ref[0] == 0, k, count - k)
        refs[count][lax.rem(place_ref[0] + step, count)] = refs[k][...]


def arrange(place, side, part, slot, packets):
    rows, width = packets[0].shape
    ordered = pl.pallas_call(
        arrange_kernel,
        out_shape=jax.ShapeDtypeStruct((len(packets), rows, width), bf16),
        in_specs=[pl.BlockSpec(memory_space=pltpu.SMEM)] * 4 + [whole_vmem] * len(packets),
        out_specs=whole_vmem,
        compiler_params=room(4),
        name="arrange",
    )(place, side, part, slot, *packets)
    return ordered.reshape(len(packets) * rows, width)


def fold(values):
    return jnp.sum(values.reshape(values.shape[0] // 8, 8, values.shape[1]), axis=0)


def row_sums(tiles):
    row = lax.broadcasted_iota(jnp.int32, tiles[0].shape, 0)
    for bit in (1, 2, 4):
        even = (row // bit) % 2 == 0
        merged = []
        for a, b in zip(tiles[::2], tiles[1::2]):
            merged.append(
                jnp.where(even, a, b) + pltpu.roll(jnp.where(even, b, a), 8 - bit, 0)
            )
        tiles = merged
    return tiles[0]


def label_table(tags):
    lane = lax.broadcasted_iota(jnp.int32, tags.shape, 1) % NCTF
    return (tags.astype(f32) == lane.astype(f32)).astype(f32)


def score_kernel(
    own_refs,
    side_ref,
    spectra_ref,
    cos_ref,
    sin_ref,
    own_ref,
    other_ref,
    transfer_ref,
    odds_ref,
    stats_ref,
    weighted_ref,
    penalty_ref,
):
    groups = spectra_ref.shape[0] // CHUNKS
    refs = groups * own_refs
    half = own_ref.shape[0]
    side = side_ref[0]

    own, other = own_ref[...], other_ref[...]
    weighted_ref[:half, :] = jnp.where(side == 0, own, other)
    weighted_ref[half:, :] = jnp.where(side == 0, other, own)
    odds_ref[...] = jnp.zeros_like(odds_ref)
    penalty_ref[...] = jnp.zeros_like(penalty_ref)
    width = 2 * UNIT * LANES

    def unit(u):
        wide = pl.ds(pl.multiple_of(u * width, width), width)
        weighted = weighted_ref[:, wide]
        tables = []
        for j in range(UNIT):
            lanes = pl.ds(pl.multiple_of((u * UNIT + j) * LANES, LANES), LANES)
            transfer = transfer_ref[:, lanes]
            tables.append((cos_ref[:, lanes], sin_ref[:, lanes], transfer * transfer))
        for g in range(groups):
            blocks = []
            for j in range(UNIT):
                d = u * UNIT + j
                line = slant_line(side, 2 * g + d % 2, d // 2, CHUNKS // 2)
                blocks.append(spectra_ref[line].astype(f32))
            for first in range(0, own_refs, WIDE):
                rows = []
                for i in range(first, first + WIDE):
                    pieces = []
                    power = 0.0
                    for j in range(UNIT):
                        cos, sin, squared = tables[j]
                        real, imag = blocks[j][i, 0:1], blocks[j][i, 1:2]
                        pieces.append((real * cos - imag * sin).astype(bf16))
                        pieces.append((real * sin + imag * cos).astype(bf16))
                        power = power + (real * real + imag * imag) * squared
                    place = (g * own_refs + i) * NCTF
                    penalty_ref[place : place + NCTF, :] += power
                    rows.append(jnp.concatenate(pieces, axis=1))
                place = (g * own_refs + first) * SHIFTS
                odds_ref[place : place + WIDE * SHIFTS, :] += lax.dot_general(
                    jnp.concatenate(rows, axis=0),
                    weighted,
                    (((1,), (1,)), ((), ())),
                    preferred_element_type=f32,
                )

    def units(k, carry):
        unit(2 * k)
        unit(2 * k + 1)
        return carry

    lax.fori_loop(0, CHUNKS // UNIT // 2, units, 0)
    tags = weighted_ref[:, 2 * F :].astype(f32).T[:NCTF]
    hot = (tags == lax.broadcasted_iota(jnp.int32, tags.shape, 0).astype(f32)).astype(f32)
    top = None
    for r in range(refs):
        charge = jnp.sum(penalty_ref[r * NCTF : (r + 1) * NCTF, :], axis=1, keepdims=True)
        cost = 0.5 * jnp.sum(charge * hot, axis=0, keepdims=True)
        place = slice(r * SHIFTS, (r + 1) * SHIFTS)
        scores = odds_ref[place, :] - cost
        odds_ref[place, :] = scores
        high = jnp.max(scores, axis=0, keepdims=True)
        top = high if top is None else jnp.maximum(top, high)
    odds = jnp.exp(odds_ref[...] - top)
    odds_ref[...] = odds
    total = jnp.sum(odds, axis=0, keepdims=True)
    stats = jnp.concatenate([top, total], axis=0)
    spare = jnp.zeros((2, LANES - stats.shape[1]), f32)
    stats = jnp.concatenate([stats, spare], axis=1)
    stats_ref[...] = jnp.broadcast_to(stats[None], stats_ref.shape)


def make_scores(side, spectra, cos_table, sin_table, own, other, transfer, own_refs, near):
    groups = spectra.shape[0] // CHUNKS
    refs = groups * own_refs
    count = 2 * own.shape[0]
    return pl.pallas_call(
        functools.partial(score_kernel, own_refs),
        out_shape=(
            jax.ShapeDtypeStruct((refs * SHIFTS, count), f32),
            jax.ShapeDtypeStruct((near, 2, LANES), f32),
            jax.ShapeDtypeStruct((count, own.shape[1]), bf16),
        ),
        in_specs=[pl.BlockSpec(memory_space=pltpu.SMEM)] + [whole_vmem] * 6,
        out_specs=(whole_vmem, whole_vmem, whole_vmem),
        scratch_shapes=[
            pltpu.VMEM((refs * NCTF, LANES), f32),
        ],
        compiler_params=room(24),
        name="scores",
    )(side, spectra, cos_table, sin_table, own, other, transfer)


def back_kernel(
    own_refs,
    slot_ref,
    odds_ref,
    stats_ref,
    packets_ref,
    cos_ref,
    sin_ref,
    parts_ref,
    log_ref,
    posterior_ref,
):
    groups = parts_ref.shape[0] // CHUNKS
    refs = groups * own_refs
    count = odds_ref.shape[1]
    slot = slot_ref[0]
    tops, sums = stats_ref[:, 0, :count], stats_ref[:, 1, :count]
    top = jnp.max(tops, axis=0, keepdims=True)
    total = jnp.sum(sums * jnp.exp(tops - top), axis=0, keepdims=True)
    log_all = top + jnp.log(total)
    own_rows = log_ref.shape[1]
    own_log = jnp.zeros_like(log_ref)
    for k in range(count // own_rows):
        piece = log_all[:, k * own_rows : (k + 1) * own_rows]
        own_log = jnp.where(slot == k, piece, own_log)
    log_ref[...] = own_log
    scale = jnp.exp(stats_ref[slot][0:1, :count] - log_all)
    weights = []
    for r in range(refs):
        place = slice(r * SHIFTS, (r + 1) * SHIFTS)
        posterior = (odds_ref[place, :] * scale).astype(bf16)
        posterior_ref[place, :] = posterior
        weights.append(jnp.sum(posterior.astype(f32), axis=0, keepdims=True))
    weights = jnp.concatenate(weights, axis=0)
    high = weights.astype(bf16)
    low = (weights - high.astype(f32)).astype(bf16)
    hot = label_table(packets_ref[:, 2 * F :]).astype(bf16)
    spread = jnp.dot(jnp.concatenate([high, low], axis=0), hot, preferred_element_type=f32)
    spread = spread[:refs] + spread[refs:]
    lane = lax.broadcasted_iota(jnp.int32, (refs, LANES), 1) // NCTF
    row = lax.broadcasted_iota(jnp.int32, (refs, LANES), 0) % own_refs
    spread = jnp.where(lane == row, spread, 0.0)
    shares = []
    for g in range(groups):
        share = jnp.sum(spread[g * own_refs : (g + 1) * own_refs], axis=0, keepdims=True)
        high = share.astype(bf16).astype(f32)
        before = jnp.zeros((2 * own_refs, LANES), f32)
        after = jnp.zeros((ROWS - 2 * own_refs - 2, LANES), f32)
        shares.append(jnp.concatenate([before, high, share - high, after], axis=0))

    def chunk(d):
        lanes = pl.ds(pl.multiple_of(d * LANES, LANES), LANES)
        wide = pl.ds(pl.multiple_of(d * 2 * LANES, 2 * LANES), 2 * LANES)
        cos, sin = cos_ref[:, lanes], sin_ref[:, lanes]
        weighted = packets_ref[:, wide]
        for g in range(groups):
            rows = []
            for first in range(0, own_refs, BATCH):
                place = (g * own_refs + first) * SHIFTS
                totals = jnp.dot(
                    posterior_ref[place : place + BATCH * SHIFTS, :],
                    weighted,
                    preferred_element_type=f32,
                )
                for i in range(BATCH):
                    real = totals[i * SHIFTS : (i + 1) * SHIFTS, :LANES]
                    imag = totals[i * SHIFTS : (i + 1) * SHIFTS, LANES:]
                    rows.append(fold(real * cos + imag * sin))
                    rows.append(fold(imag * cos - real * sin))
            blank = [jnp.zeros((8, LANES), f32)] * (ROWS - len(rows))
            rows = rows + blank
            sums = jnp.concatenate([row_sums(rows[:8]), row_sums(rows[8:])], axis=0)
            line = peer_line(2 * g + d % 2, d // 2, 2 * groups, CHUNKS // 2)
            parts_ref[line] = (sums + shares[g]).astype(bf16)

    def chunks(k, carry):
        for j in range(UNROLL):
            chunk(k * UNROLL + j)
        return carry

    lax.fori_loop(0, CHUNKS // UNROLL, chunks, 0)


def back_project(slot, odds, stats, packets, cos_table, sin_table, own_refs, rows):
    count = packets.shape[0]
    groups = odds.shape[0] // SHIFTS // own_refs
    return pl.pallas_call(
        functools.partial(back_kernel, own_refs),
        out_shape=(
            jax.ShapeDtypeStruct((groups * CHUNKS, ROWS, LANES), bf16),
            jax.ShapeDtypeStruct((1, rows), f32),
        ),
        in_specs=[pl.BlockSpec(memory_space=pltpu.SMEM)] + [whole_vmem] * 5,
        out_specs=(whole_vmem, whole_vmem),
        scratch_shapes=[pltpu.VMEM((odds.shape[0], count), bf16)],
        compiler_params=room(24),
        name="back",
    )(slot, odds, stats, packets, cos_table, sin_table)


def finish_kernel(place_ref, parts_ref, transfer_ref, out_ref):
    own_refs = out_ref.shape[0]
    sums = jnp.sum(parts_ref[...].astype(f32), axis=0)
    share = sums[2 * own_refs : 2 * own_refs + 1] + sums[2 * own_refs + 1 : 2 * own_refs + 2]
    lane = lax.broadcasted_iota(jnp.int32, (own_refs, LANES), 1) // NCTF
    row = lax.broadcasted_iota(jnp.int32, (own_refs, LANES), 0)
    shares = jnp.where(lane == row, share, 0.0)
    own = transfer_ref[:, pl.ds(pl.multiple_of(place_ref[0] * LANES, LANES), LANES)]
    squared = jnp.concatenate([own * own] * (LANES // NCTF), axis=0)
    denominator = jnp.dot(shares, squared, precision=highest) + ridge_term
    for i in range(own_refs):
        out_ref[i] = sums[2 * i : 2 * i + 2] / denominator[i : i + 1]


def finish(place, parts, transfer, own_refs):
    return pl.pallas_call(
        finish_kernel,
        out_shape=jax.ShapeDtypeStruct((own_refs, 2, LANES), f32),
        in_specs=[pl.BlockSpec(memory_space=pltpu.SMEM)] + [whole_vmem] * 2,
        out_specs=whole_vmem,
        compiler_params=room(4),
        name="finish",
    )(place, parts, transfer)


def shifted(value, axis, steps):
    count = lax.axis_size(axis)
    pairs = [(source, (source + steps) % count) for source in range(count)]
    return lax.ppermute(value, axis, pairs)


def parted(value, steps):
    count = lax.axis_size("x")
    pairs = []
    for source in range(count):
        pairs.append((2 * source, 2 * ((source - steps) % count)))
        pairs.append((2 * source + 1, 2 * ((source + steps) % count) + 1))
    return lax.ppermute(value, ("x", "core"), pairs)


def peer_line(row, plane, rows, planes):
    return (planes - 1 - plane) * rows + (row + rows // 2) % rows


def slant_line(side, row, plane, count):
    column = (plane + 1) % count
    step = count + side * column - (1 - side) * column
    return count * ((row + count // 2 + step) % count) + column


def slanted_exchange(value):
    yh, dom = lax.axis_size("yh"), lax.axis_size("dom")
    groups = []
    for side in range(2):
        order = [0] * (yh * dom)
        for y in range(yh):
            for d in range(dom):
                line = slant_line(side, 2 * y + d % 2, d // 2, dom // 2)
                order[line] = (side * yh + y) * dom + d
        groups.append(order)
    return lax.all_to_all(value, ("core", "yh", "dom"), 0, 0, axis_index_groups=groups)


def wide_exchange(value):
    yh, dom = lax.axis_size("yh"), lax.axis_size("dom")
    order = [0] * (yh * dom)
    for y in range(yh):
        for d in range(dom):
            order[peer_line(2 * y + d % 2, d // 2, 2 * yh, dom // 2)] = y * dom + d
    return lax.all_to_all(value, ("yh", "dom"), 0, 0, axis_index_groups=[order])


def body(particles, classes, template_spectra, transfer_magnitude, offsets):
    rows = particles.shape[0]
    own_refs = template_spectra.shape[0]
    near_axes = ("core", "x")
    near, far = lax.axis_size(near_axes), lax.axis_size(("yh", "dom"))
    packet, copies = prep(classes, particles, transfer_magnitude, template_spectra, far)
    spectra = slanted_exchange(copies)
    place, side, part = [lax.axis_index(name)[None] for name in ("x", "core", "dom")]
    slot = lax.axis_index(near_axes)[None]
    second, first, third = parted(packet, 2), parted(packet, 1), parted(packet, 3)
    own = arrange(place, side, part, slot, [packet, first, second, third])
    other = shifted(own, "core", 1)
    cos_table, sin_table = phase_tables(offsets)
    odds, stats, weighted = make_scores(
        side, spectra, cos_table, sin_table, own, other, transfer_magnitude, own_refs, near
    )
    stats = lax.all_to_all(stats, near_axes, 0, 0)
    parts, log_own = back_project(
        slot, odds, stats, weighted, cos_table, sin_table, own_refs, rows
    )
    parts = wide_exchange(parts)
    new_refs = finish(part, parts, transfer_magnitude, own_refs)
    return (log_own.reshape(rows), new_refs)


def solution(mesh):
    devices = mesh.devices
    names = ("yh", "x", "core", "dom")
    inner = Mesh(devices.reshape(4, 4, 2, devices.shape[1]), names)
    refs = names[:3]
    return jax.shard_map(
        body,
        mesh=inner,
        in_specs=(P(names, None, None), P(names), P(refs, None, "dom"), P(), P()),
        out_specs=(P(names), P(refs, None, "dom")),
        check_vma=False,
    )
```
